32 devices in a mesh: dp: 4 (over y, x), mp: 8 (over z, core).
Axes of the slice: x: 2, y: 2, z: 4, core: 2. Of those that a mesh axis runs over, the one named last changes fastest.
Arguments:
- token_ids: int32 [8192], P('dp'), may hold values from 0 to 50256
- targets: int32 [8192], P('dp'), may hold values from 0 to 50256
- starts: int32 [8192], P('dp'), may hold values from 0 to 1023, as said below
- sources: int32 [8192], P('dp'), may hold values from 0 to 3, as said below
- embedding: float32 [50304, 1024], P('mp', 'dp')
- w_qkv: float32 [1024, 3072], P('dp', 'mp'), may hold values from -0.1875 to 0.1875
- w_out: float32 [1024, 1024], P('mp', 'dp'), may hold values from -0.5 to 0.5
- w_fc: float32 [1024, 4096], P('dp', 'mp'), may hold values from -0.1875 to 0.1875
- w_proj: float32 [4096, 1024], P('mp', 'dp'), may hold values from -0.09375 to 0.09375
- norm_params: float32 [6, 1024], replicated
- rows_table: float32 [50304], P('mp'), may hold values from 1.4901161e-09 to 5.9604646e-09
- cols_table: float32 [1024], P('dp'), may hold values from 1.4901161e-09 to 5.9604646e-09
- rows_qkv: float32 [1024], P('dp'), may hold values from 4.7683717e-08 to 1.9073487e-07
- cols_qkv: float32 [3072], P('mp'), may hold values from 4.7683717e-08 to 1.9073487e-07
- rows_out: float32 [1024], P('mp'), may hold values from 4.7683717e-08 to 1.9073487e-07
- cols_out: float32 [1024], P('dp'), may hold values from 4.7683717e-08 to 1.9073487e-07
- rows_fc: float32 [1024], P('dp'), may hold values from 4.7683717e-08 to 1.9073487e-07
- cols_fc: float32 [4096], P('mp'), may hold values from 4.7683717e-08 to 1.9073487e-07
- rows_proj: float32 [4096], P('mp'), may hold values from 4.7683717e-08 to 1.9073487e-07
- cols_proj: float32 [1024], P('dp'), may hold values from 4.7683717e-08 to 1.9073487e-07
- second_norms: float32 [6, 1024], replicated, may hold values from 4.7683717e-08 to 1.9073487e-07
Outputs:
- loss_sums: float32 [4], replicated
- counts: float32 [4], replicated
- grad_table: float32 [50304, 1024], P('mp', 'dp')
- rows_table_new: float32 [50304], P('mp')
- cols_table_new: float32 [1024], P('dp')
- table_new: float32 [50304, 1024], P('mp', 'dp')
- grad_qkv: float32 [1024, 3072], P('dp', 'mp')
- rows_qkv_new: float32 [1024], P('dp')
- cols_qkv_new: float32 [3072], P('mp')
- qkv_new: float32 [1024, 3072], P('dp', 'mp')
- grad_out: float32 [1024, 1024], P('mp', 'dp')
- rows_out_new: float32 [1024], P('mp')
- cols_out_new: float32 [1024], P('dp')
- out_new: float32 [1024, 1024], P('mp', 'dp')
- grad_fc: float32 [1024, 4096], P('dp', 'mp')
- rows_fc_new: float32 [1024], P('dp')
- cols_fc_new: float32 [4096], P('mp')
- fc_new: float32 [1024, 4096], P('dp', 'mp')
- grad_proj: float32 [4096, 1024], P('mp', 'dp')
- rows_proj_new: float32 [4096], P('mp')
- cols_proj_new: float32 [1024], P('dp')
- proj_new: float32 [4096, 1024], P('mp', 'dp')
- grad_norms: float32 [6, 1024], replicated
- second_norms_new: float32 [6, 1024], replicated
- norms_new: float32 [6, 1024], replicated
The draws below stay inside these ranges and needn't reach their ends.
Inputs may be any that keep to these rules, and one draw needn't show every extreme that they name: starts[t] is the position within its sequence of 1024 tokens of the first token of t's document: at most t's own position, never falling along a sequence, and 0 at the first token of every sequence. One of the sources 1 to 2, which one drawn from the seed, has no token in the step.
All inputs are finite; a program needn't handle non-finite values.
Results may differ from the reference program's by a relative error of at most 0.015.
Values may be sent and summed in bfloat16 or wider, within the bound.
A program may use at most 256 MiB of HBM per device.

```python
import math
import jax
import jax.numpy as jnp
import numpy as np
from jax import lax

D = 1024
H = 16
HD = 64
FF = 4096
V = 50304
VREAL = 50257
LEN = 1024
NSRC = 4
STEP = 10
SEQS = 8
TOKENS = 8192
N_MP = 8


def draw_starts(key, part):
    key = jax.random.fold_in(key, 1)
    marks = jax.random.randint(key, (SEQS, LEN), 0, LEN)
    chosen = jax.random.randint(jax.random.fold_in(key, 7), (), 0, SEQS)
    place = jnp.arange(LEN, dtype=jnp.int32)[None, :]
    row = jnp.arange(SEQS, dtype=jnp.int32)[:, None]
    begins = (marks < 8) | (place == 0) | (place == LEN - 1) & (row == chosen)
    found = lax.cummax(jnp.where(begins, place, 0), axis=1)
    return found.reshape(TOKENS).astype(jnp.int32)


def draw_sources(key, part):
    key = jax.random.fold_in(key, 4)
    missing = jax.random.randint(jax.random.fold_in(key, 11), (), 1, NSRC - 1)
    place = jnp.arange(TOKENS, dtype=jnp.int32)
    level = jax.random.randint(jax.random.fold_in(key, 13), (TOKENS,), 0, 1000)
    rising = 150 + 600 * place // TOKENS
    middle = jax.random.randint(jax.random.fold_in(key, 17), (TOKENS,), 1, NSRC - 1)
    middle = jnp.where(middle == missing, jnp.where(missing == 1, NSRC - 2, 1), middle)
    other = jax.random.randint(jax.random.fold_in(key, 19), (TOKENS,), 0, 2)
    rest = jnp.where(other == 0, 0, middle)
    rest = jnp.where((NSRC == 3) & (other == 1), 0, rest)
    drawn = jnp.where(level < rising, NSRC - 1, rest)
    drawn = jnp.where(place == 0, 0, jnp.where(place == TOKENS - 1, NSRC - 1, drawn))
    return drawn.astype(jnp.int32)


def draw_embedding(key, part):
    key = jax.random.fold_in(key, 2)
    position = jnp.arange(V, dtype=jnp.float32)[:, None] / V
    base = jax.random.normal(key, (V, D), jnp.float32)
    rising = 1.0 + 2.0 * position
    return (base * rising * D ** (-0.5)).astype(jnp.float32)


def draw_norm_params(key, part):
    key = jax.random.fold_in(key, 3)
    width = jnp.arange(D, dtype=jnp.float32)[None, :] / D
    noise = jax.random.normal(key, (6, D), jnp.float32)
    gains = (0.6 + 0.9 * width) * (1.0 + 0.15 * noise)
    shifts = 0.3 * noise
    picks = (jnp.arange(6) % 2 == 0)[:, None]
    return jnp.where(picks, gains, shifts).astype(jnp.float32)


def place_ends(values, own_key, low, largest):
    spot = [jax.random.randint(jax.random.fold_in(own_key, axis), (), 0, length) for axis, length in enumerate(values.shape)]
    longest = values.shape.index(max(values.shape))
    neighbour = spot[:longest] + [(spot[longest] + 1) % values.shape[longest]] + spot[longest + 1:]
    return values.at[tuple(spot)].set(low).at[tuple(neighbour)].set(largest)


def block_levels(key, dims, cuts, low, top_value):
    level = 1.0
    for dim, blocks in cuts:
        heights = jax.random.uniform(jax.random.fold_in(jax.random.fold_in(key, 6), dim), (blocks,), jnp.float32, low / len(cuts), top_value / len(cuts))
        level = level * jnp.repeat(jnp.exp(heights), dims[dim] // blocks).reshape((-1,) + (1,) * (len(dims) - 1 - dim))
    return level


def cumulative_ranks(number_of, slope):
    weights = [(1 << 20) // math.isqrt(rank ** slope) + 1 for rank in range(1, number_of + 1)]
    deviation = 1 + sum(weights) // (1 << 30)
    return np.cumsum(np.array([max(1, weight // deviation) for weight in weights]))


def ranked(key, shape, count, slope):
    listing = cumulative_ranks(count, slope)
    lot = jax.random.randint(jax.random.fold_in(key, 1), shape, 0, int(listing[count - 1]))
    rank = jnp.searchsorted(jnp.asarray(listing, jnp.int32), lot, side="right")
    return jax.random.permutation(jax.random.fold_in(key, 2), count)[rank].astype(jnp.int32)


def scatter_about(rng, shape, deviation, limit, pieces=(), kind=jnp.bfloat16):
    values = deviation * jax.random.normal(rng, shape, jnp.float32)
    if pieces:
        values = values * block_levels(rng, shape, pieces, -0.22, 0.18)
    return jnp.clip(values, -limit, limit).astype(kind)


def setup_inputs(seed: int = 0) -> dict:
    splits = jax.random.split(jax.random.key(seed), 22)
    return {
        "token_ids": place_ends(ranked(splits[0], (TOKENS,), VREAL, 2), jax.random.fold_in(splits[0], 3), 0, VREAL - 1).astype(jnp.int32),
        "targets": place_ends(ranked(splits[1], (TOKENS,), VREAL, 2), jax.random.fold_in(splits[1], 3), 0, VREAL - 1).astype(jnp.int32),
        "starts": draw_starts(jax.random.fold_in(splits[21], 71), 0),
        "sources": draw_sources(jax.random.fold_in(splits[21], 71), 0),
        "embedding": draw_embedding(jax.random.fold_in(splits[21], 71), 0),
        "w_qkv": scatter_about(splits[5], (D, 3 * D), D ** -0.5, 0.1875, ((0, 4), (1, 8)), jnp.float32),
        "w_out": scatter_about(splits[6], (D, D), (D // 8) ** -0.5, 0.5, ((0, 8), (1, 4)), jnp.float32),
        "w_fc": scatter_about(splits[7], (D, FF), D ** -0.5, 0.1875, ((0, 4), (1, 8)), jnp.float32),
        "w_proj": scatter_about(splits[8], (FF, D), FF ** -0.5, 0.09375, ((0, 8), (1, 4)), jnp.float32),
        "norm_params": draw_norm_params(jax.random.fold_in(splits[21], 71), 0),
        "rows_table": jnp.clip(jnp.exp(math.log(5.9604645663569045e-09) - 1.3862944 * jax.random.uniform(splits[10], (V,), jnp.float32) ** block_levels(splits[10], (V,), ((0, 8),), -0.2, 0.2)), 1.4901161415892261e-09, 5.9604645663569045e-09),
        "cols_table": jnp.clip(jnp.exp(math.log(5.9604645663569045e-09) - 1.3862944 * jax.random.uniform(splits[11], (D,), jnp.float32) ** block_levels(splits[11], (D,), ((0, 4),), -0.2, 0.2)), 1.4901161415892261e-09, 5.9604645663569045e-09),
        "rows_qkv": jnp.clip(jnp.exp(math.log(1.9073486612342094e-07) - 1.3862944 * jax.random.uniform(splits[12], (D,), jnp.float32) ** block_levels(splits[12], (D,), ((0, 4),), -0.2, 0.2)), 4.7683716530855236e-08, 1.9073486612342094e-07),
        "cols_qkv": jnp.clip(jnp.exp(math.log(1.9073486612342094e-07) - 1.3862944 * jax.random.uniform(splits[13], (3 * D,), jnp.float32) ** block_levels(splits[13], (3 * D,), ((0, 8),), -0.2, 0.2)), 4.7683716530855236e-08, 1.9073486612342094e-07),
        "rows_out": jnp.clip(jnp.exp(math.log(1.9073486612342094e-07) - 1.3862944 * jax.random.uniform(splits[14], (D,), jnp.float32) ** block_levels(splits[14], (D,), ((0, 8),), -0.2, 0.2)), 4.7683716530855236e-08, 1.9073486612342094e-07),
        "cols_out": jnp.clip(jnp.exp(math.log(1.9073486612342094e-07) - 1.3862944 * jax.random.uniform(splits[15], (D,), jnp.float32) ** block_levels(splits[15], (D,), ((0, 4),), -0.2, 0.2)), 4.7683716530855236e-08, 1.9073486612342094e-07),
        "rows_fc": jnp.clip(jnp.exp(math.log(1.9073486612342094e-07) - 1.3862944 * jax.random.uniform(splits[16], (D,), jnp.float32) ** block_levels(splits[16], (D,), ((0, 4),), -0.2, 0.2)), 4.7683716530855236e-08, 1.9073486612342094e-07),
        "cols_fc": jnp.clip(jnp.exp(math.log(1.9073486612342094e-07) - 1.3862944 * jax.random.uniform(splits[17], (FF,), jnp.float32) ** block_levels(splits[17], (FF,), ((0, 8),), -0.2, 0.2)), 4.7683716530855236e-08, 1.9073486612342094e-07),
        "rows_proj": jnp.clip(jnp.exp(math.log(1.9073486612342094e-07) - 1.3862944 * jax.random.uniform(splits[18], (FF,), jnp.float32) ** block_levels(splits[18], (FF,), ((0, 8),), -0.2, 0.2)), 4.7683716530855236e-08, 1.9073486612342094e-07),
        "cols_proj": jnp.clip(jnp.exp(math.log(1.9073486612342094e-07) - 1.3862944 * jax.random.uniform(splits[19], (D,), jnp.float32) ** block_levels(splits[19], (D,), ((0, 4),), -0.2, 0.2)), 4.7683716530855236e-08, 1.9073486612342094e-07),
        "second_norms": jnp.clip(jnp.exp(jax.random.uniform(splits[20], (6, D), jnp.float32, math.log(4.7683716530855236e-08), math.log(1.9073486612342094e-07))), 4.7683716530855236e-08, 1.9073486612342094e-07),
    }


EPS_NORM = 1e-05
EPS_ONE = 1e-30
CLIP = 1.0
RHO = 0.5
MASKED = -1e+30
HIGHEST = lax.Precision.HIGHEST

@jax.custom_vjp
def low(v):
    return lax.optimization_barrier(v.astype(jnp.bfloat16)).astype(jnp.float32)

@jax.custom_vjp
def low_back(v):
    return v

def low_keep(v):
    return (low(v), None)

def low_pass(kept, grad):
    return (grad,)

def back_keep(v):
    return (v, None)

def back_low(kept, grad):
    return (low(grad),)
low.defvjp(low_keep, low_pass)
low_back.defvjp(back_keep, back_low)

def matmul(left, right):
    return jnp.dot(left, right, precision=HIGHEST)

def layer_norm(values, gain, shift):
    centre = lax.optimization_barrier(jnp.mean(values, axis=-1, keepdims=True))
    centred = values - centre
    spread = lax.optimization_barrier(jnp.mean(centred * centred, axis=-1, keepdims=True))
    return centred * lax.rsqrt(spread + EPS_NORM) * gain + shift

def branch_total(inner, weight):
    count = inner.shape[0]
    width = inner.shape[1] // N_MP
    parts = jnp.einsum('tgf,gfd->gtd', inner.reshape(count, N_MP, width), weight.reshape(N_MP, width, weight.shape[1]), precision=HIGHEST)
    return low_back(lax.optimization_barrier(jnp.sum(low(parts), axis=0)))

def attend(mixed_seq, start_seq):
    query = mixed_seq[:, :, 0]
    keys = mixed_seq[:, :, 1]
    values = mixed_seq[:, :, 2]
    scores = jnp.einsum('qhe,khe->hqk', query, keys, precision=HIGHEST) * HD ** (-0.5)
    place = jnp.arange(LEN, dtype=jnp.int32)
    allowed = (place[None, :] <= place[:, None]) & (place[None, :] >= start_seq[:, None])
    scores = low_back(jnp.where(allowed[None], scores, MASKED))
    highest = lax.optimization_barrier(jnp.max(scores, axis=-1, keepdims=True))
    weights = jnp.exp(scores - highest)
    weights = low(weights / lax.optimization_barrier(jnp.sum(weights, axis=-1, keepdims=True)))
    return jnp.einsum('hqk,khe->qhe', weights, values, precision=HIGHEST)

def head_block(table, rows, wanted):
    logits = low_back(jnp.dot(rows, table.T, precision=HIGHEST))
    column = jnp.arange(V, dtype=jnp.int32)
    logits = jnp.where((column < VREAL)[None, :], logits, MASKED)
    highest = lax.optimization_barrier(jnp.max(logits, axis=-1, keepdims=True))
    log_total = jnp.log(lax.optimization_barrier(jnp.sum(jnp.exp(logits - highest), axis=-1))) + highest[:, 0]
    picked = lax.optimization_barrier(jnp.sum(jnp.where(column[None, :] == wanted[:, None], logits, 0.0), axis=-1))
    return log_total - picked

def forward(embedding, w_qkv, w_out, w_fc, w_proj, norm_params, token_ids, targets, starts, sources):
    table = low(embedding)
    stream = table[token_ids]
    inner = low(layer_norm(stream, norm_params[0], norm_params[1]))
    mixed = low_back(low(matmul(inner, low(w_qkv))))
    mixed = mixed.reshape(SEQS, LEN, H, 3, HD)
    attended = lax.map(lambda paired: jax.checkpoint(attend)(paired[0], paired[1]), (mixed, starts.reshape(SEQS, LEN)))
    attended = low_back(low(attended.reshape(TOKENS, D)))
    stream = stream + branch_total(attended, low(w_out))
    inner = low(layer_norm(stream, norm_params[2], norm_params[3]))
    hidden = low(jax.nn.gelu(low_back(matmul(inner, low(w_fc))), approximate=True))
    stream = stream + branch_total(hidden, low(w_proj))
    final = low(layer_norm(stream, norm_params[4], norm_params[5]))
    block = min(512, TOKENS)
    losses = lax.map(lambda paired: jax.checkpoint(head_block)(table, paired[0], paired[1]), (final.reshape(TOKENS // block, block, D), targets.reshape(TOKENS // block, block)))
    losses = losses.reshape(TOKENS)
    member = (sources[:, None] == jnp.arange(NSRC, dtype=jnp.int32)[None, :]).astype(jnp.float32)
    loss_sums = lax.optimization_barrier(jnp.sum(member * losses[:, None], axis=0))
    counts = lax.optimization_barrier(jnp.sum(member, axis=0))
    loss = jnp.sum(loss_sums / jnp.maximum(counts, 1.0)) / NSRC
    return (loss, (loss_sums, counts))

def factored(weight, gradient, rows_old, cols_old):
    beta = 1.0 - STEP ** (-0.8)
    squares = gradient * gradient + EPS_ONE
    rows_new = beta * rows_old + (1.0 - beta) * lax.optimization_barrier(jnp.mean(squares, axis=1))
    cols_new = beta * cols_old + (1.0 - beta) * lax.optimization_barrier(jnp.mean(squares, axis=0))
    approx = rows_new[:, None] * cols_new[None, :] / jnp.mean(rows_new)
    steps = gradient * lax.rsqrt(approx)
    steps = steps / jnp.maximum(1.0, jnp.sqrt(jnp.mean(steps * steps)) / CLIP)
    rate = RHO * jnp.sqrt(jnp.mean(weight * weight))
    return (rows_new, cols_new, weight - rate * steps)

def reference(token_ids, targets, starts, sources, embedding, w_qkv, w_out, w_fc, w_proj, norm_params, rows_table, cols_table, rows_qkv, cols_qkv, rows_out, cols_out, rows_fc, cols_fc, rows_proj, cols_proj, second_norms):

    def loss_of(emb_arg, qkv_arg, out_arg, fc_arg, proj_arg, norm_arg):
        return forward(emb_arg, qkv_arg, out_arg, fc_arg, proj_arg, norm_arg, token_ids, targets, starts, sources)
    loss, pullback, aux = jax.vjp(loss_of, embedding, w_qkv, w_out, w_fc, w_proj, norm_params, has_aux=True)
    loss_sums, counts = aux
    g_table, g_qkv, g_out, g_fc, g_proj, g_norms = pullback(jnp.ones((), jnp.float32))
    r_table, c_table, n_table = factored(embedding, g_table, rows_table, cols_table)
    r_qkv, c_qkv, n_qkv = factored(w_qkv, g_qkv, rows_qkv, cols_qkv)
    r_out, c_out, n_out = factored(w_out, g_out, rows_out, cols_out)
    r_fc, c_fc, n_fc = factored(w_fc, g_fc, rows_fc, cols_fc)
    r_proj, c_proj, n_proj = factored(w_proj, g_proj, rows_proj, cols_proj)
    beta = 1.0 - STEP ** (-0.8)
    second_new = beta * second_norms + (1.0 - beta) * (g_norms * g_norms + EPS_ONE)
    steps = g_norms * lax.rsqrt(second_new)
    steps = steps / jnp.maximum(1.0, jnp.sqrt(jnp.mean(steps * steps)) / CLIP)
    norms_new = norm_params - RHO * jnp.sqrt(jnp.mean(norm_params * norm_params)) * steps
    return (loss_sums, counts, g_table, r_table, c_table, n_table, g_qkv, r_qkv, c_qkv, n_qkv, g_out, r_out, c_out, n_out, g_fc, r_fc, c_fc, n_fc, g_proj, r_proj, c_proj, n_proj, g_norms, second_new, norms_new)
```

```python
import functools
import math

import jax
import jax.numpy as jnp
from jax import lax
from jax.experimental import pallas as pl
from jax.experimental.pallas import tpu as pltpu
from jax.sharding import PartitionSpec as P

HD = 64
VREAL = 50257
LEN = 1024
NSRC = 4
STEP = 10


EPS_NORM = 1e-05
EPS_ONE = 1e-30
CLIP = 1.0
RHO = 0.5
MASKED = -1e30
MESH = pl.DeviceIdType.MESH
VMEM_CAP = 56 * 2**20


def row_slice(values, start, count):
    return lax.dynamic_slice_in_dim(values, start, count, 0)


def line_kernel(nr, ng, chunks, rows, width, n_in, n_out, step, *refs):
    part = refs[0] if nr else None
    first = 1 if nr else 0
    ins = refs[first : first + n_in]
    refs = refs[first + n_in :]
    if ng:
        whole, refs = refs[0], refs[1:]
    outs = refs[:n_out]
    scratch = refs[n_out:]
    dp = lax.axis_index("dp")
    mp = lax.axis_index("mp")
    z = mp // 2
    core = lax.rem(mp, 2)
    other = mp + 1 - 2 * core
    piece = rows // chunks
    most = max(nr, ng)
    zb = lax.rem(z, most)
    if nr:
        zr = lax.rem(z, nr)
        last_r = nr - 1
    if ng:
        zg = lax.rem(z, ng)
        last_g = ng - 1

    barrier = pltpu.get_barrier_semaphore()
    pl.semaphore_signal(barrier, inc=1, device_id=(dp, other), device_id_type=MESH)

    @pl.when(zb > 0)
    def _():
        pl.semaphore_signal(barrier, inc=1, device_id=(dp, mp - 2), device_id_type=MESH)

    @pl.when(zb < most - 1)
    def _():
        pl.semaphore_signal(barrier, inc=1, device_id=(dp, mp + 2), device_id_type=MESH)

    greeted = 1 + (zb > 0).astype(jnp.int32) + (zb < most - 1).astype(jnp.int32)
    pl.semaphore_wait(barrier, greeted)

    if nr:
        half, from_left, from_right, going = scratch[:4]
        half_send, half_recv, rs_send, left_recv, right_recv = scratch[4:9]
        scratch = scratch[9:]
    if ng:
        core_send, core_recv, to_right, to_left, ag_left, ag_right = scratch[:6]

    def part_rows(block, k):
        return pl.ds(pl.multiple_of(block * rows + k * piece, piece), piece)

    def remote(src, dst, send, recv, target):
        return pltpu.make_async_remote_copy(
            src_ref=src,
            dst_ref=dst,
            send_sem=send,
            recv_sem=recv,
            device_id=(dp, target),
            device_id_type=MESH,
        )

    if nr:

        def half_copy(dest, k):
            return remote(
                part.at[part_rows(2 * dest + 1 - core, k)],
                half.at[dest, k],
                half_send.at[dest, k],
                half_recv.at[dest, k],
                other,
            )

        def send_halves(k, carry):
            for dest in range(nr):
                half_copy(dest, k).start()
            return carry

        lax.fori_loop(0, chunks, send_halves, 0)

        def right_copy(dest, k):
            return remote(
                going.at[dest, k],
                from_left.at[dest, k],
                rs_send.at[dest, k],
                left_recv.at[dest, k],
                mp + 2,
            )

        def left_copy(dest, k):
            return remote(
                going.at[dest, k],
                from_right.at[dest, k],
                rs_send.at[dest, k],
                right_recv.at[dest, k],
                mp - 2,
            )

        def chip_sum(dest, k):
            half_copy(dest, k).wait_recv()
            mine = part[part_rows(2 * dest + core, k), :].astype(jnp.float32)
            return mine + half[dest, k].astype(jnp.float32)

        def pass_right(dest, k):
            total = chip_sum(dest, k)

            @pl.when(zr == 0)
            def _():
                going[dest, k] = total.astype(jnp.bfloat16)

            @pl.when(zr > 0)
            def _():
                right_copy(dest, k).wait_recv()
                both = total + from_left[dest, k].astype(jnp.float32)
                going[dest, k] = both.astype(jnp.bfloat16)

            right_copy(dest, k).start()

        def pass_left(dest, k):
            total = chip_sum(dest, k)

            @pl.when(zr == last_r)
            def _():
                going[dest, k] = total.astype(jnp.bfloat16)

            @pl.when(zr < last_r)
            def _():
                left_copy(dest, k).wait_recv()
                both = total + from_right[dest, k].astype(jnp.float32)
                going[dest, k] = both.astype(jnp.bfloat16)

            left_copy(dest, k).start()

    if ng:

        def gathered(block, k, send, recv, target):
            where = whole.at[part_rows(2 * block + core, k)]
            return remote(where, where, send.at[block, k], recv.at[block, k], target)

        def core_copy(block, k):
            return gathered(block, k, core_send, core_recv, other)

        def ag_right_copy(block, k):
            return gathered(block, k, to_right, ag_left, mp + 2)

        def ag_left_copy(block, k):
            return gathered(block, k, to_left, ag_right, mp - 2)

    def own_rows(k):
        total = None
        if nr:
            total = chip_sum(zr, k)
            zero = jnp.zeros((piece, width), jnp.float32)

            @pl.when(zr > 0)
            def _():
                right_copy(zr, k).wait_recv()

            @pl.when(zr < last_r)
            def _():
                left_copy(zr, k).wait_recv()

            total += jnp.where(zr > 0, from_left[zr, k].astype(jnp.float32), zero)
            total += jnp.where(zr < last_r, from_right[zr, k].astype(jnp.float32), zero)
        at = pl.ds(pl.multiple_of(k * piece, piece), piece)
        ready = step(total, at, ins, outs)
        if ng:
            whole[part_rows(2 * zg + core, k), :] = ready.astype(whole.dtype)
            core_copy(zg, k).start()

            @pl.when(zg < last_g)
            def _():
                ag_right_copy(zg, k).start()

            @pl.when(zg > 0)
            def _():
                ag_left_copy(zg, k).start()

    def inside(k):
        return (k >= 0) & (k < chunks)

    def own_lag(chip):
        if not nr:
            return 0
        at = lax.rem(chip, nr)
        return jnp.maximum(at, last_r - at)

    def tick(now, carry):
        if nr:
            k_right = now - zr
            k_left = now - (last_r - zr)
            for far in range(last_r):

                @pl.when(inside(k_right) & (last_r - far > zr))
                def _():
                    pass_right(last_r - far, k_right)

                @pl.when(inside(k_left) & (far < zr))
                def _():
                    pass_left(far, k_left)

        k_own = now - own_lag(z)

        @pl.when(inside(k_own))
        def _():
            own_rows(k_own)

        if ng:
            for block in range(ng):
                k = now - (own_lag(z - zg + block) + jnp.abs(zg - block))

                @pl.when(inside(k) & (block < zg))
                def _():
                    ag_right_copy(block, k).wait_recv()
                    core_copy(block, k).start()

                    @pl.when(zg < last_g)
                    def _():
                        ag_right_copy(block, k).start()

                @pl.when(inside(k) & (block > zg))
                def _():
                    ag_left_copy(block, k).wait_recv()
                    core_copy(block, k).start()

                    @pl.when(zg > 0)
                    def _():
                        ag_left_copy(block, k).start()

        return carry

    ticks = chunks + (nr - 1 if nr else 0) + (ng - 1 if ng else 0)
    lax.fori_loop(0, ticks, tick, 0)

    def finish(k, carry):
        if nr:
            for block in range(nr):
                half_copy(block, k).wait_send()

                @pl.when(block != zr)
                def _():
                    right_copy(block, k).wait_send()

        if ng:
            for block in range(ng):
                core_copy(block, k).wait()

                @pl.when((zg < last_g) & (block <= zg))
                def _():
                    ag_right_copy(block, k).wait_send()

                @pl.when((zg > 0) & (block >= zg))
                def _():
                    ag_left_copy(block, k).wait_send()

        return carry

    lax.fori_loop(0, chunks, finish, 0)


def line_call(name, cid, partial, ins, out_types, step, rows, width, chunks, nr, ng):
    piece = rows // chunks
    out_shape = []
    if ng:
        out_shape.append(jax.ShapeDtypeStruct((2 * ng * rows, width), jnp.bfloat16))
    out_shape += out_types
    dma = pltpu.SemaphoreType.DMA
    scratch = []
    if nr:
        scratch += [pltpu.VMEM((nr, chunks, piece, width), jnp.bfloat16)] * 4
        scratch += [dma((nr, chunks))] * 5
    if ng:
        scratch += [dma((ng, chunks))] * 6
    args = ([partial] if nr else []) + list(ins)
    vmem = pl.BlockSpec(memory_space=pltpu.VMEM)
    call = pl.pallas_call(
        functools.partial(
            line_kernel, nr, ng, chunks, rows, width, len(ins), len(out_types), step
        ),
        out_shape=out_shape,
        in_specs=[vmem] * len(args),
        out_specs=[vmem] * len(out_shape),
        scratch_shapes=scratch,
        compiler_params=pltpu.CompilerParams(
            collective_id=cid, has_side_effects=True, vmem_limit_bytes=VMEM_CAP
        ),
        name=name,
    )
    return list(call(*args))


def head_stats_kernel(block, tile, table_ref, final_ref, wanted_ref, edge_ref, exp_ref, top_ref, sum_ref, pick_ref):
    j = pl.program_id(0)
    tokens = final_ref.shape[0]
    place = j * block + lax.broadcasted_iota(jnp.int32, (block, 1), 0)
    valid = place < edge_ref[0]

    def one(i, carry):
        at = pl.ds(i * tile, tile)
        logits = lax.dot_general(
            table_ref[...],
            final_ref[at, :],
            (((1,), (1,)), ((), ())),
            preferred_element_type=jnp.float32,
        )
        logits = jnp.where(valid, logits, MASKED)
        top = jnp.max(logits, axis=0, keepdims=True)
        weights = jnp.exp(logits - top)
        exp_ref[:, at] = weights.astype(jnp.bfloat16)
        top_ref[0, :, at] = top
        sum_ref[0, :, at] = jnp.sum(weights, axis=0, keepdims=True)
        pick_ref[0, :, at] = jnp.sum(
            jnp.where(place == wanted_ref[:, at], logits, 0.0), axis=0, keepdims=True
        )
        return carry

    for i in range(tokens // tile):
        one(i, 0)


def head_stats(table, final, wanted, edge, block, tile=512):
    rows, width = table.shape
    tokens = final.shape[0]
    steps = pl.cdiv(rows, block)
    row = jax.ShapeDtypeStruct((steps, 1, tokens), jnp.float32)
    row_spec = pl.BlockSpec((1, 1, tokens), lambda j: (j, 0, 0))
    return pl.pallas_call(
        functools.partial(head_stats_kernel, block, tile),
        grid=(steps,),
        out_shape=[jax.ShapeDtypeStruct((steps * block, tokens), jnp.bfloat16), row, row, row],
        in_specs=[
            pl.BlockSpec((block, width), lambda j: (j, 0)),
            pl.BlockSpec((tokens, width), lambda j: (0, 0)),
            pl.BlockSpec((1, tokens), lambda j: (0, 0)),
            pl.BlockSpec(memory_space=pltpu.SMEM),
        ],
        out_specs=[pl.BlockSpec((block, tokens), lambda j: (j, 0)), row_spec, row_spec, row_spec],
        compiler_params=pltpu.CompilerParams(vmem_limit_bytes=56 * 2**20),
        cost_estimate=pl.CostEstimate(
            flops=2 * rows * width * tokens,
            bytes_accessed=2 * rows * (width + tokens),
            transcendentals=rows * tokens,
        ),
        name="head_stats",
    )(table, final, wanted, edge)


def head_back_kernel(rows, block, tile, exp_ref, table_ref, final_ref, scale_ref, weight_ref, wanted_ref, grad_ref, dfinal_ref, dl_ref):
    j = pl.program_id(0)
    tokens = final_ref.shape[0]
    place = j * block + lax.broadcasted_iota(jnp.int32, (block, 1), 0)

    @pl.when(j == 0)
    def _():
        dfinal_ref[...] = jnp.zeros_like(dfinal_ref)

    table = jnp.where(place < rows, table_ref[...], jnp.zeros_like(table_ref))

    def one(i, carry):
        at = pl.ds(i * tile, tile)
        weight = weight_ref[:, at]
        dl = exp_ref[:, at].astype(jnp.float32) * scale_ref[0, :, at]
        dl = dl - jnp.where(place == wanted_ref[:, at], weight, 0.0)
        dl = dl.astype(jnp.bfloat16)
        dl_ref[:, at] = dl
        dfinal_ref[at, :] += lax.dot_general(
            dl, table, (((0,), (0,)), ((), ())), preferred_element_type=jnp.float32
        )
        return carry

    for i in range(tokens // tile):
        one(i, 0)

    strip = block // max(1, block // 256)

    def two(i, carry):
        at = pl.ds(i * strip, strip)
        grad_ref[at, :] = jnp.dot(
            dl_ref[at, :], final_ref[...], preferred_element_type=jnp.float32
        ).astype(jnp.bfloat16)
        return carry

    for i in range(block // strip):
        two(i, 0)


def head_back(exps, table, final, scale, weight, wanted, block, tile=256):
    rows, width = table.shape
    tokens = final.shape[0]
    steps = pl.cdiv(rows, block)
    return pl.pallas_call(
        functools.partial(head_back_kernel, rows, block, tile),
        grid=(steps,),
        out_shape=[
            jax.ShapeDtypeStruct((rows, width), jnp.bfloat16),
            jax.ShapeDtypeStruct((tokens, width), jnp.float32),
        ],
        in_specs=[
            pl.BlockSpec((block, tokens), lambda j: (j, 0)),
            pl.BlockSpec((block, width), lambda j: (j, 0)),
            pl.BlockSpec((tokens, width), lambda j: (0, 0)),
            pl.BlockSpec((1, 1, tokens), lambda j: (j, 0, 0)),
            pl.BlockSpec((1, tokens), lambda j: (0, 0)),
            pl.BlockSpec((1, tokens), lambda j: (0, 0)),
        ],
        out_specs=[
            pl.BlockSpec((block, width), lambda j: (j, 0)),
            pl.BlockSpec((tokens, width), lambda j: (0, 0)),
        ],
        scratch_shapes=[pltpu.VMEM((block, tokens), jnp.bfloat16)],
        compiler_params=pltpu.CompilerParams(vmem_limit_bytes=60 * 2**20),
        cost_estimate=pl.CostEstimate(
            flops=4 * rows * width * tokens,
            bytes_accessed=2 * rows * (2 * width + tokens),
            transcendentals=0,
        ),
        name="head_back",
    )(exps, table, final, scale, weight, wanted)


def small_gather_kernel(axis, count, src_ref, out_ref, send, recv):
    dp = lax.axis_index("dp")
    mp = lax.axis_index("mp")
    me = dp if axis == "dp" else mp

    def device(peer):
        return (peer, mp) if axis == "dp" else (dp, peer)

    barrier = pltpu.get_barrier_semaphore()
    for hop in range(1, count):
        pl.semaphore_signal(
            barrier, inc=1, device_id=device(lax.rem(me + hop, count)), device_id_type=MESH
        )
    pl.semaphore_wait(barrier, count - 1)
    copies = []
    for hop in range(1, count):
        peer = lax.rem(me + hop, count)
        copy = pltpu.make_async_remote_copy(
            src_ref=src_ref,
            dst_ref=out_ref.at[me],
            send_sem=send.at[hop],
            recv_sem=recv.at[hop],
            device_id=device(peer),
            device_id_type=MESH,
        )
        copy.start()
        copies.append(copy)
    out_ref[me] = src_ref[...]
    for copy in copies:
        copy.wait()


def small_gather(name, cid, values, axis):
    count = lax.axis_size(axis)
    vmem = pl.BlockSpec(memory_space=pltpu.VMEM)
    return pl.pallas_call(
        functools.partial(small_gather_kernel, axis, count),
        out_shape=jax.ShapeDtypeStruct((count,) + values.shape, values.dtype),
        in_specs=[vmem],
        out_specs=vmem,
        scratch_shapes=[pltpu.SemaphoreType.DMA((count,)), pltpu.SemaphoreType.DMA((count,))],
        compiler_params=pltpu.CompilerParams(collective_id=cid, has_side_effects=True),
        name=name,
    )(values)


def packed(pieces):
    flat = []
    for piece in pieces:
        piece = piece.reshape(-1)
        flat.append(jnp.pad(piece, (0, -piece.size % 128)))
    flat = jnp.concatenate(flat)
    return jnp.pad(flat, (0, -flat.size % 1024)).reshape(-1, 128)


def unpacked(rows, shapes):
    flat = rows.reshape(-1)
    pieces, at = [], 0
    for shape in shapes:
        size = math.prod(shape)
        pieces.append(flat[at : at + size].reshape(shape))
        at += size + -size % 128
    return pieces


def small_sum(name, cid, over_dp, over_mp, over_all):
    first = small_gather(name + "_dp", cid, packed(over_dp + over_all), "dp")
    first = unpacked(jnp.sum(first, axis=0), [v.shape for v in over_dp + over_all])
    rest = first[len(over_dp) :]
    second = small_gather(name + "_mp", cid + 1, packed(over_mp + rest), "mp")
    second = unpacked(jnp.sum(second, axis=0), [v.shape for v in over_mp + over_all])
    return first[: len(over_dp)], second[: len(over_mp)], second[len(over_mp) :]


def lookup_kernel(count_ref, key_ref, table_ref, out_ref, rows_ref):
    spots = rows_ref.shape[0]
    rows_ref[...] = jnp.zeros_like(rows_ref)

    def one(i, carry):
        key = key_ref[i]
        rows_ref[pl.ds(key % spots, 1), :] = table_ref[pl.ds(key // spots, 1), :]
        return carry

    lax.fori_loop(0, count_ref[0], one, 0)

    def narrow(i, carry):
        at = pl.ds(pl.multiple_of(i * 256, 256), 256)
        out_ref[at, :] = rows_ref[at, :].astype(jnp.bfloat16)
        return carry

    lax.fori_loop(0, spots // 256, narrow, 0)


def lookup(keys, count, table, spots):
    width = table.shape[1]
    smem = pl.BlockSpec(memory_space=pltpu.SMEM)
    vmem = pl.BlockSpec(memory_space=pltpu.VMEM)
    return pl.pallas_call(
        lookup_kernel,
        out_shape=jax.ShapeDtypeStruct((spots, width), jnp.bfloat16),
        in_specs=[smem, smem, vmem],
        out_specs=vmem,
        scratch_shapes=[pltpu.VMEM((spots, width), jnp.float32)],
        compiler_params=pltpu.CompilerParams(vmem_limit_bytes=VMEM_CAP),
        cost_estimate=pl.CostEstimate(flops=0, bytes_accessed=8 * spots * width, transcendentals=0),
        name="lookup",
    )(count, keys, table)


def scatter_kernel(count_ref, key_ref, head_ref, rows_in_ref, grad_ref, rows_ref):
    spots = rows_ref.shape[0]
    vocab = grad_ref.shape[0]

    def widen(i, carry):
        at = pl.ds(pl.multiple_of(i * 256, 256), 256)
        rows_ref[at, :] = rows_in_ref[at, :].astype(jnp.float32)
        return carry

    lax.fori_loop(0, spots // 256, widen, 0)
    grad_ref[...] = head_ref[...].astype(jnp.float32)

    def one(i, carry):
        key = key_ref[i]
        grad_ref[pl.ds(key // spots, 1), :] += rows_ref[pl.ds(key % spots, 1), :]
        return carry

    lax.fori_loop(0, count_ref[0], one, 0)


def scatter(keys, count, head_grad, rows):
    spots, width = rows.shape
    vocab = head_grad.shape[0]
    smem = pl.BlockSpec(memory_space=pltpu.SMEM)
    vmem = pl.BlockSpec(memory_space=pltpu.VMEM)
    return pl.pallas_call(
        scatter_kernel,
        out_shape=jax.ShapeDtypeStruct((vocab, width), jnp.float32),
        in_specs=[smem, smem, vmem, vmem],
        out_specs=vmem,
        scratch_shapes=[pltpu.VMEM((spots, width), jnp.float32)],
        compiler_params=pltpu.CompilerParams(vmem_limit_bytes=VMEM_CAP),
        cost_estimate=pl.CostEstimate(flops=0, bytes_accessed=16 * spots * width, transcendentals=0),
        name="scatter",
    )(count, keys, head_grad, rows)


def norm_parts(values):
    centre = jnp.mean(values, axis=-1, keepdims=True)
    centred = values - centre
    scale = lax.rsqrt(jnp.mean(centred * centred, axis=-1, keepdims=True) + EPS_NORM)
    return centred * scale, scale


def norm_pull(values, gain, upstream):
    normed, scale = norm_parts(values)
    weighted = upstream * gain
    pulled = scale * (
        weighted
        - jnp.mean(weighted, axis=-1, keepdims=True)
        - normed * jnp.mean(weighted * normed, axis=-1, keepdims=True)
    )
    return (
        pulled,
        jnp.sum(upstream * normed, axis=0, keepdims=True),
        jnp.sum(upstream, axis=0, keepdims=True),
    )


def step_first(total, at, ins, outs):
    stream, norms = ins
    normed, scale = norm_parts(stream[at, :].astype(jnp.float32))
    return normed * norms[0:1, :] + norms[1:2, :]


def step_lookup(total, at, ins, outs):
    outs[0][at, :] = total.astype(jnp.bfloat16)


def step_forward(row, total, at, ins, outs):
    stream, norms = ins
    values = stream[at, :].astype(jnp.float32) + total
    outs[0][at, :] = values
    normed, scale = norm_parts(values)
    return normed * norms[row : row + 1, :] + norms[row + 1 : row + 2, :]


def step_backward(row, total, at, ins, outs):
    stream, norms = ins[:2]
    pulled, dgain, dshift = norm_pull(
        stream[at, :].astype(jnp.float32), norms[row : row + 1, :], total
    )
    if len(ins) > 2:
        pulled = pulled + ins[2][at, :]
    outs[0][at, :] = pulled.astype(outs[0].dtype)
    first = at.start == 0

    @pl.when(first)
    def _():
        outs[1][...] = jnp.zeros_like(outs[1])

    outs[1][0:1, :] += dgain
    outs[1][1:2, :] += dshift
    return pulled


def step_pass(total, at, ins, outs):
    return ins[0][at, :]


def gelu_tanh(values):
    return jax.nn.gelu(values, approximate=True)


def score_block(mixed, starts):
    place = jnp.arange(mixed.shape[0], dtype=jnp.int32)
    allowed = (place[None, :] <= place[:, None]) & (place[None, :] >= starts[:, None])
    raw = jnp.einsum(
        "qhe,khe->hqk", mixed[:, :, 0], mixed[:, :, 1], preferred_element_type=jnp.float32
    )
    return jnp.where(allowed[None], raw * HD ** (-0.5), MASKED)


def attend_forward(mixed, starts):
    scores = score_block(mixed, starts)
    highest = jnp.max(scores, axis=-1, keepdims=True)
    weights = jnp.exp(scores - highest)
    totals = jnp.sum(weights, axis=-1, keepdims=True)
    probs = (weights / totals).astype(jnp.bfloat16)
    result = jnp.einsum(
        "hqk,khe->qhe", probs, mixed[:, :, 2], preferred_element_type=jnp.float32
    )
    return (result.astype(jnp.bfloat16), highest[:, :, 0] + jnp.log(totals[:, :, 0]))


def attend_backward(mixed, starts, log_rows, upstream):
    scores = score_block(mixed, starts)
    probs = jnp.exp(scores - log_rows[:, :, None])
    dprobs = jnp.einsum(
        "qhe,khe->hqk", upstream, mixed[:, :, 2], preferred_element_type=jnp.float32
    )
    dvalues = jnp.einsum(
        "hqk,qhe->khe", probs.astype(jnp.bfloat16), upstream, preferred_element_type=jnp.float32
    )
    inner = jnp.sum(probs * dprobs, axis=-1, keepdims=True)
    dscores = (probs * (dprobs - inner)).astype(jnp.bfloat16)
    dquery = jnp.einsum(
        "hqk,khe->qhe", dscores, mixed[:, :, 1], preferred_element_type=jnp.float32
    ) * HD ** (-0.5)
    dkeys = jnp.einsum(
        "hqk,qhe->khe", dscores, mixed[:, :, 0], preferred_element_type=jnp.float32
    ) * HD ** (-0.5)
    return jnp.stack([dquery, dkeys, dvalues], axis=2).astype(jnp.bfloat16)


def local(
    token_ids,
    targets,
    starts,
    sources,
    embedding,
    w_qkv,
    w_out,
    w_fc,
    w_proj,
    norm_params,
    rows_table,
    cols_table,
    rows_qkv,
    cols_qkv,
    rows_out,
    cols_out,
    rows_fc,
    cols_fc,
    rows_proj,
    cols_proj,
    second_norms,
):
    bf16 = jnp.bfloat16
    f32 = jnp.float32
    size_mp = lax.axis_size("mp")
    size_dp = lax.axis_size("dp")
    dp = lax.axis_index("dp")
    mp = lax.axis_index("mp")
    tokens = token_ids.shape[0]
    seqs = tokens // LEN
    chips = size_mp // 2
    near = chips // seqs
    sharers = size_mp // seqs
    rows = tokens // size_mp
    vocab, part_width = embedding.shape
    width = part_width * size_dp
    first_row = mp * vocab
    spots = tokens * size_dp
    chunks_full = max(1, min(8, rows // 32))
    chunks_near = max(1, min(4, rows // 32))

    both = jnp.stack([token_ids, sources]).reshape(-1, 128)
    both = small_gather("gather_ids", 0, both, "dp").reshape(size_dp, 2, tokens)
    all_ids = both[:, 0]
    all_sources = both[:, 1].reshape(-1)
    counts = jnp.sum(
        (all_sources[:, None] == jnp.arange(NSRC, dtype=jnp.int32)[None, :]).astype(f32), axis=0
    )


    def own_and_twins(weight, axis):
        weight = weight.astype(bf16)
        found = [weight]
        for turn in range(1, seqs):
            shift = [(i, (i + turn * sharers) % size_mp) for i in range(size_mp)]
            found.append(lax.ppermute(weight, "mp", shift))
        return jnp.concatenate(found, axis=axis) if seqs > 1 else weight

    wide_qkv = lax.all_gather(own_and_twins(w_qkv, 1), "dp", axis=0, tiled=True)
    wide_out = lax.all_gather(own_and_twins(w_out, 0), "dp", axis=1, tiled=True)
    wide_fc = lax.all_gather(own_and_twins(w_fc, 1), "dp", axis=0, tiled=True)
    wide_proj = lax.all_gather(own_and_twins(w_proj, 0), "dp", axis=1, tiled=True)
    wide_table = lax.all_gather(embedding.astype(bf16), "dp", axis=1, tiled=True)

    place = (
        (jnp.arange(size_mp, dtype=jnp.int32) * size_dp)[None, :, None] * rows
        + (jnp.arange(size_dp, dtype=jnp.int32) * rows)[:, None, None]
        + jnp.arange(rows, dtype=jnp.int32)[None, None, :]
    ).reshape(size_dp, tokens)
    local_ids = all_ids - first_row
    inside = (local_ids >= 0) & (local_ids < vocab)
    keys = jnp.where(inside, local_ids * spots + place, jnp.iinfo(jnp.int32).max)
    keys = jnp.sort(keys.reshape(-1))
    owned = jnp.sum(inside.astype(jnp.int32)).reshape(1)
    found = lookup(keys, owned, embedding, spots)
    (picked_rows,) = line_call(
        "rs_lookup",
        1,
        found,
        [],
        [jax.ShapeDtypeStruct((size_dp * rows, part_width), bf16)],
        step_lookup,
        size_dp * rows,
        part_width,
        chunks_full,
        chips,
        0,
    )
    stream0 = lax.all_to_all(
        picked_rows.reshape(size_dp, rows, part_width), "dp", 0, 0, tiled=False
    )
    stream0 = jnp.swapaxes(stream0, 0, 1).reshape(rows, width)

    row_f32 = jax.ShapeDtypeStruct((rows, width), f32)
    pair_f32 = jax.ShapeDtypeStruct((8, width), f32)
    (inner_one,) = line_call(
        "ag_inner1", 2, None, [stream0, norm_params], [], step_first, rows, width, chunks_near, 0, near
    )
    heads = wide_qkv.shape[1] // (3 * HD)
    my_starts = row_slice(starts, (mp // sharers) * LEN, LEN)
    mixed = jnp.dot(inner_one, wide_qkv, preferred_element_type=f32).astype(bf16)
    mixed = mixed.reshape(LEN, heads, 3, HD)
    attended, log_sums = attend_forward(mixed, my_starts)
    attended = attended.reshape(LEN, heads * HD)
    partial = jnp.dot(attended, wide_out, preferred_element_type=f32).astype(bf16)
    inner_two, stream1 = line_call(
        "attn_sum",
        3,
        partial,
        [stream0, norm_params],
        [row_f32],
        functools.partial(step_forward, 2),
        rows,
        width,
        chunks_near,
        near,
        near,
    )
    before = jnp.dot(inner_two, wide_fc, preferred_element_type=f32)
    hidden = gelu_tanh(before).astype(bf16)
    partial = jnp.dot(hidden, wide_proj, preferred_element_type=f32).astype(bf16)
    final, stream2 = line_call(
        "mlp_sum",
        4,
        partial,
        [stream1, norm_params],
        [row_f32],
        functools.partial(step_forward, 4),
        rows,
        width,
        chunks_full,
        near,
        chips,
    )

    edge = jnp.clip(VREAL - first_row, 0, vocab).astype(jnp.int32).reshape(1)
    wanted = targets - first_row
    wanted = jnp.where((wanted >= 0) & (wanted < vocab), wanted, -1).reshape(1, tokens)
    block = 640
    exps, tops, sums, picks = head_stats(wide_table, final, wanted, edge, block)
    tops = tops[:, 0]
    top = jnp.max(tops, axis=0)
    total = jnp.sum(sums[:, 0] * jnp.exp(tops - top[None, :]), axis=0)
    pick = jnp.sum(picks[:, 0], axis=0)
    stats = small_gather("gather_stats", 5, packed([top, total, pick]), "mp")
    stats = stats.reshape(size_mp, -1)[:, : 3 * tokens].reshape(size_mp, 3, tokens)
    highest = jnp.max(stats[:, 0], axis=0)
    log_total = highest + jnp.log(
        jnp.sum(stats[:, 1] * jnp.exp(stats[:, 0] - highest[None, :]), axis=0)
    )
    token_loss = log_total - jnp.sum(stats[:, 2], axis=0)
    member = (sources[:, None] == jnp.arange(NSRC, dtype=jnp.int32)[None, :]).astype(f32)
    loss_part = jnp.sum(member * token_loss[:, None], axis=0)
    weight = jnp.sum(member / (NSRC * jnp.maximum(counts, 1.0))[None, :], axis=1)
    scale = jnp.exp(tops - log_total[None, :]) * weight[None, :]
    table_grad, dfinal = head_back(
        exps, wide_table, final, scale[:, None, :], weight[None, :], wanted, block
    )
    head_grad = lax.psum_scatter(table_grad, "dp", scatter_dimension=1, tiled=True)

    dbranch2, dstream2, norm3 = line_call(
        "final_back",
        6,
        dfinal.astype(bf16),
        [stream2, norm_params],
        [row_f32, pair_f32],
        functools.partial(step_backward, 4),
        rows,
        width,
        chunks_full,
        chips,
        near,
    )
    grad_proj = jnp.einsum("tf,td->fd", hidden, dbranch2, preferred_element_type=f32).astype(bf16)
    dhidden = jnp.einsum("td,fd->tf", dbranch2, wide_proj, preferred_element_type=f32)
    unused, gelu_pull = jax.vjp(gelu_tanh, before)
    dbefore = gelu_pull(dhidden)[0].astype(bf16)
    partial = jnp.einsum("tf,df->td", dbefore, wide_fc, preferred_element_type=f32).astype(bf16)
    dbranch1, dstream1, norm2 = line_call(
        "mlp_back",
        7,
        partial,
        [stream1, norm_params, dstream2],
        [row_f32, pair_f32],
        functools.partial(step_backward, 2),
        rows,
        width,
        chunks_near,
        near,
        near,
    )
    grad_fc = jnp.einsum("td,tf->df", inner_two, dbefore, preferred_element_type=f32).astype(bf16)
    grad_out = jnp.einsum("tf,td->fd", attended, dbranch1, preferred_element_type=f32).astype(bf16)
    dattended = jnp.einsum("td,fd->tf", dbranch1, wide_out, preferred_element_type=f32)
    dattended = dattended.astype(bf16).reshape(LEN, heads, HD)
    dmixed = attend_backward(mixed, my_starts, log_sums, dattended)
    dmixed = dmixed.reshape(LEN, heads * 3 * HD)
    partial = jnp.einsum("tc,dc->td", dmixed, wide_qkv, preferred_element_type=f32).astype(bf16)
    dstream0, norm1 = line_call(
        "attn_back",
        8,
        partial,
        [stream0, norm_params, dstream1],
        [jax.ShapeDtypeStruct((rows, width), bf16), pair_f32],
        functools.partial(step_backward, 0),
        rows,
        width,
        chunks_near,
        near,
        0,
    )
    grad_qkv = jnp.einsum("td,tc->dc", inner_one, dmixed, preferred_element_type=f32).astype(bf16)

    def to_owner(gradient, cut, axis):
        share = lax.psum_scatter(gradient, "dp", scatter_dimension=cut, tiled=True)
        pieces = jnp.split(share, seqs, axis=axis)
        mine = pieces[0].astype(f32)
        for turn in range(1, seqs):
            back = [(i, (i - turn * sharers) % size_mp) for i in range(size_mp)]
            mine = mine + lax.ppermute(pieces[turn], "mp", back).astype(f32)
        return mine

    grad_proj = to_owner(grad_proj, 1, 0)
    grad_fc = to_owner(grad_fc, 0, 1)
    grad_out = to_owner(grad_out, 1, 0)
    grad_qkv = to_owner(grad_qkv, 0, 1)

    sent = jnp.swapaxes(dstream0.reshape(rows, size_dp, part_width), 0, 1)
    sent = lax.all_to_all(sent, "dp", 0, 0, tiled=False).reshape(size_dp * rows, part_width)
    (drows,) = line_call(
        "ag_lookup",
        9,
        None,
        [sent],
        [],
        step_pass,
        size_dp * rows,
        part_width,
        chunks_full,
        0,
        chips,
    )
    grad_table = scatter(keys, owned, head_grad, drows)

    beta = 1.0 - STEP ** (-0.8)
    weights = (embedding, w_qkv, w_out, w_fc, w_proj)
    grads = (grad_table, grad_qkv, grad_out, grad_fc, grad_proj)
    rows_old = (rows_table, rows_qkv, rows_out, rows_fc, rows_proj)
    cols_old = (cols_table, cols_qkv, cols_out, cols_fc, cols_proj)
    row_span = (size_mp, size_dp, size_mp, size_dp, size_mp)
    col_span = (size_dp, size_mp, size_dp, size_mp, size_dp)
    squares = [gradient * gradient + EPS_ONE for gradient in grads]
    row_parts = [jnp.sum(square, axis=1) for square in squares]
    col_parts = [jnp.sum(square, axis=0) for square in squares]
    square_sums = jnp.stack([jnp.sum(part) for part in col_parts])
    weight_sums = jnp.stack([jnp.sum(value * value) for value in weights])
    old_sums = jnp.stack([jnp.sum(old) / span for old, span in zip(rows_old, col_span)])
    norm_partial = jnp.concatenate([norm1[:2], norm2[:2], norm3[:2]])
    on_dp, on_mp, on_all = small_sum(
        "sum_squares",
        10,
        [col_parts[1], col_parts[3], row_parts[0], row_parts[2], row_parts[4], loss_part],
        [row_parts[1], row_parts[3], col_parts[0], col_parts[2], col_parts[4]],
        [square_sums, weight_sums, old_sums, norm_partial],
    )
    square_sums, weight_sums, old_sums, grad_norms = on_all
    loss_sums = on_dp[5]
    row_full = (on_dp[2], on_mp[0], on_dp[3], on_mp[1], on_dp[4])
    col_full = (on_mp[2], on_dp[0], on_mp[3], on_dp[1], on_mp[4])
    rows_new = []
    cols_new = []
    steps = []
    entries = []
    for index in range(5):
        full_rows = grads[index].shape[0] * row_span[index]
        full_cols = grads[index].shape[1] * col_span[index]
        entries.append(full_rows * full_cols)
        rows_next = beta * rows_old[index] + (1.0 - beta) * row_full[index] / full_cols
        cols_next = beta * cols_old[index] + (1.0 - beta) * col_full[index] / full_rows
        mean = beta * old_sums[index] / full_rows + (1.0 - beta) * (
            square_sums[index] / (full_rows * full_cols)
        )
        rows_new.append(rows_next)
        cols_new.append(cols_next)
        steps.append(
            grads[index] * lax.rsqrt(rows_next[:, None] * cols_next[None, :] / mean)
        )
    step_part = jnp.stack([jnp.sum(piece * piece) for piece in steps])
    unused, unused, (step_sq,) = small_sum("sum_steps", 12, [], [], [step_part])
    updated = []
    for index in range(5):
        clipped = steps[index] / jnp.maximum(1.0, jnp.sqrt(step_sq[index] / entries[index]) / CLIP)
        rate = RHO * jnp.sqrt(weight_sums[index] / entries[index])
        updated.append(weights[index] - rate * clipped)
    second_new = beta * second_norms + (1.0 - beta) * (grad_norms * grad_norms + EPS_ONE)
    norm_steps = grad_norms * lax.rsqrt(second_new)
    norm_steps = norm_steps / jnp.maximum(1.0, jnp.sqrt(jnp.mean(norm_steps * norm_steps)) / CLIP)
    norms_new = norm_params - RHO * jnp.sqrt(jnp.mean(norm_params * norm_params)) * norm_steps
    return (
        loss_sums,
        counts,
        grad_table,
        rows_new[0],
        cols_new[0],
        updated[0],
        grad_qkv,
        rows_new[1],
        cols_new[1],
        updated[1],
        grad_out,
        rows_new[2],
        cols_new[2],
        updated[2],
        grad_fc,
        rows_new[3],
        cols_new[3],
        updated[3],
        grad_proj,
        rows_new[4],
        cols_new[4],
        updated[4],
        grad_norms,
        second_new,
        norms_new,
    )


def solution(mesh):
    placed = (
        P("dp"),
        P("dp"),
        P("dp"),
        P("dp"),
        P("mp", "dp"),
        P("dp", "mp"),
        P("mp", "dp"),
        P("dp", "mp"),
        P("mp", "dp"),
        P(),
        P("mp"),
        P("dp"),
        P("dp"),
        P("mp"),
        P("mp"),
        P("dp"),
        P("dp"),
        P("mp"),
        P("mp"),
        P("dp"),
        P(),
    )
    return jax.shard_map(
        local,
        mesh=mesh,
        in_specs=placed,
        out_specs=(
            P(),
            P(),
            P("mp", "dp"),
            P("mp"),
            P("dp"),
            P("mp", "dp"),
            P("dp", "mp"),
            P("dp"),
            P("mp"),
            P("dp", "mp"),
            P("mp", "dp"),
            P("mp"),
            P("dp"),
            P("mp", "dp"),
            P("dp", "mp"),
            P("dp"),
            P("mp"),
            P("dp", "mp"),
            P("mp", "dp"),
            P("mp"),
            P("dp"),
            P("mp", "dp"),
            P(),
            P(),
            P(),
        ),
        check_vma=False,
    )
```

```python
import functools
import math

import jax
import jax.numpy as jnp
from jax import lax
from jax.experimental import pallas as pl
from jax.experimental.pallas import tpu as pltpu
from jax.sharding import PartitionSpec as P

HD = 64
VREAL = 50257
LEN = 1024
NSRC = 4
STEP = 10


EPS_NORM = 1e-05
EPS_ONE = 1e-30
CLIP = 1.0
RHO = 0.5
MASKED = -1e30
MESH = pl.DeviceIdType.MESH
VMEM_CAP = 56 * 2**20


def cost_of(time):
    return pl.CostEstimate(
        flops=time * 1000000000, bytes_accessed=time * 3000000, transcendentals=0
    )


def row_slice(values, start, count):
    return lax.dynamic_slice_in_dim(values, start, count, 0)


def line_kernel(nr, ng, chunks, rows, width, n_in, n_out, step, sides, *refs):
    part = refs[0] if nr else None
    first = 1 if nr else 0
    ins = refs[first : first + n_in]
    refs = refs[first + n_in :]
    side_ins, refs = refs[: len(sides)], refs[len(sides) :]
    if ng:
        whole, refs = refs[0], refs[1:]
    outs = refs[:n_out]
    refs = refs[n_out:]
    side_outs, scratch = refs[: len(sides)], refs[len(sides) :]
    side_scratch, scratch = scratch[: 3 * len(sides)], scratch[3 * len(sides) :]
    size_dp = lax.axis_size("dp")
    dp = lax.axis_index("dp")
    mp = lax.axis_index("mp")
    z = mp // 2
    core = lax.rem(mp, 2)
    other = mp + 1 - 2 * core
    piece = rows // chunks
    most = max(nr, ng)
    zb = lax.rem(z, most)
    if nr:
        zr = lax.rem(z, nr)
        last_r = nr - 1
    if ng:
        zg = lax.rem(z, ng)
        last_g = ng - 1

    barrier = pltpu.get_barrier_semaphore()
    pl.semaphore_signal(barrier, inc=1, device_id=(dp, other), device_id_type=MESH)

    @pl.when(zb > 0)
    def _():
        pl.semaphore_signal(barrier, inc=1, device_id=(dp, mp - 2), device_id_type=MESH)

    @pl.when(zb < most - 1)
    def _():
        pl.semaphore_signal(barrier, inc=1, device_id=(dp, mp + 2), device_id_type=MESH)

    if sides:
        for hop in range(1, size_dp):
            pl.semaphore_signal(
                barrier,
                inc=1,
                device_id=(lax.rem(dp + hop, size_dp), mp),
                device_id_type=MESH,
            )
    greeted = (size_dp if sides else 1) + (zb > 0).astype(jnp.int32) + (zb < most - 1).astype(jnp.int32)
    pl.semaphore_wait(barrier, greeted)

    def share(axis, length, which):
        at = pl.ds(pl.multiple_of(which * length, length), length)
        return (at, slice(None)) if axis == 0 else (slice(None), at)

    side_copies = []
    for index, (kind, axis) in enumerate(sides):
        src, dst = side_ins[index], side_outs[index]
        send, recv, slots = side_scratch[3 * index : 3 * index + 3]
        length = (src if kind == "gather" else dst).shape[axis]
        for hop in range(1, size_dp):
            peer = lax.rem(dp + hop, size_dp)
            if kind == "gather":
                source, target = src, dst.at[share(axis, length, dp)]
            else:
                source, target = src.at[share(axis, length, peer)], slots.at[hop]
            copy = pltpu.make_async_remote_copy(
                src_ref=source,
                dst_ref=target,
                send_sem=send.at[hop],
                recv_sem=recv.at[hop],
                device_id=(peer, mp),
                device_id_type=MESH,
            )
            side_copies.append(copy)
            if nr == 0:
                copy.start()

    if nr:
        half, from_left, from_right, going = scratch[:4]
        half_send, half_recv, rs_send, left_recv, right_recv = scratch[4:9]
        scratch = scratch[9:]
    if ng:
        core_send, core_recv, to_right, to_left, ag_left, ag_right = scratch[:6]

    def part_rows(block, k):
        return pl.ds(pl.multiple_of(block * rows + k * piece, piece), piece)

    def remote(src, dst, send, recv, target):
        return pltpu.make_async_remote_copy(
            src_ref=src,
            dst_ref=dst,
            send_sem=send,
            recv_sem=recv,
            device_id=(dp, target),
            device_id_type=MESH,
        )

    if nr:

        def half_copy(dest, k):
            return remote(
                part.at[part_rows(2 * dest + 1 - core, k)],
                half.at[dest, k],
                half_send.at[dest, k],
                half_recv.at[dest, k],
                other,
            )

        def send_halves(k, carry):
            for dest in range(nr):
                half_copy(dest, k).start()
            return carry

        lax.fori_loop(0, chunks, send_halves, 0)
        for copy in side_copies:
            copy.start()

        def right_copy(dest, k):
            return remote(
                going.at[dest, k],
                from_left.at[dest, k],
                rs_send.at[dest, k],
                left_recv.at[dest, k],
                mp + 2,
            )

        def left_copy(dest, k):
            return remote(
                going.at[dest, k],
                from_right.at[dest, k],
                rs_send.at[dest, k],
                right_recv.at[dest, k],
                mp - 2,
            )

        def chip_sum(dest, k):
            half_copy(dest, k).wait_recv()
            mine = part[part_rows(2 * dest + core, k), :].astype(jnp.float32)
            return mine + half[dest, k].astype(jnp.float32)

        def pass_right(dest, k):
            total = chip_sum(dest, k)

            @pl.when(zr == 0)
            def _():
                going[dest, k] = total.astype(jnp.bfloat16)

            @pl.when(zr > 0)
            def _():
                right_copy(dest, k).wait_recv()
                both = total + from_left[dest, k].astype(jnp.float32)
                going[dest, k] = both.astype(jnp.bfloat16)

            right_copy(dest, k).start()

        def pass_left(dest, k):
            total = chip_sum(dest, k)

            @pl.when(zr == last_r)
            def _():
                going[dest, k] = total.astype(jnp.bfloat16)

            @pl.when(zr < last_r)
            def _():
                left_copy(dest, k).wait_recv()
                both = total + from_right[dest, k].astype(jnp.float32)
                going[dest, k] = both.astype(jnp.bfloat16)

            left_copy(dest, k).start()

    if ng:

        def gathered(block, k, send, recv, target):
            where = whole.at[part_rows(2 * block + core, k)]
            return remote(where, where, send.at[block, k], recv.at[block, k], target)

        def core_copy(block, k):
            return gathered(block, k, core_send, core_recv, other)

        def ag_right_copy(block, k):
            return gathered(block, k, to_right, ag_left, mp + 2)

        def ag_left_copy(block, k):
            return gathered(block, k, to_left, ag_right, mp - 2)

    def own_rows(k):
        total = None
        if nr:
            total = chip_sum(zr, k)
            zero = jnp.zeros((piece, width), jnp.float32)

            @pl.when(zr > 0)
            def _():
                right_copy(zr, k).wait_recv()

            @pl.when(zr < last_r)
            def _():
                left_copy(zr, k).wait_recv()

            total += jnp.where(zr > 0, from_left[zr, k].astype(jnp.float32), zero)
            total += jnp.where(zr < last_r, from_right[zr, k].astype(jnp.float32), zero)
        at = pl.ds(pl.multiple_of(k * piece, piece), piece)
        ready = step(total, at, ins, outs)
        if ng:
            whole[part_rows(2 * zg + core, k), :] = ready.astype(whole.dtype)
            core_copy(zg, k).start()

            @pl.when(zg < last_g)
            def _():
                ag_right_copy(zg, k).start()

            @pl.when(zg > 0)
            def _():
                ag_left_copy(zg, k).start()

    def inside(k):
        return (k >= 0) & (k < chunks)

    def own_lag(chip):
        if not nr:
            return 0
        at = lax.rem(chip, nr)
        return jnp.maximum(at, last_r - at)

    def tick(now, carry):
        if nr:
            k_right = now - zr
            k_left = now - (last_r - zr)
            for far in range(last_r):

                @pl.when(inside(k_right) & (last_r - far > zr))
                def _():
                    pass_right(last_r - far, k_right)

                @pl.when(inside(k_left) & (far < zr))
                def _():
                    pass_left(far, k_left)

        k_own = now - own_lag(z)

        @pl.when(inside(k_own))
        def _():
            own_rows(k_own)

        if ng:
            for block in range(ng):
                k = now - (own_lag(z - zg + block) + jnp.abs(zg - block))

                @pl.when(inside(k) & (block < zg))
                def _():
                    ag_right_copy(block, k).wait_recv()
                    core_copy(block, k).start()

                    @pl.when(zg < last_g)
                    def _():
                        ag_right_copy(block, k).start()

                @pl.when(inside(k) & (block > zg))
                def _():
                    ag_left_copy(block, k).wait_recv()
                    core_copy(block, k).start()

                    @pl.when(zg > 0)
                    def _():
                        ag_left_copy(block, k).start()

        return carry

    ticks = chunks + (nr - 1 if nr else 0) + (ng - 1 if ng else 0)
    lax.fori_loop(0, ticks, tick, 0)

    def finish(k, carry):
        if nr:
            for block in range(nr):
                half_copy(block, k).wait_send()

                @pl.when(block != zr)
                def _():
                    right_copy(block, k).wait_send()

        if ng:
            for block in range(ng):
                core_copy(block, k).wait()

                @pl.when((zg < last_g) & (block <= zg))
                def _():
                    ag_right_copy(block, k).wait_send()

                @pl.when((zg > 0) & (block >= zg))
                def _():
                    ag_left_copy(block, k).wait_send()

        return carry

    lax.fori_loop(0, chunks, finish, 0)
    for index, (kind, axis) in enumerate(sides):
        if kind == "gather":
            length = side_ins[index].shape[axis]
            side_outs[index][share(axis, length, dp)] = side_ins[index][...]
    for copy in side_copies:
        copy.wait()
    for index, (kind, axis) in enumerate(sides):
        if kind == "scatter":
            src, dst = side_ins[index], side_outs[index]
            slots = side_scratch[3 * index + 2]
            strip = 128
            height = dst.shape[0]

            def add(i, carry):
                at = pl.ds(pl.multiple_of(i * strip, strip), strip)
                length = dst.shape[axis]
                if axis == 0:
                    start = pl.multiple_of(dp * length + i * strip, strip)
                    total = src[pl.ds(start, strip), :].astype(jnp.float32)
                else:
                    start = pl.multiple_of(dp * length, length)
                    total = src[at, pl.ds(start, length)].astype(jnp.float32)
                for hop in range(1, size_dp):
                    total += slots[hop, at, :].astype(jnp.float32)
                dst[at, :] = total
                return carry

            lax.fori_loop(0, height // strip, add, 0)


def line_call(
    name, cid, partial, ins, out_types, step, rows, width, chunks, nr, ng, time, sides=()
):
    piece = rows // chunks
    out_shape = []
    if ng:
        out_shape.append(jax.ShapeDtypeStruct((2 * ng * rows, width), jnp.bfloat16))
    out_shape += out_types
    dma = pltpu.SemaphoreType.DMA
    scratch = []
    size_dp = lax.axis_size("dp")
    for kind, axis, values in sides:
        shape = list(values.shape)
        scratch += [dma((size_dp,)), dma((size_dp,))]
        if kind == "gather":
            shape[axis] *= size_dp
            out_shape.append(jax.ShapeDtypeStruct(tuple(shape), values.dtype))
            scratch.append(pltpu.VMEM((16, 128), values.dtype))
        else:
            shape[axis] //= size_dp
            out_shape.append(jax.ShapeDtypeStruct(tuple(shape), jnp.float32))
            scratch.append(pltpu.VMEM((size_dp, *shape), values.dtype))
    if nr:
        scratch += [pltpu.VMEM((nr, chunks, piece, width), jnp.bfloat16)] * 4
        scratch += [dma((nr, chunks))] * 5
    if ng:
        scratch += [dma((ng, chunks))] * 6
    args = ([partial] if nr else []) + list(ins) + [side[2] for side in sides]
    vmem = pl.BlockSpec(memory_space=pltpu.VMEM)
    call = pl.pallas_call(
        functools.partial(
            line_kernel,
            nr,
            ng,
            chunks,
            rows,
            width,
            len(ins),
            len(out_types),
            step,
            tuple(side[:2] for side in sides),
        ),
        out_shape=out_shape,
        in_specs=[vmem] * len(args),
        out_specs=[vmem] * len(out_shape),
        scratch_shapes=scratch,
        compiler_params=pltpu.CompilerParams(
            collective_id=cid, has_side_effects=True, vmem_limit_bytes=VMEM_CAP
        ),
        cost_estimate=cost_of(time),
        name=name,
    )
    return list(call(*args))


def head_stats_kernel(block, tile, table_ref, final_ref, wanted_ref, edge_ref, exp_ref, top_ref, sum_ref, pick_ref):
    j = pl.program_id(0)
    tokens = final_ref.shape[0]
    place = j * block + lax.broadcasted_iota(jnp.int32, (block, 1), 0)
    valid = place < edge_ref[0]

    def one(i, carry):
        at = pl.ds(i * tile, tile)
        logits = lax.dot_general(
            table_ref[...],
            final_ref[at, :],
            (((1,), (1,)), ((), ())),
            preferred_element_type=jnp.float32,
        )
        logits = jnp.where(valid, logits, MASKED)
        top = jnp.max(logits, axis=0, keepdims=True)
        weights = jnp.exp(logits - top)
        exp_ref[:, at] = weights.astype(jnp.bfloat16)
        top_ref[0, :, at] = top
        sum_ref[0, :, at] = jnp.sum(weights, axis=0, keepdims=True)
        pick_ref[0, :, at] = jnp.sum(
            jnp.where(place == wanted_ref[:, at], logits, 0.0), axis=0, keepdims=True
        )
        return carry

    for i in range(tokens // tile):
        one(i, 0)


def head_stats(table, final, wanted, edge, block, tile=512):
    rows, width = table.shape
    tokens = final.shape[0]
    steps = pl.cdiv(rows, block)
    row = jax.ShapeDtypeStruct((steps, 1, tokens), jnp.float32)
    row_spec = pl.BlockSpec((1, 1, tokens), lambda j: (j, 0, 0))
    return pl.pallas_call(
        functools.partial(head_stats_kernel, block, tile),
        grid=(steps,),
        out_shape=[jax.ShapeDtypeStruct((steps * block, tokens), jnp.bfloat16), row, row, row],
        in_specs=[
            pl.BlockSpec((block, width), lambda j: (j, 0)),
            pl.BlockSpec((tokens, width), lambda j: (0, 0)),
            pl.BlockSpec((1, tokens), lambda j: (0, 0)),
            pl.BlockSpec(memory_space=pltpu.SMEM),
        ],
        out_specs=[pl.BlockSpec((block, tokens), lambda j: (j, 0)), row_spec, row_spec, row_spec],
        compiler_params=pltpu.CompilerParams(vmem_limit_bytes=56 * 2**20),
        cost_estimate=pl.CostEstimate(
            flops=2 * rows * width * tokens,
            bytes_accessed=2 * rows * (width + tokens),
            transcendentals=rows * tokens,
        ),
        name="head_stats",
    )(table, final, wanted, edge)


def head_back_kernel(rows, block, tile, exp_ref, table_ref, final_ref, scale_ref, weight_ref, wanted_ref, grad_ref, dfinal_ref, dl_ref, sum_ref):
    j = pl.program_id(0)
    tokens = final_ref.shape[0]
    place = j * block + lax.broadcasted_iota(jnp.int32, (block, 1), 0)

    @pl.when(j == 0)
    def _():
        sum_ref[...] = jnp.zeros_like(sum_ref)

    table = jnp.where(place < rows, table_ref[...], jnp.zeros_like(table_ref))

    def one(i, carry):
        at = pl.ds(i * tile, tile)
        weight = weight_ref[:, at]
        dl = exp_ref[:, at].astype(jnp.float32) * scale_ref[0, :, at]
        dl = dl - jnp.where(place == wanted_ref[:, at], weight, 0.0)
        dl = dl.astype(jnp.bfloat16)
        dl_ref[:, at] = dl
        sum_ref[at, :] += lax.dot_general(
            dl, table, (((0,), (0,)), ((), ())), preferred_element_type=jnp.float32
        )
        return carry

    for i in range(tokens // tile):
        one(i, 0)

    strip = block // max(1, block // 256)

    def two(i, carry):
        at = pl.ds(i * strip, strip)
        grad_ref[at, :] = jnp.dot(
            dl_ref[at, :], final_ref[...], preferred_element_type=jnp.float32
        ).astype(jnp.bfloat16)
        return carry

    for i in range(block // strip):
        two(i, 0)

    @pl.when(j == pl.num_programs(0) - 1)
    def _():
        dfinal_ref[...] = sum_ref[...].astype(jnp.bfloat16)


def head_back(exps, table, final, scale, weight, wanted, block, tile=256):
    rows, width = table.shape
    tokens = final.shape[0]
    steps = pl.cdiv(rows, block)
    return pl.pallas_call(
        functools.partial(head_back_kernel, rows, block, tile),
        grid=(steps,),
        out_shape=[
            jax.ShapeDtypeStruct((rows, width), jnp.bfloat16),
            jax.ShapeDtypeStruct((tokens, width), jnp.bfloat16),
        ],
        in_specs=[
            pl.BlockSpec((block, tokens), lambda j: (j, 0)),
            pl.BlockSpec((block, width), lambda j: (j, 0)),
            pl.BlockSpec((tokens, width), lambda j: (0, 0)),
            pl.BlockSpec((1, 1, tokens), lambda j: (j, 0, 0)),
            pl.BlockSpec((1, tokens), lambda j: (0, 0)),
            pl.BlockSpec((1, tokens), lambda j: (0, 0)),
        ],
        out_specs=[
            pl.BlockSpec((block, width), lambda j: (j, 0)),
            pl.BlockSpec((tokens, width), lambda j: (0, 0)),
        ],
        scratch_shapes=[
            pltpu.VMEM((block, tokens), jnp.bfloat16),
            pltpu.VMEM((tokens, width), jnp.float32),
        ],
        compiler_params=pltpu.CompilerParams(vmem_limit_bytes=60 * 2**20),
        cost_estimate=pl.CostEstimate(
            flops=4 * rows * width * tokens,
            bytes_accessed=2 * rows * (2 * width + tokens),
            transcendentals=0,
        ),
        name="head_back",
    )(exps, table, final, scale, weight, wanted)


def small_gather_kernel(axis, count, src_ref, out_ref, send, recv):
    dp = lax.axis_index("dp")
    mp = lax.axis_index("mp")
    me = dp if axis == "dp" else mp

    def device(peer):
        return (peer, mp) if axis == "dp" else (dp, peer)

    barrier = pltpu.get_barrier_semaphore()
    for hop in range(1, count):
        pl.semaphore_signal(
            barrier, inc=1, device_id=device(lax.rem(me + hop, count)), device_id_type=MESH
        )
    pl.semaphore_wait(barrier, count - 1)
    copies = []
    for hop in range(1, count):
        peer = lax.rem(me + hop, count)
        copy = pltpu.make_async_remote_copy(
            src_ref=src_ref,
            dst_ref=out_ref.at[me],
            send_sem=send.at[hop],
            recv_sem=recv.at[hop],
            device_id=device(peer),
            device_id_type=MESH,
        )
        copy.start()
        copies.append(copy)
    out_ref[me] = src_ref[...]
    for copy in copies:
        copy.wait()


def small_gather(name, cid, values, axis):
    count = lax.axis_size(axis)
    vmem = pl.BlockSpec(memory_space=pltpu.VMEM)
    return pl.pallas_call(
        functools.partial(small_gather_kernel, axis, count),
        out_shape=jax.ShapeDtypeStruct((count,) + values.shape, values.dtype),
        in_specs=[vmem],
        out_specs=vmem,
        scratch_shapes=[pltpu.SemaphoreType.DMA((count,)), pltpu.SemaphoreType.DMA((count,))],
        compiler_params=pltpu.CompilerParams(collective_id=cid, has_side_effects=True),
        cost_estimate=cost_of(6),
        name=name,
    )(values)


def packed(pieces):
    flat = []
    for piece in pieces:
        piece = piece.reshape(-1)
        flat.append(jnp.pad(piece, (0, -piece.size % 128)))
    flat = jnp.concatenate(flat)
    return jnp.pad(flat, (0, -flat.size % 1024)).reshape(-1, 128)


def unpacked(rows, shapes):
    flat = rows.reshape(-1)
    pieces, at = [], 0
    for shape in shapes:
        size = math.prod(shape)
        pieces.append(flat[at : at + size].reshape(shape))
        at += size + -size % 128
    return pieces


def small_sum(name, cid, over_dp, over_mp, over_all):
    first = small_gather(name + "_dp", cid, packed(over_dp + over_all), "dp")
    first = unpacked(jnp.sum(first, axis=0), [v.shape for v in over_dp + over_all])
    rest = first[len(over_dp) :]
    second = small_gather(name + "_mp", cid + 1, packed(over_mp + rest), "mp")
    second = unpacked(jnp.sum(second, axis=0), [v.shape for v in over_mp + over_all])
    return first[: len(over_dp)], second[: len(over_mp)], second[len(over_mp) :]


def lookup_kernel(count_ref, key_ref, table_ref, out_ref, rows_ref):
    spots = rows_ref.shape[0]
    rows_ref[...] = jnp.zeros_like(rows_ref)

    def one(i, carry):
        key = key_ref[i]
        rows_ref[pl.ds(key % spots, 1), :] = table_ref[pl.ds(key // spots, 1), :]
        return carry

    lax.fori_loop(0, count_ref[0], one, 0)

    def narrow(i, carry):
        at = pl.ds(pl.multiple_of(i * 256, 256), 256)
        out_ref[at, :] = rows_ref[at, :].astype(jnp.bfloat16)
        return carry

    lax.fori_loop(0, spots // 256, narrow, 0)


def lookup(keys, count, table, spots):
    width = table.shape[1]
    smem = pl.BlockSpec(memory_space=pltpu.SMEM)
    vmem = pl.BlockSpec(memory_space=pltpu.VMEM)
    return pl.pallas_call(
        lookup_kernel,
        out_shape=jax.ShapeDtypeStruct((spots, width), jnp.bfloat16),
        in_specs=[smem, smem, vmem],
        out_specs=vmem,
        scratch_shapes=[pltpu.VMEM((spots, width), jnp.float32)],
        compiler_params=pltpu.CompilerParams(vmem_limit_bytes=VMEM_CAP),
        cost_estimate=cost_of(20),
        name="lookup",
    )(count, keys, table)


def scatter_kernel(count_ref, key_ref, head_ref, rows_in_ref, grad_ref, rows_ref):
    spots = rows_ref.shape[0]
    vocab = grad_ref.shape[0]

    def widen(i, carry):
        at = pl.ds(pl.multiple_of(i * 256, 256), 256)
        rows_ref[at, :] = rows_in_ref[at, :].astype(jnp.float32)
        return carry

    lax.fori_loop(0, spots // 256, widen, 0)
    grad_ref[...] = head_ref[...].astype(jnp.float32)

    def one(i, carry):
        key = key_ref[i]
        grad_ref[pl.ds(key // spots, 1), :] += rows_ref[pl.ds(key % spots, 1), :]
        return carry

    lax.fori_loop(0, count_ref[0], one, 0)


def scatter(keys, count, head_grad, rows):
    spots, width = rows.shape
    vocab = head_grad.shape[0]
    smem = pl.BlockSpec(memory_space=pltpu.SMEM)
    vmem = pl.BlockSpec(memory_space=pltpu.VMEM)
    return pl.pallas_call(
        scatter_kernel,
        out_shape=jax.ShapeDtypeStruct((vocab, width), jnp.float32),
        in_specs=[smem, smem, vmem, vmem],
        out_specs=vmem,
        scratch_shapes=[pltpu.VMEM((spots, width), jnp.float32)],
        compiler_params=pltpu.CompilerParams(vmem_limit_bytes=VMEM_CAP),
        cost_estimate=cost_of(23),
        name="scatter",
    )(count, keys, head_grad, rows)


def norm_parts(values):
    centre = jnp.mean(values, axis=-1, keepdims=True)
    centred = values - centre
    scale = lax.rsqrt(jnp.mean(centred * centred, axis=-1, keepdims=True) + EPS_NORM)
    return centred * scale, scale


def norm_pull(values, gain, upstream):
    normed, scale = norm_parts(values)
    weighted = upstream * gain
    pulled = scale * (
        weighted
        - jnp.mean(weighted, axis=-1, keepdims=True)
        - normed * jnp.mean(weighted * normed, axis=-1, keepdims=True)
    )
    return (
        pulled,
        jnp.sum(upstream * normed, axis=0, keepdims=True),
        jnp.sum(upstream, axis=0, keepdims=True),
    )


def step_first(total, at, ins, outs):
    stream, norms = ins
    normed, scale = norm_parts(stream[at, :].astype(jnp.float32))
    return normed * norms[0:1, :] + norms[1:2, :]


def step_lookup(total, at, ins, outs):
    outs[0][at, :] = total.astype(jnp.bfloat16)


def step_forward(row, total, at, ins, outs):
    stream, norms = ins
    values = stream[at, :].astype(jnp.float32) + total
    outs[0][at, :] = values
    normed, scale = norm_parts(values)
    return normed * norms[row : row + 1, :] + norms[row + 1 : row + 2, :]


def step_backward(row, total, at, ins, outs):
    stream, norms = ins[:2]
    pulled, dgain, dshift = norm_pull(
        stream[at, :].astype(jnp.float32), norms[row : row + 1, :], total
    )
    if len(ins) > 2:
        pulled = pulled + ins[2][at, :]
    outs[0][at, :] = pulled.astype(outs[0].dtype)
    first = at.start == 0

    @pl.when(first)
    def _():
        outs[1][...] = jnp.zeros_like(outs[1])

    outs[1][0:1, :] += dgain
    outs[1][1:2, :] += dshift
    return pulled


def step_pass(total, at, ins, outs):
    return ins[0][at, :]


def gelu_tanh(values):
    return jax.nn.gelu(values, approximate=True)


def score_block(mixed, starts):
    place = jnp.arange(mixed.shape[0], dtype=jnp.int32)
    allowed = (place[None, :] <= place[:, None]) & (place[None, :] >= starts[:, None])
    raw = jnp.einsum(
        "qhe,khe->hqk", mixed[:, :, 0], mixed[:, :, 1], preferred_element_type=jnp.float32
    )
    return jnp.where(allowed[None], raw * HD ** (-0.5), MASKED)


def attend_forward(mixed, starts):
    scores = score_block(mixed, starts)
    highest = jnp.max(scores, axis=-1, keepdims=True)
    weights = jnp.exp(scores - highest)
    totals = jnp.sum(weights, axis=-1, keepdims=True)
    probs = (weights / totals).astype(jnp.bfloat16)
    result = jnp.einsum(
        "hqk,khe->qhe", probs, mixed[:, :, 2], preferred_element_type=jnp.float32
    )
    return (result.astype(jnp.bfloat16), highest[:, :, 0] + jnp.log(totals[:, :, 0]))


def attend_backward(mixed, starts, log_rows, upstream):
    scores = score_block(mixed, starts)
    probs = jnp.exp(scores - log_rows[:, :, None])
    dprobs = jnp.einsum(
        "qhe,khe->hqk", upstream, mixed[:, :, 2], preferred_element_type=jnp.float32
    )
    dvalues = jnp.einsum(
        "hqk,qhe->khe", probs.astype(jnp.bfloat16), upstream, preferred_element_type=jnp.float32
    )
    inner = jnp.sum(probs * dprobs, axis=-1, keepdims=True)
    dscores = (probs * (dprobs - inner)).astype(jnp.bfloat16)
    dquery = jnp.einsum(
        "hqk,khe->qhe", dscores, mixed[:, :, 1], preferred_element_type=jnp.float32
    ) * HD ** (-0.5)
    dkeys = jnp.einsum(
        "hqk,qhe->khe", dscores, mixed[:, :, 0], preferred_element_type=jnp.float32
    ) * HD ** (-0.5)
    return jnp.stack([dquery, dkeys, dvalues], axis=2).astype(jnp.bfloat16)


def local(
    token_ids,
    targets,
    starts,
    sources,
    embedding,
    w_qkv,
    w_out,
    w_fc,
    w_proj,
    norm_params,
    rows_table,
    cols_table,
    rows_qkv,
    cols_qkv,
    rows_out,
    cols_out,
    rows_fc,
    cols_fc,
    rows_proj,
    cols_proj,
    second_norms,
):
    bf16 = jnp.bfloat16
    f32 = jnp.float32
    size_mp = lax.axis_size("mp")
    size_dp = lax.axis_size("dp")
    dp = lax.axis_index("dp")
    mp = lax.axis_index("mp")
    tokens = token_ids.shape[0]
    seqs = tokens // LEN
    chips = size_mp // 2
    near = chips // seqs
    sharers = size_mp // seqs
    rows = tokens // size_mp
    vocab, part_width = embedding.shape
    width = part_width * size_dp
    first_row = mp * vocab
    spots = tokens * size_dp
    chunks_full = max(1, min(8, rows // 32))
    chunks_near = max(1, min(4, rows // 32))

    both = jnp.stack([token_ids, sources]).reshape(-1, 128)
    both = small_gather("gather_ids", 0, both, "dp").reshape(size_dp, 2, tokens)
    all_ids = both[:, 0]
    all_sources = both[:, 1].reshape(-1)
    counts = jnp.sum(
        (all_sources[:, None] == jnp.arange(NSRC, dtype=jnp.int32)[None, :]).astype(f32), axis=0
    )


    def own_and_twins(weight, axis):
        weight = weight.astype(bf16)
        found = [weight]
        for turn in range(1, seqs):
            shift = [(i, (i + turn * sharers) % size_mp) for i in range(size_mp)]
            found.append(lax.ppermute(weight, "mp", shift))
        return jnp.concatenate(found, axis=axis) if seqs > 1 else weight

    pair_qkv = own_and_twins(w_qkv, 1)
    pair_out = own_and_twins(w_out, 0)
    pair_fc = own_and_twins(w_fc, 1)
    pair_proj = own_and_twins(w_proj, 0)
    wide_table = lax.all_gather(embedding.astype(bf16), "dp", axis=1, tiled=True)

    place = (
        (jnp.arange(size_mp, dtype=jnp.int32) * size_dp)[None, :, None] * rows
        + (jnp.arange(size_dp, dtype=jnp.int32) * rows)[:, None, None]
        + jnp.arange(rows, dtype=jnp.int32)[None, None, :]
    ).reshape(size_dp, tokens)
    local_ids = all_ids - first_row
    inside = (local_ids >= 0) & (local_ids < vocab)
    keys = jnp.where(inside, local_ids * spots + place, jnp.iinfo(jnp.int32).max)
    keys = jnp.sort(keys.reshape(-1))
    owned = jnp.sum(inside.astype(jnp.int32)).reshape(1)
    found = lookup(keys, owned, embedding, spots)
    picked_rows, wide_qkv, wide_out, wide_fc = line_call(
        "rs_lookup",
        1,
        found,
        [],
        [jax.ShapeDtypeStruct((size_dp * rows, part_width), bf16)],
        step_lookup,
        size_dp * rows,
        part_width,
        chunks_full,
        chips,
        0,
        50,
        [("gather", 0, pair_qkv), ("gather", 1, pair_out), ("gather", 0, pair_fc)],
    )
    stream0 = lax.all_to_all(
        picked_rows.reshape(size_dp, rows, part_width), "dp", 0, 0, tiled=False
    )
    stream0 = jnp.swapaxes(stream0, 0, 1).reshape(rows, width)

    row_f32 = jax.ShapeDtypeStruct((rows, width), f32)
    pair_f32 = jax.ShapeDtypeStruct((8, width), f32)
    (inner_one,) = line_call(
        "ag_inner1",
        2,
        None,
        [stream0, norm_params],
        [],
        step_first,
        rows,
        width,
        chunks_near,
        0,
        near,
        17,
    )
    heads = wide_qkv.shape[1] // (3 * HD)
    my_starts = row_slice(starts, (mp // sharers) * LEN, LEN)
    mixed = jnp.dot(inner_one, wide_qkv, preferred_element_type=f32).astype(bf16)
    mixed = mixed.reshape(LEN, heads, 3, HD)
    attended, log_sums = attend_forward(mixed, my_starts)
    attended = attended.reshape(LEN, heads * HD)
    partial = jnp.dot(attended, wide_out, preferred_element_type=f32).astype(bf16)
    inner_two, stream1, wide_proj = line_call(
        "attn_sum",
        3,
        partial,
        [stream0, norm_params],
        [row_f32],
        functools.partial(step_forward, 2),
        rows,
        width,
        chunks_near,
        near,
        near,
        32,
        [("gather", 1, pair_proj)],
    )
    before = jnp.dot(inner_two, wide_fc, preferred_element_type=f32)
    hidden = gelu_tanh(before).astype(bf16)
    partial = jnp.dot(hidden, wide_proj, preferred_element_type=f32).astype(bf16)
    final, stream2 = line_call(
        "mlp_sum",
        4,
        partial,
        [stream1, norm_params],
        [row_f32],
        functools.partial(step_forward, 4),
        rows,
        width,
        chunks_full,
        near,
        chips,
        58,
    )

    edge = jnp.clip(VREAL - first_row, 0, vocab).astype(jnp.int32).reshape(1)
    wanted = targets - first_row
    wanted = jnp.where((wanted >= 0) & (wanted < vocab), wanted, -1).reshape(1, tokens)
    block = 640
    exps, tops, sums, picks = head_stats(wide_table, final, wanted, edge, block)
    tops = tops[:, 0]
    top = jnp.max(tops, axis=0)
    total = jnp.sum(sums[:, 0] * jnp.exp(tops - top[None, :]), axis=0)
    pick = jnp.sum(picks[:, 0], axis=0)
    stats = small_gather("gather_stats", 5, packed([top, total, pick]), "mp")
    stats = stats.reshape(size_mp, -1)[:, : 3 * tokens].reshape(size_mp, 3, tokens)
    highest = jnp.max(stats[:, 0], axis=0)
    log_total = highest + jnp.log(
        jnp.sum(stats[:, 1] * jnp.exp(stats[:, 0] - highest[None, :]), axis=0)
    )
    token_loss = log_total - jnp.sum(stats[:, 2], axis=0)
    member = (sources[:, None] == jnp.arange(NSRC, dtype=jnp.int32)[None, :]).astype(f32)
    loss_part = jnp.sum(member * token_loss[:, None], axis=0)
    weight = jnp.sum(member / (NSRC * jnp.maximum(counts, 1.0))[None, :], axis=1)
    scale = jnp.exp(tops - log_total[None, :]) * weight[None, :]
    table_grad, dfinal = head_back(
        exps, wide_table, final, scale[:, None, :], weight[None, :], wanted, block
    )
    head_grad = lax.psum_scatter(table_grad, "dp", scatter_dimension=1, tiled=True)

    dbranch2, dstream2, norm3 = line_call(
        "final_back",
        6,
        dfinal,
        [stream2, norm_params],
        [row_f32, pair_f32],
        functools.partial(step_backward, 4),
        rows,
        width,
        chunks_full,
        chips,
        near,
        60,
    )
    grad_proj = jnp.einsum("tf,td->fd", hidden, dbranch2, preferred_element_type=f32).astype(bf16)
    dhidden = jnp.einsum("td,fd->tf", dbranch2, wide_proj, preferred_element_type=f32)
    unused, gelu_pull = jax.vjp(gelu_tanh, before)
    dbefore = gelu_pull(dhidden)[0].astype(bf16)
    partial = jnp.einsum("tf,df->td", dbefore, wide_fc, preferred_element_type=f32).astype(bf16)
    dbranch1, dstream1, norm2 = line_call(
        "mlp_back",
        7,
        partial,
        [stream1, norm_params, dstream2],
        [row_f32, pair_f32],
        functools.partial(step_backward, 2),
        rows,
        width,
        chunks_near,
        near,
        near,
        34,
    )
    grad_fc = jnp.einsum("td,tf->df", inner_two, dbefore, preferred_element_type=f32).astype(bf16)
    grad_out = jnp.einsum("tf,td->fd", attended, dbranch1, preferred_element_type=f32).astype(bf16)
    dattended = jnp.einsum("td,fd->tf", dbranch1, wide_out, preferred_element_type=f32)
    dattended = dattended.astype(bf16).reshape(LEN, heads, HD)
    dmixed = attend_backward(mixed, my_starts, log_sums, dattended)
    dmixed = dmixed.reshape(LEN, heads * 3 * HD)
    partial = jnp.einsum("tc,dc->td", dmixed, wide_qkv, preferred_element_type=f32).astype(bf16)
    dstream0, norm1, grad_proj, grad_out = line_call(
        "attn_back",
        8,
        partial,
        [stream0, norm_params, dstream1],
        [jax.ShapeDtypeStruct((rows, width), bf16), pair_f32],
        functools.partial(step_backward, 0),
        rows,
        width,
        chunks_near,
        near,
        0,
        28,
        [("scatter", 1, grad_proj), ("scatter", 1, grad_out)],
    )
    grad_qkv = jnp.einsum("td,tc->dc", inner_one, dmixed, preferred_element_type=f32).astype(bf16)

    sent = jnp.swapaxes(dstream0.reshape(rows, size_dp, part_width), 0, 1)
    sent = lax.all_to_all(sent, "dp", 0, 0, tiled=False).reshape(size_dp * rows, part_width)
    drows, grad_fc, grad_qkv = line_call(
        "ag_lookup",
        9,
        None,
        [sent],
        [],
        step_pass,
        size_dp * rows,
        part_width,
        chunks_full,
        0,
        chips,
        45,
        [("scatter", 0, grad_fc), ("scatter", 0, grad_qkv)],
    )

    def to_owner(share, axis):
        pieces = jnp.split(share, seqs, axis=axis)
        mine = pieces[0]
        for turn in range(1, seqs):
            back = [(i, (i - turn * sharers) % size_mp) for i in range(size_mp)]
            mine = mine + lax.ppermute(pieces[turn].astype(bf16), "mp", back).astype(f32)
        return mine

    grad_proj = to_owner(grad_proj, 0)
    grad_out = to_owner(grad_out, 0)
    grad_fc = to_owner(grad_fc, 1)
    grad_qkv = to_owner(grad_qkv, 1)
    grad_table = scatter(keys, owned, head_grad, drows)

    beta = 1.0 - STEP ** (-0.8)
    weights = (embedding, w_qkv, w_out, w_fc, w_proj)
    grads = (grad_table, grad_qkv, grad_out, grad_fc, grad_proj)
    rows_old = (rows_table, rows_qkv, rows_out, rows_fc, rows_proj)
    cols_old = (cols_table, cols_qkv, cols_out, cols_fc, cols_proj)
    row_span = (size_mp, size_dp, size_mp, size_dp, size_mp)
    col_span = (size_dp, size_mp, size_dp, size_mp, size_dp)
    squares = [gradient * gradient + EPS_ONE for gradient in grads]
    row_parts = [jnp.sum(square, axis=1) for square in squares]
    col_parts = [jnp.sum(square, axis=0) for square in squares]
    square_sums = jnp.stack([jnp.sum(part) for part in col_parts])
    weight_sums = jnp.stack([jnp.sum(value * value) for value in weights])
    old_sums = jnp.stack([jnp.sum(old) / span for old, span in zip(rows_old, col_span)])
    norm_partial = jnp.concatenate([norm1[:2], norm2[:2], norm3[:2]])
    on_dp, on_mp, on_all = small_sum(
        "sum_squares",
        10,
        [col_parts[1], col_parts[3], row_parts[0], row_parts[2], row_parts[4], loss_part],
        [row_parts[1], row_parts[3], col_parts[0], col_parts[2], col_parts[4]],
        [square_sums, weight_sums, old_sums, norm_partial],
    )
    square_sums, weight_sums, old_sums, grad_norms = on_all
    loss_sums = on_dp[5]
    row_full = (on_dp[2], on_mp[0], on_dp[3], on_mp[1], on_dp[4])
    col_full = (on_mp[2], on_dp[0], on_mp[3], on_dp[1], on_mp[4])
    rows_new = []
    cols_new = []
    steps = []
    entries = []
    for index in range(5):
        full_rows = grads[index].shape[0] * row_span[index]
        full_cols = grads[index].shape[1] * col_span[index]
        entries.append(full_rows * full_cols)
        rows_next = beta * rows_old[index] + (1.0 - beta) * row_full[index] / full_cols
        cols_next = beta * cols_old[index] + (1.0 - beta) * col_full[index] / full_rows
        mean = beta * old_sums[index] / full_rows + (1.0 - beta) * (
            square_sums[index] / (full_rows * full_cols)
        )
        rows_new.append(rows_next)
        cols_new.append(cols_next)
        steps.append(
            grads[index] * lax.rsqrt(rows_next[:, None] * cols_next[None, :] / mean)
        )
    step_part = jnp.stack([jnp.sum(piece * piece) for piece in steps])
    unused, unused, (step_sq,) = small_sum("sum_steps", 12, [], [], [step_part])
    updated = []
    for index in range(5):
        clipped = steps[index] / jnp.maximum(1.0, jnp.sqrt(step_sq[index] / entries[index]) / CLIP)
        rate = RHO * jnp.sqrt(weight_sums[index] / entries[index])
        updated.append(weights[index] - rate * clipped)
    second_new = beta * second_norms + (1.0 - beta) * (grad_norms * grad_norms + EPS_ONE)
    norm_steps = grad_norms * lax.rsqrt(second_new)
    norm_steps = norm_steps / jnp.maximum(1.0, jnp.sqrt(jnp.mean(norm_steps * norm_steps)) / CLIP)
    norms_new = norm_params - RHO * jnp.sqrt(jnp.mean(norm_params * norm_params)) * norm_steps
    return (
        loss_sums,
        counts,
        grad_table,
        rows_new[0],
        cols_new[0],
        updated[0],
        grad_qkv,
        rows_new[1],
        cols_new[1],
        updated[1],
        grad_out,
        rows_new[2],
        cols_new[2],
        updated[2],
        grad_fc,
        rows_new[3],
        cols_new[3],
        updated[3],
        grad_proj,
        rows_new[4],
        cols_new[4],
        updated[4],
        grad_norms,
        second_new,
        norms_new,
    )


def solution(mesh):
    placed = (
        P("dp"),
        P("dp"),
        P("dp"),
        P("dp"),
        P("mp", "dp"),
        P("dp", "mp"),
        P("mp", "dp"),
        P("dp", "mp"),
        P("mp", "dp"),
        P(),
        P("mp"),
        P("dp"),
        P("dp"),
        P("mp"),
        P("mp"),
        P("dp"),
        P("dp"),
        P("mp"),
        P("mp"),
        P("dp"),
        P(),
    )
    return jax.shard_map(
        local,
        mesh=mesh,
        in_specs=placed,
        out_specs=(
            P(),
            P(),
            P("mp", "dp"),
            P("mp"),
            P("dp"),
            P("mp", "dp"),
            P("dp", "mp"),
            P("dp"),
            P("mp"),
            P("dp", "mp"),
            P("mp", "dp"),
            P("mp"),
            P("dp"),
            P("mp", "dp"),
            P("dp", "mp"),
            P("dp"),
            P("mp"),
            P("dp", "mp"),
            P("mp", "dp"),
            P("mp"),
            P("dp"),
            P("mp", "dp"),
            P(),
            P(),
            P(),
        ),
        check_vma=False,
    )
```

```python
import functools
import math

import jax
import jax.numpy as jnp
from jax import lax
from jax.experimental import pallas as pl
from jax.experimental.pallas import tpu as pltpu
from jax.sharding import PartitionSpec as P

HD = 64
VREAL = 50257
LEN = 1024
NSRC = 4
STEP = 10


EPS_NORM = 1e-05
EPS_ONE = 1e-30
CLIP = 1.0
RHO = 0.5
MASKED = -1e30
MESH = pl.DeviceIdType.MESH
VMEM_CAP = 56 * 2**20


def cost_of(time):
    return pl.CostEstimate(
        flops=time * 1000000000, bytes_accessed=time * 3000000, transcendentals=0
    )


def row_slice(values, start, count):
    return lax.dynamic_slice_in_dim(values, start, count, 0)


def line_kernel(nr, ng, chunks, rows, width, n_in, n_out, step, sides, *refs):
    part = refs[0] if nr else None
    first = 1 if nr else 0
    ins = refs[first : first + n_in]
    refs = refs[first + n_in :]
    side_ins, refs = refs[: len(sides)], refs[len(sides) :]
    if ng:
        whole, refs = refs[0], refs[1:]
    outs = refs[:n_out]
    refs = refs[n_out:]
    side_outs, scratch = refs[: len(sides)], refs[len(sides) :]
    side_scratch, scratch = scratch[: 3 * len(sides)], scratch[3 * len(sides) :]
    size_dp = lax.axis_size("dp")
    dp = lax.axis_index("dp")
    mp = lax.axis_index("mp")
    z = mp // 2
    core = lax.rem(mp, 2)
    other = mp + 1 - 2 * core
    piece = rows // chunks
    most = max(nr, ng)
    zb = lax.rem(z, most)
    if nr:
        zr = lax.rem(z, nr)
        last_r = nr - 1
    if ng:
        zg = lax.rem(z, ng)
        last_g = ng - 1

    barrier = pltpu.get_barrier_semaphore()
    pl.semaphore_signal(barrier, inc=1, device_id=(dp, other), device_id_type=MESH)

    @pl.when(zb > 0)
    def _():
        pl.semaphore_signal(barrier, inc=1, device_id=(dp, mp - 2), device_id_type=MESH)

    @pl.when(zb < most - 1)
    def _():
        pl.semaphore_signal(barrier, inc=1, device_id=(dp, mp + 2), device_id_type=MESH)

    if sides:
        for hop in range(1, size_dp):
            pl.semaphore_signal(
                barrier,
                inc=1,
                device_id=(lax.rem(dp + hop, size_dp), mp),
                device_id_type=MESH,
            )
    greeted = (size_dp if sides else 1) + (zb > 0).astype(jnp.int32) + (zb < most - 1).astype(jnp.int32)
    pl.semaphore_wait(barrier, greeted)

    def share(axis, length, which):
        at = pl.ds(pl.multiple_of(which * length, length), length)
        return (at, slice(None)) if axis == 0 else (slice(None), at)

    side_copies = []
    for index, (kind, axis) in enumerate(sides):
        src, dst = side_ins[index], side_outs[index]
        send, recv, slots = side_scratch[3 * index : 3 * index + 3]
        length = (src if kind == "gather" else dst).shape[axis]
        for hop in range(1, size_dp):
            peer = lax.rem(dp + hop, size_dp)
            if kind == "gather":
                source, target = src, dst.at[share(axis, length, dp)]
            else:
                source, target = src.at[share(axis, length, peer)], slots.at[hop]
            copy = pltpu.make_async_remote_copy(
                src_ref=source,
                dst_ref=target,
                send_sem=send.at[hop],
                recv_sem=recv.at[hop],
                device_id=(peer, mp),
                device_id_type=MESH,
            )
            side_copies.append(copy)
            if nr == 0:
                copy.start()

    if nr:
        half, from_left, from_right, going = scratch[:4]
        half_send, half_recv, rs_send, left_recv, right_recv = scratch[4:9]
        scratch = scratch[9:]
    if ng:
        core_send, core_recv, to_right, to_left, ag_left, ag_right = scratch[:6]

    def part_rows(block, k):
        return pl.ds(pl.multiple_of(block * rows + k * piece, piece), piece)

    def remote(src, dst, send, recv, target):
        return pltpu.make_async_remote_copy(
            src_ref=src,
            dst_ref=dst,
            send_sem=send,
            recv_sem=recv,
            device_id=(dp, target),
            device_id_type=MESH,
        )

    if nr:

        def half_copy(dest, k):
            return remote(
                part.at[part_rows(2 * dest + 1 - core, k)],
                half.at[dest, k],
                half_send.at[dest, k],
                half_recv.at[dest, k],
                other,
            )

        def send_halves(k, carry):
            for dest in range(nr):
                half_copy(dest, k).start()
            return carry

        lax.fori_loop(0, chunks, send_halves, 0)
        for copy in side_copies:
            copy.start()

        def right_copy(dest, k):
            return remote(
                going.at[dest, k],
                from_left.at[dest, k],
                rs_send.at[dest, k],
                left_recv.at[dest, k],
                mp + 2,
            )

        def left_copy(dest, k):
            return remote(
                going.at[dest, k],
                from_right.at[dest, k],
                rs_send.at[dest, k],
                right_recv.at[dest, k],
                mp - 2,
            )

        def chip_sum(dest, k):
            half_copy(dest, k).wait_recv()
            mine = part[part_rows(2 * dest + core, k), :].astype(jnp.float32)
            return mine + half[dest, k].astype(jnp.float32)

        def pass_right(dest, k):
            total = chip_sum(dest, k)

            @pl.when(zr == 0)
            def _():
                going[dest, k] = total.astype(jnp.bfloat16)

            @pl.when(zr > 0)
            def _():
                right_copy(dest, k).wait_recv()
                both = total + from_left[dest, k].astype(jnp.float32)
                going[dest, k] = both.astype(jnp.bfloat16)

            right_copy(dest, k).start()

        def pass_left(dest, k):
            total = chip_sum(dest, k)

            @pl.when(zr == last_r)
            def _():
                going[dest, k] = total.astype(jnp.bfloat16)

            @pl.when(zr < last_r)
            def _():
                left_copy(dest, k).wait_recv()
                both = total + from_right[dest, k].astype(jnp.float32)
                going[dest, k] = both.astype(jnp.bfloat16)

            left_copy(dest, k).start()

    if ng:

        def gathered(block, k, send, recv, target):
            where = whole.at[part_rows(2 * block + core, k)]
            return remote(where, where, send.at[block, k], recv.at[block, k], target)

        def core_copy(block, k):
            return gathered(block, k, core_send, core_recv, other)

        def ag_right_copy(block, k):
            return gathered(block, k, to_right, ag_left, mp + 2)

        def ag_left_copy(block, k):
            return gathered(block, k, to_left, ag_right, mp - 2)

    def own_rows(k):
        total = None
        if nr:
            total = chip_sum(zr, k)
            zero = jnp.zeros((piece, width), jnp.float32)

            @pl.when(zr > 0)
            def _():
                right_copy(zr, k).wait_recv()

            @pl.when(zr < last_r)
            def _():
                left_copy(zr, k).wait_recv()

            total += jnp.where(zr > 0, from_left[zr, k].astype(jnp.float32), zero)
            total += jnp.where(zr < last_r, from_right[zr, k].astype(jnp.float32), zero)
        at = pl.ds(pl.multiple_of(k * piece, piece), piece)
        ready = step(total, at, ins, outs)
        if ng:
            whole[part_rows(2 * zg + core, k), :] = ready.astype(whole.dtype)
            core_copy(zg, k).start()

            @pl.when(zg < last_g)
            def _():
                ag_right_copy(zg, k).start()

            @pl.when(zg > 0)
            def _():
                ag_left_copy(zg, k).start()

    def inside(k):
        return (k >= 0) & (k < chunks)

    def own_lag(chip):
        if not nr:
            return 0
        at = lax.rem(chip, nr)
        return jnp.maximum(at, last_r - at)

    def tick(now, carry):
        if nr:
            k_right = now - zr
            k_left = now - (last_r - zr)
            for far in range(last_r):

                @pl.when(inside(k_right) & (last_r - far > zr))
                def _():
                    pass_right(last_r - far, k_right)

                @pl.when(inside(k_left) & (far < zr))
                def _():
                    pass_left(far, k_left)

        k_own = now - own_lag(z)

        @pl.when(inside(k_own))
        def _():
            own_rows(k_own)

        if ng:
            for block in range(ng):
                k = now - (own_lag(z - zg + block) + jnp.abs(zg - block))

                @pl.when(inside(k) & (block < zg))
                def _():
                    ag_right_copy(block, k).wait_recv()
                    core_copy(block, k).start()

                    @pl.when(zg < last_g)
                    def _():
                        ag_right_copy(block, k).start()

                @pl.when(inside(k) & (block > zg))
                def _():
                    ag_left_copy(block, k).wait_recv()
                    core_copy(block, k).start()

                    @pl.when(zg > 0)
                    def _():
                        ag_left_copy(block, k).start()

        return carry

    ticks = chunks + (nr - 1 if nr else 0) + (ng - 1 if ng else 0)
    lax.fori_loop(0, ticks, tick, 0)

    def finish(k, carry):
        if nr:
            for block in range(nr):
                half_copy(block, k).wait_send()

                @pl.when(block != zr)
                def _():
                    right_copy(block, k).wait_send()

        if ng:
            for block in range(ng):
                core_copy(block, k).wait()

                @pl.when((zg < last_g) & (block <= zg))
                def _():
                    ag_right_copy(block, k).wait_send()

                @pl.when((zg > 0) & (block >= zg))
                def _():
                    ag_left_copy(block, k).wait_send()

        return carry

    lax.fori_loop(0, chunks, finish, 0)
    for index, (kind, axis) in enumerate(sides):
        if kind == "gather":
            length = side_ins[index].shape[axis]
            side_outs[index][share(axis, length, dp)] = side_ins[index][...]
    for copy in side_copies:
        copy.wait()
    for index, (kind, axis) in enumerate(sides):
        if kind == "scatter":
            src, dst = side_ins[index], side_outs[index]
            slots = side_scratch[3 * index + 2]
            strip = 128
            height = dst.shape[0]

            def add(i, carry):
                at = pl.ds(pl.multiple_of(i * strip, strip), strip)
                length = dst.shape[axis]
                if axis == 0:
                    start = pl.multiple_of(dp * length + i * strip, strip)
                    total = src[pl.ds(start, strip), :].astype(jnp.float32)
                else:
                    start = pl.multiple_of(dp * length, length)
                    total = src[at, pl.ds(start, length)].astype(jnp.float32)
                for hop in range(1, size_dp):
                    total += slots[hop, at, :].astype(jnp.float32)
                dst[at, :] = total
                return carry

            lax.fori_loop(0, height // strip, add, 0)


def line_call(
    name, cid, partial, ins, out_types, step, rows, width, chunks, nr, ng, time, sides=()
):
    piece = rows // chunks
    out_shape = []
    if ng:
        out_shape.append(jax.ShapeDtypeStruct((2 * ng * rows, width), jnp.bfloat16))
    out_shape += out_types
    dma = pltpu.SemaphoreType.DMA
    scratch = []
    size_dp = lax.axis_size("dp")
    for kind, axis, values in sides:
        shape = list(values.shape)
        scratch += [dma((size_dp,)), dma((size_dp,))]
        if kind == "gather":
            shape[axis] *= size_dp
            out_shape.append(jax.ShapeDtypeStruct(tuple(shape), values.dtype))
            scratch.append(pltpu.VMEM((16, 128), values.dtype))
        else:
            shape[axis] //= size_dp
            out_shape.append(jax.ShapeDtypeStruct(tuple(shape), jnp.float32))
            scratch.append(pltpu.VMEM((size_dp, *shape), values.dtype))
    if nr:
        scratch += [pltpu.VMEM((nr, chunks, piece, width), jnp.bfloat16)] * 4
        scratch += [dma((nr, chunks))] * 5
    if ng:
        scratch += [dma((ng, chunks))] * 6
    args = ([partial] if nr else []) + list(ins) + [side[2] for side in sides]
    vmem = pl.BlockSpec(memory_space=pltpu.VMEM)
    call = pl.pallas_call(
        functools.partial(
            line_kernel,
            nr,
            ng,
            chunks,
            rows,
            width,
            len(ins),
            len(out_types),
            step,
            tuple(side[:2] for side in sides),
        ),
        out_shape=out_shape,
        in_specs=[vmem] * len(args),
        out_specs=[vmem] * len(out_shape),
        scratch_shapes=scratch,
        compiler_params=pltpu.CompilerParams(
            collective_id=cid, has_side_effects=True, vmem_limit_bytes=VMEM_CAP
        ),
        cost_estimate=cost_of(time),
        name=name,
    )
    return list(call(*args))


def head_stats_kernel(block, tile, table_ref, final_ref, wanted_ref, edge_ref, exp_ref, top_ref, sum_ref, pick_ref):
    j = pl.program_id(0)
    tokens = final_ref.shape[0]
    place = j * block + lax.broadcasted_iota(jnp.int32, (block, 1), 0)
    valid = place < edge_ref[0]

    def one(i, carry):
        at = pl.ds(i * tile, tile)
        logits = lax.dot_general(
            table_ref[...],
            final_ref[at, :],
            (((1,), (1,)), ((), ())),
            preferred_element_type=jnp.float32,
        )
        logits = jnp.where(valid, logits, MASKED)
        top = jnp.max(logits, axis=0, keepdims=True)
        weights = jnp.exp(logits - top)
        exp_ref[:, at] = weights.astype(jnp.bfloat16)
        top_ref[0, :, at] = top
        sum_ref[0, :, at] = jnp.sum(weights, axis=0, keepdims=True)
        pick_ref[0, :, at] = jnp.sum(
            jnp.where(place == wanted_ref[:, at], logits, 0.0), axis=0, keepdims=True
        )
        return carry

    for i in range(tokens // tile):
        one(i, 0)


def head_stats(table, final, wanted, edge, block, tile=512):
    rows, width = table.shape
    tokens = final.shape[0]
    steps = pl.cdiv(rows, block)
    row = jax.ShapeDtypeStruct((steps, 1, tokens), jnp.float32)
    row_spec = pl.BlockSpec((1, 1, tokens), lambda j: (j, 0, 0))
    return pl.pallas_call(
        functools.partial(head_stats_kernel, block, tile),
        grid=(steps,),
        out_shape=[jax.ShapeDtypeStruct((steps * block, tokens), jnp.bfloat16), row, row, row],
        in_specs=[
            pl.BlockSpec((block, width), lambda j: (j, 0)),
            pl.BlockSpec((tokens, width), lambda j: (0, 0)),
            pl.BlockSpec((1, tokens), lambda j: (0, 0)),
            pl.BlockSpec(memory_space=pltpu.SMEM),
        ],
        out_specs=[pl.BlockSpec((block, tokens), lambda j: (j, 0)), row_spec, row_spec, row_spec],
        compiler_params=pltpu.CompilerParams(vmem_limit_bytes=56 * 2**20),
        cost_estimate=pl.CostEstimate(
            flops=2 * rows * width * tokens,
            bytes_accessed=2 * rows * (width + tokens),
            transcendentals=rows * tokens,
        ),
        name="head_stats",
    )(table, final, wanted, edge)


def head_back_kernel(rows, block, tile, exp_ref, table_ref, final_ref, scale_ref, weight_ref, wanted_ref, grad_ref, dfinal_ref, dl_ref, sum_ref):
    j = pl.program_id(0)
    tokens = final_ref.shape[0]
    place = j * block + lax.broadcasted_iota(jnp.int32, (block, 1), 0)

    @pl.when(j == 0)
    def _():
        sum_ref[...] = jnp.zeros_like(sum_ref)

    table = jnp.where(place < rows, table_ref[...], jnp.zeros_like(table_ref))

    def one(i, carry):
        at = pl.ds(i * tile, tile)
        weight = weight_ref[:, at]
        dl = exp_ref[:, at].astype(jnp.float32) * scale_ref[0, :, at]
        dl = dl - jnp.where(place == wanted_ref[:, at], weight, 0.0)
        dl = dl.astype(jnp.bfloat16)
        dl_ref[:, at] = dl
        sum_ref[at, :] += lax.dot_general(
            dl, table, (((0,), (0,)), ((), ())), preferred_element_type=jnp.float32
        )
        return carry

    for i in range(tokens // tile):
        one(i, 0)

    strip = block // max(1, block // 256)

    def two(i, carry):
        at = pl.ds(i * strip, strip)
        grad_ref[at, :] = jnp.dot(
            dl_ref[at, :], final_ref[...], preferred_element_type=jnp.float32
        ).astype(jnp.bfloat16)
        return carry

    for i in range(block // strip):
        two(i, 0)

    @pl.when(j == pl.num_programs(0) - 1)
    def _():
        dfinal_ref[...] = sum_ref[...].astype(jnp.bfloat16)


def head_back(exps, table, final, scale, weight, wanted, block, tile=256):
    rows, width = table.shape
    tokens = final.shape[0]
    steps = pl.cdiv(rows, block)
    return pl.pallas_call(
        functools.partial(head_back_kernel, rows, block, tile),
        grid=(steps,),
        out_shape=[
            jax.ShapeDtypeStruct((rows, width), jnp.bfloat16),
            jax.ShapeDtypeStruct((tokens, width), jnp.bfloat16),
        ],
        in_specs=[
            pl.BlockSpec((block, tokens), lambda j: (j, 0)),
            pl.BlockSpec((block, width), lambda j: (j, 0)),
            pl.BlockSpec((tokens, width), lambda j: (0, 0)),
            pl.BlockSpec((1, 1, tokens), lambda j: (j, 0, 0)),
            pl.BlockSpec((1, tokens), lambda j: (0, 0)),
            pl.BlockSpec((1, tokens), lambda j: (0, 0)),
        ],
        out_specs=[
            pl.BlockSpec((block, width), lambda j: (j, 0)),
            pl.BlockSpec((tokens, width), lambda j: (0, 0)),
        ],
        scratch_shapes=[
            pltpu.VMEM((block, tokens), jnp.bfloat16),
            pltpu.VMEM((tokens, width), jnp.float32),
        ],
        compiler_params=pltpu.CompilerParams(vmem_limit_bytes=60 * 2**20),
        cost_estimate=pl.CostEstimate(
            flops=4 * rows * width * tokens,
            bytes_accessed=2 * rows * (2 * width + tokens),
            transcendentals=0,
        ),
        name="head_back",
    )(exps, table, final, scale, weight, wanted)


def small_gather_kernel(axis, count, src_ref, out_ref, send, recv):
    dp = lax.axis_index("dp")
    mp = lax.axis_index("mp")
    me = dp if axis == "dp" else mp

    def device(peer):
        return (peer, mp) if axis == "dp" else (dp, peer)

    barrier = pltpu.get_barrier_semaphore()
    for hop in range(1, count):
        pl.semaphore_signal(
            barrier, inc=1, device_id=device(lax.rem(me + hop, count)), device_id_type=MESH
        )
    pl.semaphore_wait(barrier, count - 1)
    copies = []
    for hop in range(1, count):
        peer = lax.rem(me + hop, count)
        copy = pltpu.make_async_remote_copy(
            src_ref=src_ref,
            dst_ref=out_ref.at[me],
            send_sem=send.at[hop],
            recv_sem=recv.at[hop],
            device_id=device(peer),
            device_id_type=MESH,
        )
        copy.start()
        copies.append(copy)
    out_ref[me] = src_ref[...]
    for copy in copies:
        copy.wait()


def small_gather(name, cid, values, axis):
    count = lax.axis_size(axis)
    vmem = pl.BlockSpec(memory_space=pltpu.VMEM)
    return pl.pallas_call(
        functools.partial(small_gather_kernel, axis, count),
        out_shape=jax.ShapeDtypeStruct((count,) + values.shape, values.dtype),
        in_specs=[vmem],
        out_specs=vmem,
        scratch_shapes=[pltpu.SemaphoreType.DMA((count,)), pltpu.SemaphoreType.DMA((count,))],
        compiler_params=pltpu.CompilerParams(collective_id=cid, has_side_effects=True),
        cost_estimate=cost_of(6),
        name=name,
    )(values)


def exchange(axis, me, here, source, slots, send, recv, first):
    count = slots.shape[0]
    copies = []
    for hop in range(1, count):
        peer = lax.rem(me + hop, count)
        copy = pltpu.make_async_remote_copy(
            src_ref=source,
            dst_ref=slots.at[me],
            send_sem=send.at[first + hop],
            recv_sem=recv.at[first + hop],
            device_id=(peer, here) if axis == "dp" else (here, peer),
            device_id_type=MESH,
        )
        copy.start()
        copies.append(copy)
    slots[me] = source[...]
    for copy in copies:
        copy.wait()
    total = slots[0]
    for index in range(1, count):
        total = total + slots[index]
    return total


def greet_all(dp, mp, size_dp, size_mp):
    barrier = pltpu.get_barrier_semaphore()
    for hop in range(1, size_dp):
        pl.semaphore_signal(
            barrier, inc=1, device_id=(lax.rem(dp + hop, size_dp), mp), device_id_type=MESH
        )
    for hop in range(1, size_mp):
        pl.semaphore_signal(
            barrier, inc=1, device_id=(dp, lax.rem(mp + hop, size_mp)), device_id_type=MESH
        )
    pl.semaphore_wait(barrier, size_dp + size_mp - 2)


def lane_rows(values):
    values = values.reshape(-1)
    return jnp.pad(values, (0, -values.size % 128)).reshape(-1, 128)


def fold(values):
    return jnp.sum(values, axis=0, keepdims=True)


def stats_kernel(full, size_dp, size_mp, *refs):
    row_part, row_old, col_part, col_old, weight_sq = (refs[5 * n : 5 * n + 5] for n in range(5))
    loss_part, norm_one, norm_two, norm_three, norms, second_old = refs[25:31]
    refs = refs[31:]
    row_out, col_out = refs[0:5], refs[5:10]
    loss_out, grads_out, second_out, norms_out, rate_out = refs[10:15]
    send_dp, slots_dp, send_mp, slots_mp, parts, part_slots, whole, send, recv = refs[15:]
    dp = lax.axis_index("dp")
    mp = lax.axis_index("mp")
    greet_all(dp, mp, size_dp, size_mp)
    beta = 1.0 - STEP ** (-0.8)
    width = norms.shape[1]

    at = 0
    marks = []

    def put(values):
        nonlocal at
        rows = values.shape[0]
        send_dp[at : at + rows, :] = values
        marks.append((at, rows))
        at += rows

    norm_rows = width // 128
    for ref in (norm_one, norm_two, norm_three):
        for which in range(2):
            for piece in range(norm_rows):
                put(ref[which : which + 1, piece * 128 : piece * 128 + 128])
    marks.clear()
    count_norm = at
    for index in (0, 2, 4):
        put(row_part[index][...])
    for index in (1, 3):
        put(col_part[index][...])
    put(loss_part[...])
    for index in (1, 3):
        put(fold(row_old[index][...]))
    for index in range(5):
        put(fold(weight_sq[index][...]))
    if at < send_dp.shape[0]:
        send_dp[at:, :] = jnp.zeros((send_dp.shape[0] - at, 128), jnp.float32)
    over_dp = exchange("dp", dp, mp, send_dp, slots_dp, send, recv, 0)
    taken = [over_dp[start : start + rows] for start, rows in marks]
    loss_out[...] = taken[5]
    row_full = {0: taken[0], 2: taken[1], 4: taken[2]}
    col_full = {1: taken[3], 3: taken[4]}
    old_total = {1: taken[6], 3: taken[7]}
    weight_rows = taken[8:13]

    at = 0
    marks = []

    def put_mp(values):
        nonlocal at
        rows = values.shape[0]
        send_mp[at : at + rows, :] = values
        marks.append((at, rows))
        at += rows

    for index in (0, 2, 4):
        put_mp(col_part[index][...])
    for index in (1, 3):
        put_mp(row_part[index][...])
    for index in range(5):
        put_mp(fold(row_full[index] if index in row_full else col_full[index]))
    for index in (0, 2, 4):
        put_mp(fold(row_old[index][...]))
    for index in range(5):
        put_mp(weight_rows[index])
    if at < send_mp.shape[0]:
        send_mp[at:, :] = jnp.zeros((send_mp.shape[0] - at, 128), jnp.float32)
    each = count_norm // size_mp
    for index in range(size_mp):
        parts[index] = over_dp[index * each : index * each + each]
    first = size_dp + size_mp
    copies = []
    for hop in range(1, size_mp):
        peer = lax.rem(mp + hop, size_mp)
        copy = pltpu.make_async_remote_copy(
            src_ref=parts.at[peer],
            dst_ref=part_slots.at[mp],
            send_sem=send.at[first + hop],
            recv_sem=recv.at[first + hop],
            device_id=(dp, peer),
            device_id_type=MESH,
        )
        copy.start()
        copies.append(copy)
    part_slots[mp] = parts[mp]
    over_mp = exchange("mp", mp, dp, send_mp, slots_mp, send, recv, size_dp)
    for copy in copies:
        copy.wait()
    summed = part_slots[0]
    for index in range(1, size_mp):
        summed = summed + part_slots[index]
    whole[mp] = summed
    first += size_mp
    copies = []
    for hop in range(1, size_mp):
        peer = lax.rem(mp + hop, size_mp)
        copy = pltpu.make_async_remote_copy(
            src_ref=whole.at[mp],
            dst_ref=whole.at[mp],
            send_sem=send.at[first + hop],
            recv_sem=recv.at[first + hop],
            device_id=(dp, peer),
            device_id_type=MESH,
        )
        copies.append(copy)
    for copy in copies:
        copy.start()
    taken = [over_mp[start : start + rows] for start, rows in marks]
    for slot, index in enumerate((0, 2, 4)):
        col_full[index] = taken[slot]
        old_total[index] = taken[10 + slot]
    for slot, index in enumerate((1, 3)):
        row_full[index] = taken[3 + slot]
    square_total = taken[5:10]
    weight_total = taken[13:18]
    for index in range(5):
        full_rows, full_cols = full[index]
        row_new = beta * row_old[index][...] + (1.0 - beta) * row_full[index] / full_cols
        col_new = beta * col_old[index][...] + (1.0 - beta) * col_full[index] / full_rows
        row_out[index][...] = row_new
        col_out[index][...] = col_new
        mean = (
            beta * jnp.sum(old_total[index], axis=1, keepdims=True)
            + (1.0 - beta) * jnp.sum(square_total[index], axis=1, keepdims=True) / full_cols
        ) / full_rows
        rate = RHO * jnp.sqrt(
            jnp.sum(weight_total[index], axis=1, keepdims=True) / (full_rows * full_cols)
        )
        rate_out[index : index + 1, :] = jnp.broadcast_to(mean, (1, 128))
        rate_out[8 + index : 9 + index, :] = jnp.broadcast_to(rate, (1, 128))
    for copy in copies:
        copy.wait()
    for row in range(6):
        for piece in range(norm_rows):
            place = row * norm_rows + piece
            grads_out[row : row + 1, piece * 128 : piece * 128 + 128] = whole[
                place // each, place % each : place % each + 1, :
            ]
    grad = grads_out[...]
    second = beta * second_old[...] + (1.0 - beta) * (grad * grad + EPS_ONE)
    second_out[...] = second
    step = grad * lax.rsqrt(second)
    entries = step.size

    def mean_square(values):
        return jnp.sum(jnp.sum(values * values, axis=0, keepdims=True), axis=1, keepdims=True) / (
            entries
        )

    step = step / jnp.maximum(1.0, jnp.sqrt(mean_square(step)) / CLIP)
    old = norms[...]
    norms_out[...] = old - RHO * jnp.sqrt(mean_square(old)) * step


def update_stats(cid, row_parts, rows_old, col_parts, cols_old, weight_sq, loss, norm_parts, norms, second, full):
    size_dp = lax.axis_size("dp")
    size_mp = lax.axis_size("mp")
    f32 = jnp.float32
    rows_old2 = [lane_rows(v) for v in rows_old]
    cols_old2 = [lane_rows(v) for v in cols_old]
    args = (
        [lane_rows(v) for v in row_parts]
        + rows_old2
        + [lane_rows(v) for v in col_parts]
        + cols_old2
        + [v if v.ndim == 2 else lane_rows(v) for v in weight_sq]
        + [lane_rows(loss)]
        + list(norm_parts)
        + [norms, second]
    )
    width = norms.shape[1]
    count_norm = 6 * width // 128
    size_a = count_norm + sum(rows_old2[n].shape[0] for n in (0, 2, 4))
    size_a += sum(cols_old2[n].shape[0] for n in (1, 3)) + 8
    size_a += -size_a % 8
    size_b = sum(cols_old2[n].shape[0] for n in (0, 2, 4))
    size_b += sum(rows_old2[n].shape[0] for n in (1, 3)) + 13
    size_b += -size_b % 8
    each = count_norm // size_mp
    out_shape = [jax.ShapeDtypeStruct(v.shape, f32) for v in rows_old2 + cols_old2]
    out_shape += [
        jax.ShapeDtypeStruct((1, 128), f32),
        jax.ShapeDtypeStruct(norms.shape, f32),
        jax.ShapeDtypeStruct(norms.shape, f32),
        jax.ShapeDtypeStruct(norms.shape, f32),
        jax.ShapeDtypeStruct((16, 128), f32),
    ]
    sems = size_dp + 3 * size_mp
    vmem = pl.BlockSpec(memory_space=pltpu.VMEM)
    found = pl.pallas_call(
        functools.partial(stats_kernel, full, size_dp, size_mp),
        out_shape=out_shape,
        in_specs=[vmem] * len(args),
        out_specs=[vmem] * len(out_shape),
        scratch_shapes=[
            pltpu.VMEM((size_a, 128), f32),
            pltpu.VMEM((size_dp, size_a, 128), f32),
            pltpu.VMEM((size_b, 128), f32),
            pltpu.VMEM((size_mp, size_b, 128), f32),
            pltpu.VMEM((size_mp, each, 128), f32),
            pltpu.VMEM((size_mp, each, 128), f32),
            pltpu.VMEM((size_mp, each, 128), f32),
            pltpu.SemaphoreType.DMA((sems,)),
            pltpu.SemaphoreType.DMA((sems,)),
        ],
        compiler_params=pltpu.CompilerParams(collective_id=cid, has_side_effects=True),
        cost_estimate=cost_of(12),
        name="update_stats",
    )(*args)
    rows_new = [found[n].reshape(-1)[: rows_old[n].size] for n in range(5)]
    cols_new = [found[5 + n].reshape(-1)[: cols_old[n].size] for n in range(5)]
    loss_sums = found[10][0, :NSRC]
    return rows_new, cols_new, loss_sums, found[11], found[12], found[13], found[14]


def clip_kernel(entries, size_dp, size_mp, *refs):
    parts, rate = refs[:5], refs[5]
    out, mine, slots_dp, slots_mp, send, recv = refs[6:]
    dp = lax.axis_index("dp")
    mp = lax.axis_index("mp")
    greet_all(dp, mp, size_dp, size_mp)
    mine[...] = jnp.zeros_like(mine)
    for index in range(5):
        mine[index : index + 1, :] = fold(parts[index][...])
    mine[...] = exchange("dp", dp, mp, mine, slots_dp, send, recv, 0)
    total = exchange("mp", mp, dp, mine, slots_mp, send, recv, size_dp)
    total = jnp.sum(total, axis=1, keepdims=True)
    for index in range(5):
        clip = jnp.maximum(1.0, jnp.sqrt(total[index : index + 1] / entries[index]) / CLIP)
        out[index : index + 1, :] = rate[8 + index : 9 + index, :] / clip


def clip_rates(cid, step_parts, rate, entries):
    size_dp = lax.axis_size("dp")
    size_mp = lax.axis_size("mp")
    vmem = pl.BlockSpec(memory_space=pltpu.VMEM)
    sems = size_dp + size_mp
    return pl.pallas_call(
        functools.partial(clip_kernel, entries, size_dp, size_mp),
        out_shape=jax.ShapeDtypeStruct((8, 128), jnp.float32),
        in_specs=[vmem] * 6,
        out_specs=vmem,
        scratch_shapes=[
            pltpu.VMEM((8, 128), jnp.float32),
            pltpu.VMEM((size_dp, 8, 128), jnp.float32),
            pltpu.VMEM((size_mp, 8, 128), jnp.float32),
            pltpu.SemaphoreType.DMA((sems,)),
            pltpu.SemaphoreType.DMA((sems,)),
        ],
        compiler_params=pltpu.CompilerParams(collective_id=cid, has_side_effects=True),
        cost_estimate=cost_of(8),
        name="clip_rates",
    )(*[lane_rows(v) for v in step_parts], rate)


UNROLL = 8


def lookup_kernel(shift, count_ref, key_ref, table_ref, out_ref, low_ref, square_ref, rows_ref):
    spots = out_ref.shape[0]
    vocab, width = table_ref.shape
    rows_ref[...] = jnp.zeros_like(rows_ref)

    def some(i, carry):
        for j in range(UNROLL):
            key = key_ref[i * UNROLL + j]
            place = key & ((1 << shift) - 1)
            rows_ref[pl.ds(place, 1), :] = table_ref[pl.ds(key >> shift, 1), :]
        return carry

    lax.fori_loop(0, (count_ref[0] + UNROLL - 1) // UNROLL, some, 0)

    def narrow(i, carry):
        at = pl.ds(pl.multiple_of(i * 256, 256), 256)
        out_ref[at, :] = rows_ref[at, :].astype(jnp.bfloat16)
        return carry

    lax.fori_loop(0, spots // 256, narrow, 0)
    strip = 48 if vocab % 48 == 0 else 8

    def lower(i, total):
        at = pl.ds(pl.multiple_of(i * strip, strip), strip)
        values = table_ref[at, :]
        low_ref[at, :] = values.astype(jnp.bfloat16)
        for row in range(0, strip, 8):
            piece = values[row : row + 8, :]
            total = total + piece * piece
        return total

    total = lax.fori_loop(0, vocab // strip, lower, jnp.zeros((8, width), jnp.float32))
    folded = total[:, 0:128]
    for start in range(128, width, 128):
        folded = folded + total[:, start : start + 128]
    square_ref[...] = folded


def lookup(keys, count, table, spots, shift):
    vocab, width = table.shape
    smem = pl.BlockSpec(memory_space=pltpu.SMEM)
    vmem = pl.BlockSpec(memory_space=pltpu.VMEM)
    return pl.pallas_call(
        functools.partial(lookup_kernel, shift),
        out_shape=[
            jax.ShapeDtypeStruct((spots, width), jnp.bfloat16),
            jax.ShapeDtypeStruct((vocab, width), jnp.bfloat16),
            jax.ShapeDtypeStruct((8, 128), jnp.float32),
        ],
        in_specs=[smem, smem, vmem],
        out_specs=[vmem] * 3,
        scratch_shapes=[pltpu.VMEM((spots + 8, width), jnp.float32)],
        compiler_params=pltpu.CompilerParams(vmem_limit_bytes=VMEM_CAP),
        cost_estimate=cost_of(20),
        name="lookup",
    )(count, keys, table)


def scatter_kernel(shift, count_ref, key_ref, head_ref, rows_in_ref, grad_ref, rows_ref):
    spots = rows_in_ref.shape[0]
    width = grad_ref.shape[1]

    def widen(i, carry):
        at = pl.ds(pl.multiple_of(i * 256, 256), 256)
        rows_ref[at, :] = rows_in_ref[at, :].astype(jnp.float32)
        return carry

    lax.fori_loop(0, spots // 256, widen, 0)
    rows_ref[spots:, :] = jnp.zeros((8, width), jnp.float32)
    grad_ref[...] = head_ref[...].astype(jnp.float32)

    def some(i, carry):
        for j in range(UNROLL):
            key = key_ref[i * UNROLL + j]
            place = key & ((1 << shift) - 1)
            grad_ref[pl.ds(key >> shift, 1), :] += rows_ref[pl.ds(place, 1), :]
        return carry

    lax.fori_loop(0, (count_ref[0] + UNROLL - 1) // UNROLL, some, 0)


def scatter(keys, count, head_grad, rows, shift):
    spots, width = rows.shape
    vocab = head_grad.shape[0]
    smem = pl.BlockSpec(memory_space=pltpu.SMEM)
    vmem = pl.BlockSpec(memory_space=pltpu.VMEM)
    return pl.pallas_call(
        functools.partial(scatter_kernel, shift),
        out_shape=jax.ShapeDtypeStruct((vocab, width), jnp.float32),
        in_specs=[smem, smem, vmem, vmem],
        out_specs=vmem,
        scratch_shapes=[pltpu.VMEM((spots + 8, width), jnp.float32)],
        compiler_params=pltpu.CompilerParams(vmem_limit_bytes=VMEM_CAP),
        cost_estimate=cost_of(23),
        name="scatter",
    )(count, keys, head_grad, rows)


def norm_parts(values):
    centre = jnp.mean(values, axis=-1, keepdims=True)
    centred = values - centre
    scale = lax.rsqrt(jnp.mean(centred * centred, axis=-1, keepdims=True) + EPS_NORM)
    return centred * scale, scale


def norm_pull(values, gain, upstream):
    normed, scale = norm_parts(values)
    weighted = upstream * gain
    pulled = scale * (
        weighted
        - jnp.mean(weighted, axis=-1, keepdims=True)
        - normed * jnp.mean(weighted * normed, axis=-1, keepdims=True)
    )
    return (
        pulled,
        jnp.sum(upstream * normed, axis=0, keepdims=True),
        jnp.sum(upstream, axis=0, keepdims=True),
    )


def step_first(total, at, ins, outs):
    stream, norms = ins
    normed, scale = norm_parts(stream[at, :].astype(jnp.float32))
    return normed * norms[0:1, :] + norms[1:2, :]


def step_lookup(total, at, ins, outs):
    outs[0][at, :] = total.astype(jnp.bfloat16)


def step_forward(row, total, at, ins, outs):
    stream, norms = ins
    values = stream[at, :].astype(jnp.float32) + total
    outs[0][at, :] = values
    normed, scale = norm_parts(values)
    return normed * norms[row : row + 1, :] + norms[row + 1 : row + 2, :]


def step_backward(row, total, at, ins, outs):
    stream, norms = ins[:2]
    pulled, dgain, dshift = norm_pull(
        stream[at, :].astype(jnp.float32), norms[row : row + 1, :], total
    )
    if len(ins) > 2:
        pulled = pulled + ins[2][at, :]
    outs[0][at, :] = pulled.astype(outs[0].dtype)
    first = at.start == 0

    @pl.when(first)
    def _():
        outs[1][...] = jnp.zeros_like(outs[1])

    outs[1][0:1, :] += dgain
    outs[1][1:2, :] += dshift
    return pulled


def step_pass(total, at, ins, outs):
    return ins[0][at, :]


def gelu_tanh(values):
    return jax.nn.gelu(values, approximate=True)


def score_block(mixed, starts):
    place = jnp.arange(mixed.shape[0], dtype=jnp.int32)
    allowed = (place[None, :] <= place[:, None]) & (place[None, :] >= starts[:, None])
    raw = jnp.einsum(
        "qhe,khe->hqk", mixed[:, :, 0], mixed[:, :, 1], preferred_element_type=jnp.float32
    )
    return jnp.where(allowed[None], raw * HD ** (-0.5), MASKED)


def attend_forward(mixed, starts):
    scores = score_block(mixed, starts)
    highest = jnp.max(scores, axis=-1, keepdims=True)
    weights = jnp.exp(scores - highest)
    totals = jnp.sum(weights, axis=-1, keepdims=True)
    probs = (weights / totals).astype(jnp.bfloat16)
    result = jnp.einsum(
        "hqk,khe->qhe", probs, mixed[:, :, 2], preferred_element_type=jnp.float32
    )
    return (result.astype(jnp.bfloat16), highest[:, :, 0] + jnp.log(totals[:, :, 0]))


def attend_backward(mixed, starts, log_rows, upstream):
    scores = score_block(mixed, starts)
    probs = jnp.exp(scores - log_rows[:, :, None])
    dprobs = jnp.einsum(
        "qhe,khe->hqk", upstream, mixed[:, :, 2], preferred_element_type=jnp.float32
    )
    dvalues = jnp.einsum(
        "hqk,qhe->khe", probs.astype(jnp.bfloat16), upstream, preferred_element_type=jnp.float32
    )
    inner = jnp.sum(probs * dprobs, axis=-1, keepdims=True)
    dscores = (probs * (dprobs - inner)).astype(jnp.bfloat16)
    dquery = jnp.einsum(
        "hqk,khe->qhe", dscores, mixed[:, :, 1], preferred_element_type=jnp.float32
    ) * HD ** (-0.5)
    dkeys = jnp.einsum(
        "hqk,qhe->khe", dscores, mixed[:, :, 0], preferred_element_type=jnp.float32
    ) * HD ** (-0.5)
    return jnp.stack([dquery, dkeys, dvalues], axis=2).astype(jnp.bfloat16)


def local(
    token_ids,
    targets,
    starts,
    sources,
    embedding,
    w_qkv,
    w_out,
    w_fc,
    w_proj,
    norm_params,
    rows_table,
    cols_table,
    rows_qkv,
    cols_qkv,
    rows_out,
    cols_out,
    rows_fc,
    cols_fc,
    rows_proj,
    cols_proj,
    second_norms,
):
    bf16 = jnp.bfloat16
    f32 = jnp.float32
    size_mp = lax.axis_size("mp")
    size_dp = lax.axis_size("dp")
    dp = lax.axis_index("dp")
    mp = lax.axis_index("mp")
    tokens = token_ids.shape[0]
    seqs = tokens // LEN
    chips = size_mp // 2
    near = chips // seqs
    sharers = size_mp // seqs
    rows = tokens // size_mp
    vocab, part_width = embedding.shape
    width = part_width * size_dp
    first_row = mp * vocab
    spots = tokens * size_dp
    chunks_full = max(1, min(8, rows // 32))
    chunks_near = max(1, min(4, rows // 32))

    both = jnp.stack([token_ids, sources]).reshape(-1, 128)
    both = small_gather("gather_ids", 0, both, "dp").reshape(size_dp, 2, tokens)
    all_ids = both[:, 0]
    all_sources = both[:, 1].reshape(-1)
    counts = jnp.sum(
        (all_sources[:, None] == jnp.arange(NSRC, dtype=jnp.int32)[None, :]).astype(f32), axis=0
    )

    w_qkv, w_out, w_fc, w_proj, all_ids = lax.optimization_barrier(
        (w_qkv, w_out, w_fc, w_proj, all_ids)
    )


    def own_and_twins(weight, axis):
        weight = weight.astype(bf16)
        found = [weight]
        for turn in range(1, seqs):
            shift = [(i, (i + turn * sharers) % size_mp) for i in range(size_mp)]
            found.append(lax.ppermute(weight, "mp", shift))
        return jnp.concatenate(found, axis=axis) if seqs > 1 else weight

    pair_qkv = own_and_twins(w_qkv, 1)
    pair_out = own_and_twins(w_out, 0)
    pair_fc = own_and_twins(w_fc, 1)
    pair_proj = own_and_twins(w_proj, 0)
    place = (
        (jnp.arange(size_mp, dtype=jnp.int32) * size_dp)[None, :, None] * rows
        + (jnp.arange(size_dp, dtype=jnp.int32) * rows)[:, None, None]
        + jnp.arange(rows, dtype=jnp.int32)[None, None, :]
    ).reshape(size_dp, tokens)
    local_ids = all_ids - first_row
    inside = (local_ids >= 0) & (local_ids < vocab)
    shift = spots.bit_length()
    idle = ((vocab - 1) << shift) + spots
    keys = jnp.where(inside, (local_ids << shift) + place, idle)
    keys = jnp.sort(keys.reshape(-1))
    owned = jnp.sum(inside.astype(jnp.int32)).reshape(1)
    found, low_table, table_sq = lookup(keys, owned, embedding, spots, shift)
    picked_rows, wide_qkv, wide_out, wide_fc = line_call(
        "rs_lookup",
        1,
        found,
        [],
        [jax.ShapeDtypeStruct((size_dp * rows, part_width), bf16)],
        step_lookup,
        size_dp * rows,
        part_width,
        chunks_full,
        chips,
        0,
        50,
        [("gather", 0, pair_qkv), ("gather", 1, pair_out), ("gather", 0, pair_fc)],
    )
    stream0 = lax.all_to_all(
        picked_rows.reshape(size_dp, rows, part_width), "dp", 0, 0, tiled=False
    )
    stream0 = jnp.swapaxes(stream0, 0, 1).reshape(rows, width)

    low_table, picked_rows = lax.optimization_barrier((low_table, picked_rows))
    wide_table = lax.all_gather(low_table, "dp", axis=1, tiled=True)
    row_f32 = jax.ShapeDtypeStruct((rows, width), f32)
    pair_f32 = jax.ShapeDtypeStruct((8, width), f32)
    (inner_one,) = line_call(
        "ag_inner1",
        2,
        None,
        [stream0, norm_params],
        [],
        step_first,
        rows,
        width,
        chunks_near,
        0,
        near,
        17,
    )
    heads = wide_qkv.shape[1] // (3 * HD)
    my_starts = row_slice(starts, (mp // sharers) * LEN, LEN)
    mixed = jnp.dot(inner_one, wide_qkv, preferred_element_type=f32).astype(bf16)
    mixed = mixed.reshape(LEN, heads, 3, HD)
    attended, log_sums = attend_forward(mixed, my_starts)
    attended = attended.reshape(LEN, heads * HD)
    partial = jnp.dot(attended, wide_out, preferred_element_type=f32).astype(bf16)
    inner_two, stream1, wide_proj = line_call(
        "attn_sum",
        3,
        partial,
        [stream0, norm_params],
        [row_f32],
        functools.partial(step_forward, 2),
        rows,
        width,
        chunks_near,
        near,
        near,
        32,
        [("gather", 1, pair_proj)],
    )
    before = jnp.dot(inner_two, wide_fc, preferred_element_type=f32)
    hidden = gelu_tanh(before).astype(bf16)
    partial = jnp.dot(hidden, wide_proj, preferred_element_type=f32).astype(bf16)
    final, stream2 = line_call(
        "mlp_sum",
        4,
        partial,
        [stream1, norm_params],
        [row_f32],
        functools.partial(step_forward, 4),
        rows,
        width,
        chunks_full,
        near,
        chips,
        58,
    )

    edge = jnp.clip(VREAL - first_row, 0, vocab).astype(jnp.int32).reshape(1)
    wanted = targets - first_row
    wanted = jnp.where((wanted >= 0) & (wanted < vocab), wanted, -1).reshape(1, tokens)
    block = 640
    exps, tops, sums, picks = head_stats(wide_table, final, wanted, edge, block)
    tops = tops[:, 0]
    top = jnp.max(tops, axis=0)
    total = jnp.sum(sums[:, 0] * jnp.exp(tops - top[None, :]), axis=0)
    pick = jnp.sum(picks[:, 0], axis=0)
    stats = jnp.concatenate([v.reshape(-1, 128) for v in (top, total, pick)])
    stats = small_gather("gather_stats", 5, stats, "mp").reshape(size_mp, 3, tokens)
    highest = jnp.max(stats[:, 0], axis=0)
    log_total = highest + jnp.log(
        jnp.sum(stats[:, 1] * jnp.exp(stats[:, 0] - highest[None, :]), axis=0)
    )
    token_loss = log_total - jnp.sum(stats[:, 2], axis=0)
    member = (sources[:, None] == jnp.arange(NSRC, dtype=jnp.int32)[None, :]).astype(f32)
    loss_part = jnp.sum(member * token_loss[:, None], axis=0)
    weight = jnp.sum(member / (NSRC * jnp.maximum(counts, 1.0))[None, :], axis=1)
    scale = jnp.exp(tops - log_total[None, :]) * weight[None, :]
    table_grad, dfinal = head_back(
        exps, wide_table, final, scale[:, None, :], weight[None, :], wanted, block
    )
    head_grad = lax.psum_scatter(table_grad, "dp", scatter_dimension=1, tiled=True)

    dbranch2, dstream2, norm3 = line_call(
        "final_back",
        6,
        dfinal,
        [stream2, norm_params],
        [row_f32, pair_f32],
        functools.partial(step_backward, 4),
        rows,
        width,
        chunks_full,
        chips,
        near,
        60,
    )
    grad_proj = jnp.einsum("tf,td->fd", hidden, dbranch2, preferred_element_type=f32).astype(bf16)
    dhidden = jnp.einsum("td,fd->tf", dbranch2, wide_proj, preferred_element_type=f32)
    unused, gelu_pull = jax.vjp(gelu_tanh, before)
    dbefore = gelu_pull(dhidden)[0].astype(bf16)
    partial = jnp.einsum("tf,df->td", dbefore, wide_fc, preferred_element_type=f32).astype(bf16)
    dbranch1, dstream1, norm2 = line_call(
        "mlp_back",
        7,
        partial,
        [stream1, norm_params, dstream2],
        [row_f32, pair_f32],
        functools.partial(step_backward, 2),
        rows,
        width,
        chunks_near,
        near,
        near,
        34,
    )
    grad_fc = jnp.einsum("td,tf->df", inner_two, dbefore, preferred_element_type=f32).astype(bf16)
    grad_out = jnp.einsum("tf,td->fd", attended, dbranch1, preferred_element_type=f32).astype(bf16)
    dattended = jnp.einsum("td,fd->tf", dbranch1, wide_out, preferred_element_type=f32)
    dattended = dattended.astype(bf16).reshape(LEN, heads, HD)
    dmixed = attend_backward(mixed, my_starts, log_sums, dattended)
    dmixed = dmixed.reshape(LEN, heads * 3 * HD)
    partial = jnp.einsum("tc,dc->td", dmixed, wide_qkv, preferred_element_type=f32).astype(bf16)
    dstream0, norm1, grad_proj, grad_out = line_call(
        "attn_back",
        8,
        partial,
        [stream0, norm_params, dstream1],
        [jax.ShapeDtypeStruct((rows, width), bf16), pair_f32],
        functools.partial(step_backward, 0),
        rows,
        width,
        chunks_near,
        near,
        0,
        28,
        [("scatter", 1, grad_proj), ("scatter", 1, grad_out)],
    )
    grad_qkv = jnp.einsum("td,tc->dc", inner_one, dmixed, preferred_element_type=f32).astype(bf16)

    sent = jnp.swapaxes(dstream0.reshape(rows, size_dp, part_width), 0, 1)
    sent = lax.all_to_all(sent, "dp", 0, 0, tiled=False).reshape(size_dp * rows, part_width)
    drows, grad_fc, grad_qkv = line_call(
        "ag_lookup",
        9,
        None,
        [sent],
        [],
        step_pass,
        size_dp * rows,
        part_width,
        chunks_full,
        0,
        chips,
        45,
        [("scatter", 0, grad_fc), ("scatter", 0, grad_qkv)],
    )

    def to_twins(share, axis):
        pieces = jnp.split(share, seqs, axis=axis)
        found = []
        for turn in range(1, seqs):
            back = [(i, (i - turn * sharers) % size_mp) for i in range(size_mp)]
            found.append(lax.ppermute(pieces[turn].astype(bf16), "mp", back))
        return pieces[0], found

    shares = [
        to_twins(grad_qkv, 1),
        to_twins(grad_out, 0),
        to_twins(grad_fc, 1),
        to_twins(grad_proj, 0),
    ]
    grad_table = scatter(keys, owned, head_grad, drows, shift)
    shares, grad_table = lax.optimization_barrier((shares, grad_table))
    grad_qkv, grad_out, grad_fc, grad_proj = [
        sum((piece.astype(f32) for piece in found), mine) for mine, found in shares
    ]

    weights = (embedding, w_qkv, w_out, w_fc, w_proj)
    grads = (grad_table, grad_qkv, grad_out, grad_fc, grad_proj)
    row_span = (size_mp, size_dp, size_mp, size_dp, size_mp)
    col_span = (size_dp, size_mp, size_dp, size_mp, size_dp)
    full = tuple(
        (g.shape[0] * r, g.shape[1] * c) for g, r, c in zip(grads, row_span, col_span)
    )
    squares = [gradient * gradient + EPS_ONE for gradient in grads]
    rows_new, cols_new, loss_sums, grad_norms, second_new, norms_new, rates = update_stats(
        10,
        [jnp.sum(square, axis=1) for square in squares],
        (rows_table, rows_qkv, rows_out, rows_fc, rows_proj),
        [jnp.sum(square, axis=0) for square in squares],
        (cols_table, cols_qkv, cols_out, cols_fc, cols_proj),
        [table_sq] + [jnp.sum(value * value, axis=0) for value in weights[1:]],
        loss_part,
        (norm1, norm2, norm3),
        norm_params,
        second_norms,
        full,
    )
    steps = [
        grads[n] * lax.rsqrt(rows_new[n][:, None] * cols_new[n][None, :] / rates[n, 0])
        for n in range(5)
    ]
    factors = clip_rates(
        11, [jnp.sum(step * step, axis=0) for step in steps], rates, [r * c for r, c in full]
    )
    updated = [weights[n] - factors[n, 0] * steps[n] for n in range(5)]
    return (
        loss_sums,
        counts,
        grad_table,
        rows_new[0],
        cols_new[0],
        updated[0],
        grad_qkv,
        rows_new[1],
        cols_new[1],
        updated[1],
        grad_out,
        rows_new[2],
        cols_new[2],
        updated[2],
        grad_fc,
        rows_new[3],
        cols_new[3],
        updated[3],
        grad_proj,
        rows_new[4],
        cols_new[4],
        updated[4],
        grad_norms,
        second_new,
        norms_new,
    )


def solution(mesh):
    placed = (
        P("dp"),
        P("dp"),
        P("dp"),
        P("dp"),
        P("mp", "dp"),
        P("dp", "mp"),
        P("mp", "dp"),
        P("dp", "mp"),
        P("mp", "dp"),
        P(),
        P("mp"),
        P("dp"),
        P("dp"),
        P("mp"),
        P("mp"),
        P("dp"),
        P("dp"),
        P("mp"),
        P("mp"),
        P("dp"),
        P(),
    )
    return jax.shard_map(
        local,
        mesh=mesh,
        in_specs=placed,
        out_specs=(
            P(),
            P(),
            P("mp", "dp"),
            P("mp"),
            P("dp"),
            P("mp", "dp"),
            P("dp", "mp"),
            P("dp"),
            P("mp"),
            P("dp", "mp"),
            P("mp", "dp"),
            P("mp"),
            P("dp"),
            P("mp", "dp"),
            P("dp", "mp"),
            P("dp"),
            P("mp"),
            P("dp", "mp"),
            P("mp", "dp"),
            P("mp"),
            P("dp"),
            P("mp", "dp"),
            P(),
            P(),
            P(),
        ),
        check_vma=False,
    )
```

```python
import functools
import math

import jax
import jax.numpy as jnp
from jax import lax
from jax.experimental import pallas as pl
from jax.experimental.pallas import tpu as pltpu
from jax.sharding import PartitionSpec as P

HD = 64
VREAL = 50257
LEN = 1024
NSRC = 4
STEP = 10


EPS_NORM = 1e-05
EPS_ONE = 1e-30
CLIP = 1.0
RHO = 0.5
MASKED = -1e30
QUERIES = 256
MESH = pl.DeviceIdType.MESH
VMEM_CAP = 56 * 2**20


def cost_of(time):
    return pl.CostEstimate(
        flops=time * 1000000000, bytes_accessed=time * 3000000, transcendentals=0
    )


def row_slice(values, start, count):
    return lax.dynamic_slice_in_dim(values, start, count, 0)


def line_kernel(nr, ng, chunks, shapes, n_in, n_out, step, sides, turn, relay_tick, *refs):
    (rows_r, width_r), (rows_g, width_g) = shapes
    part = refs[0] if nr else None
    first = 1 if nr else 0
    ins = refs[first : first + n_in]
    refs = refs[first + n_in :]
    side_ins, refs = refs[: len(sides)], refs[len(sides) :]
    if ng:
        whole, refs = refs[0], refs[1:]
    outs = refs[:n_out]
    refs = refs[n_out:]
    side_outs, scratch = refs[: len(sides)], refs[len(sides) :]
    side_scratch, scratch = scratch[: 3 * len(sides)], scratch[3 * len(sides) :]
    if turn:
        cast, turn_send, turn_recv = scratch[-3:]
    size_dp = lax.axis_size("dp")
    dp = lax.axis_index("dp")
    mp = lax.axis_index("mp")
    z = mp // 2
    core = lax.rem(mp, 2)
    other = mp + 1 - 2 * core
    piece_r = rows_r // chunks
    piece_g = rows_g // chunks
    small = min(piece_r, piece_g)
    late = 1 if turn else 0
    most = max(nr, ng)
    zb = lax.rem(z, most)
    if nr:
        zr = lax.rem(z, nr)
        last_r = nr - 1
    if ng:
        zg = lax.rem(z, ng)
        last_g = ng - 1

    barrier = pltpu.get_barrier_semaphore()
    pl.semaphore_signal(barrier, inc=1, device_id=(dp, other), device_id_type=MESH)

    @pl.when(zb > 0)
    def _():
        pl.semaphore_signal(barrier, inc=1, device_id=(dp, mp - 2), device_id_type=MESH)

    @pl.when(zb < most - 1)
    def _():
        pl.semaphore_signal(barrier, inc=1, device_id=(dp, mp + 2), device_id_type=MESH)

    if sides or turn:
        for hop in range(1, size_dp):
            pl.semaphore_signal(
                barrier,
                inc=1,
                device_id=(lax.rem(dp + hop, size_dp), mp),
                device_id_type=MESH,
            )
    greeted = (size_dp if sides or turn else 1) + (zb > 0).astype(jnp.int32) + (zb < most - 1).astype(jnp.int32)
    pl.semaphore_wait(barrier, greeted)

    def share(axis, length, which):
        at = pl.ds(pl.multiple_of(which * length, length), length)
        return (at, slice(None)) if axis == 0 else (slice(None), at)

    def to_peer(src, dst, send, recv, peer):
        return pltpu.make_async_remote_copy(
            src_ref=src,
            dst_ref=dst,
            send_sem=send,
            recv_sem=recv,
            device_id=(peer, mp),
            device_id_type=MESH,
        )

    relay = size_dp == 4
    beside_x = dp + 1 - 2 * lax.rem(dp, 2)
    beside_y = lax.rem(dp + 2, 4)
    across = 3 - dp

    def half_share(axis, length, which, height, part):
        if axis == 0:
            return (pl.ds(pl.multiple_of(which * length + part * height, height), height), slice(None))
        at = pl.ds(pl.multiple_of(which * length, length), length)
        return (pl.ds(part * height, height), at)

    first_copies, more_copies, relays = [], [], []
    for index, (kind, axis) in enumerate(sides):
        src, dst = side_ins[index], side_outs[index]
        send, recv, slots = side_scratch[3 * index : 3 * index + 3]
        shard = src if kind == "gather" else dst
        length, height = shard.shape[axis], shard.shape[0] // 2
        if not relay:
            for hop in range(1, size_dp):
                peer = lax.rem(dp + hop, size_dp)
                if kind == "gather":
                    source, target = src, dst.at[share(axis, length, dp)]
                else:
                    source, target = src.at[share(axis, length, peer)], slots.at[hop]
                more_copies.append(to_peer(source, target, send.at[hop], recv.at[hop], peer))
            continue
        for side, near_one, far_one in ((0, beside_x, beside_y), (1, beside_y, beside_x)):
            sems = [(send.at[3 * side + n], recv.at[3 * side + n]) for n in range(3)]
            if kind == "gather":
                mine = src.at[pl.ds(side * height, height)]
                here = dst.at[half_share(axis, length, dp, height, side)]
                passed = dst.at[half_share(axis, length, near_one, height, side)]
                arrives = to_peer(mine, here, *sems[0], near_one)
                first_copies.append(arrives)
                more_copies.append(to_peer(mine, here, *sems[1], far_one))
                relays.append((arrives, None, to_peer(passed, passed, *sems[2], far_one)))
            else:
                arrives = to_peer(
                    src.at[half_share(axis, length, across, height, side)],
                    slots.at[4 * side],
                    *sems[0],
                    near_one,
                )
                first_copies.append(arrives)
                more_copies.append(
                    to_peer(
                        src.at[half_share(axis, length, near_one, height, side)],
                        slots.at[4 * side + 1],
                        *sems[1],
                        near_one,
                    )
                )
                summed = to_peer(
                    slots.at[4 * side + 2], slots.at[4 * side + 3], *sems[2], far_one
                )
                own = src.at[half_share(axis, length, far_one, height, side)]
                relays.append((arrives, (own, slots, 4 * side, height), summed))

    def start_sides():
        for copy in first_copies + more_copies:
            copy.start()

    def pass_on():
        for arrives, adding, copy in relays:
            arrives.wait_recv()
            if adding is not None:
                own, slots, at, height = adding
                both = own[...].astype(jnp.float32) + slots[at].astype(jnp.float32)
                slots[at + 2] = both.astype(slots.dtype)
            copy.start()

    if nr == 0:
        start_sides()

    if nr:
        half, from_left, from_right, going = scratch[:4]
        half_send, half_recv, rs_send, left_recv, right_recv = scratch[4:9]
        scratch = scratch[9:]
    if ng:
        core_send, core_recv, to_right, to_left, ag_left, ag_right = scratch[:6]

    def part_rows(block, k):
        return pl.ds(pl.multiple_of(block * rows_r + k * piece_r, piece_r), piece_r)

    def whole_rows(block, k):
        return pl.ds(pl.multiple_of(block * rows_g + k * piece_g, piece_g), piece_g)

    def remote(src, dst, send, recv, target):
        return pltpu.make_async_remote_copy(
            src_ref=src,
            dst_ref=dst,
            send_sem=send,
            recv_sem=recv,
            device_id=(dp, target),
            device_id_type=MESH,
        )

    if nr:

        def half_copy(dest, k):
            return remote(
                part.at[part_rows(2 * dest + 1 - core, k)],
                half.at[dest, k],
                half_send.at[dest, k],
                half_recv.at[dest, k],
                other,
            )

        def send_halves(k, carry):
            for dest in range(nr):
                half_copy(dest, k).start()
            return carry

        lax.fori_loop(0, chunks, send_halves, 0)
        start_sides()

        def right_copy(dest, k):
            return remote(
                going.at[dest, k],
                from_left.at[dest, k],
                rs_send.at[dest, k],
                left_recv.at[dest, k],
                mp + 2,
            )

        def left_copy(dest, k):
            return remote(
                going.at[dest, k],
                from_right.at[dest, k],
                rs_send.at[dest, k],
                right_recv.at[dest, k],
                mp - 2,
            )

        def chip_sum(dest, k):
            half_copy(dest, k).wait_recv()
            mine = part[part_rows(2 * dest + core, k), :].astype(jnp.float32)
            return mine + half[dest, k].astype(jnp.float32)

        def pass_right(dest, k):
            total = chip_sum(dest, k)

            @pl.when(zr == 0)
            def _():
                going[dest, k] = total.astype(jnp.bfloat16)

            @pl.when(zr > 0)
            def _():
                right_copy(dest, k).wait_recv()
                both = total + from_left[dest, k].astype(jnp.float32)
                going[dest, k] = both.astype(jnp.bfloat16)

            right_copy(dest, k).start()

        def pass_left(dest, k):
            total = chip_sum(dest, k)

            @pl.when(zr == last_r)
            def _():
                going[dest, k] = total.astype(jnp.bfloat16)

            @pl.when(zr < last_r)
            def _():
                left_copy(dest, k).wait_recv()
                both = total + from_right[dest, k].astype(jnp.float32)
                going[dest, k] = both.astype(jnp.bfloat16)

            left_copy(dest, k).start()

    if ng:

        def gathered(block, k, send, recv, target):
            where = whole.at[whole_rows(2 * block + core, k)]
            return remote(where, where, send.at[block, k], recv.at[block, k], target)

        def core_copy(block, k):
            return gathered(block, k, core_send, core_recv, other)

        def ag_right_copy(block, k):
            return gathered(block, k, to_right, ag_left, mp + 2)

        def ag_left_copy(block, k):
            return gathered(block, k, to_left, ag_right, mp - 2)

    def own_rows(k):
        total = None
        if nr:
            total = chip_sum(zr, k)
            zero = jnp.zeros((piece_r, width_r), jnp.float32)

            @pl.when(zr > 0)
            def _():
                right_copy(zr, k).wait_recv()

            @pl.when(zr < last_r)
            def _():
                left_copy(zr, k).wait_recv()

            total += jnp.where(zr > 0, from_left[zr, k].astype(jnp.float32), zero)
            total += jnp.where(zr < last_r, from_right[zr, k].astype(jnp.float32), zero)
        if turn == "gather":
            cast[k] = total.astype(cast.dtype)
            for hop in range(1, size_dp):
                turn_copy(hop, k).start()
            mine = pl.ds(pl.multiple_of(dp * small, small), small)
            outs[0][own_place(k, dp)] = cast[k, mine, :]
            return
        at = pl.ds(pl.multiple_of(k * piece_r, piece_r), piece_r)
        ready = step(total, at, ins, outs)
        if turn == "spread":
            cast[k] = ready.astype(cast.dtype)
            for hop in range(1, size_dp):
                turn_copy(hop, k).start()
            whole[own_place(k, dp)] = cast[
                k, :, pl.ds(pl.multiple_of(dp * width_g, width_g), width_g)
            ]
        elif ng:
            whole[whole_rows(2 * zg + core, k), :] = ready.astype(whole.dtype)
            start_gather(k)

    def own_place(k, peer):
        if turn == "gather":
            return (
                pl.ds(pl.multiple_of(k * small, small), small),
                pl.ds(pl.multiple_of(peer * width_r, width_r), width_r),
            )
        start = (2 * zg + core) * rows_g + k * piece_g + peer * small
        return (pl.ds(pl.multiple_of(start, small), small), slice(None))

    def turn_copy(hop, k):
        peer = lax.rem(dp + hop, size_dp)
        if turn == "gather":
            src = cast.at[k, pl.ds(pl.multiple_of(peer * small, small), small)]
            dst = outs[0].at[own_place(k, dp)]
        else:
            src = cast.at[k, :, pl.ds(pl.multiple_of(peer * width_g, width_g), width_g)]
            dst = whole.at[own_place(k, dp)]
        return to_peer(src, dst, turn_send.at[hop, k], turn_recv.at[hop, k], peer)

    def turned_rows(k):
        for hop in range(1, size_dp):
            turn_copy(hop, k).wait_recv()
        if turn == "gather":
            at = pl.ds(pl.multiple_of(k * piece_g, piece_g), piece_g)
            ready = step(None, at, ins, outs)
            whole[whole_rows(2 * zg + core, k), :] = ready.astype(whole.dtype)
        start_gather(k)

    def start_gather(k):
        core_copy(zg, k).start()

        @pl.when(zg < last_g)
        def _():
            ag_right_copy(zg, k).start()

        @pl.when(zg > 0)
        def _():
            ag_left_copy(zg, k).start()

    def inside(k):
        return (k >= 0) & (k < chunks)

    def own_lag(chip):
        if not nr:
            return 0
        at = lax.rem(chip, nr)
        return jnp.maximum(at, last_r - at)

    def tick(now, carry):
        if nr:
            k_right = now - zr
            k_left = now - (last_r - zr)
            for far in range(last_r):

                @pl.when(inside(k_right) & (last_r - far > zr))
                def _():
                    pass_right(last_r - far, k_right)

                @pl.when(inside(k_left) & (far < zr))
                def _():
                    pass_left(far, k_left)

        k_own = now - own_lag(z)

        @pl.when(inside(k_own))
        def _():
            own_rows(k_own)

        if turn:

            @pl.when(inside(k_own - 1))
            def _():
                turned_rows(k_own - 1)

        if relays:

            @pl.when(now == relay_tick)
            def _():
                pass_on()

        if ng:
            for block in range(ng):
                k = now - (own_lag(z - zg + block) + late + jnp.abs(zg - block))

                @pl.when(inside(k) & (block < zg))
                def _():
                    ag_right_copy(block, k).wait_recv()
                    core_copy(block, k).start()

                    @pl.when(zg < last_g)
                    def _():
                        ag_right_copy(block, k).start()

                @pl.when(inside(k) & (block > zg))
                def _():
                    ag_left_copy(block, k).wait_recv()
                    core_copy(block, k).start()

                    @pl.when(zg > 0)
                    def _():
                        ag_left_copy(block, k).start()

        return carry

    ticks = chunks + (nr - 1 if nr else 0) + (ng - 1 if ng else 0) + late
    lax.fori_loop(0, ticks, tick, 0)

    def finish(k, carry):
        if turn:
            for hop in range(1, size_dp):
                turn_copy(hop, k).wait_send()
        if nr:
            for block in range(nr):
                half_copy(block, k).wait_send()

                @pl.when(block != zr)
                def _():
                    right_copy(block, k).wait_send()

        if ng:
            for block in range(ng):
                core_copy(block, k).wait()

                @pl.when((zg < last_g) & (block <= zg))
                def _():
                    ag_right_copy(block, k).wait_send()

                @pl.when((zg > 0) & (block >= zg))
                def _():
                    ag_left_copy(block, k).wait_send()

        return carry

    lax.fori_loop(0, chunks, finish, 0)
    for index, (kind, axis) in enumerate(sides):
        if kind == "gather":
            length = side_ins[index].shape[axis]
            side_outs[index][share(axis, length, dp)] = side_ins[index][...]
    for copy in first_copies:
        copy.wait_send()
    for copy in more_copies:
        copy.wait()
    for unused, unused, copy in relays:
        copy.wait()
    for index, (kind, axis) in enumerate(sides):
        if kind == "scatter":
            src, dst = side_ins[index], side_outs[index]
            slots = side_scratch[3 * index + 2]
            length, height = dst.shape[axis], dst.shape[0] // 2
            if relay:
                for side in range(2):
                    total = src[half_share(axis, length, dp, height, side)].astype(jnp.float32)
                    total += slots[4 * side + 1].astype(jnp.float32)
                    total += slots[4 * side + 3].astype(jnp.float32)
                    dst[pl.ds(side * height, height), :] = total
            else:
                total = src[share(axis, length, dp)].astype(jnp.float32)
                for hop in range(1, size_dp):
                    total += slots[hop].astype(jnp.float32)
                dst[...] = total


def line_call(
    name,
    cid,
    partial,
    ins,
    out_types,
    step,
    rows,
    width,
    chunks,
    nr,
    ng,
    time,
    sides=(),
    turn=None,
    relay_tick=0,
):
    piece = rows // chunks
    size_dp = lax.axis_size("dp")
    reduced = gathered = (rows, width)
    if turn == "gather":
        gathered = (rows // size_dp, width * size_dp)
    elif turn == "spread":
        gathered = (rows * size_dp, width // size_dp)
    out_shape = []
    if ng:
        out_shape.append(
            jax.ShapeDtypeStruct((2 * ng * gathered[0], gathered[1]), jnp.bfloat16)
        )
    out_shape += out_types
    dma = pltpu.SemaphoreType.DMA
    scratch = []
    for kind, axis, values in sides:
        shape = list(values.shape)
        scratch += [dma((max(size_dp, 6),)), dma((max(size_dp, 6),))]
        if kind == "gather":
            shape[axis] *= size_dp
            out_shape.append(jax.ShapeDtypeStruct(tuple(shape), values.dtype))
            scratch.append(pltpu.VMEM((16, 128), values.dtype))
        else:
            shape[axis] //= size_dp
            out_shape.append(jax.ShapeDtypeStruct(tuple(shape), jnp.float32))
            slots = (8, shape[0] // 2, shape[1]) if size_dp == 4 else (size_dp, *shape)
            scratch.append(pltpu.VMEM(slots, values.dtype))
    if nr:
        scratch += [pltpu.VMEM((nr, chunks, piece, width), jnp.bfloat16)] * 4
        scratch += [dma((nr, chunks))] * 5
    if ng:
        scratch += [dma((ng, chunks))] * 6
    if turn:
        scratch.append(pltpu.VMEM((chunks, piece, width), jnp.bfloat16))
        scratch += [dma((size_dp, chunks))] * 2
    args = ([partial] if nr else []) + list(ins) + [side[2] for side in sides]
    vmem = pl.BlockSpec(memory_space=pltpu.VMEM)
    call = pl.pallas_call(
        functools.partial(
            line_kernel,
            nr,
            ng,
            chunks,
            (reduced, gathered),
            len(ins),
            len(out_types),
            step,
            tuple(side[:2] for side in sides),
            turn,
            relay_tick,
        ),
        out_shape=out_shape,
        in_specs=[vmem] * len(args),
        out_specs=[vmem] * len(out_shape),
        scratch_shapes=scratch,
        compiler_params=pltpu.CompilerParams(
            collective_id=cid, has_side_effects=True, vmem_limit_bytes=VMEM_CAP
        ),
        cost_estimate=cost_of(time),
        name=name,
    )
    return list(call(*args))


def head_stats_kernel(block, tile, table_ref, final_ref, wanted_ref, edge_ref, exp_ref, top_ref, sum_ref, pick_ref):
    j = pl.program_id(0)
    tokens = final_ref.shape[0]
    place = j * block + lax.broadcasted_iota(jnp.int32, (block, 1), 0)
    valid = place < edge_ref[0]

    def one(i, carry):
        at = pl.ds(i * tile, tile)
        logits = lax.dot_general(
            table_ref[...],
            final_ref[at, :],
            (((1,), (1,)), ((), ())),
            preferred_element_type=jnp.float32,
        )
        logits = jnp.where(valid, logits, MASKED)
        top = jnp.max(logits, axis=0, keepdims=True)
        weights = jnp.exp(logits - top)
        exp_ref[:, at] = weights.astype(jnp.bfloat16)
        top_ref[0, :, at] = top
        sum_ref[0, :, at] = jnp.sum(weights, axis=0, keepdims=True)
        pick_ref[0, :, at] = jnp.sum(
            jnp.where(place == wanted_ref[:, at], logits, 0.0), axis=0, keepdims=True
        )
        return carry

    for i in range(tokens // tile):
        one(i, 0)


def head_stats(table, final, wanted, edge, block, tile=512):
    rows, width = table.shape
    tokens = final.shape[0]
    steps = pl.cdiv(rows, block)
    row = jax.ShapeDtypeStruct((steps, 1, tokens), jnp.float32)
    row_spec = pl.BlockSpec((1, 1, tokens), lambda j: (j, 0, 0))
    return pl.pallas_call(
        functools.partial(head_stats_kernel, block, tile),
        grid=(steps,),
        out_shape=[jax.ShapeDtypeStruct((steps * block, tokens), jnp.bfloat16), row, row, row],
        in_specs=[
            pl.BlockSpec((block, width), lambda j: (j, 0)),
            pl.BlockSpec((tokens, width), lambda j: (0, 0)),
            pl.BlockSpec((1, tokens), lambda j: (0, 0)),
            pl.BlockSpec(memory_space=pltpu.SMEM),
        ],
        out_specs=[pl.BlockSpec((block, tokens), lambda j: (j, 0)), row_spec, row_spec, row_spec],
        compiler_params=pltpu.CompilerParams(vmem_limit_bytes=56 * 2**20),
        cost_estimate=pl.CostEstimate(
            flops=2 * rows * width * tokens,
            bytes_accessed=2 * rows * (width + tokens),
            transcendentals=rows * tokens,
        ),
        name="head_stats",
    )(table, final, wanted, edge)


def head_back_kernel(rows, block, tile, exp_ref, table_ref, final_ref, scale_ref, weight_ref, wanted_ref, grad_ref, dfinal_ref, dl_ref, sum_ref):
    j = pl.program_id(0)
    tokens = final_ref.shape[0]
    place = j * block + lax.broadcasted_iota(jnp.int32, (block, 1), 0)

    @pl.when(j == 0)
    def _():
        sum_ref[...] = jnp.zeros_like(sum_ref)

    table = jnp.where(place < rows, table_ref[...], jnp.zeros_like(table_ref))

    def one(i, carry):
        at = pl.ds(i * tile, tile)
        weight = weight_ref[:, at]
        dl = exp_ref[:, at].astype(jnp.float32) * scale_ref[0, :, at]
        dl = dl - jnp.where(place == wanted_ref[:, at], weight, 0.0)
        dl = dl.astype(jnp.bfloat16)
        dl_ref[:, at] = dl
        sum_ref[at, :] += lax.dot_general(
            dl, table, (((0,), (0,)), ((), ())), preferred_element_type=jnp.float32
        )
        return carry

    for i in range(tokens // tile):
        one(i, 0)

    strip = block // max(1, block // 256)

    def two(i, carry):
        at = pl.ds(i * strip, strip)
        grad_ref[at, :] = jnp.dot(
            dl_ref[at, :], final_ref[...], preferred_element_type=jnp.float32
        ).astype(jnp.bfloat16)
        return carry

    for i in range(block // strip):
        two(i, 0)

    @pl.when(j == pl.num_programs(0) - 1)
    def _():
        dfinal_ref[...] = sum_ref[...].astype(jnp.bfloat16)


def head_back(exps, table, final, scale, weight, wanted, block, tile=256):
    rows, width = table.shape
    tokens = final.shape[0]
    steps = pl.cdiv(rows, block)
    return pl.pallas_call(
        functools.partial(head_back_kernel, rows, block, tile),
        grid=(steps,),
        out_shape=[
            jax.ShapeDtypeStruct((rows, width), jnp.bfloat16),
            jax.ShapeDtypeStruct((tokens, width), jnp.bfloat16),
        ],
        in_specs=[
            pl.BlockSpec((block, tokens), lambda j: (j, 0)),
            pl.BlockSpec((block, width), lambda j: (j, 0)),
            pl.BlockSpec((tokens, width), lambda j: (0, 0)),
            pl.BlockSpec((1, 1, tokens), lambda j: (j, 0, 0)),
            pl.BlockSpec((1, tokens), lambda j: (0, 0)),
            pl.BlockSpec((1, tokens), lambda j: (0, 0)),
        ],
        out_specs=[
            pl.BlockSpec((block, width), lambda j: (j, 0)),
            pl.BlockSpec((tokens, width), lambda j: (0, 0)),
        ],
        scratch_shapes=[
            pltpu.VMEM((block, tokens), jnp.bfloat16),
            pltpu.VMEM((tokens, width), jnp.float32),
        ],
        compiler_params=pltpu.CompilerParams(vmem_limit_bytes=60 * 2**20),
        cost_estimate=pl.CostEstimate(
            flops=4 * rows * width * tokens,
            bytes_accessed=2 * rows * (2 * width + tokens),
            transcendentals=0,
        ),
        name="head_back",
    )(exps, table, final, scale, weight, wanted)


def head_weights(mixed_ref, starts_ref, base, at, seen):
    query = mixed_ref[at : at + QUERIES, base : base + HD]
    keys = mixed_ref[0:seen, base + HD : base + 2 * HD]
    values = mixed_ref[0:seen, base + 2 * HD : base + 3 * HD]
    scores = lax.dot_general(
        query, keys, (((1,), (1,)), ((), ())), preferred_element_type=jnp.float32
    )
    row = at + lax.broadcasted_iota(jnp.int32, (QUERIES, seen), 0)
    column = lax.broadcasted_iota(jnp.int32, (QUERIES, seen), 1)
    allowed = (column <= row) & (column >= starts_ref[at : at + QUERIES, :])
    scores = jnp.where(allowed, scores * HD ** (-0.5), MASKED)
    weights = jnp.exp(scores - jnp.max(scores, axis=1, keepdims=True))
    probs = weights / jnp.sum(weights, axis=1, keepdims=True)
    return query, keys, values, probs


def attend_kernel(mixed_ref, starts_ref, out_ref):
    length = mixed_ref.shape[0]
    for at in range(0, length, QUERIES):
        found = []
        for head in range(2):
            unused, unused, values, probs = head_weights(
                mixed_ref, starts_ref, head * 3 * HD, at, at + QUERIES
            )
            found.append(
                jnp.dot(probs.astype(jnp.bfloat16), values, preferred_element_type=jnp.float32)
            )
        out_ref[at : at + QUERIES, :] = jnp.concatenate(found, axis=1).astype(jnp.bfloat16)


def attend(mixed, starts):
    length, columns = mixed.shape
    pairs = columns // (6 * HD)
    return pl.pallas_call(
        attend_kernel,
        grid=(pairs,),
        out_shape=jax.ShapeDtypeStruct((length, pairs * 2 * HD), jnp.bfloat16),
        in_specs=[
            pl.BlockSpec((length, 6 * HD), lambda j: (0, j)),
            pl.BlockSpec((length, 1), lambda j: (0, 0)),
        ],
        out_specs=pl.BlockSpec((length, 2 * HD), lambda j: (0, j)),
        compiler_params=pltpu.CompilerParams(vmem_limit_bytes=40 * 2**20),
        cost_estimate=pl.CostEstimate(
            flops=8 * pairs * length * length * HD,
            bytes_accessed=2 * length * columns,
            transcendentals=pairs * length * length,
        ),
        name="attend",
    )(mixed, starts)


def attend_back_kernel(mixed_ref, starts_ref, upstream_ref, out_ref, sums_ref):
    length = mixed_ref.shape[0]
    sums_ref[...] = jnp.zeros_like(sums_ref)
    rows = (((0,), (0,)), ((), ()))
    for at in range(0, length, QUERIES):
        seen = at + QUERIES
        for head in range(2):
            base = head * 3 * HD
            query, keys, values, probs = head_weights(mixed_ref, starts_ref, base, at, seen)
            upstream = upstream_ref[at:seen, head * HD : head * HD + HD]
            dprobs = lax.dot_general(
                upstream, values, (((1,), (1,)), ((), ())), preferred_element_type=jnp.float32
            )
            inner = jnp.sum(probs * dprobs, axis=1, keepdims=True)
            dscores = (probs * (dprobs - inner)).astype(jnp.bfloat16)
            dquery = jnp.dot(dscores, keys, preferred_element_type=jnp.float32)
            dkeys = lax.dot_general(dscores, query, rows, preferred_element_type=jnp.float32)
            dvalues = lax.dot_general(
                probs.astype(jnp.bfloat16), upstream, rows, preferred_element_type=jnp.float32
            )
            sums_ref[at:seen, base : base + HD] = dquery * HD ** (-0.5)
            sums_ref[0:seen, base + HD : base + 2 * HD] += dkeys * HD ** (-0.5)
            sums_ref[0:seen, base + 2 * HD : base + 3 * HD] += dvalues
    out_ref[...] = sums_ref[...].astype(jnp.bfloat16)


def attend_back(mixed, starts, upstream):
    length, columns = mixed.shape
    pairs = columns // (6 * HD)
    return pl.pallas_call(
        attend_back_kernel,
        grid=(pairs,),
        out_shape=jax.ShapeDtypeStruct((length, columns), jnp.bfloat16),
        in_specs=[
            pl.BlockSpec((length, 6 * HD), lambda j: (0, j)),
            pl.BlockSpec((length, 1), lambda j: (0, 0)),
            pl.BlockSpec((length, 2 * HD), lambda j: (0, j)),
        ],
        out_specs=pl.BlockSpec((length, 6 * HD), lambda j: (0, j)),
        scratch_shapes=[pltpu.VMEM((length, 6 * HD), jnp.float32)],
        compiler_params=pltpu.CompilerParams(vmem_limit_bytes=40 * 2**20),
        cost_estimate=pl.CostEstimate(
            flops=20 * pairs * length * length * HD,
            bytes_accessed=4 * length * columns,
            transcendentals=pairs * length * length,
        ),
        name="attend_back",
    )(mixed, starts, upstream)


def small_gather_kernel(axis, count, src_ref, out_ref, send, recv):
    dp = lax.axis_index("dp")
    mp = lax.axis_index("mp")
    me = dp if axis == "dp" else mp

    def device(peer):
        return (peer, mp) if axis == "dp" else (dp, peer)

    barrier = pltpu.get_barrier_semaphore()
    for hop in range(1, count):
        pl.semaphore_signal(
            barrier, inc=1, device_id=device(lax.rem(me + hop, count)), device_id_type=MESH
        )
    pl.semaphore_wait(barrier, count - 1)
    copies = []
    for hop in range(1, count):
        peer = lax.rem(me + hop, count)
        copy = pltpu.make_async_remote_copy(
            src_ref=src_ref,
            dst_ref=out_ref.at[me],
            send_sem=send.at[hop],
            recv_sem=recv.at[hop],
            device_id=device(peer),
            device_id_type=MESH,
        )
        copy.start()
        copies.append(copy)
    out_ref[me] = src_ref[...]
    for copy in copies:
        copy.wait()


def small_gather(name, cid, values, axis):
    count = lax.axis_size(axis)
    vmem = pl.BlockSpec(memory_space=pltpu.VMEM)
    return pl.pallas_call(
        functools.partial(small_gather_kernel, axis, count),
        out_shape=jax.ShapeDtypeStruct((count,) + values.shape, values.dtype),
        in_specs=[vmem],
        out_specs=vmem,
        scratch_shapes=[pltpu.SemaphoreType.DMA((count,)), pltpu.SemaphoreType.DMA((count,))],
        compiler_params=pltpu.CompilerParams(collective_id=cid, has_side_effects=True),
        cost_estimate=cost_of(6),
        name=name,
    )(values)


def exchange(axis, me, here, source, slots, send, recv, first):
    count = slots.shape[0]
    copies = []
    for hop in range(1, count):
        peer = lax.rem(me + hop, count)
        copy = pltpu.make_async_remote_copy(
            src_ref=source,
            dst_ref=slots.at[me],
            send_sem=send.at[first + hop],
            recv_sem=recv.at[first + hop],
            device_id=(peer, here) if axis == "dp" else (here, peer),
            device_id_type=MESH,
        )
        copy.start()
        copies.append(copy)
    slots[me] = source[...]
    for copy in copies:
        copy.wait()
    total = slots[0]
    for index in range(1, count):
        total = total + slots[index]
    return total


def greet_all(dp, mp, size_dp, size_mp):
    barrier = pltpu.get_barrier_semaphore()
    for hop in range(1, size_dp):
        pl.semaphore_signal(
            barrier, inc=1, device_id=(lax.rem(dp + hop, size_dp), mp), device_id_type=MESH
        )
    for hop in range(1, size_mp):
        pl.semaphore_signal(
            barrier, inc=1, device_id=(dp, lax.rem(mp + hop, size_mp)), device_id_type=MESH
        )
    pl.semaphore_wait(barrier, size_dp + size_mp - 2)


def lane_rows(values):
    values = values.reshape(-1)
    return jnp.pad(values, (0, -values.size % 128)).reshape(-1, 128)


def fold(values):
    return jnp.sum(values, axis=0, keepdims=True)


def stats_kernel(full, size_dp, size_mp, *refs):
    row_part, row_old, col_part, col_old, weight_sq = (refs[5 * n : 5 * n + 5] for n in range(5))
    loss_part, norm_one, norm_two, norm_three, norms, second_old = refs[25:31]
    refs = refs[31:]
    row_out, col_out = refs[0:5], refs[5:10]
    loss_out, grads_out, second_out, norms_out, rate_out = refs[10:15]
    send_dp, slots_dp, send_mp, slots_mp, parts, part_slots, whole, send, recv = refs[15:]
    dp = lax.axis_index("dp")
    mp = lax.axis_index("mp")
    greet_all(dp, mp, size_dp, size_mp)
    beta = 1.0 - STEP ** (-0.8)
    width = norms.shape[1]

    at = 0
    marks = []

    def put(values):
        nonlocal at
        rows = values.shape[0]
        send_dp[at : at + rows, :] = values
        marks.append((at, rows))
        at += rows

    norm_rows = width // 128
    for ref in (norm_one, norm_two, norm_three):
        for which in range(2):
            for piece in range(norm_rows):
                put(ref[which : which + 1, piece * 128 : piece * 128 + 128])
    marks.clear()
    count_norm = at
    for index in (0, 2, 4):
        put(row_part[index][...])
    for index in (1, 3):
        put(col_part[index][...])
    put(loss_part[...])
    for index in (1, 3):
        put(fold(row_old[index][...]))
    for index in range(5):
        put(fold(weight_sq[index][...]))
    if at < send_dp.shape[0]:
        send_dp[at:, :] = jnp.zeros((send_dp.shape[0] - at, 128), jnp.float32)
    over_dp = exchange("dp", dp, mp, send_dp, slots_dp, send, recv, 0)
    taken = [over_dp[start : start + rows] for start, rows in marks]
    loss_out[...] = taken[5]
    row_full = {0: taken[0], 2: taken[1], 4: taken[2]}
    col_full = {1: taken[3], 3: taken[4]}
    old_total = {1: taken[6], 3: taken[7]}
    weight_rows = taken[8:13]

    at = 0
    marks = []

    def put_mp(values):
        nonlocal at
        rows = values.shape[0]
        send_mp[at : at + rows, :] = values
        marks.append((at, rows))
        at += rows

    for index in (0, 2, 4):
        put_mp(col_part[index][...])
    for index in (1, 3):
        put_mp(row_part[index][...])
    for index in range(5):
        put_mp(fold(row_full[index] if index in row_full else col_full[index]))
    for index in (0, 2, 4):
        put_mp(fold(row_old[index][...]))
    for index in range(5):
        put_mp(weight_rows[index])
    if at < send_mp.shape[0]:
        send_mp[at:, :] = jnp.zeros((send_mp.shape[0] - at, 128), jnp.float32)
    each = count_norm // size_mp
    for index in range(size_mp):
        parts[index] = over_dp[index * each : index * each + each]
    first = size_dp + size_mp
    copies = []
    for hop in range(1, size_mp):
        peer = lax.rem(mp + hop, size_mp)
        copy = pltpu.make_async_remote_copy(
            src_ref=parts.at[peer],
            dst_ref=part_slots.at[mp],
            send_sem=send.at[first + hop],
            recv_sem=recv.at[first + hop],
            device_id=(dp, peer),
            device_id_type=MESH,
        )
        copy.start()
        copies.append(copy)
    part_slots[mp] = parts[mp]
    over_mp = exchange("mp", mp, dp, send_mp, slots_mp, send, recv, size_dp)
    for copy in copies:
        copy.wait()
    summed = part_slots[0]
    for index in range(1, size_mp):
        summed = summed + part_slots[index]
    whole[mp] = summed
    first += size_mp
    copies = []
    for hop in range(1, size_mp):
        peer = lax.rem(mp + hop, size_mp)
        copy = pltpu.make_async_remote_copy(
            src_ref=whole.at[mp],
            dst_ref=whole.at[mp],
            send_sem=send.at[first + hop],
            recv_sem=recv.at[first + hop],
            device_id=(dp, peer),
            device_id_type=MESH,
        )
        copies.append(copy)
    for copy in copies:
        copy.start()
    taken = [over_mp[start : start + rows] for start, rows in marks]
    for slot, index in enumerate((0, 2, 4)):
        col_full[index] = taken[slot]
        old_total[index] = taken[10 + slot]
    for slot, index in enumerate((1, 3)):
        row_full[index] = taken[3 + slot]
    square_total = taken[5:10]
    weight_total = taken[13:18]
    for index in range(5):
        full_rows, full_cols = full[index]
        row_new = beta * row_old[index][...] + (1.0 - beta) * row_full[index] / full_cols
        col_new = beta * col_old[index][...] + (1.0 - beta) * col_full[index] / full_rows
        row_out[index][...] = row_new
        col_out[index][...] = col_new
        mean = (
            beta * jnp.sum(old_total[index], axis=1, keepdims=True)
            + (1.0 - beta) * jnp.sum(square_total[index], axis=1, keepdims=True) / full_cols
        ) / full_rows
        rate = RHO * jnp.sqrt(
            jnp.sum(weight_total[index], axis=1, keepdims=True) / (full_rows * full_cols)
        )
        rate_out[index : index + 1, :] = jnp.broadcast_to(mean, (1, 128))
        rate_out[8 + index : 9 + index, :] = jnp.broadcast_to(rate, (1, 128))
    for copy in copies:
        copy.wait()
    for row in range(6):
        for piece in range(norm_rows):
            place = row * norm_rows + piece
            grads_out[row : row + 1, piece * 128 : piece * 128 + 128] = whole[
                place // each, place % each : place % each + 1, :
            ]
    grad = grads_out[...]
    second = beta * second_old[...] + (1.0 - beta) * (grad * grad + EPS_ONE)
    second_out[...] = second
    step = grad * lax.rsqrt(second)
    entries = step.size

    def mean_square(values):
        return jnp.sum(jnp.sum(values * values, axis=0, keepdims=True), axis=1, keepdims=True) / (
            entries
        )

    step = step / jnp.maximum(1.0, jnp.sqrt(mean_square(step)) / CLIP)
    old = norms[...]
    norms_out[...] = old - RHO * jnp.sqrt(mean_square(old)) * step


def update_stats(cid, row_parts, rows_old, col_parts, cols_old, weight_sq, loss, norm_parts, norms, second, full):
    size_dp = lax.axis_size("dp")
    size_mp = lax.axis_size("mp")
    f32 = jnp.float32
    rows_old2 = [lane_rows(v) for v in rows_old]
    cols_old2 = [lane_rows(v) for v in cols_old]
    args = (
        [lane_rows(v) for v in row_parts]
        + rows_old2
        + [lane_rows(v) for v in col_parts]
        + cols_old2
        + [v if v.ndim == 2 else lane_rows(v) for v in weight_sq]
        + [lane_rows(loss)]
        + list(norm_parts)
        + [norms, second]
    )
    width = norms.shape[1]
    count_norm = 6 * width // 128
    size_a = count_norm + sum(rows_old2[n].shape[0] for n in (0, 2, 4))
    size_a += sum(cols_old2[n].shape[0] for n in (1, 3)) + 8
    size_a += -size_a % 8
    size_b = sum(cols_old2[n].shape[0] for n in (0, 2, 4))
    size_b += sum(rows_old2[n].shape[0] for n in (1, 3)) + 13
    size_b += -size_b % 8
    each = count_norm // size_mp
    out_shape = [jax.ShapeDtypeStruct(v.shape, f32) for v in rows_old2 + cols_old2]
    out_shape += [
        jax.ShapeDtypeStruct((1, 128), f32),
        jax.ShapeDtypeStruct(norms.shape, f32),
        jax.ShapeDtypeStruct(norms.shape, f32),
        jax.ShapeDtypeStruct(norms.shape, f32),
        jax.ShapeDtypeStruct((16, 128), f32),
    ]
    sems = size_dp + 3 * size_mp
    vmem = pl.BlockSpec(memory_space=pltpu.VMEM)
    found = pl.pallas_call(
        functools.partial(stats_kernel, full, size_dp, size_mp),
        out_shape=out_shape,
        in_specs=[vmem] * len(args),
        out_specs=[vmem] * len(out_shape),
        scratch_shapes=[
            pltpu.VMEM((size_a, 128), f32),
            pltpu.VMEM((size_dp, size_a, 128), f32),
            pltpu.VMEM((size_b, 128), f32),
            pltpu.VMEM((size_mp, size_b, 128), f32),
            pltpu.VMEM((size_mp, each, 128), f32),
            pltpu.VMEM((size_mp, each, 128), f32),
            pltpu.VMEM((size_mp, each, 128), f32),
            pltpu.SemaphoreType.DMA((sems,)),
            pltpu.SemaphoreType.DMA((sems,)),
        ],
        compiler_params=pltpu.CompilerParams(collective_id=cid, has_side_effects=True),
        cost_estimate=cost_of(12),
        name="update_stats",
    )(*args)
    rows_new = [found[n].reshape(-1)[: rows_old[n].size] for n in range(5)]
    cols_new = [found[5 + n].reshape(-1)[: cols_old[n].size] for n in range(5)]
    loss_sums = found[10][0, :NSRC]
    return rows_new, cols_new, loss_sums, found[11], found[12], found[13], found[14]


def clip_kernel(entries, size_dp, size_mp, *refs):
    parts, rate = refs[:5], refs[5]
    out, mine, slots_dp, slots_mp, send, recv = refs[6:]
    dp = lax.axis_index("dp")
    mp = lax.axis_index("mp")
    greet_all(dp, mp, size_dp, size_mp)
    mine[...] = jnp.zeros_like(mine)
    for index in range(5):
        mine[index : index + 1, :] = fold(parts[index][...])
    mine[...] = exchange("dp", dp, mp, mine, slots_dp, send, recv, 0)
    total = exchange("mp", mp, dp, mine, slots_mp, send, recv, size_dp)
    total = jnp.sum(total, axis=1, keepdims=True)
    for index in range(5):
        clip = jnp.maximum(1.0, jnp.sqrt(total[index : index + 1] / entries[index]) / CLIP)
        out[index : index + 1, :] = rate[8 + index : 9 + index, :] / clip


def clip_rates(cid, step_parts, rate, entries):
    size_dp = lax.axis_size("dp")
    size_mp = lax.axis_size("mp")
    vmem = pl.BlockSpec(memory_space=pltpu.VMEM)
    sems = size_dp + size_mp
    return pl.pallas_call(
        functools.partial(clip_kernel, entries, size_dp, size_mp),
        out_shape=jax.ShapeDtypeStruct((8, 128), jnp.float32),
        in_specs=[vmem] * 6,
        out_specs=vmem,
        scratch_shapes=[
            pltpu.VMEM((8, 128), jnp.float32),
            pltpu.VMEM((size_dp, 8, 128), jnp.float32),
            pltpu.VMEM((size_mp, 8, 128), jnp.float32),
            pltpu.SemaphoreType.DMA((sems,)),
            pltpu.SemaphoreType.DMA((sems,)),
        ],
        compiler_params=pltpu.CompilerParams(collective_id=cid, has_side_effects=True),
        cost_estimate=cost_of(8),
        name="clip_rates",
    )(*[lane_rows(v) for v in step_parts], rate)


UNROLL = 8


def lookup_kernel(shift, count_ref, key_ref, table_ref, out_ref, low_ref, square_ref, rows_ref):
    spots = out_ref.shape[0]
    vocab, width = table_ref.shape
    rows_ref[...] = jnp.zeros_like(rows_ref)

    def some(i, carry):
        for j in range(UNROLL):
            key = key_ref[i * UNROLL + j]
            place = key & ((1 << shift) - 1)
            rows_ref[pl.ds(place, 1), :] = table_ref[pl.ds(key >> shift, 1), :]
        return carry

    lax.fori_loop(0, (count_ref[0] + UNROLL - 1) // UNROLL, some, 0)

    def narrow(i, carry):
        at = pl.ds(pl.multiple_of(i * 256, 256), 256)
        out_ref[at, :] = rows_ref[at, :].astype(jnp.bfloat16)
        return carry

    lax.fori_loop(0, spots // 256, narrow, 0)
    strip = 48 if vocab % 48 == 0 else 8

    def lower(i, total):
        at = pl.ds(pl.multiple_of(i * strip, strip), strip)
        values = table_ref[at, :]
        low_ref[at, :] = values.astype(jnp.bfloat16)
        for row in range(0, strip, 8):
            piece = values[row : row + 8, :]
            total = total + piece * piece
        return total

    total = lax.fori_loop(0, vocab // strip, lower, jnp.zeros((8, width), jnp.float32))
    folded = total[:, 0:128]
    for start in range(128, width, 128):
        folded = folded + total[:, start : start + 128]
    square_ref[...] = folded


def lookup(keys, count, table, spots, shift):
    vocab, width = table.shape
    smem = pl.BlockSpec(memory_space=pltpu.SMEM)
    vmem = pl.BlockSpec(memory_space=pltpu.VMEM)
    return pl.pallas_call(
        functools.partial(lookup_kernel, shift),
        out_shape=[
            jax.ShapeDtypeStruct((spots, width), jnp.bfloat16),
            jax.ShapeDtypeStruct((vocab, width), jnp.bfloat16),
            jax.ShapeDtypeStruct((8, 128), jnp.float32),
        ],
        in_specs=[smem, smem, vmem],
        out_specs=[vmem] * 3,
        scratch_shapes=[pltpu.VMEM((spots + 8, width), jnp.float32)],
        compiler_params=pltpu.CompilerParams(vmem_limit_bytes=VMEM_CAP),
        cost_estimate=cost_of(20),
        name="lookup",
    )(count, keys, table)


def scatter_kernel(shift, count_ref, key_ref, head_ref, rows_in_ref, grad_ref, rows_ref):
    spots = rows_in_ref.shape[0]
    width = grad_ref.shape[1]

    def widen(i, carry):
        at = pl.ds(pl.multiple_of(i * 256, 256), 256)
        rows_ref[at, :] = rows_in_ref[at, :].astype(jnp.float32)
        return carry

    lax.fori_loop(0, spots // 256, widen, 0)
    rows_ref[spots:, :] = jnp.zeros((8, width), jnp.float32)
    grad_ref[...] = head_ref[...].astype(jnp.float32)

    def some(i, carry):
        for j in range(UNROLL):
            key = key_ref[i * UNROLL + j]
            place = key & ((1 << shift) - 1)
            grad_ref[pl.ds(key >> shift, 1), :] += rows_ref[pl.ds(place, 1), :]
        return carry

    lax.fori_loop(0, (count_ref[0] + UNROLL - 1) // UNROLL, some, 0)


def scatter(keys, count, head_grad, rows, shift):
    spots, width = rows.shape
    vocab = head_grad.shape[0]
    smem = pl.BlockSpec(memory_space=pltpu.SMEM)
    vmem = pl.BlockSpec(memory_space=pltpu.VMEM)
    return pl.pallas_call(
        functools.partial(scatter_kernel, shift),
        out_shape=jax.ShapeDtypeStruct((vocab, width), jnp.float32),
        in_specs=[smem, smem, vmem, vmem],
        out_specs=vmem,
        scratch_shapes=[pltpu.VMEM((spots + 8, width), jnp.float32)],
        compiler_params=pltpu.CompilerParams(vmem_limit_bytes=VMEM_CAP),
        cost_estimate=cost_of(23),
        name="scatter",
    )(count, keys, head_grad, rows)


def norm_parts(values):
    centre = jnp.mean(values, axis=-1, keepdims=True)
    centred = values - centre
    scale = lax.rsqrt(jnp.mean(centred * centred, axis=-1, keepdims=True) + EPS_NORM)
    return centred * scale, scale


def norm_pull(values, gain, upstream):
    normed, scale = norm_parts(values)
    weighted = upstream * gain
    pulled = scale * (
        weighted
        - jnp.mean(weighted, axis=-1, keepdims=True)
        - normed * jnp.mean(weighted * normed, axis=-1, keepdims=True)
    )
    return (
        pulled,
        jnp.sum(upstream * normed, axis=0, keepdims=True),
        jnp.sum(upstream, axis=0, keepdims=True),
    )


def step_first(total, at, ins, outs):
    stream, norms = outs[0], ins[0]
    normed, scale = norm_parts(stream[at, :].astype(jnp.float32))
    return normed * norms[0:1, :] + norms[1:2, :]


def step_forward(row, total, at, ins, outs):
    stream, norms = ins
    values = stream[at, :].astype(jnp.float32) + total
    outs[0][at, :] = values
    normed, scale = norm_parts(values)
    return normed * norms[row : row + 1, :] + norms[row + 1 : row + 2, :]


def step_backward(row, total, at, ins, outs):
    stream, norms = ins[:2]
    pulled, dgain, dshift = norm_pull(
        stream[at, :].astype(jnp.float32), norms[row : row + 1, :], total
    )
    if len(ins) > 2:
        pulled = pulled + ins[2][at, :]
    if len(outs) > 1:
        outs[0][at, :] = pulled
    sums = outs[-1]

    @pl.when(at.start == 0)
    def _():
        sums[...] = jnp.zeros_like(sums)

    sums[0:1, :] += dgain
    sums[1:2, :] += dshift
    return pulled


def gelu_tanh(values):
    return jax.nn.gelu(values, approximate=True)


def local(
    token_ids,
    targets,
    starts,
    sources,
    embedding,
    w_qkv,
    w_out,
    w_fc,
    w_proj,
    norm_params,
    rows_table,
    cols_table,
    rows_qkv,
    cols_qkv,
    rows_out,
    cols_out,
    rows_fc,
    cols_fc,
    rows_proj,
    cols_proj,
    second_norms,
):
    bf16 = jnp.bfloat16
    f32 = jnp.float32
    size_mp = lax.axis_size("mp")
    size_dp = lax.axis_size("dp")
    dp = lax.axis_index("dp")
    mp = lax.axis_index("mp")
    tokens = token_ids.shape[0]
    seqs = tokens // LEN
    chips = size_mp // 2
    near = chips // seqs
    sharers = size_mp // seqs
    rows = tokens // size_mp
    vocab, part_width = embedding.shape
    width = part_width * size_dp
    first_row = mp * vocab
    spots = tokens * size_dp
    chunks_full = max(1, min(8, rows // 32))
    chunks_near = max(1, min(4, rows // 32))

    both = jnp.stack([token_ids, sources]).reshape(-1, 128)
    both = small_gather("gather_ids", 0, both, "dp").reshape(size_dp, 2, tokens)
    all_ids = both[:, 0]
    all_sources = both[:, 1].reshape(-1)
    counts = jnp.sum(
        (all_sources[:, None] == jnp.arange(NSRC, dtype=jnp.int32)[None, :]).astype(f32), axis=0
    )

    w_qkv, w_out, w_fc, w_proj, all_ids = lax.optimization_barrier(
        (w_qkv, w_out, w_fc, w_proj, all_ids)
    )


    def own_and_twins(weight, axis):
        weight = weight.astype(bf16)
        found = [weight]
        for turn in range(1, seqs):
            shift = [(i, (i + turn * sharers) % size_mp) for i in range(size_mp)]
            found.append(lax.ppermute(weight, "mp", shift))
        return jnp.concatenate(found, axis=axis) if seqs > 1 else weight

    pair_qkv = own_and_twins(w_qkv, 1)
    pair_out = own_and_twins(w_out, 0)
    pair_fc = own_and_twins(w_fc, 1)
    pair_proj = own_and_twins(w_proj, 0)
    piece = rows // chunks_full
    token = jnp.arange(tokens, dtype=jnp.int32)
    place = (
        token // piece * (size_dp * piece)
        + (jnp.arange(size_dp, dtype=jnp.int32) * piece)[:, None]
        + token % piece
    )
    local_ids = all_ids - first_row
    inside = (local_ids >= 0) & (local_ids < vocab)
    shift = spots.bit_length()
    idle = ((vocab - 1) << shift) + spots
    keys = jnp.where(inside, (local_ids << shift) + place, idle)
    keys = jnp.sort(keys.reshape(-1))
    owned = jnp.sum(inside.astype(jnp.int32)).reshape(1)
    found, low_table, table_sq = lookup(keys, owned, embedding, spots, shift)
    inner_one, stream0, wide_qkv, wide_out, wide_fc, wide_proj = line_call(
        "lookup_sum",
        1,
        found,
        [norm_params],
        [jax.ShapeDtypeStruct((rows, width), bf16)],
        step_first,
        size_dp * rows,
        part_width,
        chunks_full,
        chips,
        near,
        70,
        [
            ("gather", 0, pair_qkv),
            ("gather", 1, pair_out),
            ("gather", 0, pair_fc),
            ("gather", 1, pair_proj),
        ],
        "gather",
        4,
    )
    low_table, inner_one = lax.optimization_barrier((low_table, inner_one))
    wide_table = lax.all_gather(low_table, "dp", axis=1, tiled=True)
    row_f32 = jax.ShapeDtypeStruct((rows, width), f32)
    pair_f32 = jax.ShapeDtypeStruct((8, width), f32)
    my_starts = row_slice(starts, (mp // sharers) * LEN, LEN)[:, None]
    mixed = jnp.dot(inner_one, wide_qkv, preferred_element_type=f32).astype(bf16)
    attended = attend(mixed, my_starts)
    partial = jnp.dot(attended, wide_out, preferred_element_type=f32).astype(bf16)
    inner_two, stream1 = line_call(
        "attn_sum",
        3,
        partial,
        [stream0, norm_params],
        [row_f32],
        functools.partial(step_forward, 2),
        rows,
        width,
        chunks_near,
        near,
        near,
        32,
    )
    before = jnp.dot(inner_two, wide_fc, preferred_element_type=f32)
    hidden = gelu_tanh(before).astype(bf16)
    partial = jnp.dot(hidden, wide_proj, preferred_element_type=f32).astype(bf16)
    final, stream2 = line_call(
        "mlp_sum",
        4,
        partial,
        [stream1, norm_params],
        [row_f32],
        functools.partial(step_forward, 4),
        rows,
        width,
        chunks_full,
        near,
        chips,
        58,
    )

    edge = jnp.clip(VREAL - first_row, 0, vocab).astype(jnp.int32).reshape(1)
    wanted = targets - first_row
    wanted = jnp.where((wanted >= 0) & (wanted < vocab), wanted, -1).reshape(1, tokens)
    block = 640
    exps, tops, sums, picks = head_stats(wide_table, final, wanted, edge, block)
    tops = tops[:, 0]
    top = jnp.max(tops, axis=0)
    total = jnp.sum(sums[:, 0] * jnp.exp(tops - top[None, :]), axis=0)
    pick = jnp.sum(picks[:, 0], axis=0)
    stats = jnp.concatenate([v.reshape(-1, 128) for v in (top, total, pick)])
    stats = small_gather("gather_stats", 5, stats, "mp").reshape(size_mp, 3, tokens)
    highest = jnp.max(stats[:, 0], axis=0)
    log_total = highest + jnp.log(
        jnp.sum(stats[:, 1] * jnp.exp(stats[:, 0] - highest[None, :]), axis=0)
    )
    token_loss = log_total - jnp.sum(stats[:, 2], axis=0)
    member = (sources[:, None] == jnp.arange(NSRC, dtype=jnp.int32)[None, :]).astype(f32)
    loss_part = jnp.sum(member * token_loss[:, None], axis=0)
    weight = jnp.sum(member / (NSRC * jnp.maximum(counts, 1.0))[None, :], axis=1)
    scale = jnp.exp(tops - log_total[None, :]) * weight[None, :]
    table_grad, dfinal = head_back(
        exps, wide_table, final, scale[:, None, :], weight[None, :], wanted, block
    )
    head_grad = lax.psum_scatter(table_grad, "dp", scatter_dimension=1, tiled=True)

    dbranch2, dstream2, norm3 = line_call(
        "final_back",
        6,
        dfinal,
        [stream2, norm_params],
        [row_f32, pair_f32],
        functools.partial(step_backward, 4),
        rows,
        width,
        chunks_full,
        chips,
        near,
        60,
    )
    grad_proj = jnp.einsum("tf,td->fd", hidden, dbranch2, preferred_element_type=f32).astype(bf16)
    dhidden = jnp.einsum("td,fd->tf", dbranch2, wide_proj, preferred_element_type=f32)
    unused, gelu_pull = jax.vjp(gelu_tanh, before)
    dbefore = gelu_pull(dhidden)[0].astype(bf16)
    partial = jnp.einsum("tf,df->td", dbefore, wide_fc, preferred_element_type=f32).astype(bf16)
    dbranch1, dstream1, norm2 = line_call(
        "mlp_back",
        7,
        partial,
        [stream1, norm_params, dstream2],
        [row_f32, pair_f32],
        functools.partial(step_backward, 2),
        rows,
        width,
        chunks_near,
        near,
        near,
        34,
    )
    grad_fc = jnp.einsum("td,tf->df", inner_two, dbefore, preferred_element_type=f32).astype(bf16)
    grad_out = jnp.einsum("tf,td->fd", attended, dbranch1, preferred_element_type=f32).astype(bf16)
    dattended = jnp.einsum("td,fd->tf", dbranch1, wide_out, preferred_element_type=f32)
    dmixed = attend_back(mixed, my_starts, dattended.astype(bf16))
    partial = jnp.einsum("tc,dc->td", dmixed, wide_qkv, preferred_element_type=f32).astype(bf16)
    grad_qkv = jnp.einsum("td,tc->dc", inner_one, dmixed, preferred_element_type=f32).astype(bf16)
    drows, norm1, grad_proj, grad_out, grad_fc, grad_qkv = line_call(
        "attn_back",
        8,
        partial,
        [stream0, norm_params, dstream1],
        [pair_f32],
        functools.partial(step_backward, 0),
        rows,
        width,
        chunks_full,
        near,
        chips,
        70,
        [
            ("scatter", 1, grad_proj),
            ("scatter", 1, grad_out),
            ("scatter", 0, grad_fc),
            ("scatter", 0, grad_qkv),
        ],
        "spread",
        5,
    )

    def to_twins(share, axis):
        pieces = jnp.split(share, seqs, axis=axis)
        found = []
        for turn in range(1, seqs):
            back = [(i, (i - turn * sharers) % size_mp) for i in range(size_mp)]
            found.append(lax.ppermute(pieces[turn].astype(bf16), "mp", back))
        return pieces[0], found

    shares = [
        to_twins(grad_qkv, 1),
        to_twins(grad_out, 0),
        to_twins(grad_fc, 1),
        to_twins(grad_proj, 0),
    ]
    grad_table = scatter(keys, owned, head_grad, drows, shift)
    shares, grad_table = lax.optimization_barrier((shares, grad_table))
    grad_qkv, grad_out, grad_fc, grad_proj = [
        sum((piece.astype(f32) for piece in found), mine) for mine, found in shares
    ]

    weights = (embedding, w_qkv, w_out, w_fc, w_proj)
    grads = (grad_table, grad_qkv, grad_out, grad_fc, grad_proj)
    row_span = (size_mp, size_dp, size_mp, size_dp, size_mp)
    col_span = (size_dp, size_mp, size_dp, size_mp, size_dp)
    full = tuple(
        (g.shape[0] * r, g.shape[1] * c) for g, r, c in zip(grads, row_span, col_span)
    )
    squares = [gradient * gradient + EPS_ONE for gradient in grads]
    rows_new, cols_new, loss_sums, grad_norms, second_new, norms_new, rates = update_stats(
        10,
        [jnp.sum(square, axis=1) for square in squares],
        (rows_table, rows_qkv, rows_out, rows_fc, rows_proj),
        [jnp.sum(square, axis=0) for square in squares],
        (cols_table, cols_qkv, cols_out, cols_fc, cols_proj),
        [table_sq] + [jnp.sum(value * value, axis=0) for value in weights[1:]],
        loss_part,
        (norm1, norm2, norm3),
        norm_params,
        second_norms,
        full,
    )
    steps = [
        grads[n] * lax.rsqrt(rows_new[n][:, None] * cols_new[n][None, :] / rates[n, 0])
        for n in range(5)
    ]
    factors = clip_rates(
        11, [jnp.sum(step * step, axis=0) for step in steps], rates, [r * c for r, c in full]
    )
    updated = [weights[n] - factors[n, 0] * steps[n] for n in range(5)]
    return (
        loss_sums,
        counts,
        grad_table,
        rows_new[0],
        cols_new[0],
        updated[0],
        grad_qkv,
        rows_new[1],
        cols_new[1],
        updated[1],
        grad_out,
        rows_new[2],
        cols_new[2],
        updated[2],
        grad_fc,
        rows_new[3],
        cols_new[3],
        updated[3],
        grad_proj,
        rows_new[4],
        cols_new[4],
        updated[4],
        grad_norms,
        second_new,
        norms_new,
    )


def solution(mesh):
    placed = (
        P("dp"),
        P("dp"),
        P("dp"),
        P("dp"),
        P("mp", "dp"),
        P("dp", "mp"),
        P("mp", "dp"),
        P("dp", "mp"),
        P("mp", "dp"),
        P(),
        P("mp"),
        P("dp"),
        P("dp"),
        P("mp"),
        P("mp"),
        P("dp"),
        P("dp"),
        P("mp"),
        P("mp"),
        P("dp"),
        P(),
    )
    return jax.shard_map(
        local,
        mesh=mesh,
        in_specs=placed,
        out_specs=(
            P(),
            P(),
            P("mp", "dp"),
            P("mp"),
            P("dp"),
            P("mp", "dp"),
            P("dp", "mp"),
            P("dp"),
            P("mp"),
            P("dp", "mp"),
            P("mp", "dp"),
            P("mp"),
            P("dp"),
            P("mp", "dp"),
            P("dp", "mp"),
            P("dp"),
            P("mp"),
            P("dp", "mp"),
            P("mp", "dp"),
            P("mp"),
            P("dp"),
            P("mp", "dp"),
            P(),
            P(),
            P(),
        ),
        check_vma=False,
    )
```

```python
import functools
import math

import jax
import jax.numpy as jnp
from jax import lax
from jax.experimental import pallas as pl
from jax.experimental.pallas import tpu as pltpu
from jax.sharding import PartitionSpec as P

HD = 64
VREAL = 50257
LEN = 1024
NSRC = 4
STEP = 10


EPS_NORM = 1e-05
EPS_ONE = 1e-30
CLIP = 1.0
RHO = 0.5
MASKED = -1e30
QUERIES = 256
MESH = pl.DeviceIdType.MESH
VMEM_CAP = 56 * 2**20


def cost_of(time):
    return pl.CostEstimate(
        flops=time * 1000000000, bytes_accessed=time * 3000000, transcendentals=0
    )


def row_slice(values, start, count):
    return lax.dynamic_slice_in_dim(values, start, count, 0)


def line_kernel(nr, ng, chunks, shapes, n_in, n_out, step, sides, turn, side_ticks, *refs):
    (rows_r, width_r), (rows_g, width_g) = shapes
    part = refs[0] if nr else None
    first = 1 if nr else 0
    ins = refs[first : first + n_in]
    refs = refs[first + n_in :]
    side_ins, refs = refs[: len(sides)], refs[len(sides) :]
    if ng:
        whole, refs = refs[0], refs[1:]
    outs = refs[:n_out]
    refs = refs[n_out:]
    side_outs, scratch = refs[: len(sides)], refs[len(sides) :]
    side_scratch, scratch = scratch[: 3 * len(sides)], scratch[3 * len(sides) :]
    if turn:
        cast, turn_send, turn_recv = scratch[-3:]
    size_dp = lax.axis_size("dp")
    dp = lax.axis_index("dp")
    mp = lax.axis_index("mp")
    z = mp // 2
    core = lax.rem(mp, 2)
    other = mp + 1 - 2 * core
    piece_r = rows_r // chunks
    piece_g = rows_g // chunks
    small = min(piece_r, piece_g)
    late = 1 if turn else 0
    most = max(nr, ng)
    zb = lax.rem(z, most)
    if nr:
        zr = lax.rem(z, nr)
        last_r = nr - 1
    if ng:
        zg = lax.rem(z, ng)
        last_g = ng - 1

    barrier = pltpu.get_barrier_semaphore()
    pl.semaphore_signal(barrier, inc=1, device_id=(dp, other), device_id_type=MESH)

    @pl.when(zb > 0)
    def _():
        pl.semaphore_signal(barrier, inc=1, device_id=(dp, mp - 2), device_id_type=MESH)

    @pl.when(zb < most - 1)
    def _():
        pl.semaphore_signal(barrier, inc=1, device_id=(dp, mp + 2), device_id_type=MESH)

    if sides or turn:
        for hop in range(1, size_dp):
            pl.semaphore_signal(
                barrier,
                inc=1,
                device_id=(lax.rem(dp + hop, size_dp), mp),
                device_id_type=MESH,
            )
    greeted = (size_dp if sides or turn else 1) + (zb > 0).astype(jnp.int32) + (zb < most - 1).astype(jnp.int32)
    pl.semaphore_wait(barrier, greeted)

    def share(axis, length, which):
        at = pl.ds(pl.multiple_of(which * length, length), length)
        return (at, slice(None)) if axis == 0 else (slice(None), at)

    def to_peer(src, dst, send, recv, peer):
        return pltpu.make_async_remote_copy(
            src_ref=src,
            dst_ref=dst,
            send_sem=send,
            recv_sem=recv,
            device_id=(peer, mp),
            device_id_type=MESH,
        )

    relay = size_dp == 4
    beside_x = dp + 1 - 2 * lax.rem(dp, 2)
    beside_y = lax.rem(dp + 2, 4)
    across = 3 - dp

    def half_share(axis, length, which, height, part):
        if axis == 0:
            return (pl.ds(pl.multiple_of(which * length + part * height, height), height), slice(None))
        at = pl.ds(pl.multiple_of(which * length, length), length)
        return (pl.ds(part * height, height), at)

    first_copies, more_copies, relays = [], [], []
    for index, (kind, axis) in enumerate(sides):
        src, dst = side_ins[index], side_outs[index]
        send, recv, slots = side_scratch[3 * index : 3 * index + 3]
        shard = src if kind == "gather" else dst
        length, height = shard.shape[axis], shard.shape[0] // 2
        if not relay:
            for hop in range(1, size_dp):
                peer = lax.rem(dp + hop, size_dp)
                if kind == "gather":
                    source, target = src, dst.at[share(axis, length, dp)]
                else:
                    source, target = src.at[share(axis, length, peer)], slots.at[hop]
                more_copies.append(to_peer(source, target, send.at[hop], recv.at[hop], peer))
            continue
        for side, near_one, far_one in ((0, beside_x, beside_y), (1, beside_y, beside_x)):
            sems = [(send.at[3 * side + n], recv.at[3 * side + n]) for n in range(3)]
            if kind == "gather":
                mine = src.at[pl.ds(side * height, height)]
                here = dst.at[half_share(axis, length, dp, height, side)]
                passed = dst.at[half_share(axis, length, near_one, height, side)]
                arrives = to_peer(mine, here, *sems[0], near_one)
                first_copies.append(arrives)
                more_copies.append(to_peer(mine, here, *sems[1], far_one))
                relays.append((arrives, None, to_peer(passed, passed, *sems[2], far_one)))
            else:
                arrives = to_peer(
                    src.at[half_share(axis, length, across, height, side)],
                    slots.at[4 * side],
                    *sems[0],
                    near_one,
                )
                first_copies.append(arrives)
                more_copies.append(
                    to_peer(
                        src.at[half_share(axis, length, near_one, height, side)],
                        slots.at[4 * side + 1],
                        *sems[1],
                        near_one,
                    )
                )
                summed = to_peer(
                    slots.at[4 * side + 2], slots.at[4 * side + 3], *sems[2], far_one
                )
                own = src.at[half_share(axis, length, far_one, height, side)]
                relays.append((arrives, (own, slots, 4 * side, height), summed))

    def pass_on(arrives, adding, copy):
        arrives.wait_recv()
        if adding is not None:
            own, slots, at, height = adding
            both = own[...].astype(jnp.float32) + slots[at].astype(jnp.float32)
            slots[at + 2] = both.astype(slots.dtype)
        copy.start()

    jobs = [copy.start for copy in first_copies + more_copies]
    jobs += [functools.partial(pass_on, *one) for one in relays]

    def side_jobs(now):
        for spot in range(side_ticks if jobs else 0):
            chosen = jobs[len(jobs) * spot // side_ticks : len(jobs) * (spot + 1) // side_ticks]

            @pl.when(now == spot)
            def _():
                for job in chosen:
                    job()

    if nr:
        half, from_left, from_right, going = scratch[:4]
        half_send, half_recv, rs_send, left_recv, right_recv = scratch[4:9]
        scratch = scratch[9:]
    if ng:
        core_send, core_recv, to_right, to_left, ag_left, ag_right = scratch[:6]

    def part_rows(block, k):
        return pl.ds(pl.multiple_of(block * rows_r + k * piece_r, piece_r), piece_r)

    def whole_rows(block, k):
        return pl.ds(pl.multiple_of(block * rows_g + k * piece_g, piece_g), piece_g)

    def remote(src, dst, send, recv, target):
        return pltpu.make_async_remote_copy(
            src_ref=src,
            dst_ref=dst,
            send_sem=send,
            recv_sem=recv,
            device_id=(dp, target),
            device_id_type=MESH,
        )

    if nr:

        def half_copy(dest, k):
            return remote(
                part.at[part_rows(2 * dest + 1 - core, k)],
                half.at[dest, k],
                half_send.at[dest, k],
                half_recv.at[dest, k],
                other,
            )

        def send_halves(k, carry):
            for dest in range(nr):
                half_copy(dest, k).start()
            return carry

        lax.fori_loop(0, chunks, send_halves, 0)

        def right_copy(dest, k):
            return remote(
                going.at[dest, k],
                from_left.at[dest, k],
                rs_send.at[dest, k],
                left_recv.at[dest, k],
                mp + 2,
            )

        def left_copy(dest, k):
            return remote(
                going.at[dest, k],
                from_right.at[dest, k],
                rs_send.at[dest, k],
                right_recv.at[dest, k],
                mp - 2,
            )

        def chip_sum(dest, k):
            half_copy(dest, k).wait_recv()
            mine = part[part_rows(2 * dest + core, k), :].astype(jnp.float32)
            return mine + half[dest, k].astype(jnp.float32)

        def pass_right(dest, k):
            total = chip_sum(dest, k)

            @pl.when(zr == 0)
            def _():
                going[dest, k] = total.astype(jnp.bfloat16)

            @pl.when(zr > 0)
            def _():
                right_copy(dest, k).wait_recv()
                both = total + from_left[dest, k].astype(jnp.float32)
                going[dest, k] = both.astype(jnp.bfloat16)

            right_copy(dest, k).start()

        def pass_left(dest, k):
            total = chip_sum(dest, k)

            @pl.when(zr == last_r)
            def _():
                going[dest, k] = total.astype(jnp.bfloat16)

            @pl.when(zr < last_r)
            def _():
                left_copy(dest, k).wait_recv()
                both = total + from_right[dest, k].astype(jnp.float32)
                going[dest, k] = both.astype(jnp.bfloat16)

            left_copy(dest, k).start()

    if ng:

        def gathered(block, k, send, recv, target):
            where = whole.at[whole_rows(2 * block + core, k)]
            return remote(where, where, send.at[block, k], recv.at[block, k], target)

        def core_copy(block, k):
            return gathered(block, k, core_send, core_recv, other)

        def ag_right_copy(block, k):
            return gathered(block, k, to_right, ag_left, mp + 2)

        def ag_left_copy(block, k):
            return gathered(block, k, to_left, ag_right, mp - 2)

    def own_rows(k):
        total = None
        if nr:
            total = chip_sum(zr, k)
            zero = jnp.zeros((piece_r, width_r), jnp.float32)

            @pl.when(zr > 0)
            def _():
                right_copy(zr, k).wait_recv()

            @pl.when(zr < last_r)
            def _():
                left_copy(zr, k).wait_recv()

            total += jnp.where(zr > 0, from_left[zr, k].astype(jnp.float32), zero)
            total += jnp.where(zr < last_r, from_right[zr, k].astype(jnp.float32), zero)
        if turn == "gather":
            cast[k] = total.astype(cast.dtype)
            for hop in range(1, size_dp):
                turn_copy(hop, k).start()
            mine = pl.ds(pl.multiple_of(dp * small, small), small)
            outs[0][own_place(k, dp)] = cast[k, mine, :]
            return
        at = pl.ds(pl.multiple_of(k * piece_r, piece_r), piece_r)
        ready = step(total, at, ins, outs)
        if turn == "spread":
            cast[k] = ready.astype(cast.dtype)
            for hop in range(1, size_dp):
                turn_copy(hop, k).start()
            whole[own_place(k, dp)] = cast[
                k, :, pl.ds(pl.multiple_of(dp * width_g, width_g), width_g)
            ]
        elif ng:
            whole[whole_rows(2 * zg + core, k), :] = ready.astype(whole.dtype)
            start_gather(k)

    def own_place(k, peer):
        if turn == "gather":
            return (
                pl.ds(pl.multiple_of(k * small, small), small),
                pl.ds(pl.multiple_of(peer * width_r, width_r), width_r),
            )
        start = (2 * zg + core) * rows_g + k * piece_g + peer * small
        return (pl.ds(pl.multiple_of(start, small), small), slice(None))

    def turn_copy(hop, k):
        peer = lax.rem(dp + hop, size_dp)
        if turn == "gather":
            src = cast.at[k, pl.ds(pl.multiple_of(peer * small, small), small)]
            dst = outs[0].at[own_place(k, dp)]
        else:
            src = cast.at[k, :, pl.ds(pl.multiple_of(peer * width_g, width_g), width_g)]
            dst = whole.at[own_place(k, dp)]
        return to_peer(src, dst, turn_send.at[hop, k], turn_recv.at[hop, k], peer)

    def turned_rows(k):
        for hop in range(1, size_dp):
            turn_copy(hop, k).wait_recv()
        if turn == "gather":
            at = pl.ds(pl.multiple_of(k * piece_g, piece_g), piece_g)
            ready = step(None, at, ins, outs)
            whole[whole_rows(2 * zg + core, k), :] = ready.astype(whole.dtype)
        start_gather(k)

    def start_gather(k):
        core_copy(zg, k).start()

        @pl.when(zg < last_g)
        def _():
            ag_right_copy(zg, k).start()

        @pl.when(zg > 0)
        def _():
            ag_left_copy(zg, k).start()

    def inside(k):
        return (k >= 0) & (k < chunks)

    def own_lag(chip):
        if not nr:
            return 0
        at = lax.rem(chip, nr)
        return jnp.maximum(at, last_r - at)

    def tick(now, carry):
        side_jobs(now)
        if nr:
            k_right = now - zr
            k_left = now - (last_r - zr)
            for far in range(last_r):

                @pl.when(inside(k_right) & (last_r - far > zr))
                def _():
                    pass_right(last_r - far, k_right)

                @pl.when(inside(k_left) & (far < zr))
                def _():
                    pass_left(far, k_left)

        k_own = now - own_lag(z)

        @pl.when(inside(k_own))
        def _():
            own_rows(k_own)

        if turn:

            @pl.when(inside(k_own - 1))
            def _():
                turned_rows(k_own - 1)

        if ng:
            for block in range(ng):
                k = now - (own_lag(z - zg + block) + late + jnp.abs(zg - block))

                @pl.when(inside(k) & (block < zg))
                def _():
                    ag_right_copy(block, k).wait_recv()
                    core_copy(block, k).start()

                    @pl.when(zg < last_g)
                    def _():
                        ag_right_copy(block, k).start()

                @pl.when(inside(k) & (block > zg))
                def _():
                    ag_left_copy(block, k).wait_recv()
                    core_copy(block, k).start()

                    @pl.when(zg > 0)
                    def _():
                        ag_left_copy(block, k).start()

        return carry

    ticks = chunks + (nr - 1 if nr else 0) + (ng - 1 if ng else 0) + late
    lax.fori_loop(0, ticks, tick, 0)

    def finish(k, carry):
        if turn:
            for hop in range(1, size_dp):
                turn_copy(hop, k).wait_send()
        if nr:
            for block in range(nr):
                half_copy(block, k).wait_send()

                @pl.when(block != zr)
                def _():
                    right_copy(block, k).wait_send()

        if ng:
            for block in range(ng):
                core_copy(block, k).wait()

                @pl.when((zg < last_g) & (block <= zg))
                def _():
                    ag_right_copy(block, k).wait_send()

                @pl.when((zg > 0) & (block >= zg))
                def _():
                    ag_left_copy(block, k).wait_send()

        return carry

    lax.fori_loop(0, chunks, finish, 0)
    for index, (kind, axis) in enumerate(sides):
        if kind == "gather":
            length = side_ins[index].shape[axis]
            side_outs[index][share(axis, length, dp)] = side_ins[index][...]
    for copy in first_copies:
        copy.wait_send()
    for copy in more_copies:
        copy.wait()
    for unused, unused, copy in relays:
        copy.wait()
    for index, (kind, axis) in enumerate(sides):
        if kind == "scatter":
            src, dst = side_ins[index], side_outs[index]
            slots = side_scratch[3 * index + 2]
            length, height = dst.shape[axis], dst.shape[0] // 2
            if relay:
                for side in range(2):
                    total = src[half_share(axis, length, dp, height, side)].astype(jnp.float32)
                    total += slots[4 * side + 1].astype(jnp.float32)
                    total += slots[4 * side + 3].astype(jnp.float32)
                    dst[pl.ds(side * height, height), :] = total
            else:
                total = src[share(axis, length, dp)].astype(jnp.float32)
                for hop in range(1, size_dp):
                    total += slots[hop].astype(jnp.float32)
                dst[...] = total


def line_call(
    name,
    cid,
    partial,
    ins,
    out_types,
    step,
    rows,
    width,
    chunks,
    nr,
    ng,
    time,
    sides=(),
    turn=None,
    side_ticks=0,
):
    piece = rows // chunks
    size_dp = lax.axis_size("dp")
    reduced = gathered = (rows, width)
    if turn == "gather":
        gathered = (rows // size_dp, width * size_dp)
    elif turn == "spread":
        gathered = (rows * size_dp, width // size_dp)
    out_shape = []
    if ng:
        out_shape.append(
            jax.ShapeDtypeStruct((2 * ng * gathered[0], gathered[1]), jnp.bfloat16)
        )
    out_shape += out_types
    dma = pltpu.SemaphoreType.DMA
    scratch = []
    for kind, axis, values in sides:
        shape = list(values.shape)
        scratch += [dma((max(size_dp, 6),)), dma((max(size_dp, 6),))]
        if kind == "gather":
            shape[axis] *= size_dp
            out_shape.append(jax.ShapeDtypeStruct(tuple(shape), values.dtype))
            scratch.append(pltpu.VMEM((16, 128), values.dtype))
        else:
            shape[axis] //= size_dp
            out_shape.append(jax.ShapeDtypeStruct(tuple(shape), jnp.float32))
            slots = (8, shape[0] // 2, shape[1]) if size_dp == 4 else (size_dp, *shape)
            scratch.append(pltpu.VMEM(slots, values.dtype))
    if nr:
        scratch += [pltpu.VMEM((nr, chunks, piece, width), jnp.bfloat16)] * 4
        scratch += [dma((nr, chunks))] * 5
    if ng:
        scratch += [dma((ng, chunks))] * 6
    if turn:
        scratch.append(pltpu.VMEM((chunks, piece, width), jnp.bfloat16))
        scratch += [dma((size_dp, chunks))] * 2
    args = ([partial] if nr else []) + list(ins) + [side[2] for side in sides]
    vmem = pl.BlockSpec(memory_space=pltpu.VMEM)
    call = pl.pallas_call(
        functools.partial(
            line_kernel,
            nr,
            ng,
            chunks,
            (reduced, gathered),
            len(ins),
            len(out_types),
            step,
            tuple(side[:2] for side in sides),
            turn,
            side_ticks,
        ),
        out_shape=out_shape,
        in_specs=[vmem] * len(args),
        out_specs=[vmem] * len(out_shape),
        scratch_shapes=scratch,
        compiler_params=pltpu.CompilerParams(
            collective_id=cid, has_side_effects=True, vmem_limit_bytes=VMEM_CAP
        ),
        cost_estimate=cost_of(time),
        name=name,
    )
    return list(call(*args))


def head_stats_kernel(block, tile, table_ref, final_ref, wanted_ref, edge_ref, exp_ref, top_ref, sum_ref, pick_ref):
    j = pl.program_id(0)
    tokens = final_ref.shape[0]
    place = j * block + lax.broadcasted_iota(jnp.int32, (block, 1), 0)
    valid = place < edge_ref[0]

    def one(i, carry):
        at = pl.ds(i * tile, tile)
        logits = lax.dot_general(
            table_ref[...],
            final_ref[at, :],
            (((1,), (1,)), ((), ())),
            preferred_element_type=jnp.float32,
        )
        logits = jnp.where(valid, logits, MASKED)
        top = jnp.max(logits, axis=0, keepdims=True)
        weights = jnp.exp(logits - top)
        exp_ref[:, at] = weights.astype(jnp.bfloat16)
        top_ref[0, :, at] = top
        sum_ref[0, :, at] = jnp.sum(weights, axis=0, keepdims=True)
        pick_ref[0, :, at] = jnp.sum(
            jnp.where(place == wanted_ref[:, at], logits, 0.0), axis=0, keepdims=True
        )
        return carry

    for i in range(tokens // tile):
        one(i, 0)


def head_stats(table, final, wanted, edge, block, tile=512):
    rows, width = table.shape
    tokens = final.shape[0]
    steps = pl.cdiv(rows, block)
    row = jax.ShapeDtypeStruct((steps, 1, tokens), jnp.float32)
    row_spec = pl.BlockSpec((1, 1, tokens), lambda j: (j, 0, 0))
    return pl.pallas_call(
        functools.partial(head_stats_kernel, block, tile),
        grid=(steps,),
        out_shape=[jax.ShapeDtypeStruct((steps * block, tokens), jnp.bfloat16), row, row, row],
        in_specs=[
            pl.BlockSpec((block, width), lambda j: (j, 0)),
            pl.BlockSpec((tokens, width), lambda j: (0, 0)),
            pl.BlockSpec((1, tokens), lambda j: (0, 0)),
            pl.BlockSpec(memory_space=pltpu.SMEM),
        ],
        out_specs=[pl.BlockSpec((block, tokens), lambda j: (j, 0)), row_spec, row_spec, row_spec],
        compiler_params=pltpu.CompilerParams(vmem_limit_bytes=56 * 2**20),
        cost_estimate=pl.CostEstimate(
            flops=2 * rows * width * tokens,
            bytes_accessed=2 * rows * (width + tokens),
            transcendentals=rows * tokens,
        ),
        name="head_stats",
    )(table, final, wanted, edge)


def head_back_kernel(rows, block, tile, exp_ref, table_ref, final_ref, scale_ref, weight_ref, wanted_ref, grad_ref, dfinal_ref, dl_ref, sum_ref):
    j = pl.program_id(0)
    tokens = final_ref.shape[0]
    place = j * block + lax.broadcasted_iota(jnp.int32, (block, 1), 0)

    @pl.when(j == 0)
    def _():
        sum_ref[...] = jnp.zeros_like(sum_ref)

    table = jnp.where(place < rows, table_ref[...], jnp.zeros_like(table_ref))

    def one(i, carry):
        at = pl.ds(i * tile, tile)
        weight = weight_ref[:, at]
        dl = exp_ref[:, at].astype(jnp.float32) * scale_ref[0, :, at]
        dl = dl - jnp.where(place == wanted_ref[:, at], weight, 0.0)
        dl = dl.astype(jnp.bfloat16)
        dl_ref[:, at] = dl
        sum_ref[at, :] += lax.dot_general(
            dl, table, (((0,), (0,)), ((), ())), preferred_element_type=jnp.float32
        )
        return carry

    for i in range(tokens // tile):
        one(i, 0)

    strip = block // max(1, block // 256)

    def two(i, carry):
        at = pl.ds(i * strip, strip)
        grad_ref[at, :] = jnp.dot(
            dl_ref[at, :], final_ref[...], preferred_element_type=jnp.float32
        ).astype(jnp.bfloat16)
        return carry

    for i in range(block // strip):
        two(i, 0)

    @pl.when(j == pl.num_programs(0) - 1)
    def _():
        dfinal_ref[...] = sum_ref[...].astype(jnp.bfloat16)


def head_back(exps, table, final, scale, weight, wanted, block, tile=256):
    rows, width = table.shape
    tokens = final.shape[0]
    steps = pl.cdiv(rows, block)
    return pl.pallas_call(
        functools.partial(head_back_kernel, rows, block, tile),
        grid=(steps,),
        out_shape=[
            jax.ShapeDtypeStruct((rows, width), jnp.bfloat16),
            jax.ShapeDtypeStruct((tokens, width), jnp.bfloat16),
        ],
        in_specs=[
            pl.BlockSpec((block, tokens), lambda j: (j, 0)),
            pl.BlockSpec((block, width), lambda j: (j, 0)),
            pl.BlockSpec((tokens, width), lambda j: (0, 0)),
            pl.BlockSpec((1, 1, tokens), lambda j: (j, 0, 0)),
            pl.BlockSpec((1, tokens), lambda j: (0, 0)),
            pl.BlockSpec((1, tokens), lambda j: (0, 0)),
        ],
        out_specs=[
            pl.BlockSpec((block, width), lambda j: (j, 0)),
            pl.BlockSpec((tokens, width), lambda j: (0, 0)),
        ],
        scratch_shapes=[
            pltpu.VMEM((block, tokens), jnp.bfloat16),
            pltpu.VMEM((tokens, width), jnp.float32),
        ],
        compiler_params=pltpu.CompilerParams(vmem_limit_bytes=60 * 2**20),
        cost_estimate=pl.CostEstimate(
            flops=4 * rows * width * tokens,
            bytes_accessed=2 * rows * (2 * width + tokens),
            transcendentals=0,
        ),
        name="head_back",
    )(exps, table, final, scale, weight, wanted)


def head_weights(mixed_ref, starts_ref, base, at, seen):
    query = mixed_ref[at : at + QUERIES, base : base + HD]
    keys = mixed_ref[0:seen, base + HD : base + 2 * HD]
    values = mixed_ref[0:seen, base + 2 * HD : base + 3 * HD]
    scores = lax.dot_general(
        query, keys, (((1,), (1,)), ((), ())), preferred_element_type=jnp.float32
    )
    row = at + lax.broadcasted_iota(jnp.int32, (QUERIES, seen), 0)
    column = lax.broadcasted_iota(jnp.int32, (QUERIES, seen), 1)
    allowed = (column <= row) & (column >= starts_ref[at : at + QUERIES, :])
    scores = jnp.where(allowed, scores * HD ** (-0.5), MASKED)
    weights = jnp.exp(scores - jnp.max(scores, axis=1, keepdims=True))
    probs = weights / jnp.sum(weights, axis=1, keepdims=True)
    return query, keys, values, probs


def attend_kernel(mixed_ref, starts_ref, out_ref):
    length = mixed_ref.shape[0]
    for at in range(0, length, QUERIES):
        found = []
        for head in range(2):
            unused, unused, values, probs = head_weights(
                mixed_ref, starts_ref, head * 3 * HD, at, at + QUERIES
            )
            found.append(
                jnp.dot(probs.astype(jnp.bfloat16), values, preferred_element_type=jnp.float32)
            )
        out_ref[at : at + QUERIES, :] = jnp.concatenate(found, axis=1).astype(jnp.bfloat16)


def attend(mixed, starts):
    length, columns = mixed.shape
    pairs = columns // (6 * HD)
    return pl.pallas_call(
        attend_kernel,
        grid=(pairs,),
        out_shape=jax.ShapeDtypeStruct((length, pairs * 2 * HD), jnp.bfloat16),
        in_specs=[
            pl.BlockSpec((length, 6 * HD), lambda j: (0, j)),
            pl.BlockSpec((length, 1), lambda j: (0, 0)),
        ],
        out_specs=pl.BlockSpec((length, 2 * HD), lambda j: (0, j)),
        compiler_params=pltpu.CompilerParams(vmem_limit_bytes=40 * 2**20),
        cost_estimate=pl.CostEstimate(
            flops=8 * pairs * length * length * HD,
            bytes_accessed=2 * length * columns,
            transcendentals=pairs * length * length,
        ),
        name="attend",
    )(mixed, starts)


def attend_back_kernel(mixed_ref, starts_ref, upstream_ref, out_ref, sums_ref):
    length = mixed_ref.shape[0]
    sums_ref[...] = jnp.zeros_like(sums_ref)
    rows = (((0,), (0,)), ((), ()))
    for at in range(0, length, QUERIES):
        seen = at + QUERIES
        for head in range(2):
            base = head * 3 * HD
            query, keys, values, probs = head_weights(mixed_ref, starts_ref, base, at, seen)
            upstream = upstream_ref[at:seen, head * HD : head * HD + HD]
            dprobs = lax.dot_general(
                upstream, values, (((1,), (1,)), ((), ())), preferred_element_type=jnp.float32
            )
            inner = jnp.sum(probs * dprobs, axis=1, keepdims=True)
            dscores = (probs * (dprobs - inner)).astype(jnp.bfloat16)
            dquery = jnp.dot(dscores, keys, preferred_element_type=jnp.float32)
            dkeys = lax.dot_general(dscores, query, rows, preferred_element_type=jnp.float32)
            dvalues = lax.dot_general(
                probs.astype(jnp.bfloat16), upstream, rows, preferred_element_type=jnp.float32
            )
            sums_ref[at:seen, base : base + HD] = dquery * HD ** (-0.5)
            sums_ref[0:seen, base + HD : base + 2 * HD] += dkeys * HD ** (-0.5)
            sums_ref[0:seen, base + 2 * HD : base + 3 * HD] += dvalues
    out_ref[...] = sums_ref[...].astype(jnp.bfloat16)


def attend_back(mixed, starts, upstream):
    length, columns = mixed.shape
    pairs = columns // (6 * HD)
    return pl.pallas_call(
        attend_back_kernel,
        grid=(pairs,),
        out_shape=jax.ShapeDtypeStruct((length, columns), jnp.bfloat16),
        in_specs=[
            pl.BlockSpec((length, 6 * HD), lambda j: (0, j)),
            pl.BlockSpec((length, 1), lambda j: (0, 0)),
            pl.BlockSpec((length, 2 * HD), lambda j: (0, j)),
        ],
        out_specs=pl.BlockSpec((length, 6 * HD), lambda j: (0, j)),
        scratch_shapes=[pltpu.VMEM((length, 6 * HD), jnp.float32)],
        compiler_params=pltpu.CompilerParams(vmem_limit_bytes=40 * 2**20),
        cost_estimate=pl.CostEstimate(
            flops=20 * pairs * length * length * HD,
            bytes_accessed=4 * length * columns,
            transcendentals=pairs * length * length,
        ),
        name="attend_back",
    )(mixed, starts, upstream)


def small_gather_kernel(axis, count, src_ref, out_ref, send, recv):
    dp = lax.axis_index("dp")
    mp = lax.axis_index("mp")
    me = dp if axis == "dp" else mp

    def device(peer):
        return (peer, mp) if axis == "dp" else (dp, peer)

    barrier = pltpu.get_barrier_semaphore()
    for hop in range(1, count):
        pl.semaphore_signal(
            barrier, inc=1, device_id=device(lax.rem(me + hop, count)), device_id_type=MESH
        )
    pl.semaphore_wait(barrier, count - 1)
    copies = []
    for hop in range(1, count):
        peer = lax.rem(me + hop, count)
        copy = pltpu.make_async_remote_copy(
            src_ref=src_ref,
            dst_ref=out_ref.at[me],
            send_sem=send.at[hop],
            recv_sem=recv.at[hop],
            device_id=device(peer),
            device_id_type=MESH,
        )
        copy.start()
        copies.append(copy)
    out_ref[me] = src_ref[...]
    for copy in copies:
        copy.wait()


def small_gather(name, cid, values, axis):
    count = lax.axis_size(axis)
    vmem = pl.BlockSpec(memory_space=pltpu.VMEM)
    return pl.pallas_call(
        functools.partial(small_gather_kernel, axis, count),
        out_shape=jax.ShapeDtypeStruct((count,) + values.shape, values.dtype),
        in_specs=[vmem],
        out_specs=vmem,
        scratch_shapes=[pltpu.SemaphoreType.DMA((count,)), pltpu.SemaphoreType.DMA((count,))],
        compiler_params=pltpu.CompilerParams(collective_id=cid, has_side_effects=True),
        cost_estimate=cost_of(6),
        name=name,
    )(values)


def exchange(axis, me, here, source, slots, send, recv, first):
    count = slots.shape[0]
    copies = []
    for hop in range(1, count):
        peer = lax.rem(me + hop, count)
        copy = pltpu.make_async_remote_copy(
            src_ref=source,
            dst_ref=slots.at[me],
            send_sem=send.at[first + hop],
            recv_sem=recv.at[first + hop],
            device_id=(peer, here) if axis == "dp" else (here, peer),
            device_id_type=MESH,
        )
        copy.start()
        copies.append(copy)
    slots[me] = source[...]
    for copy in copies:
        copy.wait()
    total = slots[0]
    for index in range(1, count):
        total = total + slots[index]
    return total


def greet_all(dp, mp, size_dp, size_mp):
    barrier = pltpu.get_barrier_semaphore()
    for hop in range(1, size_dp):
        pl.semaphore_signal(
            barrier, inc=1, device_id=(lax.rem(dp + hop, size_dp), mp), device_id_type=MESH
        )
    for hop in range(1, size_mp):
        pl.semaphore_signal(
            barrier, inc=1, device_id=(dp, lax.rem(mp + hop, size_mp)), device_id_type=MESH
        )
    pl.semaphore_wait(barrier, size_dp + size_mp - 2)


def lane_rows(values):
    values = values.reshape(-1)
    return jnp.pad(values, (0, -values.size % 128)).reshape(-1, 128)


def fold(values):
    return jnp.sum(values, axis=0, keepdims=True)


def stats_kernel(full, size_dp, size_mp, *refs):
    row_part, row_old, col_part, col_old, weight_sq = (refs[5 * n : 5 * n + 5] for n in range(5))
    loss_part, norm_one, norm_two, norm_three, norms, second_old = refs[25:31]
    refs = refs[31:]
    row_out, col_out = refs[0:5], refs[5:10]
    loss_out, grads_out, second_out, norms_out, rate_out = refs[10:15]
    send_dp, slots_dp, send_mp, slots_mp, parts, part_slots, whole, send, recv = refs[15:]
    dp = lax.axis_index("dp")
    mp = lax.axis_index("mp")
    greet_all(dp, mp, size_dp, size_mp)
    beta = 1.0 - STEP ** (-0.8)
    width = norms.shape[1]

    at = 0
    marks = []

    def put(values):
        nonlocal at
        rows = values.shape[0]
        send_dp[at : at + rows, :] = values
        marks.append((at, rows))
        at += rows

    norm_rows = width // 128
    for ref in (norm_one, norm_two, norm_three):
        for which in range(2):
            for piece in range(norm_rows):
                put(ref[which : which + 1, piece * 128 : piece * 128 + 128])
    marks.clear()
    count_norm = at
    for index in (0, 2, 4):
        put(row_part[index][...])
    for index in (1, 3):
        put(col_part[index][...])
    put(loss_part[...])
    for index in (1, 3):
        put(fold(row_old[index][...]))
    for index in range(5):
        put(fold(weight_sq[index][...]))
    if at < send_dp.shape[0]:
        send_dp[at:, :] = jnp.zeros((send_dp.shape[0] - at, 128), jnp.float32)
    over_dp = exchange("dp", dp, mp, send_dp, slots_dp, send, recv, 0)
    taken = [over_dp[start : start + rows] for start, rows in marks]
    loss_out[...] = taken[5]
    row_full = {0: taken[0], 2: taken[1], 4: taken[2]}
    col_full = {1: taken[3], 3: taken[4]}
    old_total = {1: taken[6], 3: taken[7]}
    weight_rows = taken[8:13]

    at = 0
    marks = []

    def put_mp(values):
        nonlocal at
        rows = values.shape[0]
        send_mp[at : at + rows, :] = values
        marks.append((at, rows))
        at += rows

    for index in (0, 2, 4):
        put_mp(col_part[index][...])
    for index in (1, 3):
        put_mp(row_part[index][...])
    for index in range(5):
        put_mp(fold(row_full[index] if index in row_full else col_full[index]))
    for index in (0, 2, 4):
        put_mp(fold(row_old[index][...]))
    for index in range(5):
        put_mp(weight_rows[index])
    if at < send_mp.shape[0]:
        send_mp[at:, :] = jnp.zeros((send_mp.shape[0] - at, 128), jnp.float32)
    each = count_norm // size_mp
    for index in range(size_mp):
        parts[index] = over_dp[index * each : index * each + each]
    first = size_dp + size_mp
    copies = []
    for hop in range(1, size_mp):
        peer = lax.rem(mp + hop, size_mp)
        copy = pltpu.make_async_remote_copy(
            src_ref=parts.at[peer],
            dst_ref=part_slots.at[mp],
            send_sem=send.at[first + hop],
            recv_sem=recv.at[first + hop],
            device_id=(dp, peer),
            device_id_type=MESH,
        )
        copy.start()
        copies.append(copy)
    part_slots[mp] = parts[mp]
    over_mp = exchange("mp", mp, dp, send_mp, slots_mp, send, recv, size_dp)
    for copy in copies:
        copy.wait()
    summed = part_slots[0]
    for index in range(1, size_mp):
        summed = summed + part_slots[index]
    whole[mp] = summed
    first += size_mp
    copies = []
    for hop in range(1, size_mp):
        peer = lax.rem(mp + hop, size_mp)
        copy = pltpu.make_async_remote_copy(
            src_ref=whole.at[mp],
            dst_ref=whole.at[mp],
            send_sem=send.at[first + hop],
            recv_sem=recv.at[first + hop],
            device_id=(dp, peer),
            device_id_type=MESH,
        )
        copies.append(copy)
    for copy in copies:
        copy.start()
    taken = [over_mp[start : start + rows] for start, rows in marks]
    for slot, index in enumerate((0, 2, 4)):
        col_full[index] = taken[slot]
        old_total[index] = taken[10 + slot]
    for slot, index in enumerate((1, 3)):
        row_full[index] = taken[3 + slot]
    square_total = taken[5:10]
    weight_total = taken[13:18]
    for index in range(5):
        full_rows, full_cols = full[index]
        row_new = beta * row_old[index][...] + (1.0 - beta) * row_full[index] / full_cols
        col_new = beta * col_old[index][...] + (1.0 - beta) * col_full[index] / full_rows
        row_out[index][...] = row_new
        col_out[index][...] = col_new
        mean = (
            beta * jnp.sum(old_total[index], axis=1, keepdims=True)
            + (1.0 - beta) * jnp.sum(square_total[index], axis=1, keepdims=True) / full_cols
        ) / full_rows
        rate = RHO * jnp.sqrt(
            jnp.sum(weight_total[index], axis=1, keepdims=True) / (full_rows * full_cols)
        )
        rate_out[index : index + 1, :] = jnp.broadcast_to(mean, (1, 128))
        rate_out[8 + index : 9 + index, :] = jnp.broadcast_to(rate, (1, 128))
    for copy in copies:
        copy.wait()
    for row in range(6):
        for piece in range(norm_rows):
            place = row * norm_rows + piece
            grads_out[row : row + 1, piece * 128 : piece * 128 + 128] = whole[
                place // each, place % each : place % each + 1, :
            ]
    grad = grads_out[...]
    second = beta * second_old[...] + (1.0 - beta) * (grad * grad + EPS_ONE)
    second_out[...] = second
    step = grad * lax.rsqrt(second)
    entries = step.size

    def mean_square(values):
        return jnp.sum(jnp.sum(values * values, axis=0, keepdims=True), axis=1, keepdims=True) / (
            entries
        )

    step = step / jnp.maximum(1.0, jnp.sqrt(mean_square(step)) / CLIP)
    old = norms[...]
    norms_out[...] = old - RHO * jnp.sqrt(mean_square(old)) * step


def update_stats(cid, row_parts, rows_old, col_parts, cols_old, weight_sq, loss, norm_parts, norms, second, full):
    size_dp = lax.axis_size("dp")
    size_mp = lax.axis_size("mp")
    f32 = jnp.float32
    rows_old2 = [lane_rows(v) for v in rows_old]
    cols_old2 = [lane_rows(v) for v in cols_old]
    args = (
        [lane_rows(v) for v in row_parts]
        + rows_old2
        + [lane_rows(v) for v in col_parts]
        + cols_old2
        + [v if v.ndim == 2 else lane_rows(v) for v in weight_sq]
        + [lane_rows(loss)]
        + list(norm_parts)
        + [norms, second]
    )
    width = norms.shape[1]
    count_norm = 6 * width // 128
    size_a = count_norm + sum(rows_old2[n].shape[0] for n in (0, 2, 4))
    size_a += sum(cols_old2[n].shape[0] for n in (1, 3)) + 8
    size_a += -size_a % 8
    size_b = sum(cols_old2[n].shape[0] for n in (0, 2, 4))
    size_b += sum(rows_old2[n].shape[0] for n in (1, 3)) + 13
    size_b += -size_b % 8
    each = count_norm // size_mp
    out_shape = [jax.ShapeDtypeStruct(v.shape, f32) for v in rows_old2 + cols_old2]
    out_shape += [
        jax.ShapeDtypeStruct((1, 128), f32),
        jax.ShapeDtypeStruct(norms.shape, f32),
        jax.ShapeDtypeStruct(norms.shape, f32),
        jax.ShapeDtypeStruct(norms.shape, f32),
        jax.ShapeDtypeStruct((16, 128), f32),
    ]
    sems = size_dp + 3 * size_mp
    vmem = pl.BlockSpec(memory_space=pltpu.VMEM)
    found = pl.pallas_call(
        functools.partial(stats_kernel, full, size_dp, size_mp),
        out_shape=out_shape,
        in_specs=[vmem] * len(args),
        out_specs=[vmem] * len(out_shape),
        scratch_shapes=[
            pltpu.VMEM((size_a, 128), f32),
            pltpu.VMEM((size_dp, size_a, 128), f32),
            pltpu.VMEM((size_b, 128), f32),
            pltpu.VMEM((size_mp, size_b, 128), f32),
            pltpu.VMEM((size_mp, each, 128), f32),
            pltpu.VMEM((size_mp, each, 128), f32),
            pltpu.VMEM((size_mp, each, 128), f32),
            pltpu.SemaphoreType.DMA((sems,)),
            pltpu.SemaphoreType.DMA((sems,)),
        ],
        compiler_params=pltpu.CompilerParams(collective_id=cid, has_side_effects=True),
        cost_estimate=cost_of(12),
        name="update_stats",
    )(*args)
    rows_new = [found[n].reshape(-1)[: rows_old[n].size] for n in range(5)]
    cols_new = [found[5 + n].reshape(-1)[: cols_old[n].size] for n in range(5)]
    loss_sums = found[10][0, :NSRC]
    return rows_new, cols_new, loss_sums, found[11], found[12], found[13], found[14]


def clip_kernel(entries, size_dp, size_mp, *refs):
    parts, rate = refs[:5], refs[5]
    out, mine, slots_dp, slots_mp, send, recv = refs[6:]
    dp = lax.axis_index("dp")
    mp = lax.axis_index("mp")
    greet_all(dp, mp, size_dp, size_mp)
    mine[...] = jnp.zeros_like(mine)
    for index in range(5):
        mine[index : index + 1, :] = fold(parts[index][...])
    mine[...] = exchange("dp", dp, mp, mine, slots_dp, send, recv, 0)
    total = exchange("mp", mp, dp, mine, slots_mp, send, recv, size_dp)
    total = jnp.sum(total, axis=1, keepdims=True)
    for index in range(5):
        clip = jnp.maximum(1.0, jnp.sqrt(total[index : index + 1] / entries[index]) / CLIP)
        out[index : index + 1, :] = rate[8 + index : 9 + index, :] / clip


def clip_rates(cid, step_parts, rate, entries):
    size_dp = lax.axis_size("dp")
    size_mp = lax.axis_size("mp")
    vmem = pl.BlockSpec(memory_space=pltpu.VMEM)
    sems = size_dp + size_mp
    return pl.pallas_call(
        functools.partial(clip_kernel, entries, size_dp, size_mp),
        out_shape=jax.ShapeDtypeStruct((8, 128), jnp.float32),
        in_specs=[vmem] * 6,
        out_specs=vmem,
        scratch_shapes=[
            pltpu.VMEM((8, 128), jnp.float32),
            pltpu.VMEM((size_dp, 8, 128), jnp.float32),
            pltpu.VMEM((size_mp, 8, 128), jnp.float32),
            pltpu.SemaphoreType.DMA((sems,)),
            pltpu.SemaphoreType.DMA((sems,)),
        ],
        compiler_params=pltpu.CompilerParams(collective_id=cid, has_side_effects=True),
        cost_estimate=cost_of(8),
        name="clip_rates",
    )(*[lane_rows(v) for v in step_parts], rate)


UNROLL = 8


def lookup_kernel(shift, count_ref, key_ref, table_ref, out_ref, low_ref, square_ref, rows_ref):
    spots = out_ref.shape[0]
    vocab, width = table_ref.shape
    rows_ref[...] = jnp.zeros_like(rows_ref)

    def some(i, carry):
        for j in range(UNROLL):
            key = key_ref[i * UNROLL + j]
            place = key & ((1 << shift) - 1)
            rows_ref[pl.ds(place, 1), :] = table_ref[pl.ds(key >> shift, 1), :]
        return carry

    lax.fori_loop(0, (count_ref[0] + UNROLL - 1) // UNROLL, some, 0)

    def narrow(i, carry):
        at = pl.ds(pl.multiple_of(i * 256, 256), 256)
        out_ref[at, :] = rows_ref[at, :].astype(jnp.bfloat16)
        return carry

    lax.fori_loop(0, spots // 256, narrow, 0)
    strip = 48 if vocab % 48 == 0 else 8

    def lower(i, total):
        at = pl.ds(pl.multiple_of(i * strip, strip), strip)
        values = table_ref[at, :]
        low_ref[at, :] = values.astype(jnp.bfloat16)
        for row in range(0, strip, 8):
            piece = values[row : row + 8, :]
            total = total + piece * piece
        return total

    total = lax.fori_loop(0, vocab // strip, lower, jnp.zeros((8, width), jnp.float32))
    folded = total[:, 0:128]
    for start in range(128, width, 128):
        folded = folded + total[:, start : start + 128]
    square_ref[...] = folded


def lookup(keys, count, table, spots, shift):
    vocab, width = table.shape
    smem = pl.BlockSpec(memory_space=pltpu.SMEM)
    vmem = pl.BlockSpec(memory_space=pltpu.VMEM)
    return pl.pallas_call(
        functools.partial(lookup_kernel, shift),
        out_shape=[
            jax.ShapeDtypeStruct((spots, width), jnp.bfloat16),
            jax.ShapeDtypeStruct((vocab, width), jnp.bfloat16),
            jax.ShapeDtypeStruct((8, 128), jnp.float32),
        ],
        in_specs=[smem, smem, vmem],
        out_specs=[vmem] * 3,
        scratch_shapes=[pltpu.VMEM((spots + 8, width), jnp.float32)],
        compiler_params=pltpu.CompilerParams(vmem_limit_bytes=VMEM_CAP),
        cost_estimate=cost_of(20),
        name="lookup",
    )(count, keys, table)


def scatter_kernel(shift, count_ref, key_ref, head_ref, rows_in_ref, grad_ref, rows_ref):
    spots = rows_in_ref.shape[0]
    width = grad_ref.shape[1]

    def widen(i, carry):
        at = pl.ds(pl.multiple_of(i * 256, 256), 256)
        rows_ref[at, :] = rows_in_ref[at, :].astype(jnp.float32)
        return carry

    lax.fori_loop(0, spots // 256, widen, 0)
    rows_ref[spots:, :] = jnp.zeros((8, width), jnp.float32)
    grad_ref[...] = head_ref[...].astype(jnp.float32)

    def some(i, carry):
        for j in range(UNROLL):
            key = key_ref[i * UNROLL + j]
            place = key & ((1 << shift) - 1)
            grad_ref[pl.ds(key >> shift, 1), :] += rows_ref[pl.ds(place, 1), :]
        return carry

    lax.fori_loop(0, (count_ref[0] + UNROLL - 1) // UNROLL, some, 0)


def scatter(keys, count, head_grad, rows, shift):
    spots, width = rows.shape
    vocab = head_grad.shape[0]
    smem = pl.BlockSpec(memory_space=pltpu.SMEM)
    vmem = pl.BlockSpec(memory_space=pltpu.VMEM)
    return pl.pallas_call(
        functools.partial(scatter_kernel, shift),
        out_shape=jax.ShapeDtypeStruct((vocab, width), jnp.float32),
        in_specs=[smem, smem, vmem, vmem],
        out_specs=vmem,
        scratch_shapes=[pltpu.VMEM((spots + 8, width), jnp.float32)],
        compiler_params=pltpu.CompilerParams(vmem_limit_bytes=VMEM_CAP),
        cost_estimate=cost_of(23),
        name="scatter",
    )(count, keys, head_grad, rows)


def norm_parts(values):
    centre = jnp.mean(values, axis=-1, keepdims=True)
    centred = values - centre
    scale = lax.rsqrt(jnp.mean(centred * centred, axis=-1, keepdims=True) + EPS_NORM)
    return centred * scale, scale


def norm_pull(values, gain, upstream):
    normed, scale = norm_parts(values)
    weighted = upstream * gain
    pulled = scale * (
        weighted
        - jnp.mean(weighted, axis=-1, keepdims=True)
        - normed * jnp.mean(weighted * normed, axis=-1, keepdims=True)
    )
    return (
        pulled,
        jnp.sum(upstream * normed, axis=0, keepdims=True),
        jnp.sum(upstream, axis=0, keepdims=True),
    )


def step_first(total, at, ins, outs):
    stream, norms = outs[0], ins[0]
    normed, scale = norm_parts(stream[at, :].astype(jnp.float32))
    return normed * norms[0:1, :] + norms[1:2, :]


def step_forward(row, total, at, ins, outs):
    stream, norms = ins
    values = stream[at, :].astype(jnp.float32) + total
    outs[0][at, :] = values
    normed, scale = norm_parts(values)
    return normed * norms[row : row + 1, :] + norms[row + 1 : row + 2, :]


def step_backward(row, total, at, ins, outs):
    stream, norms = ins[:2]
    pulled, dgain, dshift = norm_pull(
        stream[at, :].astype(jnp.float32), norms[row : row + 1, :], total
    )
    if len(ins) > 2:
        pulled = pulled + ins[2][at, :]
    if len(outs) > 1:
        outs[0][at, :] = pulled
    sums = outs[-1]

    @pl.when(at.start == 0)
    def _():
        sums[...] = jnp.zeros_like(sums)

    sums[0:1, :] += dgain
    sums[1:2, :] += dshift
    return pulled


def gelu_tanh(values):
    return jax.nn.gelu(values, approximate=True)


def local(
    token_ids,
    targets,
    starts,
    sources,
    embedding,
    w_qkv,
    w_out,
    w_fc,
    w_proj,
    norm_params,
    rows_table,
    cols_table,
    rows_qkv,
    cols_qkv,
    rows_out,
    cols_out,
    rows_fc,
    cols_fc,
    rows_proj,
    cols_proj,
    second_norms,
):
    bf16 = jnp.bfloat16
    f32 = jnp.float32
    size_mp = lax.axis_size("mp")
    size_dp = lax.axis_size("dp")
    dp = lax.axis_index("dp")
    mp = lax.axis_index("mp")
    tokens = token_ids.shape[0]
    seqs = tokens // LEN
    chips = size_mp // 2
    near = chips // seqs
    sharers = size_mp // seqs
    rows = tokens // size_mp
    vocab, part_width = embedding.shape
    width = part_width * size_dp
    first_row = mp * vocab
    spots = tokens * size_dp
    chunks_full = max(1, min(8, rows // 32))
    chunks_near = max(1, min(4, rows // 32))
    chunks_turn = max(1, min(4, rows // 32))

    both = jnp.stack([token_ids, sources]).reshape(-1, 128)
    both = small_gather("gather_ids", 0, both, "dp").reshape(size_dp, 2, tokens)
    all_ids = both[:, 0]
    all_sources = both[:, 1].reshape(-1)
    counts = jnp.sum(
        (all_sources[:, None] == jnp.arange(NSRC, dtype=jnp.int32)[None, :]).astype(f32), axis=0
    )

    w_qkv, w_out, w_fc, w_proj, all_ids = lax.optimization_barrier(
        (w_qkv, w_out, w_fc, w_proj, all_ids)
    )


    def own_and_twins(weight, axis):
        weight = weight.astype(bf16)
        found = [weight]
        for turn in range(1, seqs):
            shift = [(i, (i + turn * sharers) % size_mp) for i in range(size_mp)]
            found.append(lax.ppermute(weight, "mp", shift))
        return jnp.concatenate(found, axis=axis) if seqs > 1 else weight

    pair_qkv = own_and_twins(w_qkv, 1)
    pair_out = own_and_twins(w_out, 0)
    pair_fc = own_and_twins(w_fc, 1)
    pair_proj = own_and_twins(w_proj, 0)
    piece = rows // chunks_turn
    token = jnp.arange(tokens, dtype=jnp.int32)
    place = (
        token // piece * (size_dp * piece)
        + (jnp.arange(size_dp, dtype=jnp.int32) * piece)[:, None]
        + token % piece
    )
    local_ids = all_ids - first_row
    inside = (local_ids >= 0) & (local_ids < vocab)
    shift = spots.bit_length()
    idle = ((vocab - 1) << shift) + spots
    keys = jnp.where(inside, (local_ids << shift) + place, idle)
    keys = jnp.sort(keys.reshape(-1))
    owned = jnp.sum(inside.astype(jnp.int32)).reshape(1)
    found, low_table, table_sq = lookup(keys, owned, embedding, spots, shift)
    inner_one, stream0, wide_qkv, wide_out, wide_fc, wide_proj = line_call(
        "lookup_sum",
        1,
        found,
        [norm_params],
        [jax.ShapeDtypeStruct((rows, width), bf16)],
        step_first,
        size_dp * rows,
        part_width,
        chunks_turn,
        chips,
        near,
        70,
        [
            ("gather", 0, pair_qkv),
            ("gather", 1, pair_out),
            ("gather", 0, pair_fc),
            ("gather", 1, pair_proj),
        ],
        "gather",
        8,
    )
    low_table, inner_one = lax.optimization_barrier((low_table, inner_one))
    wide_table = lax.all_gather(low_table, "dp", axis=1, tiled=True)
    row_f32 = jax.ShapeDtypeStruct((rows, width), f32)
    pair_f32 = jax.ShapeDtypeStruct((8, width), f32)
    my_starts = row_slice(starts, (mp // sharers) * LEN, LEN)[:, None]
    mixed = jnp.dot(inner_one, wide_qkv, preferred_element_type=f32).astype(bf16)
    attended = attend(mixed, my_starts)
    partial = jnp.dot(attended, wide_out, preferred_element_type=f32).astype(bf16)
    inner_two, stream1 = line_call(
        "attn_sum",
        3,
        partial,
        [stream0, norm_params],
        [row_f32],
        functools.partial(step_forward, 2),
        rows,
        width,
        chunks_near,
        near,
        near,
        32,
    )
    before = jnp.dot(inner_two, wide_fc, preferred_element_type=f32)
    hidden = gelu_tanh(before).astype(bf16)
    partial = jnp.dot(hidden, wide_proj, preferred_element_type=f32).astype(bf16)
    final, stream2 = line_call(
        "mlp_sum",
        4,
        partial,
        [stream1, norm_params],
        [row_f32],
        functools.partial(step_forward, 4),
        rows,
        width,
        chunks_full,
        near,
        chips,
        58,
    )

    edge = jnp.clip(VREAL - first_row, 0, vocab).astype(jnp.int32).reshape(1)
    wanted = targets - first_row
    wanted = jnp.where((wanted >= 0) & (wanted < vocab), wanted, -1).reshape(1, tokens)
    block = 640
    exps, tops, sums, picks = head_stats(wide_table, final, wanted, edge, block)
    tops = tops[:, 0]
    top = jnp.max(tops, axis=0)
    total = jnp.sum(sums[:, 0] * jnp.exp(tops - top[None, :]), axis=0)
    pick = jnp.sum(picks[:, 0], axis=0)
    stats = jnp.concatenate([v.reshape(-1, 128) for v in (top, total, pick)])
    stats = small_gather("gather_stats", 5, stats, "mp").reshape(size_mp, 3, tokens)
    highest = jnp.max(stats[:, 0], axis=0)
    log_total = highest + jnp.log(
        jnp.sum(stats[:, 1] * jnp.exp(stats[:, 0] - highest[None, :]), axis=0)
    )
    token_loss = log_total - jnp.sum(stats[:, 2], axis=0)
    member = (sources[:, None] == jnp.arange(NSRC, dtype=jnp.int32)[None, :]).astype(f32)
    loss_part = jnp.sum(member * token_loss[:, None], axis=0)
    weight = jnp.sum(member / (NSRC * jnp.maximum(counts, 1.0))[None, :], axis=1)
    scale = jnp.exp(tops - log_total[None, :]) * weight[None, :]
    table_grad, dfinal = head_back(
        exps, wide_table, final, scale[:, None, :], weight[None, :], wanted, block
    )
    head_grad = lax.psum_scatter(table_grad, "dp", scatter_dimension=1, tiled=True)

    dbranch2, dstream2, norm3 = line_call(
        "final_back",
        6,
        dfinal,
        [stream2, norm_params],
        [row_f32, pair_f32],
        functools.partial(step_backward, 4),
        rows,
        width,
        chunks_full,
        chips,
        near,
        60,
    )
    grad_proj = jnp.einsum("tf,td->fd", hidden, dbranch2, preferred_element_type=f32).astype(bf16)
    dhidden = jnp.einsum("td,fd->tf", dbranch2, wide_proj, preferred_element_type=f32)
    unused, gelu_pull = jax.vjp(gelu_tanh, before)
    dbefore = gelu_pull(dhidden)[0].astype(bf16)
    partial = jnp.einsum("tf,df->td", dbefore, wide_fc, preferred_element_type=f32).astype(bf16)
    dbranch1, dstream1, norm2 = line_call(
        "mlp_back",
        7,
        partial,
        [stream1, norm_params, dstream2],
        [row_f32, pair_f32],
        functools.partial(step_backward, 2),
        rows,
        width,
        chunks_near,
        near,
        near,
        34,
    )
    grad_fc = jnp.einsum("td,tf->df", inner_two, dbefore, preferred_element_type=f32).astype(bf16)
    grad_out = jnp.einsum("tf,td->fd", attended, dbranch1, preferred_element_type=f32).astype(bf16)
    dattended = jnp.einsum("td,fd->tf", dbranch1, wide_out, preferred_element_type=f32)
    dmixed = attend_back(mixed, my_starts, dattended.astype(bf16))
    partial = jnp.einsum("tc,dc->td", dmixed, wide_qkv, preferred_element_type=f32).astype(bf16)
    grad_qkv = jnp.einsum("td,tc->dc", inner_one, dmixed, preferred_element_type=f32).astype(bf16)
    drows, norm1, grad_proj, grad_out, grad_fc, grad_qkv = line_call(
        "attn_back",
        8,
        partial,
        [stream0, norm_params, dstream1],
        [pair_f32],
        functools.partial(step_backward, 0),
        rows,
        width,
        chunks_turn,
        near,
        chips,
        70,
        [
            ("scatter", 1, grad_proj),
            ("scatter", 1, grad_out),
            ("scatter", 0, grad_fc),
            ("scatter", 0, grad_qkv),
        ],
        "spread",
        9,
    )

    def to_twins(share, axis):
        pieces = jnp.split(share, seqs, axis=axis)
        found = []
        for turn in range(1, seqs):
            back = [(i, (i - turn * sharers) % size_mp) for i in range(size_mp)]
            found.append(lax.ppermute(pieces[turn].astype(bf16), "mp", back))
        return pieces[0], found

    shares = [
        to_twins(grad_qkv, 1),
        to_twins(grad_out, 0),
        to_twins(grad_fc, 1),
        to_twins(grad_proj, 0),
    ]
    grad_table = scatter(keys, owned, head_grad, drows, shift)
    shares, grad_table = lax.optimization_barrier((shares, grad_table))
    grad_qkv, grad_out, grad_fc, grad_proj = [
        sum((piece.astype(f32) for piece in found), mine) for mine, found in shares
    ]

    weights = (embedding, w_qkv, w_out, w_fc, w_proj)
    grads = (grad_table, grad_qkv, grad_out, grad_fc, grad_proj)
    row_span = (size_mp, size_dp, size_mp, size_dp, size_mp)
    col_span = (size_dp, size_mp, size_dp, size_mp, size_dp)
    full = tuple(
        (g.shape[0] * r, g.shape[1] * c) for g, r, c in zip(grads, row_span, col_span)
    )
    squares = [gradient * gradient + EPS_ONE for gradient in grads]
    rows_new, cols_new, loss_sums, grad_norms, second_new, norms_new, rates = update_stats(
        10,
        [jnp.sum(square, axis=1) for square in squares],
        (rows_table, rows_qkv, rows_out, rows_fc, rows_proj),
        [jnp.sum(square, axis=0) for square in squares],
        (cols_table, cols_qkv, cols_out, cols_fc, cols_proj),
        [table_sq] + [jnp.sum(value * value, axis=0) for value in weights[1:]],
        loss_part,
        (norm1, norm2, norm3),
        norm_params,
        second_norms,
        full,
    )
    steps = [
        grads[n] * lax.rsqrt(rows_new[n][:, None] * cols_new[n][None, :] / rates[n, 0])
        for n in range(5)
    ]
    factors = clip_rates(
        11, [jnp.sum(step * step, axis=0) for step in steps], rates, [r * c for r, c in full]
    )
    updated = [weights[n] - factors[n, 0] * steps[n] for n in range(5)]
    return (
        loss_sums,
        counts,
        grad_table,
        rows_new[0],
        cols_new[0],
        updated[0],
        grad_qkv,
        rows_new[1],
        cols_new[1],
        updated[1],
        grad_out,
        rows_new[2],
        cols_new[2],
        updated[2],
        grad_fc,
        rows_new[3],
        cols_new[3],
        updated[3],
        grad_proj,
        rows_new[4],
        cols_new[4],
        updated[4],
        grad_norms,
        second_new,
        norms_new,
    )


def solution(mesh):
    placed = (
        P("dp"),
        P("dp"),
        P("dp"),
        P("dp"),
        P("mp", "dp"),
        P("dp", "mp"),
        P("mp", "dp"),
        P("dp", "mp"),
        P("mp", "dp"),
        P(),
        P("mp"),
        P("dp"),
        P("dp"),
        P("mp"),
        P("mp"),
        P("dp"),
        P("dp"),
        P("mp"),
        P("mp"),
        P("dp"),
        P(),
    )
    return jax.shard_map(
        local,
        mesh=mesh,
        in_specs=placed,
        out_specs=(
            P(),
            P(),
            P("mp", "dp"),
            P("mp"),
            P("dp"),
            P("mp", "dp"),
            P("dp", "mp"),
            P("dp"),
            P("mp"),
            P("dp", "mp"),
            P("mp", "dp"),
            P("mp"),
            P("dp"),
            P("mp", "dp"),
            P("dp", "mp"),
            P("dp"),
            P("mp"),
            P("dp", "mp"),
            P("mp", "dp"),
            P("mp"),
            P("dp"),
            P("mp", "dp"),
            P(),
            P(),
            P(),
        ),
        check_vma=False,
    )
```

```python
import functools
import math

import jax
import jax.numpy as jnp
from jax import lax
from jax.experimental import pallas as pl
from jax.experimental.pallas import tpu as pltpu
from jax.sharding import PartitionSpec as P

HD = 64
VREAL = 50257
LEN = 1024
NSRC = 4
STEP = 10


EPS_NORM = 1e-05
EPS_ONE = 1e-30
CLIP = 1.0
RHO = 0.5
MASKED = -1e30
QUERIES = 256
HEAD_BLOCK = 640
MESH = pl.DeviceIdType.MESH
VMEM_CAP = 56 * 2**20


def cost_of(time):
    return pl.CostEstimate(
        flops=time * 1000000000, bytes_accessed=time * 3000000, transcendentals=0
    )


def row_slice(values, start, count):
    return lax.dynamic_slice_in_dim(values, start, count, 0)


def line_kernel(
    nr, ng, chunks, shapes, n_in, n_out, step, sides, turn, side_ticks, product, chunk_major, *refs
):
    (rows_r, width_r), (rows_g, width_g) = shapes
    if product:
        dl, table = refs[:2]
        first = 2
    else:
        part = refs[0] if nr else None
        first = 1 if nr else 0
    ins = refs[first : first + n_in]
    refs = refs[first + n_in :]
    side_ins, refs = refs[: len(sides)], refs[len(sides) :]
    if ng:
        whole, refs = refs[0], refs[1:]
    outs = refs[:n_out]
    refs = refs[n_out:]
    side_outs, scratch = refs[: len(sides)], refs[len(sides) :]
    side_scratch, scratch = scratch[: 3 * len(sides)], scratch[3 * len(sides) :]
    if turn:
        cast, turn_send, turn_recv = scratch[-3:]
    if product:
        part, dl_buf, total_ref, dl_sem = scratch[-4:]
    size_dp = lax.axis_size("dp")
    dp = lax.axis_index("dp")
    mp = lax.axis_index("mp")
    z = mp // 2
    core = lax.rem(mp, 2)
    other = mp + 1 - 2 * core
    piece_r = rows_r // chunks
    piece_g = rows_g // chunks
    small = min(piece_r, piece_g)
    late = 1 if turn else 0
    ahead = 1 if product else 0
    most = max(nr, ng)
    zb = lax.rem(z, most)
    if nr:
        zr = lax.rem(z, nr)
        last_r = nr - 1
    if ng:
        zg = lax.rem(z, ng)
        last_g = ng - 1

    barrier = pltpu.get_barrier_semaphore()
    pl.semaphore_signal(barrier, inc=1, device_id=(dp, other), device_id_type=MESH)

    @pl.when(zb > 0)
    def _():
        pl.semaphore_signal(barrier, inc=1, device_id=(dp, mp - 2), device_id_type=MESH)

    @pl.when(zb < most - 1)
    def _():
        pl.semaphore_signal(barrier, inc=1, device_id=(dp, mp + 2), device_id_type=MESH)

    if sides or turn:
        for hop in range(1, size_dp):
            pl.semaphore_signal(
                barrier,
                inc=1,
                device_id=(lax.rem(dp + hop, size_dp), mp),
                device_id_type=MESH,
            )
    greeted = (size_dp if sides or turn else 1) + (zb > 0).astype(jnp.int32) + (zb < most - 1).astype(jnp.int32)
    pl.semaphore_wait(barrier, greeted)

    def share(axis, length, which):
        at = pl.ds(pl.multiple_of(which * length, length), length)
        return (at, slice(None)) if axis == 0 else (slice(None), at)

    def to_peer(src, dst, send, recv, peer):
        return pltpu.make_async_remote_copy(
            src_ref=src,
            dst_ref=dst,
            send_sem=send,
            recv_sem=recv,
            device_id=(peer, mp),
            device_id_type=MESH,
        )

    relay = size_dp == 4
    beside_x = dp + 1 - 2 * lax.rem(dp, 2)
    beside_y = lax.rem(dp + 2, 4)
    across = 3 - dp

    def half_share(axis, length, which, height, part):
        if axis == 0:
            return (pl.ds(pl.multiple_of(which * length + part * height, height), height), slice(None))
        at = pl.ds(pl.multiple_of(which * length, length), length)
        return (pl.ds(part * height, height), at)

    first_copies, more_copies, relays = [], [], []
    for index, (kind, axis) in enumerate(sides):
        src, dst = side_ins[index], side_outs[index]
        send, recv, slots = side_scratch[3 * index : 3 * index + 3]
        shard = src if kind == "gather" else dst
        length, height = shard.shape[axis], shard.shape[0] // 2
        if not relay:
            for hop in range(1, size_dp):
                peer = lax.rem(dp + hop, size_dp)
                if kind == "gather":
                    source, target = src, dst.at[share(axis, length, dp)]
                else:
                    source, target = src.at[share(axis, length, peer)], slots.at[hop]
                more_copies.append(to_peer(source, target, send.at[hop], recv.at[hop], peer))
            continue
        for side, near_one, far_one in ((0, beside_x, beside_y), (1, beside_y, beside_x)):
            sems = [(send.at[3 * side + n], recv.at[3 * side + n]) for n in range(3)]
            if kind == "gather":
                mine = src.at[pl.ds(side * height, height)]
                here = dst.at[half_share(axis, length, dp, height, side)]
                passed = dst.at[half_share(axis, length, near_one, height, side)]
                arrives = to_peer(mine, here, *sems[0], near_one)
                first_copies.append(arrives)
                more_copies.append(to_peer(mine, here, *sems[1], far_one))
                relays.append((arrives, None, to_peer(passed, passed, *sems[2], far_one)))
            else:
                arrives = to_peer(
                    src.at[half_share(axis, length, across, height, side)],
                    slots.at[4 * side],
                    *sems[0],
                    near_one,
                )
                first_copies.append(arrives)
                more_copies.append(
                    to_peer(
                        src.at[half_share(axis, length, near_one, height, side)],
                        slots.at[4 * side + 1],
                        *sems[1],
                        near_one,
                    )
                )
                summed = to_peer(
                    slots.at[4 * side + 2], slots.at[4 * side + 3], *sems[2], far_one
                )
                own = src.at[half_share(axis, length, far_one, height, side)]
                relays.append((arrives, (own, slots, 4 * side, height), summed))

    def pass_on(arrives, adding, copy):
        arrives.wait_recv()
        if adding is not None:
            own, slots, at, height = adding
            both = own[...].astype(jnp.float32) + slots[at].astype(jnp.float32)
            slots[at + 2] = both.astype(slots.dtype)
        copy.start()

    jobs = [copy.start for copy in first_copies + more_copies]
    jobs += [functools.partial(pass_on, *one) for one in relays]

    def side_jobs(now):
        for spot in range(side_ticks if jobs else 0):
            chosen = jobs[len(jobs) * spot // side_ticks : len(jobs) * (spot + 1) // side_ticks]

            @pl.when(now == spot)
            def _():
                for job in chosen:
                    job()

    if nr:
        half, from_left, from_right, going = scratch[:4]
        half_send, half_recv, rs_send, left_recv, right_recv = scratch[4:9]
        scratch = scratch[9:]
    if ng:
        core_send, core_recv, to_right, to_left, ag_left, ag_right = scratch[:6]

    def part_rows(block, k):
        return pl.ds(pl.multiple_of(block * rows_r + k * piece_r, piece_r), piece_r)

    def whole_rows(block, k):
        if chunk_major:
            start = k * (2 * ng * piece_g) + block * piece_g
            return pl.ds(pl.multiple_of(start, piece_g), piece_g)
        return pl.ds(pl.multiple_of(block * rows_g + k * piece_g, piece_g), piece_g)

    def remote(src, dst, send, recv, target):
        return pltpu.make_async_remote_copy(
            src_ref=src,
            dst_ref=dst,
            send_sem=send,
            recv_sem=recv,
            device_id=(dp, target),
            device_id_type=MESH,
        )

    if nr:

        def half_copy(dest, k):
            return remote(
                part.at[part_rows(2 * dest + 1 - core, k)],
                half.at[dest, k],
                half_send.at[dest, k],
                half_recv.at[dest, k],
                other,
            )

        def send_halves(k, carry):
            for dest in range(nr):
                half_copy(dest, k).start()
            return carry

        if not product:
            lax.fori_loop(0, chunks, send_halves, 0)

        def right_copy(dest, k):
            return remote(
                going.at[dest, k],
                from_left.at[dest, k],
                rs_send.at[dest, k],
                left_recv.at[dest, k],
                mp + 2,
            )

        def left_copy(dest, k):
            return remote(
                going.at[dest, k],
                from_right.at[dest, k],
                rs_send.at[dest, k],
                right_recv.at[dest, k],
                mp - 2,
            )

        def chip_sum(dest, k):
            half_copy(dest, k).wait_recv()
            mine = part[part_rows(2 * dest + core, k), :].astype(jnp.float32)
            return mine + half[dest, k].astype(jnp.float32)

        def pass_right(dest, k):
            total = chip_sum(dest, k)

            @pl.when(zr == 0)
            def _():
                going[dest, k] = total.astype(jnp.bfloat16)

            @pl.when(zr > 0)
            def _():
                right_copy(dest, k).wait_recv()
                both = total + from_left[dest, k].astype(jnp.float32)
                going[dest, k] = both.astype(jnp.bfloat16)

            right_copy(dest, k).start()

        def pass_left(dest, k):
            total = chip_sum(dest, k)

            @pl.when(zr == last_r)
            def _():
                going[dest, k] = total.astype(jnp.bfloat16)

            @pl.when(zr < last_r)
            def _():
                left_copy(dest, k).wait_recv()
                both = total + from_right[dest, k].astype(jnp.float32)
                going[dest, k] = both.astype(jnp.bfloat16)

            left_copy(dest, k).start()

    if ng:

        def gathered(block, k, send, recv, target):
            where = whole.at[whole_rows(2 * block + core, k)]
            return remote(where, where, send.at[block, k], recv.at[block, k], target)

        def core_copy(block, k):
            return gathered(block, k, core_send, core_recv, other)

        def ag_right_copy(block, k):
            return gathered(block, k, to_right, ag_left, mp + 2)

        def ag_left_copy(block, k):
            return gathered(block, k, to_left, ag_right, mp - 2)

    def own_rows(k):
        total = None
        if nr:
            total = chip_sum(zr, k)
            zero = jnp.zeros((piece_r, width_r), jnp.float32)

            @pl.when(zr > 0)
            def _():
                right_copy(zr, k).wait_recv()

            @pl.when(zr < last_r)
            def _():
                left_copy(zr, k).wait_recv()

            total += jnp.where(zr > 0, from_left[zr, k].astype(jnp.float32), zero)
            total += jnp.where(zr < last_r, from_right[zr, k].astype(jnp.float32), zero)
        if turn == "gather":
            cast[k] = total.astype(cast.dtype)
            for hop in range(1, size_dp):
                turn_copy(hop, k).start()
            mine = pl.ds(pl.multiple_of(dp * small, small), small)
            outs[0][own_place(k, dp)] = cast[k, mine, :]
            return
        at = pl.ds(pl.multiple_of(k * piece_r, piece_r), piece_r)
        ready = step(total, at, ins, outs)
        if turn == "spread":
            cast[k] = ready.astype(cast.dtype)
            for hop in range(1, size_dp):
                turn_copy(hop, k).start()
            whole[own_place(k, dp)] = cast[
                k, :, pl.ds(pl.multiple_of(dp * width_g, width_g), width_g)
            ]
        elif ng:
            whole[whole_rows(2 * zg + core, k), :] = ready.astype(whole.dtype)
            start_gather(k)

    def own_place(k, peer):
        if turn == "gather":
            return (
                pl.ds(pl.multiple_of(k * small, small), small),
                pl.ds(pl.multiple_of(peer * width_r, width_r), width_r),
            )
        start = (2 * zg + core) * rows_g + k * piece_g + peer * small
        return (pl.ds(pl.multiple_of(start, small), small), slice(None))

    def turn_copy(hop, k):
        peer = lax.rem(dp + hop, size_dp)
        if turn == "gather":
            src = cast.at[k, pl.ds(pl.multiple_of(peer * small, small), small)]
            dst = outs[0].at[own_place(k, dp)]
        else:
            src = cast.at[k, :, pl.ds(pl.multiple_of(peer * width_g, width_g), width_g)]
            dst = whole.at[own_place(k, dp)]
        return to_peer(src, dst, turn_send.at[hop, k], turn_recv.at[hop, k], peer)

    def turned_rows(k):
        for hop in range(1, size_dp):
            turn_copy(hop, k).wait_recv()
        if turn == "gather":
            at = pl.ds(pl.multiple_of(k * piece_g, piece_g), piece_g)
            ready = step(None, at, ins, outs)
            whole[whole_rows(2 * zg + core, k), :] = ready.astype(whole.dtype)
        start_gather(k)

    def start_gather(k):
        core_copy(zg, k).start()

        @pl.when(zg < last_g)
        def _():
            ag_right_copy(zg, k).start()

        @pl.when(zg > 0)
        def _():
            ag_left_copy(zg, k).start()

    def inside(k):
        return (k >= 0) & (k < chunks)

    def own_lag(chip):
        if not nr:
            return 0
        at = lax.rem(chip, nr)
        return jnp.maximum(at, last_r - at) + ahead

    def dl_copy(k):
        columns = dl_buf.shape[2]
        return pltpu.make_async_copy(
            dl.at[:, pl.ds(pl.multiple_of(k * columns, columns), columns)],
            dl_buf.at[lax.rem(k, 2)],
            dl_sem.at[lax.rem(k, 2)],
        )

    def make_part(k):
        dl_copy(k).wait()

        @pl.when(k + 1 < chunks)
        def _():
            dl_copy(k + 1).start()

        slot = lax.rem(k, 2)

        def add(i, carry):
            at = pl.ds(pl.multiple_of(i * HEAD_BLOCK, HEAD_BLOCK), HEAD_BLOCK)
            found = lax.dot_general(
                dl_buf[slot, at, :],
                table[at, :],
                (((0,), (0,)), ((), ())),
                preferred_element_type=jnp.float32,
            )

            @pl.when(i == 0)
            def _():
                total_ref[...] = found

            @pl.when(i > 0)
            def _():
                total_ref[...] += found

            return carry

        lax.fori_loop(0, table.shape[0] // HEAD_BLOCK, add, 0)
        for block in range(2 * nr):
            part[part_rows(block, k), :] = total_ref[
                block * piece_r : block * piece_r + piece_r, :
            ].astype(jnp.bfloat16)
        send_halves(k, 0)

    if product:
        dl_copy(0).start()

    def tick(now, carry):
        side_jobs(now)
        if nr:
            k_right = now - zr - ahead
            k_left = now - (last_r - zr) - ahead
            for far in range(last_r):

                @pl.when(inside(k_right) & (last_r - far > zr))
                def _():
                    pass_right(last_r - far, k_right)

                @pl.when(inside(k_left) & (far < zr))
                def _():
                    pass_left(far, k_left)

        k_own = now - own_lag(z)

        @pl.when(inside(k_own))
        def _():
            own_rows(k_own)

        if turn:

            @pl.when(inside(k_own - 1))
            def _():
                turned_rows(k_own - 1)

        if ng:
            for block in range(ng):
                k = now - (own_lag(z - zg + block) + late + jnp.abs(zg - block))

                @pl.when(inside(k) & (block < zg))
                def _():
                    ag_right_copy(block, k).wait_recv()
                    core_copy(block, k).start()

                    @pl.when(zg < last_g)
                    def _():
                        ag_right_copy(block, k).start()

                @pl.when(inside(k) & (block > zg))
                def _():
                    ag_left_copy(block, k).wait_recv()
                    core_copy(block, k).start()

                    @pl.when(zg > 0)
                    def _():
                        ag_left_copy(block, k).start()

        if product:

            @pl.when(now < chunks)
            def _():
                make_part(now)

        return carry

    ticks = ahead + chunks + (nr - 1 if nr else 0) + (ng - 1 if ng else 0) + late
    lax.fori_loop(0, ticks, tick, 0)

    def finish(k, carry):
        if turn:
            for hop in range(1, size_dp):
                turn_copy(hop, k).wait_send()
        if nr:
            for block in range(nr):
                half_copy(block, k).wait_send()

                @pl.when(block != zr)
                def _():
                    right_copy(block, k).wait_send()

        if ng:
            for block in range(ng):
                core_copy(block, k).wait()

                @pl.when((zg < last_g) & (block <= zg))
                def _():
                    ag_right_copy(block, k).wait_send()

                @pl.when((zg > 0) & (block >= zg))
                def _():
                    ag_left_copy(block, k).wait_send()

        return carry

    lax.fori_loop(0, chunks, finish, 0)
    for index, (kind, axis) in enumerate(sides):
        if kind == "gather":
            length = side_ins[index].shape[axis]
            side_outs[index][share(axis, length, dp)] = side_ins[index][...]
    for copy in first_copies:
        copy.wait_send()
    for copy in more_copies:
        copy.wait()
    for unused, unused, copy in relays:
        copy.wait()
    for index, (kind, axis) in enumerate(sides):
        if kind == "scatter":
            src, dst = side_ins[index], side_outs[index]
            slots = side_scratch[3 * index + 2]
            length, height = dst.shape[axis], dst.shape[0] // 2
            if relay:
                for side in range(2):
                    total = src[half_share(axis, length, dp, height, side)].astype(jnp.float32)
                    total += slots[4 * side + 1].astype(jnp.float32)
                    total += slots[4 * side + 3].astype(jnp.float32)
                    dst[pl.ds(side * height, height), :] = total
            else:
                total = src[share(axis, length, dp)].astype(jnp.float32)
                for hop in range(1, size_dp):
                    total += slots[hop].astype(jnp.float32)
                dst[...] = total


def line_call(
    name,
    cid,
    partial,
    ins,
    out_types,
    step,
    rows,
    width,
    chunks,
    nr,
    ng,
    time,
    sides=(),
    turn=None,
    side_ticks=0,
    product=False,
    chunk_major=False,
):
    piece = rows // chunks
    size_dp = lax.axis_size("dp")
    reduced = gathered = (rows, width)
    if turn == "gather":
        gathered = (rows // size_dp, width * size_dp)
    elif turn == "spread":
        gathered = (rows * size_dp, width // size_dp)
    out_shape = []
    if ng:
        out_shape.append(
            jax.ShapeDtypeStruct((2 * ng * gathered[0], gathered[1]), jnp.bfloat16)
        )
    out_shape += out_types
    dma = pltpu.SemaphoreType.DMA
    scratch = []
    for kind, axis, values in sides:
        shape = list(values.shape)
        scratch += [dma((max(size_dp, 6),)), dma((max(size_dp, 6),))]
        if kind == "gather":
            shape[axis] *= size_dp
            out_shape.append(jax.ShapeDtypeStruct(tuple(shape), values.dtype))
            scratch.append(pltpu.VMEM((16, 128), values.dtype))
        else:
            shape[axis] //= size_dp
            out_shape.append(jax.ShapeDtypeStruct(tuple(shape), jnp.float32))
            slots = (8, shape[0] // 2, shape[1]) if size_dp == 4 else (size_dp, *shape)
            scratch.append(pltpu.VMEM(slots, values.dtype))
    if nr:
        scratch += [pltpu.VMEM((nr, chunks, piece, width), jnp.bfloat16)] * 4
        scratch += [dma((nr, chunks))] * 5
    if ng:
        scratch += [dma((ng, chunks))] * 6
    if turn:
        scratch.append(pltpu.VMEM((chunks, piece, width), jnp.bfloat16))
        scratch += [dma((size_dp, chunks))] * 2
    if product:
        dl, table = partial
        columns = dl.shape[1] // chunks
        scratch += [
            pltpu.VMEM((2 * nr * rows, width), jnp.bfloat16),
            pltpu.VMEM((2, dl.shape[0], columns), jnp.bfloat16),
            pltpu.VMEM((columns, width), jnp.float32),
            dma((2,)),
        ]
        partial = [dl, table]
    else:
        partial = [partial] if nr else []
    args = partial + list(ins) + [side[2] for side in sides]
    vmem = pl.BlockSpec(memory_space=pltpu.VMEM)
    call = pl.pallas_call(
        functools.partial(
            line_kernel,
            nr,
            ng,
            chunks,
            (reduced, gathered),
            len(ins),
            len(out_types),
            step,
            tuple(side[:2] for side in sides),
            turn,
            side_ticks,
            product,
            chunk_major,
        ),
        out_shape=out_shape,
        in_specs=[pl.BlockSpec(memory_space=pl.ANY) if product and n == 0 else vmem for n in range(len(args))],
        out_specs=[vmem] * len(out_shape),
        scratch_shapes=scratch,
        compiler_params=pltpu.CompilerParams(
            collective_id=cid, has_side_effects=True, vmem_limit_bytes=VMEM_CAP
        ),
        cost_estimate=cost_of(time),
        name=name,
    )
    return list(call(*args))


def head_stats_kernel(block, tile, table_ref, final_ref, wanted_ref, edge_ref, exp_ref, top_ref, sum_ref, pick_ref):
    j = pl.program_id(0)
    tokens = final_ref.shape[0]
    place = j * block + lax.broadcasted_iota(jnp.int32, (block, 1), 0)
    valid = place < edge_ref[0]

    def one(i, carry):
        at = pl.ds(i * tile, tile)
        logits = lax.dot_general(
            table_ref[...],
            final_ref[at, :],
            (((1,), (1,)), ((), ())),
            preferred_element_type=jnp.float32,
        )
        logits = jnp.where(valid, logits, MASKED)
        top = jnp.max(logits, axis=0, keepdims=True)
        weights = jnp.exp(logits - top)
        exp_ref[:, at] = weights.astype(jnp.bfloat16)
        top_ref[0, :, at] = top
        sum_ref[0, :, at] = jnp.sum(weights, axis=0, keepdims=True)
        pick_ref[0, :, at] = jnp.sum(
            jnp.where(place == wanted_ref[:, at], logits, 0.0), axis=0, keepdims=True
        )
        return carry

    for i in range(tokens // tile):
        one(i, 0)


def head_stats(table, final, wanted, edge, block, tile=512):
    rows, width = table.shape
    tokens = final.shape[0]
    steps = rows // block
    row = jax.ShapeDtypeStruct((steps, 1, tokens), jnp.float32)
    row_spec = pl.BlockSpec((1, 1, tokens), lambda j: (j, 0, 0))
    return pl.pallas_call(
        functools.partial(head_stats_kernel, block, tile),
        grid=(steps,),
        out_shape=[jax.ShapeDtypeStruct((steps * block, tokens), jnp.bfloat16), row, row, row],
        in_specs=[
            pl.BlockSpec((block, width), lambda j: (j, 0)),
            pl.BlockSpec((tokens, width), lambda j: (0, 0)),
            pl.BlockSpec((1, tokens), lambda j: (0, 0)),
            pl.BlockSpec(memory_space=pltpu.SMEM),
        ],
        out_specs=[pl.BlockSpec((block, tokens), lambda j: (j, 0)), row_spec, row_spec, row_spec],
        compiler_params=pltpu.CompilerParams(vmem_limit_bytes=56 * 2**20),
        cost_estimate=pl.CostEstimate(
            flops=2 * rows * width * tokens,
            bytes_accessed=2 * rows * (width + tokens),
            transcendentals=rows * tokens,
        ),
        name="head_stats",
    )(table, final, wanted, edge)


def head_back_kernel(block, tile, exp_ref, final_ref, scale_ref, weight_ref, wanted_ref, dl_ref, grad_ref):
    j = pl.program_id(0)
    tokens = final_ref.shape[0]
    place = j * block + lax.broadcasted_iota(jnp.int32, (block, 1), 0)
    for start in range(0, tokens, tile):
        at = pl.ds(start, tile)
        dl = exp_ref[:, at].astype(jnp.float32) * scale_ref[0, :, at]
        dl = dl - jnp.where(place == wanted_ref[:, at], weight_ref[:, at], 0.0)
        dl_ref[:, at] = dl.astype(jnp.bfloat16)
    strip = block // max(1, block // 256)
    for start in range(0, block, strip):
        at = pl.ds(start, strip)
        grad_ref[at, :] = jnp.dot(
            dl_ref[at, :], final_ref[...], preferred_element_type=jnp.float32
        ).astype(jnp.bfloat16)


def head_back(exps, final, scale, weight, wanted, block, tile=256):
    rows, tokens = exps.shape
    width = final.shape[1]
    return pl.pallas_call(
        functools.partial(head_back_kernel, block, tile),
        grid=(rows // block,),
        out_shape=[
            jax.ShapeDtypeStruct((rows, tokens), jnp.bfloat16),
            jax.ShapeDtypeStruct((rows, width), jnp.bfloat16),
        ],
        in_specs=[
            pl.BlockSpec((block, tokens), lambda j: (j, 0)),
            pl.BlockSpec((tokens, width), lambda j: (0, 0)),
            pl.BlockSpec((1, 1, tokens), lambda j: (j, 0, 0)),
            pl.BlockSpec((1, tokens), lambda j: (0, 0)),
            pl.BlockSpec((1, tokens), lambda j: (0, 0)),
        ],
        out_specs=[
            pl.BlockSpec((block, tokens), lambda j: (j, 0)),
            pl.BlockSpec((block, width), lambda j: (j, 0)),
        ],
        compiler_params=pltpu.CompilerParams(vmem_limit_bytes=56 * 2**20),
        cost_estimate=pl.CostEstimate(
            flops=2 * rows * width * tokens,
            bytes_accessed=2 * rows * (width + 2 * tokens),
            transcendentals=0,
        ),
        name="head_back",
    )(exps, final, scale, weight, wanted)


def head_weights(mixed_ref, starts_ref, base, at, seen):
    query = mixed_ref[at : at + QUERIES, base : base + HD]
    keys = mixed_ref[0:seen, base + HD : base + 2 * HD]
    values = mixed_ref[0:seen, base + 2 * HD : base + 3 * HD]
    scores = lax.dot_general(
        query, keys, (((1,), (1,)), ((), ())), preferred_element_type=jnp.float32
    )
    row = at + lax.broadcasted_iota(jnp.int32, (QUERIES, seen), 0)
    column = lax.broadcasted_iota(jnp.int32, (QUERIES, seen), 1)
    allowed = (column <= row) & (column >= starts_ref[at : at + QUERIES, :])
    scores = jnp.where(allowed, scores * HD ** (-0.5), MASKED)
    weights = jnp.exp(scores - jnp.max(scores, axis=1, keepdims=True))
    probs = weights / jnp.sum(weights, axis=1, keepdims=True)
    return query, keys, values, probs


def attend_kernel(mixed_ref, starts_ref, out_ref):
    length = mixed_ref.shape[0]
    for at in range(0, length, QUERIES):
        found = []
        for head in range(2):
            unused, unused, values, probs = head_weights(
                mixed_ref, starts_ref, head * 3 * HD, at, at + QUERIES
            )
            found.append(
                jnp.dot(probs.astype(jnp.bfloat16), values, preferred_element_type=jnp.float32)
            )
        out_ref[at : at + QUERIES, :] = jnp.concatenate(found, axis=1).astype(jnp.bfloat16)


def attend(mixed, starts):
    length, columns = mixed.shape
    pairs = columns // (6 * HD)
    return pl.pallas_call(
        attend_kernel,
        grid=(pairs,),
        out_shape=jax.ShapeDtypeStruct((length, pairs * 2 * HD), jnp.bfloat16),
        in_specs=[
            pl.BlockSpec((length, 6 * HD), lambda j: (0, j)),
            pl.BlockSpec((length, 1), lambda j: (0, 0)),
        ],
        out_specs=pl.BlockSpec((length, 2 * HD), lambda j: (0, j)),
        compiler_params=pltpu.CompilerParams(vmem_limit_bytes=40 * 2**20),
        cost_estimate=pl.CostEstimate(
            flops=8 * pairs * length * length * HD,
            bytes_accessed=2 * length * columns,
            transcendentals=pairs * length * length,
        ),
        name="attend",
    )(mixed, starts)


def attend_back_kernel(mixed_ref, starts_ref, upstream_ref, out_ref, sums_ref):
    length = mixed_ref.shape[0]
    sums_ref[...] = jnp.zeros_like(sums_ref)
    rows = (((0,), (0,)), ((), ()))
    for at in range(0, length, QUERIES):
        seen = at + QUERIES
        for head in range(2):
            base = head * 3 * HD
            query, keys, values, probs = head_weights(mixed_ref, starts_ref, base, at, seen)
            upstream = upstream_ref[at:seen, head * HD : head * HD + HD]
            dprobs = lax.dot_general(
                upstream, values, (((1,), (1,)), ((), ())), preferred_element_type=jnp.float32
            )
            inner = jnp.sum(probs * dprobs, axis=1, keepdims=True)
            dscores = (probs * (dprobs - inner)).astype(jnp.bfloat16)
            dquery = jnp.dot(dscores, keys, preferred_element_type=jnp.float32)
            dkeys = lax.dot_general(dscores, query, rows, preferred_element_type=jnp.float32)
            dvalues = lax.dot_general(
                probs.astype(jnp.bfloat16), upstream, rows, preferred_element_type=jnp.float32
            )
            sums_ref[at:seen, base : base + HD] = dquery * HD ** (-0.5)
            sums_ref[0:seen, base + HD : base + 2 * HD] += dkeys * HD ** (-0.5)
            sums_ref[0:seen, base + 2 * HD : base + 3 * HD] += dvalues
    out_ref[...] = sums_ref[...].astype(jnp.bfloat16)


def attend_back(mixed, starts, upstream):
    length, columns = mixed.shape
    pairs = columns // (6 * HD)
    return pl.pallas_call(
        attend_back_kernel,
        grid=(pairs,),
        out_shape=jax.ShapeDtypeStruct((length, columns), jnp.bfloat16),
        in_specs=[
            pl.BlockSpec((length, 6 * HD), lambda j: (0, j)),
            pl.BlockSpec((length, 1), lambda j: (0, 0)),
            pl.BlockSpec((length, 2 * HD), lambda j: (0, j)),
        ],
        out_specs=pl.BlockSpec((length, 6 * HD), lambda j: (0, j)),
        scratch_shapes=[pltpu.VMEM((length, 6 * HD), jnp.float32)],
        compiler_params=pltpu.CompilerParams(vmem_limit_bytes=40 * 2**20),
        cost_estimate=pl.CostEstimate(
            flops=20 * pairs * length * length * HD,
            bytes_accessed=4 * length * columns,
            transcendentals=pairs * length * length,
        ),
        name="attend_back",
    )(mixed, starts, upstream)


def small_gather_kernel(axis, count, src_ref, out_ref, send, recv):
    dp = lax.axis_index("dp")
    mp = lax.axis_index("mp")
    me = dp if axis == "dp" else mp

    def device(peer):
        return (peer, mp) if axis == "dp" else (dp, peer)

    barrier = pltpu.get_barrier_semaphore()
    for hop in range(1, count):
        pl.semaphore_signal(
            barrier, inc=1, device_id=device(lax.rem(me + hop, count)), device_id_type=MESH
        )
    pl.semaphore_wait(barrier, count - 1)
    copies = []
    for hop in range(1, count):
        peer = lax.rem(me + hop, count)
        copy = pltpu.make_async_remote_copy(
            src_ref=src_ref,
            dst_ref=out_ref.at[me],
            send_sem=send.at[hop],
            recv_sem=recv.at[hop],
            device_id=device(peer),
            device_id_type=MESH,
        )
        copy.start()
        copies.append(copy)
    out_ref[me] = src_ref[...]
    for copy in copies:
        copy.wait()


def small_gather(name, cid, values, axis):
    count = lax.axis_size(axis)
    vmem = pl.BlockSpec(memory_space=pltpu.VMEM)
    return pl.pallas_call(
        functools.partial(small_gather_kernel, axis, count),
        out_shape=jax.ShapeDtypeStruct((count,) + values.shape, values.dtype),
        in_specs=[vmem],
        out_specs=vmem,
        scratch_shapes=[pltpu.SemaphoreType.DMA((count,)), pltpu.SemaphoreType.DMA((count,))],
        compiler_params=pltpu.CompilerParams(collective_id=cid, has_side_effects=True),
        cost_estimate=cost_of(6),
        name=name,
    )(values)


def exchange(axis, me, here, source, slots, send, recv, first):
    count = slots.shape[0]
    copies = []
    for hop in range(1, count):
        peer = lax.rem(me + hop, count)
        copy = pltpu.make_async_remote_copy(
            src_ref=source,
            dst_ref=slots.at[me],
            send_sem=send.at[first + hop],
            recv_sem=recv.at[first + hop],
            device_id=(peer, here) if axis == "dp" else (here, peer),
            device_id_type=MESH,
        )
        copy.start()
        copies.append(copy)
    slots[me] = source[...]
    for copy in copies:
        copy.wait()
    total = slots[0]
    for index in range(1, count):
        total = total + slots[index]
    return total


def greet_all(dp, mp, size_dp, size_mp):
    barrier = pltpu.get_barrier_semaphore()
    for hop in range(1, size_dp):
        pl.semaphore_signal(
            barrier, inc=1, device_id=(lax.rem(dp + hop, size_dp), mp), device_id_type=MESH
        )
    for hop in range(1, size_mp):
        pl.semaphore_signal(
            barrier, inc=1, device_id=(dp, lax.rem(mp + hop, size_mp)), device_id_type=MESH
        )
    pl.semaphore_wait(barrier, size_dp + size_mp - 2)


def lane_rows(values):
    values = values.reshape(-1)
    return jnp.pad(values, (0, -values.size % 128)).reshape(-1, 128)


def fold(values):
    return jnp.sum(values, axis=0, keepdims=True)


def stats_kernel(full, size_dp, size_mp, *refs):
    row_part, row_old, col_part, col_old, weight_sq = (refs[5 * n : 5 * n + 5] for n in range(5))
    loss_part, norm_one, norm_two, norm_three, norms, second_old = refs[25:31]
    refs = refs[31:]
    row_out, col_out = refs[0:5], refs[5:10]
    loss_out, grads_out, second_out, norms_out, rate_out = refs[10:15]
    send_dp, slots_dp, send_mp, slots_mp, parts, part_slots, whole, send, recv = refs[15:]
    dp = lax.axis_index("dp")
    mp = lax.axis_index("mp")
    greet_all(dp, mp, size_dp, size_mp)
    beta = 1.0 - STEP ** (-0.8)
    width = norms.shape[1]

    at = 0
    marks = []

    def put(values):
        nonlocal at
        rows = values.shape[0]
        send_dp[at : at + rows, :] = values
        marks.append((at, rows))
        at += rows

    norm_rows = width // 128
    for ref in (norm_one, norm_two, norm_three):
        for which in range(2):
            for piece in range(norm_rows):
                put(ref[which : which + 1, piece * 128 : piece * 128 + 128])
    marks.clear()
    count_norm = at
    for index in (0, 2, 4):
        put(row_part[index][...])
    for index in (1, 3):
        put(col_part[index][...])
    put(loss_part[...])
    for index in (1, 3):
        put(fold(row_old[index][...]))
    for index in range(5):
        put(fold(weight_sq[index][...]))
    if at < send_dp.shape[0]:
        send_dp[at:, :] = jnp.zeros((send_dp.shape[0] - at, 128), jnp.float32)
    over_dp = exchange("dp", dp, mp, send_dp, slots_dp, send, recv, 0)
    taken = [over_dp[start : start + rows] for start, rows in marks]
    loss_out[...] = taken[5]
    row_full = {0: taken[0], 2: taken[1], 4: taken[2]}
    col_full = {1: taken[3], 3: taken[4]}
    old_total = {1: taken[6], 3: taken[7]}
    weight_rows = taken[8:13]

    at = 0
    marks = []

    def put_mp(values):
        nonlocal at
        rows = values.shape[0]
        send_mp[at : at + rows, :] = values
        marks.append((at, rows))
        at += rows

    for index in (0, 2, 4):
        put_mp(col_part[index][...])
    for index in (1, 3):
        put_mp(row_part[index][...])
    for index in range(5):
        put_mp(fold(row_full[index] if index in row_full else col_full[index]))
    for index in (0, 2, 4):
        put_mp(fold(row_old[index][...]))
    for index in range(5):
        put_mp(weight_rows[index])
    if at < send_mp.shape[0]:
        send_mp[at:, :] = jnp.zeros((send_mp.shape[0] - at, 128), jnp.float32)
    each = count_norm // size_mp
    for index in range(size_mp):
        parts[index] = over_dp[index * each : index * each + each]
    first = size_dp + size_mp
    copies = []
    for hop in range(1, size_mp):
        peer = lax.rem(mp + hop, size_mp)
        copy = pltpu.make_async_remote_copy(
            src_ref=parts.at[peer],
            dst_ref=part_slots.at[mp],
            send_sem=send.at[first + hop],
            recv_sem=recv.at[first + hop],
            device_id=(dp, peer),
            device_id_type=MESH,
        )
        copy.start()
        copies.append(copy)
    part_slots[mp] = parts[mp]
    over_mp = exchange("mp", mp, dp, send_mp, slots_mp, send, recv, size_dp)
    for copy in copies:
        copy.wait()
    summed = part_slots[0]
    for index in range(1, size_mp):
        summed = summed + part_slots[index]
    whole[mp] = summed
    first += size_mp
    copies = []
    for hop in range(1, size_mp):
        peer = lax.rem(mp + hop, size_mp)
        copy = pltpu.make_async_remote_copy(
            src_ref=whole.at[mp],
            dst_ref=whole.at[mp],
            send_sem=send.at[first + hop],
            recv_sem=recv.at[first + hop],
            device_id=(dp, peer),
            device_id_type=MESH,
        )
        copies.append(copy)
    for copy in copies:
        copy.start()
    taken = [over_mp[start : start + rows] for start, rows in marks]
    for slot, index in enumerate((0, 2, 4)):
        col_full[index] = taken[slot]
        old_total[index] = taken[10 + slot]
    for slot, index in enumerate((1, 3)):
        row_full[index] = taken[3 + slot]
    square_total = taken[5:10]
    weight_total = taken[13:18]
    for index in range(5):
        full_rows, full_cols = full[index]
        row_new = beta * row_old[index][...] + (1.0 - beta) * row_full[index] / full_cols
        col_new = beta * col_old[index][...] + (1.0 - beta) * col_full[index] / full_rows
        row_out[index][...] = row_new
        col_out[index][...] = col_new
        mean = (
            beta * jnp.sum(old_total[index], axis=1, keepdims=True)
            + (1.0 - beta) * jnp.sum(square_total[index], axis=1, keepdims=True) / full_cols
        ) / full_rows
        rate = RHO * jnp.sqrt(
            jnp.sum(weight_total[index], axis=1, keepdims=True) / (full_rows * full_cols)
        )
        rate_out[index : index + 1, :] = jnp.broadcast_to(mean, (1, 128))
        rate_out[8 + index : 9 + index, :] = jnp.broadcast_to(rate, (1, 128))
    for copy in copies:
        copy.wait()
    for row in range(6):
        for piece in range(norm_rows):
            place = row * norm_rows + piece
            grads_out[row : row + 1, piece * 128 : piece * 128 + 128] = whole[
                place // each, place % each : place % each + 1, :
            ]
    grad = grads_out[...]
    second = beta * second_old[...] + (1.0 - beta) * (grad * grad + EPS_ONE)
    second_out[...] = second
    step = grad * lax.rsqrt(second)
    entries = step.size

    def mean_square(values):
        return jnp.sum(jnp.sum(values * values, axis=0, keepdims=True), axis=1, keepdims=True) / (
            entries
        )

    step = step / jnp.maximum(1.0, jnp.sqrt(mean_square(step)) / CLIP)
    old = norms[...]
    norms_out[...] = old - RHO * jnp.sqrt(mean_square(old)) * step


def update_stats(cid, row_parts, rows_old, col_parts, cols_old, weight_sq, loss, norm_parts, norms, second, full):
    size_dp = lax.axis_size("dp")
    size_mp = lax.axis_size("mp")
    f32 = jnp.float32
    rows_old2 = [lane_rows(v) for v in rows_old]
    cols_old2 = [lane_rows(v) for v in cols_old]
    args = (
        [lane_rows(v) for v in row_parts]
        + rows_old2
        + [lane_rows(v) for v in col_parts]
        + cols_old2
        + [v if v.ndim == 2 else lane_rows(v) for v in weight_sq]
        + [lane_rows(loss)]
        + list(norm_parts)
        + [norms, second]
    )
    width = norms.shape[1]
    count_norm = 6 * width // 128
    size_a = count_norm + sum(rows_old2[n].shape[0] for n in (0, 2, 4))
    size_a += sum(cols_old2[n].shape[0] for n in (1, 3)) + 8
    size_a += -size_a % 8
    size_b = sum(cols_old2[n].shape[0] for n in (0, 2, 4))
    size_b += sum(rows_old2[n].shape[0] for n in (1, 3)) + 13
    size_b += -size_b % 8
    each = count_norm // size_mp
    out_shape = [jax.ShapeDtypeStruct(v.shape, f32) for v in rows_old2 + cols_old2]
    out_shape += [
        jax.ShapeDtypeStruct((1, 128), f32),
        jax.ShapeDtypeStruct(norms.shape, f32),
        jax.ShapeDtypeStruct(norms.shape, f32),
        jax.ShapeDtypeStruct(norms.shape, f32),
        jax.ShapeDtypeStruct((16, 128), f32),
    ]
    sems = size_dp + 3 * size_mp
    vmem = pl.BlockSpec(memory_space=pltpu.VMEM)
    found = pl.pallas_call(
        functools.partial(stats_kernel, full, size_dp, size_mp),
        out_shape=out_shape,
        in_specs=[vmem] * len(args),
        out_specs=[vmem] * len(out_shape),
        scratch_shapes=[
            pltpu.VMEM((size_a, 128), f32),
            pltpu.VMEM((size_dp, size_a, 128), f32),
            pltpu.VMEM((size_b, 128), f32),
            pltpu.VMEM((size_mp, size_b, 128), f32),
            pltpu.VMEM((size_mp, each, 128), f32),
            pltpu.VMEM((size_mp, each, 128), f32),
            pltpu.VMEM((size_mp, each, 128), f32),
            pltpu.SemaphoreType.DMA((sems,)),
            pltpu.SemaphoreType.DMA((sems,)),
        ],
        compiler_params=pltpu.CompilerParams(collective_id=cid, has_side_effects=True),
        cost_estimate=cost_of(12),
        name="update_stats",
    )(*args)
    rows_new = [found[n].reshape(-1)[: rows_old[n].size] for n in range(5)]
    cols_new = [found[5 + n].reshape(-1)[: cols_old[n].size] for n in range(5)]
    loss_sums = found[10][0, :NSRC]
    return rows_new, cols_new, loss_sums, found[11], found[12], found[13], found[14]


def clip_kernel(entries, size_dp, size_mp, *refs):
    parts, rate = refs[:5], refs[5]
    out, mine, slots_dp, slots_mp, send, recv = refs[6:]
    dp = lax.axis_index("dp")
    mp = lax.axis_index("mp")
    greet_all(dp, mp, size_dp, size_mp)
    mine[...] = jnp.zeros_like(mine)
    for index in range(5):
        mine[index : index + 1, :] = fold(parts[index][...])
    mine[...] = exchange("dp", dp, mp, mine, slots_dp, send, recv, 0)
    total = exchange("mp", mp, dp, mine, slots_mp, send, recv, size_dp)
    total = jnp.sum(total, axis=1, keepdims=True)
    for index in range(5):
        clip = jnp.maximum(1.0, jnp.sqrt(total[index : index + 1] / entries[index]) / CLIP)
        out[index : index + 1, :] = rate[8 + index : 9 + index, :] / clip


def clip_rates(cid, step_parts, rate, entries):
    size_dp = lax.axis_size("dp")
    size_mp = lax.axis_size("mp")
    vmem = pl.BlockSpec(memory_space=pltpu.VMEM)
    sems = size_dp + size_mp
    return pl.pallas_call(
        functools.partial(clip_kernel, entries, size_dp, size_mp),
        out_shape=jax.ShapeDtypeStruct((8, 128), jnp.float32),
        in_specs=[vmem] * 6,
        out_specs=vmem,
        scratch_shapes=[
            pltpu.VMEM((8, 128), jnp.float32),
            pltpu.VMEM((size_dp, 8, 128), jnp.float32),
            pltpu.VMEM((size_mp, 8, 128), jnp.float32),
            pltpu.SemaphoreType.DMA((sems,)),
            pltpu.SemaphoreType.DMA((sems,)),
        ],
        compiler_params=pltpu.CompilerParams(collective_id=cid, has_side_effects=True),
        cost_estimate=cost_of(8),
        name="clip_rates",
    )(*[lane_rows(v) for v in step_parts], rate)


UNROLL = 8


def lookup_kernel(shift, count_ref, key_ref, table_ref, out_ref, low_ref, square_ref, rows_ref):
    spots = out_ref.shape[0]
    vocab, width = table_ref.shape
    rows_ref[...] = jnp.zeros_like(rows_ref)

    def some(i, carry):
        for j in range(UNROLL):
            key = key_ref[i * UNROLL + j]
            place = key & ((1 << shift) - 1)
            rows_ref[pl.ds(place, 1), :] = table_ref[pl.ds(key >> shift, 1), :]
        return carry

    lax.fori_loop(0, (count_ref[0] + UNROLL - 1) // UNROLL, some, 0)

    def narrow(i, carry):
        at = pl.ds(pl.multiple_of(i * 256, 256), 256)
        out_ref[at, :] = rows_ref[at, :].astype(jnp.bfloat16)
        return carry

    lax.fori_loop(0, spots // 256, narrow, 0)
    strip = 48
    rest = vocab % strip
    done = vocab - rest
    low_ref[done:, :] = jnp.zeros((low_ref.shape[0] - done, width), jnp.bfloat16)

    def squares(values, total):
        for row in range(0, values.shape[0], 8):
            piece = values[row : row + 8, :]
            total = total + piece * piece
        return total

    def lower(i, total):
        at = pl.ds(pl.multiple_of(i * strip, strip), strip)
        values = table_ref[at, :]
        low_ref[at, :] = values.astype(jnp.bfloat16)
        return squares(values, total)

    total = lax.fori_loop(0, done // strip, lower, jnp.zeros((8, width), jnp.float32))
    if rest:
        values = table_ref[done:, :]
        total = squares(values, total)
        values = jnp.concatenate([values, jnp.zeros((strip - rest, width), jnp.float32)])
        low_ref[done : done + strip, :] = values.astype(jnp.bfloat16)
    folded = total[:, 0:128]
    for start in range(128, width, 128):
        folded = folded + total[:, start : start + 128]
    square_ref[...] = folded


def lookup(keys, count, table, spots, shift):
    vocab, width = table.shape
    smem = pl.BlockSpec(memory_space=pltpu.SMEM)
    vmem = pl.BlockSpec(memory_space=pltpu.VMEM)
    return pl.pallas_call(
        functools.partial(lookup_kernel, shift),
        out_shape=[
            jax.ShapeDtypeStruct((spots, width), jnp.bfloat16),
            jax.ShapeDtypeStruct((vocab + -vocab % HEAD_BLOCK, width), jnp.bfloat16),
            jax.ShapeDtypeStruct((8, 128), jnp.float32),
        ],
        in_specs=[smem, smem, vmem],
        out_specs=[vmem] * 3,
        scratch_shapes=[pltpu.VMEM((spots + 8, width), jnp.float32)],
        compiler_params=pltpu.CompilerParams(vmem_limit_bytes=VMEM_CAP),
        cost_estimate=cost_of(20),
        name="lookup",
    )(count, keys, table)


def scatter_kernel(shift, count_ref, key_ref, head_ref, rows_in_ref, grad_ref, rows_ref):
    spots = rows_in_ref.shape[0]
    width = grad_ref.shape[1]

    def widen(i, carry):
        at = pl.ds(pl.multiple_of(i * 256, 256), 256)
        rows_ref[at, :] = rows_in_ref[at, :].astype(jnp.float32)
        return carry

    lax.fori_loop(0, spots // 256, widen, 0)
    rows_ref[spots:, :] = jnp.zeros((8, width), jnp.float32)
    grad_ref[...] = head_ref[...].astype(jnp.float32)[: grad_ref.shape[0]]

    def some(i, carry):
        for j in range(UNROLL):
            key = key_ref[i * UNROLL + j]
            place = key & ((1 << shift) - 1)
            grad_ref[pl.ds(key >> shift, 1), :] += rows_ref[pl.ds(place, 1), :]
        return carry

    lax.fori_loop(0, (count_ref[0] + UNROLL - 1) // UNROLL, some, 0)


def scatter(keys, count, head_grad, rows, vocab, shift):
    spots, width = rows.shape
    smem = pl.BlockSpec(memory_space=pltpu.SMEM)
    vmem = pl.BlockSpec(memory_space=pltpu.VMEM)
    return pl.pallas_call(
        functools.partial(scatter_kernel, shift),
        out_shape=jax.ShapeDtypeStruct((vocab, width), jnp.float32),
        in_specs=[smem, smem, vmem, vmem],
        out_specs=vmem,
        scratch_shapes=[pltpu.VMEM((spots + 8, width), jnp.float32)],
        compiler_params=pltpu.CompilerParams(vmem_limit_bytes=VMEM_CAP),
        cost_estimate=cost_of(23),
        name="scatter",
    )(count, keys, head_grad, rows)


def norm_parts(values):
    centre = jnp.mean(values, axis=-1, keepdims=True)
    centred = values - centre
    scale = lax.rsqrt(jnp.mean(centred * centred, axis=-1, keepdims=True) + EPS_NORM)
    return centred * scale, scale


def norm_pull(values, gain, upstream):
    normed, scale = norm_parts(values)
    weighted = upstream * gain
    pulled = scale * (
        weighted
        - jnp.mean(weighted, axis=-1, keepdims=True)
        - normed * jnp.mean(weighted * normed, axis=-1, keepdims=True)
    )
    return (
        pulled,
        jnp.sum(upstream * normed, axis=0, keepdims=True),
        jnp.sum(upstream, axis=0, keepdims=True),
    )


def step_first(total, at, ins, outs):
    stream, norms = outs[0], ins[0]
    normed, scale = norm_parts(stream[at, :].astype(jnp.float32))
    return normed * norms[0:1, :] + norms[1:2, :]


def step_forward(row, total, at, ins, outs):
    stream, norms = ins
    values = stream[at, :].astype(jnp.float32) + total
    outs[0][at, :] = values
    normed, scale = norm_parts(values)
    return normed * norms[row : row + 1, :] + norms[row + 1 : row + 2, :]


def step_backward(row, total, at, ins, outs):
    stream, norms = ins[:2]
    pulled, dgain, dshift = norm_pull(
        stream[at, :].astype(jnp.float32), norms[row : row + 1, :], total
    )
    if len(ins) > 2:
        pulled = pulled + ins[2][at, :]
    if len(outs) > 1:
        outs[0][at, :] = pulled
    sums = outs[-1]

    @pl.when(at.start == 0)
    def _():
        sums[...] = jnp.zeros_like(sums)

    sums[0:1, :] += dgain
    sums[1:2, :] += dshift
    return pulled


def gelu_tanh(values):
    return jax.nn.gelu(values, approximate=True)


def local(
    token_ids,
    targets,
    starts,
    sources,
    embedding,
    w_qkv,
    w_out,
    w_fc,
    w_proj,
    norm_params,
    rows_table,
    cols_table,
    rows_qkv,
    cols_qkv,
    rows_out,
    cols_out,
    rows_fc,
    cols_fc,
    rows_proj,
    cols_proj,
    second_norms,
):
    bf16 = jnp.bfloat16
    f32 = jnp.float32
    size_mp = lax.axis_size("mp")
    size_dp = lax.axis_size("dp")
    dp = lax.axis_index("dp")
    mp = lax.axis_index("mp")
    tokens = token_ids.shape[0]
    seqs = tokens // LEN
    chips = size_mp // 2
    near = chips // seqs
    sharers = size_mp // seqs
    rows = tokens // size_mp
    vocab, part_width = embedding.shape
    width = part_width * size_dp
    first_row = mp * vocab
    spots = tokens * size_dp
    chunks_full = max(1, min(8, rows // 32))
    chunks_near = max(1, min(4, rows // 32))
    chunks_turn = max(1, min(4, rows // 32))

    both = jnp.stack([token_ids, sources]).reshape(-1, 128)
    both = small_gather("gather_ids", 0, both, "dp").reshape(size_dp, 2, tokens)
    all_ids = both[:, 0]
    all_sources = both[:, 1].reshape(-1)
    counts = jnp.sum(
        (all_sources[:, None] == jnp.arange(NSRC, dtype=jnp.int32)[None, :]).astype(f32), axis=0
    )

    w_qkv, w_out, w_fc, w_proj, all_ids = lax.optimization_barrier(
        (w_qkv, w_out, w_fc, w_proj, all_ids)
    )


    def own_and_twins(weight, axis):
        weight = weight.astype(bf16)
        found = [weight]
        for turn in range(1, seqs):
            shift = [(i, (i + turn * sharers) % size_mp) for i in range(size_mp)]
            found.append(lax.ppermute(weight, "mp", shift))
        return jnp.concatenate(found, axis=axis) if seqs > 1 else weight

    pair_qkv = own_and_twins(w_qkv, 1)
    pair_out = own_and_twins(w_out, 0)
    pair_fc = own_and_twins(w_fc, 1)
    pair_proj = own_and_twins(w_proj, 0)
    piece = rows // chunks_turn
    token = jnp.arange(tokens, dtype=jnp.int32)
    place = (
        token // piece * (size_dp * piece)
        + (jnp.arange(size_dp, dtype=jnp.int32) * piece)[:, None]
        + token % piece
    )
    local_ids = all_ids - first_row
    inside = (local_ids >= 0) & (local_ids < vocab)
    shift = spots.bit_length()
    idle = ((vocab - 1) << shift) + spots
    keys = jnp.where(inside, (local_ids << shift) + place, idle)
    keys = jnp.sort(keys.reshape(-1))
    owned = jnp.sum(inside.astype(jnp.int32)).reshape(1)
    found, low_table, table_sq = lookup(keys, owned, embedding, spots, shift)
    inner_one, stream0, wide_qkv, wide_out, wide_fc, wide_proj = line_call(
        "lookup_sum",
        1,
        found,
        [norm_params],
        [jax.ShapeDtypeStruct((rows, width), bf16)],
        step_first,
        size_dp * rows,
        part_width,
        chunks_turn,
        chips,
        near,
        70,
        [
            ("gather", 0, pair_qkv),
            ("gather", 1, pair_out),
            ("gather", 0, pair_fc),
            ("gather", 1, pair_proj),
        ],
        "gather",
        8,
    )
    low_table, inner_one = lax.optimization_barrier((low_table, inner_one))
    wide_table = lax.all_gather(low_table, "dp", axis=1, tiled=True)
    row_f32 = jax.ShapeDtypeStruct((rows, width), f32)
    pair_f32 = jax.ShapeDtypeStruct((8, width), f32)
    my_starts = row_slice(starts, (mp // sharers) * LEN, LEN)[:, None]
    mixed = jnp.dot(inner_one, wide_qkv, preferred_element_type=f32).astype(bf16)
    attended = attend(mixed, my_starts)
    partial = jnp.dot(attended, wide_out, preferred_element_type=f32).astype(bf16)
    inner_two, stream1 = line_call(
        "attn_sum",
        3,
        partial,
        [stream0, norm_params],
        [row_f32],
        functools.partial(step_forward, 2),
        rows,
        width,
        chunks_near,
        near,
        near,
        32,
    )
    before = jnp.dot(inner_two, wide_fc, preferred_element_type=f32)
    hidden = gelu_tanh(before).astype(bf16)
    partial = jnp.dot(hidden, wide_proj, preferred_element_type=f32).astype(bf16)
    final, stream2 = line_call(
        "mlp_sum",
        4,
        partial,
        [stream1, norm_params],
        [row_f32],
        functools.partial(step_forward, 4),
        rows,
        width,
        chunks_full,
        near,
        chips,
        58,
        chunk_major=True,
    )

    edge = jnp.clip(VREAL - first_row, 0, vocab).astype(jnp.int32).reshape(1)

    def by_chunk(values):
        return values.reshape(size_mp, chunks_full, -1).swapaxes(0, 1).reshape(tokens)

    sources = by_chunk(sources)
    wanted = by_chunk(targets) - first_row
    wanted = jnp.where((wanted >= 0) & (wanted < vocab), wanted, -1).reshape(1, tokens)
    block = HEAD_BLOCK
    exps, tops, sums, picks = head_stats(wide_table, final, wanted, edge, block)
    tops = tops[:, 0]
    top = jnp.max(tops, axis=0)
    total = jnp.sum(sums[:, 0] * jnp.exp(tops - top[None, :]), axis=0)
    pick = jnp.sum(picks[:, 0], axis=0)
    stats = jnp.concatenate([v.reshape(-1, 128) for v in (top, total, pick)])
    stats = small_gather("gather_stats", 5, stats, "mp").reshape(size_mp, 3, tokens)
    highest = jnp.max(stats[:, 0], axis=0)
    log_total = highest + jnp.log(
        jnp.sum(stats[:, 1] * jnp.exp(stats[:, 0] - highest[None, :]), axis=0)
    )
    token_loss = log_total - jnp.sum(stats[:, 2], axis=0)
    member = (sources[:, None] == jnp.arange(NSRC, dtype=jnp.int32)[None, :]).astype(f32)
    loss_part = jnp.sum(member * token_loss[:, None], axis=0)
    weight = jnp.sum(member / (NSRC * jnp.maximum(counts, 1.0))[None, :], axis=1)
    scale = jnp.exp(tops - log_total[None, :]) * weight[None, :]
    dlogits, table_grad = head_back(
        exps, final, scale[:, None, :], weight[None, :], wanted, block
    )
    head_grad = lax.psum_scatter(table_grad, "dp", scatter_dimension=1, tiled=True)

    dbranch2, dstream2, norm3 = line_call(
        "final_back",
        6,
        (dlogits, wide_table),
        [stream2, norm_params],
        [row_f32, pair_f32],
        functools.partial(step_backward, 4),
        rows,
        width,
        chunks_full,
        chips,
        near,
        65,
        product=True,
    )
    grad_proj = jnp.einsum("tf,td->fd", hidden, dbranch2, preferred_element_type=f32).astype(bf16)
    dhidden = jnp.einsum("td,fd->tf", dbranch2, wide_proj, preferred_element_type=f32)
    unused, gelu_pull = jax.vjp(gelu_tanh, before)
    dbefore = gelu_pull(dhidden)[0].astype(bf16)
    partial = jnp.einsum("tf,df->td", dbefore, wide_fc, preferred_element_type=f32).astype(bf16)
    dbranch1, dstream1, norm2 = line_call(
        "mlp_back",
        7,
        partial,
        [stream1, norm_params, dstream2],
        [row_f32, pair_f32],
        functools.partial(step_backward, 2),
        rows,
        width,
        chunks_near,
        near,
        near,
        34,
    )
    grad_fc = jnp.einsum("td,tf->df", inner_two, dbefore, preferred_element_type=f32).astype(bf16)
    grad_out = jnp.einsum("tf,td->fd", attended, dbranch1, preferred_element_type=f32).astype(bf16)
    dattended = jnp.einsum("td,fd->tf", dbranch1, wide_out, preferred_element_type=f32)
    dmixed = attend_back(mixed, my_starts, dattended.astype(bf16))
    partial = jnp.einsum("tc,dc->td", dmixed, wide_qkv, preferred_element_type=f32).astype(bf16)
    grad_qkv = jnp.einsum("td,tc->dc", inner_one, dmixed, preferred_element_type=f32).astype(bf16)
    drows, norm1, grad_proj, grad_out, grad_fc, grad_qkv = line_call(
        "attn_back",
        8,
        partial,
        [stream0, norm_params, dstream1],
        [pair_f32],
        functools.partial(step_backward, 0),
        rows,
        width,
        chunks_turn,
        near,
        chips,
        70,
        [
            ("scatter", 1, grad_proj),
            ("scatter", 1, grad_out),
            ("scatter", 0, grad_fc),
            ("scatter", 0, grad_qkv),
        ],
        "spread",
        9,
    )

    def to_twins(share, axis):
        pieces = jnp.split(share, seqs, axis=axis)
        found = []
        for turn in range(1, seqs):
            back = [(i, (i - turn * sharers) % size_mp) for i in range(size_mp)]
            found.append(lax.ppermute(pieces[turn].astype(bf16), "mp", back))
        return pieces[0], found

    shares = [
        to_twins(grad_qkv, 1),
        to_twins(grad_out, 0),
        to_twins(grad_fc, 1),
        to_twins(grad_proj, 0),
    ]
    grad_table = scatter(keys, owned, head_grad, drows, vocab, shift)
    shares, grad_table = lax.optimization_barrier((shares, grad_table))
    grad_qkv, grad_out, grad_fc, grad_proj = [
        sum((piece.astype(f32) for piece in found), mine) for mine, found in shares
    ]

    weights = (embedding, w_qkv, w_out, w_fc, w_proj)
    grads = (grad_table, grad_qkv, grad_out, grad_fc, grad_proj)
    row_span = (size_mp, size_dp, size_mp, size_dp, size_mp)
    col_span = (size_dp, size_mp, size_dp, size_mp, size_dp)
    full = tuple(
        (g.shape[0] * r, g.shape[1] * c) for g, r, c in zip(grads, row_span, col_span)
    )
    squares = [gradient * gradient + EPS_ONE for gradient in grads]
    rows_new, cols_new, loss_sums, grad_norms, second_new, norms_new, rates = update_stats(
        10,
        [jnp.sum(square, axis=1) for square in squares],
        (rows_table, rows_qkv, rows_out, rows_fc, rows_proj),
        [jnp.sum(square, axis=0) for square in squares],
        (cols_table, cols_qkv, cols_out, cols_fc, cols_proj),
        [table_sq] + [jnp.sum(value * value, axis=0) for value in weights[1:]],
        loss_part,
        (norm1, norm2, norm3),
        norm_params,
        second_norms,
        full,
    )
    steps = [
        grads[n] * lax.rsqrt(rows_new[n][:, None] * cols_new[n][None, :] / rates[n, 0])
        for n in range(5)
    ]
    factors = clip_rates(
        11, [jnp.sum(step * step, axis=0) for step in steps], rates, [r * c for r, c in full]
    )
    updated = [weights[n] - factors[n, 0] * steps[n] for n in range(5)]
    return (
        loss_sums,
        counts,
        grad_table,
        rows_new[0],
        cols_new[0],
        updated[0],
        grad_qkv,
        rows_new[1],
        cols_new[1],
        updated[1],
        grad_out,
        rows_new[2],
        cols_new[2],
        updated[2],
        grad_fc,
        rows_new[3],
        cols_new[3],
        updated[3],
        grad_proj,
        rows_new[4],
        cols_new[4],
        updated[4],
        grad_norms,
        second_new,
        norms_new,
    )


def solution(mesh):
    placed = (
        P("dp"),
        P("dp"),
        P("dp"),
        P("dp"),
        P("mp", "dp"),
        P("dp", "mp"),
        P("mp", "dp"),
        P("dp", "mp"),
        P("mp", "dp"),
        P(),
        P("mp"),
        P("dp"),
        P("dp"),
        P("mp"),
        P("mp"),
        P("dp"),
        P("dp"),
        P("mp"),
        P("mp"),
        P("dp"),
        P(),
    )
    return jax.shard_map(
        local,
        mesh=mesh,
        in_specs=placed,
        out_specs=(
            P(),
            P(),
            P("mp", "dp"),
            P("mp"),
            P("dp"),
            P("mp", "dp"),
            P("dp", "mp"),
            P("dp"),
            P("mp"),
            P("dp", "mp"),
            P("mp", "dp"),
            P("mp"),
            P("dp"),
            P("mp", "dp"),
            P("dp", "mp"),
            P("dp"),
            P("mp"),
            P("dp", "mp"),
            P("mp", "dp"),
            P("mp"),
            P("dp"),
            P("mp", "dp"),
            P(),
            P(),
            P(),
        ),
        check_vma=False,
    )
```

```python
import functools
import math

import jax
import jax.numpy as jnp
from jax import lax
from jax.experimental import pallas as pl
from jax.experimental.pallas import tpu as pltpu
from jax.sharding import PartitionSpec as P

HD = 64
VREAL = 50257
LEN = 1024
NSRC = 4
STEP = 10


EPS_NORM = 1e-05
EPS_ONE = 1e-30
CLIP = 1.0
RHO = 0.5
MASKED = -1e30
QUERIES = 256
HEAD_BLOCK = 640
MESH = pl.DeviceIdType.MESH
VMEM_CAP = 56 * 2**20


def cost_of(time):
    return pl.CostEstimate(
        flops=time * 1000000000, bytes_accessed=time * 3000000, transcendentals=0
    )


def row_slice(values, start, count):
    return lax.dynamic_slice_in_dim(values, start, count, 0)


def line_kernel(
    nr, ng, chunks, shapes, n_in, n_out, step, sides, turn, side_ticks, product, chunk_major, *refs
):
    (rows_r, width_r), (rows_g, width_g) = shapes
    if product:
        dl, *tables = refs[:3]
        first = 3
    else:
        part = refs[0] if nr else None
        first = 1 if nr else 0
    ins = refs[first : first + n_in]
    refs = refs[first + n_in :]
    side_ins, refs = refs[: len(sides)], refs[len(sides) :]
    if ng:
        whole, refs = refs[0], refs[1:]
    outs = refs[:n_out]
    refs = refs[n_out:]
    scatters = [index for index, (kind, unused) in enumerate(sides) if kind == "scatter"]
    side_outs, refs = refs[: len(sides)], refs[len(sides) :]
    twin_outs, scratch = (refs[:2], refs[2:]) if scatters else ([], refs)
    side_scratch, scratch = scratch[: 3 * len(sides)], scratch[3 * len(sides) :]
    if turn:
        cast, turn_send, turn_recv = scratch[-3:]
    if product:
        part, dl_buf, total_ref, dl_sem = scratch[-4:]
    size_dp = lax.axis_size("dp")
    dp = lax.axis_index("dp")
    mp = lax.axis_index("mp")
    z = mp // 2
    core = lax.rem(mp, 2)
    other = mp + 1 - 2 * core
    piece_r = rows_r // chunks
    piece_g = rows_g // chunks
    small = min(piece_r, piece_g)
    late = 1 if turn else 0
    ahead = 1 if product else 0
    most = max(nr, ng)
    zb = lax.rem(z, most)
    if nr:
        zr = lax.rem(z, nr)
        last_r = nr - 1
    if ng:
        zg = lax.rem(z, ng)
        last_g = ng - 1

    barrier = pltpu.get_barrier_semaphore()
    pl.semaphore_signal(barrier, inc=1, device_id=(dp, other), device_id_type=MESH)

    @pl.when(zb > 0)
    def _():
        pl.semaphore_signal(barrier, inc=1, device_id=(dp, mp - 2), device_id_type=MESH)

    @pl.when(zb < most - 1)
    def _():
        pl.semaphore_signal(barrier, inc=1, device_id=(dp, mp + 2), device_id_type=MESH)

    if sides or turn:
        for hop in range(1, size_dp):
            pl.semaphore_signal(
                barrier,
                inc=1,
                device_id=(lax.rem(dp + hop, size_dp), mp),
                device_id_type=MESH,
            )
    greeted = (size_dp if sides or turn else 1) + (zb > 0).astype(jnp.int32) + (zb < most - 1).astype(jnp.int32)
    pl.semaphore_wait(barrier, greeted)

    def share(axis, length, which):
        at = pl.ds(pl.multiple_of(which * length, length), length)
        return (at, slice(None)) if axis == 0 else (slice(None), at)

    def to_peer(src, dst, send, recv, peer):
        return pltpu.make_async_remote_copy(
            src_ref=src,
            dst_ref=dst,
            send_sem=send,
            recv_sem=recv,
            device_id=(peer, mp),
            device_id_type=MESH,
        )

    relay = size_dp == 4
    beside_x = dp + 1 - 2 * lax.rem(dp, 2)
    beside_y = lax.rem(dp + 2, 4)
    across = 3 - dp

    def half_share(axis, length, which, height, part):
        if axis == 0:
            return (pl.ds(pl.multiple_of(which * length + part * height, height), height), slice(None))
        at = pl.ds(pl.multiple_of(which * length, length), length)
        return (pl.ds(part * height, height), at)

    first_copies, more_copies, relays = [], [], []
    for index, (kind, axis) in enumerate(sides):
        src, dst = side_ins[index], side_outs[index]
        send, recv, slots = side_scratch[3 * index : 3 * index + 3]
        if kind == "gather":
            length, height = src.shape[axis], src.shape[0] // 2
        else:
            length = src.shape[axis] // size_dp
            height = (length if axis == 0 else src.shape[0]) // 2
        if not relay:
            for hop in range(1, size_dp):
                peer = lax.rem(dp + hop, size_dp)
                if kind == "gather":
                    source, target = src, dst.at[share(axis, length, dp)]
                else:
                    source, target = src.at[share(axis, length, peer)], slots.at[hop]
                more_copies.append(to_peer(source, target, send.at[hop], recv.at[hop], peer))
            continue
        for side, near_one, far_one in ((0, beside_x, beside_y), (1, beside_y, beside_x)):
            sems = [(send.at[3 * side + n], recv.at[3 * side + n]) for n in range(3)]
            if kind == "gather":
                mine = src.at[pl.ds(side * height, height)]
                here = dst.at[half_share(axis, length, dp, height, side)]
                passed = dst.at[half_share(axis, length, near_one, height, side)]
                arrives = to_peer(mine, here, *sems[0], near_one)
                first_copies.append(arrives)
                more_copies.append(to_peer(mine, here, *sems[1], far_one))
                relays.append((arrives, None, to_peer(passed, passed, *sems[2], far_one)))
            else:
                arrives = to_peer(
                    src.at[half_share(axis, length, across, height, side)],
                    slots.at[4 * side],
                    *sems[0],
                    near_one,
                )
                first_copies.append(arrives)
                more_copies.append(
                    to_peer(
                        src.at[half_share(axis, length, near_one, height, side)],
                        slots.at[4 * side + 1],
                        *sems[1],
                        near_one,
                    )
                )
                summed = to_peer(
                    slots.at[4 * side + 2], slots.at[4 * side + 3], *sems[2], far_one
                )
                own = src.at[half_share(axis, length, far_one, height, side)]
                relays.append((arrives, (own, slots, 4 * side, height), summed))

    def pass_on(arrives, adding, copy):
        arrives.wait_recv()
        if adding is not None:
            own, slots, at, height = adding
            both = own[...].astype(jnp.float32) + slots[at].astype(jnp.float32)
            slots[at + 2] = both.astype(slots.dtype)
        copy.start()

    jobs = [copy.start for copy in first_copies + more_copies]
    jobs += [functools.partial(pass_on, *one) for one in relays]

    def side_jobs(now):
        for spot in range(side_ticks if jobs else 0):
            chosen = jobs[len(jobs) * spot // side_ticks : len(jobs) * (spot + 1) // side_ticks]

            @pl.when(now == spot)
            def _():
                for job in chosen:
                    job()

    if nr:
        half, from_left, from_right, going = scratch[:4]
        half_send, half_recv, rs_send, left_recv, right_recv = scratch[4:9]
        scratch = scratch[9:]
    if ng:
        core_send, core_recv, to_right, to_left, ag_left, ag_right = scratch[:6]

    def part_rows(block, k):
        return pl.ds(pl.multiple_of(block * rows_r + k * piece_r, piece_r), piece_r)

    def whole_rows(block, k):
        if chunk_major:
            start = k * (2 * ng * piece_g) + block * piece_g
            return pl.ds(pl.multiple_of(start, piece_g), piece_g)
        return pl.ds(pl.multiple_of(block * rows_g + k * piece_g, piece_g), piece_g)

    def remote(src, dst, send, recv, target):
        return pltpu.make_async_remote_copy(
            src_ref=src,
            dst_ref=dst,
            send_sem=send,
            recv_sem=recv,
            device_id=(dp, target),
            device_id_type=MESH,
        )

    if nr:

        def half_copy(dest, k):
            return remote(
                part.at[part_rows(2 * dest + 1 - core, k)],
                half.at[dest, k],
                half_send.at[dest, k],
                half_recv.at[dest, k],
                other,
            )

        def send_halves(k, carry):
            for dest in range(nr):
                half_copy(dest, k).start()
            return carry

        if not product:
            lax.fori_loop(0, chunks, send_halves, 0)

        def right_copy(dest, k):
            return remote(
                going.at[dest, k],
                from_left.at[dest, k],
                rs_send.at[dest, k],
                left_recv.at[dest, k],
                mp + 2,
            )

        def left_copy(dest, k):
            return remote(
                going.at[dest, k],
                from_right.at[dest, k],
                rs_send.at[dest, k],
                right_recv.at[dest, k],
                mp - 2,
            )

        def chip_sum(dest, k):
            half_copy(dest, k).wait_recv()
            mine = part[part_rows(2 * dest + core, k), :].astype(jnp.float32)
            return mine + half[dest, k].astype(jnp.float32)

        def pass_right(dest, k):
            total = chip_sum(dest, k)

            @pl.when(zr == 0)
            def _():
                going[dest, k] = total.astype(jnp.bfloat16)

            @pl.when(zr > 0)
            def _():
                right_copy(dest, k).wait_recv()
                both = total + from_left[dest, k].astype(jnp.float32)
                going[dest, k] = both.astype(jnp.bfloat16)

            right_copy(dest, k).start()

        def pass_left(dest, k):
            total = chip_sum(dest, k)

            @pl.when(zr == last_r)
            def _():
                going[dest, k] = total.astype(jnp.bfloat16)

            @pl.when(zr < last_r)
            def _():
                left_copy(dest, k).wait_recv()
                both = total + from_right[dest, k].astype(jnp.float32)
                going[dest, k] = both.astype(jnp.bfloat16)

            left_copy(dest, k).start()

    if ng:

        def gathered(block, k, send, recv, target):
            where = whole.at[whole_rows(2 * block + core, k)]
            return remote(where, where, send.at[block, k], recv.at[block, k], target)

        def core_copy(block, k):
            return gathered(block, k, core_send, core_recv, other)

        def ag_right_copy(block, k):
            return gathered(block, k, to_right, ag_left, mp + 2)

        def ag_left_copy(block, k):
            return gathered(block, k, to_left, ag_right, mp - 2)

    def own_rows(k):
        total = None
        if nr:
            total = chip_sum(zr, k)
            zero = jnp.zeros((piece_r, width_r), jnp.float32)

            @pl.when(zr > 0)
            def _():
                right_copy(zr, k).wait_recv()

            @pl.when(zr < last_r)
            def _():
                left_copy(zr, k).wait_recv()

            total += jnp.where(zr > 0, from_left[zr, k].astype(jnp.float32), zero)
            total += jnp.where(zr < last_r, from_right[zr, k].astype(jnp.float32), zero)
        if turn == "gather":
            cast[k] = total.astype(cast.dtype)
            for hop in range(1, size_dp):
                turn_copy(hop, k).start()
            mine = pl.ds(pl.multiple_of(dp * small, small), small)
            outs[0][own_place(k, dp)] = cast[k, mine, :]
            return
        at = pl.ds(pl.multiple_of(k * piece_r, piece_r), piece_r)
        ready = step(total, at, ins, outs)
        if turn == "spread":
            cast[k] = ready.astype(cast.dtype)
            for hop in range(1, size_dp):
                turn_copy(hop, k).start()
            whole[own_place(k, dp)] = cast[
                k, :, pl.ds(pl.multiple_of(dp * width_g, width_g), width_g)
            ]
        elif ng:
            whole[whole_rows(2 * zg + core, k), :] = ready.astype(whole.dtype)
            start_gather(k)

    def own_place(k, peer):
        if turn == "gather":
            return (
                pl.ds(pl.multiple_of(k * small, small), small),
                pl.ds(pl.multiple_of(peer * width_r, width_r), width_r),
            )
        start = (2 * zg + core) * rows_g + k * piece_g + peer * small
        return (pl.ds(pl.multiple_of(start, small), small), slice(None))

    def turn_copy(hop, k):
        peer = lax.rem(dp + hop, size_dp)
        if turn == "gather":
            src = cast.at[k, pl.ds(pl.multiple_of(peer * small, small), small)]
            dst = outs[0].at[own_place(k, dp)]
        else:
            src = cast.at[k, :, pl.ds(pl.multiple_of(peer * width_g, width_g), width_g)]
            dst = whole.at[own_place(k, dp)]
        return to_peer(src, dst, turn_send.at[hop, k], turn_recv.at[hop, k], peer)

    def turned_rows(k):
        for hop in range(1, size_dp):
            turn_copy(hop, k).wait_recv()
        if turn == "gather":
            at = pl.ds(pl.multiple_of(k * piece_g, piece_g), piece_g)
            ready = step(None, at, ins, outs)
            whole[whole_rows(2 * zg + core, k), :] = ready.astype(whole.dtype)
        start_gather(k)

    def start_gather(k):
        core_copy(zg, k).start()

        @pl.when(zg < last_g)
        def _():
            ag_right_copy(zg, k).start()

        @pl.when(zg > 0)
        def _():
            ag_left_copy(zg, k).start()

    def inside(k):
        return (k >= 0) & (k < chunks)

    def own_lag(chip):
        if not nr:
            return 0
        at = lax.rem(chip, nr)
        return jnp.maximum(at, last_r - at) + ahead

    def dl_copy(k):
        columns = dl_buf.shape[2]
        return pltpu.make_async_copy(
            dl.at[:, pl.ds(pl.multiple_of(k * columns, columns), columns)],
            dl_buf.at[lax.rem(k, 2)],
            dl_sem.at[lax.rem(k, 2)],
        )

    def make_part(k):
        dl_copy(k).wait()

        @pl.when(k + 1 < chunks)
        def _():
            dl_copy(k + 1).start()

        slot = lax.rem(k, 2)

        start = 0
        for piece in tables:
            found = lax.dot_general(
                dl_buf[slot, start : start + piece.shape[0], :],
                piece[...],
                (((0,), (0,)), ((), ())),
                preferred_element_type=jnp.float32,
            )
            if start:
                total_ref[...] += found
            else:
                total_ref[...] = found
            start += piece.shape[0]
        for block in range(2 * nr):
            part[part_rows(block, k), :] = total_ref[
                block * piece_r : block * piece_r + piece_r, :
            ].astype(jnp.bfloat16)
        send_halves(k, 0)

    if product:
        dl_copy(0).start()

    def tick(now, carry):
        side_jobs(now)
        if nr:
            k_right = now - zr - ahead
            k_left = now - (last_r - zr) - ahead
            for far in range(last_r):

                @pl.when(inside(k_right) & (last_r - far > zr))
                def _():
                    pass_right(last_r - far, k_right)

                @pl.when(inside(k_left) & (far < zr))
                def _():
                    pass_left(far, k_left)

        k_own = now - own_lag(z)

        @pl.when(inside(k_own))
        def _():
            own_rows(k_own)

        if turn:

            @pl.when(inside(k_own - 1))
            def _():
                turned_rows(k_own - 1)

        if ng:
            for block in range(ng):
                k = now - (own_lag(z - zg + block) + late + jnp.abs(zg - block))

                @pl.when(inside(k) & (block < zg))
                def _():
                    ag_right_copy(block, k).wait_recv()
                    core_copy(block, k).start()

                    @pl.when(zg < last_g)
                    def _():
                        ag_right_copy(block, k).start()

                @pl.when(inside(k) & (block > zg))
                def _():
                    ag_left_copy(block, k).wait_recv()
                    core_copy(block, k).start()

                    @pl.when(zg > 0)
                    def _():
                        ag_left_copy(block, k).start()

        if product:

            @pl.when(now < chunks)
            def _():
                make_part(now)

        return carry

    ticks = ahead + chunks + (nr - 1 if nr else 0) + (ng - 1 if ng else 0) + late
    lax.fori_loop(0, ticks, tick, 0)

    def finish(k, carry):
        if turn:
            for hop in range(1, size_dp):
                turn_copy(hop, k).wait_send()
        if nr:
            for block in range(nr):
                half_copy(block, k).wait_send()

                @pl.when(block != zr)
                def _():
                    right_copy(block, k).wait_send()

        if ng:
            for block in range(ng):
                core_copy(block, k).wait()

                @pl.when((zg < last_g) & (block <= zg))
                def _():
                    ag_right_copy(block, k).wait_send()

                @pl.when((zg > 0) & (block >= zg))
                def _():
                    ag_left_copy(block, k).wait_send()

        return carry

    lax.fori_loop(0, chunks, finish, 0)
    for index, (kind, axis) in enumerate(sides):
        if kind == "gather":
            length = side_ins[index].shape[axis]
            side_outs[index][share(axis, length, dp)] = side_ins[index][...]
    for copy in first_copies:
        copy.wait_send()
    for copy in more_copies:
        copy.wait()
    for unused, unused, copy in relays:
        copy.wait()
    placed = [0, 0]
    for index in scatters:
        axis = sides[index][1]
        src, dst = side_ins[index], side_outs[index]
        slots = side_scratch[3 * index + 2]
        length = src.shape[axis] // size_dp
        height = (length if axis == 0 else src.shape[0]) // 2
        if relay:
            total = []
            for side in range(2):
                one = src[half_share(axis, length, dp, height, side)].astype(jnp.float32)
                one += slots[4 * side + 1].astype(jnp.float32)
                one += slots[4 * side + 3].astype(jnp.float32)
                total.append(one)
            total = jnp.concatenate(total)
        else:
            total = src[share(axis, length, dp)].astype(jnp.float32)
            for hop in range(1, size_dp):
                total += slots[hop].astype(jnp.float32)
        twins = twin_outs[axis]
        at = placed[axis]
        if axis == 0:
            own = dst.shape[1]
            dst[...] = total[:, :own]
            more = total.shape[1] - own
            twins[:, at : at + more] = total[:, own:].astype(twins.dtype)
        else:
            own = dst.shape[0]
            dst[...] = total[:own, :]
            more = total.shape[0] - own
            twins[at : at + more, :] = total[own:, :].astype(twins.dtype)
        placed[axis] += more


def line_call(
    name,
    cid,
    partial,
    ins,
    out_types,
    step,
    rows,
    width,
    chunks,
    nr,
    ng,
    time,
    sides=(),
    turn=None,
    side_ticks=0,
    product=False,
    chunk_major=False,
    seqs=1,
):
    piece = rows // chunks
    size_dp = lax.axis_size("dp")
    reduced = gathered = (rows, width)
    if turn == "gather":
        gathered = (rows // size_dp, width * size_dp)
    elif turn == "spread":
        gathered = (rows * size_dp, width // size_dp)
    out_shape = []
    if ng:
        out_shape.append(
            jax.ShapeDtypeStruct((2 * ng * gathered[0], gathered[1]), jnp.bfloat16)
        )
    out_shape += out_types
    dma = pltpu.SemaphoreType.DMA
    scratch = []
    twin_shapes = [[0, 0], [0, 0]]
    for kind, axis, values in sides:
        shape = list(values.shape)
        scratch += [dma((max(size_dp, 6),)), dma((max(size_dp, 6),))]
        if kind == "gather":
            shape[axis] *= size_dp
            out_shape.append(jax.ShapeDtypeStruct(tuple(shape), values.dtype))
            scratch.append(pltpu.VMEM((16, 128), values.dtype))
        else:
            shape[axis] //= size_dp
            own = list(shape)
            own[1 - axis] //= seqs
            out_shape.append(jax.ShapeDtypeStruct(tuple(own), jnp.float32))
            twin_shapes[axis][axis] = shape[axis]
            twin_shapes[axis][1 - axis] += shape[1 - axis] - own[1 - axis]
            slots = (8, shape[0] // 2, shape[1]) if size_dp == 4 else (size_dp, *shape)
            scratch.append(pltpu.VMEM(slots, values.dtype))
    if any(side[0] == "scatter" for side in sides):
        out_shape += [jax.ShapeDtypeStruct(tuple(shape), jnp.bfloat16) for shape in twin_shapes]
    if nr:
        scratch += [pltpu.VMEM((nr, chunks, piece, width), jnp.bfloat16)] * 4
        scratch += [dma((nr, chunks))] * 5
    if ng:
        scratch += [dma((ng, chunks))] * 6
    if turn:
        scratch.append(pltpu.VMEM((chunks, piece, width), jnp.bfloat16))
        scratch += [dma((size_dp, chunks))] * 2
    if product:
        dl = partial[0]
        columns = dl.shape[1] // chunks
        scratch += [
            pltpu.VMEM((2 * nr * rows, width), jnp.bfloat16),
            pltpu.VMEM((2, dl.shape[0], columns), jnp.bfloat16),
            pltpu.VMEM((columns, width), jnp.float32),
            dma((2,)),
        ]
        partial = list(partial)
    else:
        partial = [partial] if nr else []
    args = partial + list(ins) + [side[2] for side in sides]
    vmem = pl.BlockSpec(memory_space=pltpu.VMEM)
    call = pl.pallas_call(
        functools.partial(
            line_kernel,
            nr,
            ng,
            chunks,
            (reduced, gathered),
            len(ins),
            len(out_types),
            step,
            tuple(side[:2] for side in sides),
            turn,
            side_ticks,
            product,
            chunk_major,
        ),
        out_shape=out_shape,
        in_specs=[pl.BlockSpec(memory_space=pl.ANY) if product and n == 0 else vmem for n in range(len(args))],
        out_specs=[vmem] * len(out_shape),
        scratch_shapes=scratch,
        compiler_params=pltpu.CompilerParams(
            collective_id=cid, has_side_effects=True, vmem_limit_bytes=VMEM_CAP
        ),
        cost_estimate=cost_of(time),
        name=name,
    )
    return list(call(*args))


def head_stats_kernel(block, tile, early, early_ref, late_ref, final_ref, wanted_ref, edge_ref, exp_ref, top_ref, sum_ref, pick_ref):
    j = pl.program_id(0)
    tokens = final_ref.shape[0]
    place = j * block + lax.broadcasted_iota(jnp.int32, (block, 1), 0)
    valid = place < edge_ref[0]
    table = jnp.where(j < early, early_ref[...], late_ref[...])

    def one(i, carry):
        at = pl.ds(i * tile, tile)
        logits = lax.dot_general(
            table,
            final_ref[at, :],
            (((1,), (1,)), ((), ())),
            preferred_element_type=jnp.float32,
        )
        logits = jnp.where(valid, logits, MASKED)
        top = jnp.max(logits, axis=0, keepdims=True)
        weights = jnp.exp(logits - top)
        exp_ref[:, at] = weights.astype(jnp.bfloat16)
        top_ref[0, :, at] = top
        sum_ref[0, :, at] = jnp.sum(weights, axis=0, keepdims=True)
        pick_ref[0, :, at] = jnp.sum(
            jnp.where(place == wanted_ref[:, at], logits, 0.0), axis=0, keepdims=True
        )
        return carry

    for i in range(tokens // tile):
        one(i, 0)


def head_stats(tables, final, wanted, edge, block, tile=512):
    early = tables[0].shape[0] // block
    rows = sum(table.shape[0] for table in tables)
    width = tables[0].shape[1]
    tokens = final.shape[0]
    steps = rows // block
    row = jax.ShapeDtypeStruct((steps, 1, tokens), jnp.float32)
    row_spec = pl.BlockSpec((1, 1, tokens), lambda j: (j, 0, 0))
    return pl.pallas_call(
        functools.partial(head_stats_kernel, block, tile, early),
        grid=(steps,),
        out_shape=[jax.ShapeDtypeStruct((steps * block, tokens), jnp.bfloat16), row, row, row],
        in_specs=[
            pl.BlockSpec((block, width), lambda j: (jnp.minimum(j, early - 1), 0)),
            pl.BlockSpec((block, width), lambda j: (jnp.maximum(j - early, 0), 0)),
            pl.BlockSpec((tokens, width), lambda j: (0, 0)),
            pl.BlockSpec((1, tokens), lambda j: (0, 0)),
            pl.BlockSpec(memory_space=pltpu.SMEM),
        ],
        out_specs=[pl.BlockSpec((block, tokens), lambda j: (j, 0)), row_spec, row_spec, row_spec],
        compiler_params=pltpu.CompilerParams(vmem_limit_bytes=56 * 2**20),
        cost_estimate=pl.CostEstimate(
            flops=2 * rows * width * tokens,
            bytes_accessed=2 * rows * (width + tokens),
            transcendentals=rows * tokens,
        ),
        name="head_stats",
    )(*tables, final, wanted, edge)


def head_back_kernel(block, tile, exp_ref, final_ref, scale_ref, weight_ref, wanted_ref, dl_ref, grad_ref):
    j = pl.program_id(0)
    tokens = final_ref.shape[0]
    place = j * block + lax.broadcasted_iota(jnp.int32, (block, 1), 0)
    for start in range(0, tokens, tile):
        at = pl.ds(start, tile)
        dl = exp_ref[:, at].astype(jnp.float32) * scale_ref[0, :, at]
        dl = dl - jnp.where(place == wanted_ref[:, at], weight_ref[:, at], 0.0)
        dl_ref[:, at] = dl.astype(jnp.bfloat16)
    strip = block // max(1, block // 256)
    for start in range(0, block, strip):
        at = pl.ds(start, strip)
        grad_ref[at, :] = jnp.dot(
            dl_ref[at, :], final_ref[...], preferred_element_type=jnp.float32
        ).astype(jnp.bfloat16)


def head_back(exps, final, scale, weight, wanted, block, tile=256):
    rows, tokens = exps.shape
    width = final.shape[1]
    return pl.pallas_call(
        functools.partial(head_back_kernel, block, tile),
        grid=(rows // block,),
        out_shape=[
            jax.ShapeDtypeStruct((rows, tokens), jnp.bfloat16),
            jax.ShapeDtypeStruct((rows, width), jnp.bfloat16),
        ],
        in_specs=[
            pl.BlockSpec((block, tokens), lambda j: (j, 0)),
            pl.BlockSpec((tokens, width), lambda j: (0, 0)),
            pl.BlockSpec((1, 1, tokens), lambda j: (j, 0, 0)),
            pl.BlockSpec((1, tokens), lambda j: (0, 0)),
            pl.BlockSpec((1, tokens), lambda j: (0, 0)),
        ],
        out_specs=[
            pl.BlockSpec((block, tokens), lambda j: (j, 0)),
            pl.BlockSpec((block, width), lambda j: (j, 0)),
        ],
        compiler_params=pltpu.CompilerParams(vmem_limit_bytes=56 * 2**20),
        cost_estimate=pl.CostEstimate(
            flops=2 * rows * width * tokens,
            bytes_accessed=2 * rows * (width + 2 * tokens),
            transcendentals=0,
        ),
        name="head_back",
    )(exps, final, scale, weight, wanted)


def head_weights(mixed_ref, starts_ref, base, at, seen):
    query = mixed_ref[at : at + QUERIES, base : base + HD]
    keys = mixed_ref[0:seen, base + HD : base + 2 * HD]
    values = mixed_ref[0:seen, base + 2 * HD : base + 3 * HD]
    scores = lax.dot_general(
        query, keys, (((1,), (1,)), ((), ())), preferred_element_type=jnp.float32
    )
    row = at + lax.broadcasted_iota(jnp.int32, (QUERIES, seen), 0)
    column = lax.broadcasted_iota(jnp.int32, (QUERIES, seen), 1)
    allowed = (column <= row) & (column >= starts_ref[at : at + QUERIES, :])
    scores = jnp.where(allowed, scores * HD ** (-0.5), MASKED)
    weights = jnp.exp(scores - jnp.max(scores, axis=1, keepdims=True))
    probs = weights / jnp.sum(weights, axis=1, keepdims=True)
    return query, keys, values, probs


def attend_kernel(mixed_ref, starts_ref, out_ref):
    length = mixed_ref.shape[0]
    for at in range(0, length, QUERIES):
        found = []
        for head in range(2):
            unused, unused, values, probs = head_weights(
                mixed_ref, starts_ref, head * 3 * HD, at, at + QUERIES
            )
            found.append(
                jnp.dot(probs.astype(jnp.bfloat16), values, preferred_element_type=jnp.float32)
            )
        out_ref[at : at + QUERIES, :] = jnp.concatenate(found, axis=1).astype(jnp.bfloat16)


def attend(mixed, starts):
    length, columns = mixed.shape
    pairs = columns // (6 * HD)
    return pl.pallas_call(
        attend_kernel,
        grid=(pairs,),
        out_shape=jax.ShapeDtypeStruct((length, pairs * 2 * HD), jnp.bfloat16),
        in_specs=[
            pl.BlockSpec((length, 6 * HD), lambda j: (0, j)),
            pl.BlockSpec((length, 1), lambda j: (0, 0)),
        ],
        out_specs=pl.BlockSpec((length, 2 * HD), lambda j: (0, j)),
        compiler_params=pltpu.CompilerParams(vmem_limit_bytes=40 * 2**20),
        cost_estimate=pl.CostEstimate(
            flops=8 * pairs * length * length * HD,
            bytes_accessed=2 * length * columns,
            transcendentals=pairs * length * length,
        ),
        name="attend",
    )(mixed, starts)


def attend_back_kernel(mixed_ref, starts_ref, upstream_ref, out_ref, sums_ref):
    length = mixed_ref.shape[0]
    sums_ref[...] = jnp.zeros_like(sums_ref)
    rows = (((0,), (0,)), ((), ()))
    for at in range(0, length, QUERIES):
        seen = at + QUERIES
        for head in range(2):
            base = head * 3 * HD
            query, keys, values, probs = head_weights(mixed_ref, starts_ref, base, at, seen)
            upstream = upstream_ref[at:seen, head * HD : head * HD + HD]
            dprobs = lax.dot_general(
                upstream, values, (((1,), (1,)), ((), ())), preferred_element_type=jnp.float32
            )
            inner = jnp.sum(probs * dprobs, axis=1, keepdims=True)
            dscores = (probs * (dprobs - inner)).astype(jnp.bfloat16)
            dquery = jnp.dot(dscores, keys, preferred_element_type=jnp.float32)
            dkeys = lax.dot_general(dscores, query, rows, preferred_element_type=jnp.float32)
            dvalues = lax.dot_general(
                probs.astype(jnp.bfloat16), upstream, rows, preferred_element_type=jnp.float32
            )
            sums_ref[at:seen, base : base + HD] = dquery * HD ** (-0.5)
            sums_ref[0:seen, base + HD : base + 2 * HD] += dkeys * HD ** (-0.5)
            sums_ref[0:seen, base + 2 * HD : base + 3 * HD] += dvalues
    out_ref[...] = sums_ref[...].astype(jnp.bfloat16)


def attend_back(mixed, starts, upstream):
    length, columns = mixed.shape
    pairs = columns // (6 * HD)
    return pl.pallas_call(
        attend_back_kernel,
        grid=(pairs,),
        out_shape=jax.ShapeDtypeStruct((length, columns), jnp.bfloat16),
        in_specs=[
            pl.BlockSpec((length, 6 * HD), lambda j: (0, j)),
            pl.BlockSpec((length, 1), lambda j: (0, 0)),
            pl.BlockSpec((length, 2 * HD), lambda j: (0, j)),
        ],
        out_specs=pl.BlockSpec((length, 6 * HD), lambda j: (0, j)),
        scratch_shapes=[pltpu.VMEM((length, 6 * HD), jnp.float32)],
        compiler_params=pltpu.CompilerParams(vmem_limit_bytes=40 * 2**20),
        cost_estimate=pl.CostEstimate(
            flops=20 * pairs * length * length * HD,
            bytes_accessed=4 * length * columns,
            transcendentals=pairs * length * length,
        ),
        name="attend_back",
    )(mixed, starts, upstream)


def small_gather_kernel(axis, count, src_ref, out_ref, send, recv):
    dp = lax.axis_index("dp")
    mp = lax.axis_index("mp")
    me = dp if axis == "dp" else mp

    def device(peer):
        return (peer, mp) if axis == "dp" else (dp, peer)

    barrier = pltpu.get_barrier_semaphore()
    for hop in range(1, count):
        pl.semaphore_signal(
            barrier, inc=1, device_id=device(lax.rem(me + hop, count)), device_id_type=MESH
        )
    pl.semaphore_wait(barrier, count - 1)
    copies = []
    for hop in range(1, count):
        peer = lax.rem(me + hop, count)
        copy = pltpu.make_async_remote_copy(
            src_ref=src_ref,
            dst_ref=out_ref.at[me],
            send_sem=send.at[hop],
            recv_sem=recv.at[hop],
            device_id=device(peer),
            device_id_type=MESH,
        )
        copy.start()
        copies.append(copy)
    out_ref[me] = src_ref[...]
    for copy in copies:
        copy.wait()


def small_gather(name, cid, values, axis):
    count = lax.axis_size(axis)
    vmem = pl.BlockSpec(memory_space=pltpu.VMEM)
    return pl.pallas_call(
        functools.partial(small_gather_kernel, axis, count),
        out_shape=jax.ShapeDtypeStruct((count,) + values.shape, values.dtype),
        in_specs=[vmem],
        out_specs=vmem,
        scratch_shapes=[pltpu.SemaphoreType.DMA((count,)), pltpu.SemaphoreType.DMA((count,))],
        compiler_params=pltpu.CompilerParams(collective_id=cid, has_side_effects=True),
        cost_estimate=cost_of(6),
        name=name,
    )(values)


def exchange(axis, me, here, source, slots, send, recv, first):
    count = slots.shape[0]
    copies = []
    for hop in range(1, count):
        peer = lax.rem(me + hop, count)
        copy = pltpu.make_async_remote_copy(
            src_ref=source,
            dst_ref=slots.at[me],
            send_sem=send.at[first + hop],
            recv_sem=recv.at[first + hop],
            device_id=(peer, here) if axis == "dp" else (here, peer),
            device_id_type=MESH,
        )
        copy.start()
        copies.append(copy)
    slots[me] = source[...]
    for copy in copies:
        copy.wait()
    total = slots[0]
    for index in range(1, count):
        total = total + slots[index]
    return total


def greet_all(dp, mp, size_dp, size_mp):
    barrier = pltpu.get_barrier_semaphore()
    for hop in range(1, size_dp):
        pl.semaphore_signal(
            barrier, inc=1, device_id=(lax.rem(dp + hop, size_dp), mp), device_id_type=MESH
        )
    for hop in range(1, size_mp):
        pl.semaphore_signal(
            barrier, inc=1, device_id=(dp, lax.rem(mp + hop, size_mp)), device_id_type=MESH
        )
    pl.semaphore_wait(barrier, size_dp + size_mp - 2)


def lane_rows(values):
    values = values.reshape(-1)
    return jnp.pad(values, (0, -values.size % 128)).reshape(-1, 128)


def fold(values):
    return jnp.sum(values, axis=0, keepdims=True)


def stats_kernel(full, size_dp, size_mp, *refs):
    row_part, row_old, col_part, col_old, weight_sq = (refs[5 * n : 5 * n + 5] for n in range(5))
    loss_part, norm_one, norm_two, norm_three, norms, second_old = refs[25:31]
    refs = refs[31:]
    row_out, col_out = refs[0:5], refs[5:10]
    loss_out, grads_out, second_out, norms_out, rate_out = refs[10:15]
    send_dp, slots_dp, send_mp, slots_mp, parts, part_slots, whole, send, recv = refs[15:]
    dp = lax.axis_index("dp")
    mp = lax.axis_index("mp")
    greet_all(dp, mp, size_dp, size_mp)
    beta = 1.0 - STEP ** (-0.8)
    width = norms.shape[1]

    at = 0
    marks = []

    def put(values):
        nonlocal at
        rows = values.shape[0]
        send_dp[at : at + rows, :] = values
        marks.append((at, rows))
        at += rows

    norm_rows = width // 128
    for ref in (norm_one, norm_two, norm_three):
        for which in range(2):
            for piece in range(norm_rows):
                put(ref[which : which + 1, piece * 128 : piece * 128 + 128])
    marks.clear()
    count_norm = at
    for index in (0, 2, 4):
        put(row_part[index][...])
    for index in (1, 3):
        put(col_part[index][...])
    put(loss_part[...])
    for index in (1, 3):
        put(fold(row_old[index][...]))
    for index in range(5):
        put(fold(weight_sq[index][...]))
    if at < send_dp.shape[0]:
        send_dp[at:, :] = jnp.zeros((send_dp.shape[0] - at, 128), jnp.float32)
    over_dp = exchange("dp", dp, mp, send_dp, slots_dp, send, recv, 0)
    taken = [over_dp[start : start + rows] for start, rows in marks]
    loss_out[...] = taken[5]
    row_full = {0: taken[0], 2: taken[1], 4: taken[2]}
    col_full = {1: taken[3], 3: taken[4]}
    old_total = {1: taken[6], 3: taken[7]}
    weight_rows = taken[8:13]

    at = 0
    marks = []

    def put_mp(values):
        nonlocal at
        rows = values.shape[0]
        send_mp[at : at + rows, :] = values
        marks.append((at, rows))
        at += rows

    for index in (0, 2, 4):
        put_mp(col_part[index][...])
    for index in (1, 3):
        put_mp(row_part[index][...])
    for index in range(5):
        put_mp(fold(row_full[index] if index in row_full else col_full[index]))
    for index in (0, 2, 4):
        put_mp(fold(row_old[index][...]))
    for index in range(5):
        put_mp(weight_rows[index])
    if at < send_mp.shape[0]:
        send_mp[at:, :] = jnp.zeros((send_mp.shape[0] - at, 128), jnp.float32)
    each = count_norm // size_mp
    for index in range(size_mp):
        parts[index] = over_dp[index * each : index * each + each]
    first = size_dp + size_mp
    copies = []
    for hop in range(1, size_mp):
        peer = lax.rem(mp + hop, size_mp)
        copy = pltpu.make_async_remote_copy(
            src_ref=parts.at[peer],
            dst_ref=part_slots.at[mp],
            send_sem=send.at[first + hop],
            recv_sem=recv.at[first + hop],
            device_id=(dp, peer),
            device_id_type=MESH,
        )
        copy.start()
        copies.append(copy)
    part_slots[mp] = parts[mp]
    over_mp = exchange("mp", mp, dp, send_mp, slots_mp, send, recv, size_dp)
    for copy in copies:
        copy.wait()
    summed = part_slots[0]
    for index in range(1, size_mp):
        summed = summed + part_slots[index]
    whole[mp] = summed
    first += size_mp
    copies = []
    for hop in range(1, size_mp):
        peer = lax.rem(mp + hop, size_mp)
        copy = pltpu.make_async_remote_copy(
            src_ref=whole.at[mp],
            dst_ref=whole.at[mp],
            send_sem=send.at[first + hop],
            recv_sem=recv.at[first + hop],
            device_id=(dp, peer),
            device_id_type=MESH,
        )
        copies.append(copy)
    for copy in copies:
        copy.start()
    taken = [over_mp[start : start + rows] for start, rows in marks]
    for slot, index in enumerate((0, 2, 4)):
        col_full[index] = taken[slot]
        old_total[index] = taken[10 + slot]
    for slot, index in enumerate((1, 3)):
        row_full[index] = taken[3 + slot]
    square_total = taken[5:10]
    weight_total = taken[13:18]
    for index in range(5):
        full_rows, full_cols = full[index]
        row_new = beta * row_old[index][...] + (1.0 - beta) * row_full[index] / full_cols
        col_new = beta * col_old[index][...] + (1.0 - beta) * col_full[index] / full_rows
        row_out[index][...] = row_new
        col_out[index][...] = col_new
        mean = (
            beta * jnp.sum(old_total[index], axis=1, keepdims=True)
            + (1.0 - beta) * jnp.sum(square_total[index], axis=1, keepdims=True) / full_cols
        ) / full_rows
        rate = RHO * jnp.sqrt(
            jnp.sum(weight_total[index], axis=1, keepdims=True) / (full_rows * full_cols)
        )
        rate_out[index : index + 1, :] = jnp.broadcast_to(mean, (1, 128))
        rate_out[8 + index : 9 + index, :] = jnp.broadcast_to(rate, (1, 128))
    for copy in copies:
        copy.wait()
    for row in range(6):
        for piece in range(norm_rows):
            place = row * norm_rows + piece
            grads_out[row : row + 1, piece * 128 : piece * 128 + 128] = whole[
                place // each, place % each : place % each + 1, :
            ]
    grad = grads_out[...]
    second = beta * second_old[...] + (1.0 - beta) * (grad * grad + EPS_ONE)
    second_out[...] = second
    step = grad * lax.rsqrt(second)
    entries = step.size

    def mean_square(values):
        return jnp.sum(jnp.sum(values * values, axis=0, keepdims=True), axis=1, keepdims=True) / (
            entries
        )

    step = step / jnp.maximum(1.0, jnp.sqrt(mean_square(step)) / CLIP)
    old = norms[...]
    norms_out[...] = old - RHO * jnp.sqrt(mean_square(old)) * step


def update_stats(cid, row_parts, rows_old, col_parts, cols_old, weight_sq, loss, norm_parts, norms, second, full):
    size_dp = lax.axis_size("dp")
    size_mp = lax.axis_size("mp")
    f32 = jnp.float32
    rows_old2 = [lane_rows(v) for v in rows_old]
    cols_old2 = [lane_rows(v) for v in cols_old]
    args = (
        [lane_rows(v) for v in row_parts]
        + rows_old2
        + [lane_rows(v) for v in col_parts]
        + cols_old2
        + [v if v.ndim == 2 else lane_rows(v) for v in weight_sq]
        + [lane_rows(loss)]
        + list(norm_parts)
        + [norms, second]
    )
    width = norms.shape[1]
    count_norm = 6 * width // 128
    size_a = count_norm + sum(rows_old2[n].shape[0] for n in (0, 2, 4))
    size_a += sum(cols_old2[n].shape[0] for n in (1, 3)) + 8
    size_a += -size_a % 8
    size_b = sum(cols_old2[n].shape[0] for n in (0, 2, 4))
    size_b += sum(rows_old2[n].shape[0] for n in (1, 3)) + 13
    size_b += -size_b % 8
    each = count_norm // size_mp
    out_shape = [jax.ShapeDtypeStruct(v.shape, f32) for v in rows_old2 + cols_old2]
    out_shape += [
        jax.ShapeDtypeStruct((1, 128), f32),
        jax.ShapeDtypeStruct(norms.shape, f32),
        jax.ShapeDtypeStruct(norms.shape, f32),
        jax.ShapeDtypeStruct(norms.shape, f32),
        jax.ShapeDtypeStruct((16, 128), f32),
    ]
    sems = size_dp + 3 * size_mp
    vmem = pl.BlockSpec(memory_space=pltpu.VMEM)
    found = pl.pallas_call(
        functools.partial(stats_kernel, full, size_dp, size_mp),
        out_shape=out_shape,
        in_specs=[vmem] * len(args),
        out_specs=[vmem] * len(out_shape),
        scratch_shapes=[
            pltpu.VMEM((size_a, 128), f32),
            pltpu.VMEM((size_dp, size_a, 128), f32),
            pltpu.VMEM((size_b, 128), f32),
            pltpu.VMEM((size_mp, size_b, 128), f32),
            pltpu.VMEM((size_mp, each, 128), f32),
            pltpu.VMEM((size_mp, each, 128), f32),
            pltpu.VMEM((size_mp, each, 128), f32),
            pltpu.SemaphoreType.DMA((sems,)),
            pltpu.SemaphoreType.DMA((sems,)),
        ],
        compiler_params=pltpu.CompilerParams(collective_id=cid, has_side_effects=True),
        cost_estimate=cost_of(12),
        name="update_stats",
    )(*args)
    rows_new = [found[n].reshape(-1)[: rows_old[n].size] for n in range(5)]
    cols_new = [found[5 + n].reshape(-1)[: cols_old[n].size] for n in range(5)]
    loss_sums = found[10][0, :NSRC]
    return rows_new, cols_new, loss_sums, found[11], found[12], found[13], found[14]


def clip_kernel(entries, size_dp, size_mp, *refs):
    parts, rate = refs[:5], refs[5]
    out, mine, slots_dp, slots_mp, send, recv = refs[6:]
    dp = lax.axis_index("dp")
    mp = lax.axis_index("mp")
    greet_all(dp, mp, size_dp, size_mp)
    mine[...] = jnp.zeros_like(mine)
    for index in range(5):
        mine[index : index + 1, :] = fold(parts[index][...])
    mine[...] = exchange("dp", dp, mp, mine, slots_dp, send, recv, 0)
    total = exchange("mp", mp, dp, mine, slots_mp, send, recv, size_dp)
    total = jnp.sum(total, axis=1, keepdims=True)
    for index in range(5):
        clip = jnp.maximum(1.0, jnp.sqrt(total[index : index + 1] / entries[index]) / CLIP)
        out[index : index + 1, :] = rate[8 + index : 9 + index, :] / clip


def clip_rates(cid, step_parts, rate, entries):
    size_dp = lax.axis_size("dp")
    size_mp = lax.axis_size("mp")
    vmem = pl.BlockSpec(memory_space=pltpu.VMEM)
    sems = size_dp + size_mp
    return pl.pallas_call(
        functools.partial(clip_kernel, entries, size_dp, size_mp),
        out_shape=jax.ShapeDtypeStruct((8, 128), jnp.float32),
        in_specs=[vmem] * 6,
        out_specs=vmem,
        scratch_shapes=[
            pltpu.VMEM((8, 128), jnp.float32),
            pltpu.VMEM((size_dp, 8, 128), jnp.float32),
            pltpu.VMEM((size_mp, 8, 128), jnp.float32),
            pltpu.SemaphoreType.DMA((sems,)),
            pltpu.SemaphoreType.DMA((sems,)),
        ],
        compiler_params=pltpu.CompilerParams(collective_id=cid, has_side_effects=True),
        cost_estimate=cost_of(8),
        name="clip_rates",
    )(*[lane_rows(v) for v in step_parts], rate)


UNROLL = 8


def lookup_kernel(shift, early, count_ref, key_ref, table_ref, out_ref, low_ref, square_ref, rows_ref):
    spots = out_ref.shape[0]
    vocab, width = table_ref.shape
    rows_ref[...] = jnp.zeros_like(rows_ref)

    def some(i, carry):
        for j in range(UNROLL):
            key = key_ref[i * UNROLL + j]
            place = key & ((1 << shift) - 1)
            rows_ref[pl.ds(place, 1), :] = table_ref[pl.ds(key >> shift, 1), :]
        return carry

    lax.fori_loop(0, (count_ref[0] + UNROLL - 1) // UNROLL, some, 0)

    def narrow(i, carry):
        at = pl.ds(pl.multiple_of(i * 256, 256), 256)
        out_ref[at, :] = rows_ref[at, :].astype(jnp.bfloat16)
        return carry

    lax.fori_loop(0, spots // 256, narrow, 0)
    strip = 48
    rest = vocab % strip
    done = vocab - rest
    low_ref[done - early :, :] = jnp.zeros(
        (low_ref.shape[0] - done + early, width), jnp.bfloat16
    )

    def squares(values, total):
        for row in range(0, values.shape[0], 8):
            piece = values[row : row + 8, :]
            total = total + piece * piece
        return total

    def lower(i, total):
        at = pl.ds(pl.multiple_of(i * strip, strip), strip)
        values = table_ref[at, :]

        @pl.when(i >= early // strip)
        def _():
            start = pl.multiple_of(i * strip - early, 16)
            low_ref[pl.ds(start, strip), :] = values.astype(jnp.bfloat16)

        return squares(values, total)

    total = lax.fori_loop(0, done // strip, lower, jnp.zeros((8, width), jnp.float32))
    if rest:
        values = table_ref[done:, :]
        total = squares(values, total)
        values = jnp.concatenate([values, jnp.zeros((strip - rest, width), jnp.float32)])
        low_ref[done - early : done - early + strip, :] = values.astype(jnp.bfloat16)
    folded = total[:, 0:128]
    for start in range(128, width, 128):
        folded = folded + total[:, start : start + 128]
    square_ref[...] = folded


def lookup(keys, count, table, spots, shift, early):
    vocab, width = table.shape
    smem = pl.BlockSpec(memory_space=pltpu.SMEM)
    vmem = pl.BlockSpec(memory_space=pltpu.VMEM)
    return pl.pallas_call(
        functools.partial(lookup_kernel, shift, early),
        out_shape=[
            jax.ShapeDtypeStruct((spots, width), jnp.bfloat16),
            jax.ShapeDtypeStruct((vocab + -vocab % HEAD_BLOCK - early, width), jnp.bfloat16),
            jax.ShapeDtypeStruct((8, 128), jnp.float32),
        ],
        in_specs=[smem, smem, vmem],
        out_specs=[vmem] * 3,
        scratch_shapes=[pltpu.VMEM((spots + 8, width), jnp.float32)],
        compiler_params=pltpu.CompilerParams(vmem_limit_bytes=VMEM_CAP),
        cost_estimate=cost_of(20),
        name="lookup",
    )(count, keys, table)


def scatter_kernel(shift, count_ref, key_ref, head_ref, rows_in_ref, grad_ref, rows_ref):
    spots = rows_in_ref.shape[0]
    width = grad_ref.shape[1]

    def widen(i, carry):
        at = pl.ds(pl.multiple_of(i * 256, 256), 256)
        rows_ref[at, :] = rows_in_ref[at, :].astype(jnp.float32)
        return carry

    lax.fori_loop(0, spots // 256, widen, 0)
    rows_ref[spots:, :] = jnp.zeros((8, width), jnp.float32)
    grad_ref[...] = head_ref[...].astype(jnp.float32)[: grad_ref.shape[0]]

    def some(i, carry):
        for j in range(UNROLL):
            key = key_ref[i * UNROLL + j]
            place = key & ((1 << shift) - 1)
            grad_ref[pl.ds(key >> shift, 1), :] += rows_ref[pl.ds(place, 1), :]
        return carry

    lax.fori_loop(0, (count_ref[0] + UNROLL - 1) // UNROLL, some, 0)


def scatter(keys, count, head_grad, rows, vocab, shift):
    spots, width = rows.shape
    smem = pl.BlockSpec(memory_space=pltpu.SMEM)
    vmem = pl.BlockSpec(memory_space=pltpu.VMEM)
    return pl.pallas_call(
        functools.partial(scatter_kernel, shift),
        out_shape=jax.ShapeDtypeStruct((vocab, width), jnp.float32),
        in_specs=[smem, smem, vmem, vmem],
        out_specs=vmem,
        scratch_shapes=[pltpu.VMEM((spots + 8, width), jnp.float32)],
        compiler_params=pltpu.CompilerParams(vmem_limit_bytes=VMEM_CAP),
        cost_estimate=cost_of(23),
        name="scatter",
    )(count, keys, head_grad, rows)


def norm_parts(values):
    centre = jnp.mean(values, axis=-1, keepdims=True)
    centred = values - centre
    scale = lax.rsqrt(jnp.mean(centred * centred, axis=-1, keepdims=True) + EPS_NORM)
    return centred * scale, scale


def norm_pull(values, gain, upstream):
    normed, scale = norm_parts(values)
    weighted = upstream * gain
    pulled = scale * (
        weighted
        - jnp.mean(weighted, axis=-1, keepdims=True)
        - normed * jnp.mean(weighted * normed, axis=-1, keepdims=True)
    )
    return (
        pulled,
        jnp.sum(upstream * normed, axis=0, keepdims=True),
        jnp.sum(upstream, axis=0, keepdims=True),
    )


def step_first(total, at, ins, outs):
    stream, norms = outs[0], ins[0]
    normed, scale = norm_parts(stream[at, :].astype(jnp.float32))
    return normed * norms[0:1, :] + norms[1:2, :]


def step_forward(row, total, at, ins, outs):
    stream, norms = ins
    values = stream[at, :].astype(jnp.float32) + total
    outs[0][at, :] = values
    normed, scale = norm_parts(values)
    return normed * norms[row : row + 1, :] + norms[row + 1 : row + 2, :]


def step_backward(row, total, at, ins, outs):
    stream, norms = ins[:2]
    pulled, dgain, dshift = norm_pull(
        stream[at, :].astype(jnp.float32), norms[row : row + 1, :], total
    )
    if len(ins) > 2:
        pulled = pulled + ins[2][at, :]
    if len(outs) > 1:
        outs[0][at, :] = pulled
    sums = outs[-1]

    @pl.when(at.start == 0)
    def _():
        sums[...] = jnp.zeros_like(sums)

    sums[0:1, :] += dgain
    sums[1:2, :] += dshift
    return pulled


def gelu_tanh(values):
    return jax.nn.gelu(values, approximate=True)


def local(
    token_ids,
    targets,
    starts,
    sources,
    embedding,
    w_qkv,
    w_out,
    w_fc,
    w_proj,
    norm_params,
    rows_table,
    cols_table,
    rows_qkv,
    cols_qkv,
    rows_out,
    cols_out,
    rows_fc,
    cols_fc,
    rows_proj,
    cols_proj,
    second_norms,
):
    bf16 = jnp.bfloat16
    f32 = jnp.float32
    size_mp = lax.axis_size("mp")
    size_dp = lax.axis_size("dp")
    dp = lax.axis_index("dp")
    mp = lax.axis_index("mp")
    tokens = token_ids.shape[0]
    seqs = tokens // LEN
    chips = size_mp // 2
    near = chips // seqs
    sharers = size_mp // seqs
    rows = tokens // size_mp
    vocab, part_width = embedding.shape
    width = part_width * size_dp
    first_row = mp * vocab
    spots = tokens * size_dp
    chunks_full = max(1, min(8, rows // 32))
    chunks_near = max(1, min(4, rows // 32))
    chunks_turn = max(1, min(4, rows // 32))

    early = (vocab + -vocab % HEAD_BLOCK) * 3 // (10 * HEAD_BLOCK) * HEAD_BLOCK
    early_table = lax.all_gather(embedding[:early].astype(bf16), "dp", axis=1, tiled=True)

    both = jnp.stack([token_ids, sources]).reshape(-1, 128)
    both = small_gather("gather_ids", 0, both, "dp").reshape(size_dp, 2, tokens)
    all_ids = both[:, 0]
    all_sources = both[:, 1].reshape(-1)
    counts = jnp.sum(
        (all_sources[:, None] == jnp.arange(NSRC, dtype=jnp.int32)[None, :]).astype(f32), axis=0
    )

    w_qkv, w_out, w_fc, w_proj, all_ids = lax.optimization_barrier(
        (w_qkv, w_out, w_fc, w_proj, all_ids)
    )


    def own_and_twins(weight, axis):
        weight = weight.astype(bf16)
        found = [weight]
        for turn in range(1, seqs):
            shift = [(i, (i + turn * sharers) % size_mp) for i in range(size_mp)]
            found.append(lax.ppermute(weight, "mp", shift))
        return jnp.concatenate(found, axis=axis) if seqs > 1 else weight

    pair_qkv = own_and_twins(w_qkv, 1)
    pair_out = own_and_twins(w_out, 0)
    pair_fc = own_and_twins(w_fc, 1)
    pair_proj = own_and_twins(w_proj, 0)
    piece = rows // chunks_turn
    token = jnp.arange(tokens, dtype=jnp.int32)
    place = (
        token // piece * (size_dp * piece)
        + (jnp.arange(size_dp, dtype=jnp.int32) * piece)[:, None]
        + token % piece
    )
    local_ids = all_ids - first_row
    inside = (local_ids >= 0) & (local_ids < vocab)
    shift = spots.bit_length()
    idle = ((vocab - 1) << shift) + spots
    keys = jnp.where(inside, (local_ids << shift) + place, idle)
    keys = jnp.sort(keys.reshape(-1))
    owned = jnp.sum(inside.astype(jnp.int32)).reshape(1)
    found, low_table, table_sq = lookup(keys, owned, embedding, spots, shift, early)
    found, early_table = lax.optimization_barrier((found, early_table))
    inner_one, stream0, wide_qkv, wide_out, wide_fc, wide_proj = line_call(
        "lookup_sum",
        1,
        found,
        [norm_params],
        [jax.ShapeDtypeStruct((rows, width), bf16)],
        step_first,
        size_dp * rows,
        part_width,
        chunks_turn,
        chips,
        near,
        70,
        [
            ("gather", 0, pair_qkv),
            ("gather", 1, pair_out),
            ("gather", 0, pair_fc),
            ("gather", 1, pair_proj),
        ],
        "gather",
        8,
    )
    low_table, inner_one = lax.optimization_barrier((low_table, inner_one))
    wide_table = (early_table, lax.all_gather(low_table, "dp", axis=1, tiled=True))
    row_f32 = jax.ShapeDtypeStruct((rows, width), f32)
    pair_f32 = jax.ShapeDtypeStruct((8, width), f32)
    my_starts = row_slice(starts, (mp // sharers) * LEN, LEN)[:, None]
    mixed = jnp.dot(inner_one, wide_qkv, preferred_element_type=f32).astype(bf16)
    attended = attend(mixed, my_starts)
    partial = jnp.dot(attended, wide_out, preferred_element_type=f32).astype(bf16)
    inner_two, stream1 = line_call(
        "attn_sum",
        3,
        partial,
        [stream0, norm_params],
        [row_f32],
        functools.partial(step_forward, 2),
        rows,
        width,
        chunks_near,
        near,
        near,
        32,
    )
    before = jnp.dot(inner_two, wide_fc, preferred_element_type=f32)
    hidden = gelu_tanh(before).astype(bf16)
    partial = jnp.dot(hidden, wide_proj, preferred_element_type=f32).astype(bf16)
    final, stream2 = line_call(
        "mlp_sum",
        4,
        partial,
        [stream1, norm_params],
        [row_f32],
        functools.partial(step_forward, 4),
        rows,
        width,
        chunks_full,
        near,
        chips,
        58,
        chunk_major=True,
    )

    edge = jnp.clip(VREAL - first_row, 0, vocab).astype(jnp.int32).reshape(1)

    def by_chunk(values):
        return values.reshape(size_mp, chunks_full, -1).swapaxes(0, 1).reshape(tokens)

    sources = by_chunk(sources)
    wanted = by_chunk(targets) - first_row
    wanted = jnp.where((wanted >= 0) & (wanted < vocab), wanted, -1).reshape(1, tokens)
    block = HEAD_BLOCK
    exps, tops, sums, picks = head_stats(wide_table, final, wanted, edge, block)
    tops = tops[:, 0]
    top = jnp.max(tops, axis=0)
    total = jnp.sum(sums[:, 0] * jnp.exp(tops - top[None, :]), axis=0)
    pick = jnp.sum(picks[:, 0], axis=0)
    stats = jnp.concatenate([v.reshape(-1, 128) for v in (top, total, pick)])
    stats = small_gather("gather_stats", 5, stats, "mp").reshape(size_mp, 3, tokens)
    highest = jnp.max(stats[:, 0], axis=0)
    log_total = highest + jnp.log(
        jnp.sum(stats[:, 1] * jnp.exp(stats[:, 0] - highest[None, :]), axis=0)
    )
    token_loss = log_total - jnp.sum(stats[:, 2], axis=0)
    member = (sources[:, None] == jnp.arange(NSRC, dtype=jnp.int32)[None, :]).astype(f32)
    loss_part = jnp.sum(member * token_loss[:, None], axis=0)
    weight = jnp.sum(member / (NSRC * jnp.maximum(counts, 1.0))[None, :], axis=1)
    scale = jnp.exp(tops - log_total[None, :]) * weight[None, :]
    dlogits, table_grad = head_back(
        exps, final, scale[:, None, :], weight[None, :], wanted, block
    )
    head_grad = lax.psum_scatter(table_grad, "dp", scatter_dimension=1, tiled=True)

    dbranch2, dstream2, norm3 = line_call(
        "final_back",
        6,
        (dlogits, *wide_table),
        [stream2, norm_params],
        [row_f32, pair_f32],
        functools.partial(step_backward, 4),
        rows,
        width,
        chunks_full,
        chips,
        near,
        65,
        product=True,
    )
    grad_proj = jnp.einsum("tf,td->fd", hidden, dbranch2, preferred_element_type=f32).astype(bf16)
    dhidden = jnp.einsum("td,fd->tf", dbranch2, wide_proj, preferred_element_type=f32)
    unused, gelu_pull = jax.vjp(gelu_tanh, before)
    dbefore = gelu_pull(dhidden)[0].astype(bf16)
    partial = jnp.einsum("tf,df->td", dbefore, wide_fc, preferred_element_type=f32).astype(bf16)
    dbranch1, dstream1, norm2 = line_call(
        "mlp_back",
        7,
        partial,
        [stream1, norm_params, dstream2],
        [row_f32, pair_f32],
        functools.partial(step_backward, 2),
        rows,
        width,
        chunks_near,
        near,
        near,
        34,
    )
    grad_fc = jnp.einsum("td,tf->df", inner_two, dbefore, preferred_element_type=f32).astype(bf16)
    grad_out = jnp.einsum("tf,td->fd", attended, dbranch1, preferred_element_type=f32).astype(bf16)
    dattended = jnp.einsum("td,fd->tf", dbranch1, wide_out, preferred_element_type=f32)
    dmixed = attend_back(mixed, my_starts, dattended.astype(bf16))
    partial = jnp.einsum("tc,dc->td", dmixed, wide_qkv, preferred_element_type=f32).astype(bf16)
    grad_qkv = jnp.einsum("td,tc->dc", inner_one, dmixed, preferred_element_type=f32).astype(bf16)
    drows, norm1, grad_proj, grad_out, grad_fc, grad_qkv, twins_wide, twins_tall = line_call(
        "attn_back",
        8,
        partial,
        [stream0, norm_params, dstream1],
        [pair_f32],
        functools.partial(step_backward, 0),
        rows,
        width,
        chunks_turn,
        near,
        chips,
        70,
        [
            ("scatter", 1, grad_proj),
            ("scatter", 1, grad_out),
            ("scatter", 0, grad_fc),
            ("scatter", 0, grad_qkv),
        ],
        "spread",
        9,
        seqs=seqs,
    )

    def from_twins(values, axis, sizes):
        starts = [(seqs - 1) * sum(sizes[:n]) for n in range(len(sizes))]
        found = []
        for turn in range(1, seqs):
            pieces = [
                lax.slice_in_dim(values, at + (turn - 1) * size, at + turn * size, axis=axis)
                for at, size in zip(starts, sizes)
            ]
            back = [(i, (i - turn * sharers) % size_mp) for i in range(size_mp)]
            found.append(lax.ppermute(jnp.concatenate(pieces, axis=axis), "mp", back))
        return found

    tall = [grad_proj.shape[0], grad_out.shape[0]]
    wide = [grad_fc.shape[1], grad_qkv.shape[1]]
    found_tall = from_twins(twins_tall, 0, tall)
    found_wide = from_twins(twins_wide, 1, wide)
    grad_table = scatter(keys, owned, head_grad, drows, vocab, shift)
    found_tall, found_wide, grad_table = lax.optimization_barrier(
        (found_tall, found_wide, grad_table)
    )
    for values in found_tall:
        grad_proj += values[: tall[0]].astype(f32)
        grad_out += values[tall[0] :].astype(f32)
    for values in found_wide:
        grad_fc += values[:, : wide[0]].astype(f32)
        grad_qkv += values[:, wide[0] :].astype(f32)

    weights = (embedding, w_qkv, w_out, w_fc, w_proj)
    grads = (grad_table, grad_qkv, grad_out, grad_fc, grad_proj)
    row_span = (size_mp, size_dp, size_mp, size_dp, size_mp)
    col_span = (size_dp, size_mp, size_dp, size_mp, size_dp)
    full = tuple(
        (g.shape[0] * r, g.shape[1] * c) for g, r, c in zip(grads, row_span, col_span)
    )
    squares = [gradient * gradient + EPS_ONE for gradient in grads]
    rows_new, cols_new, loss_sums, grad_norms, second_new, norms_new, rates = update_stats(
        10,
        [jnp.sum(square, axis=1) for square in squares],
        (rows_table, rows_qkv, rows_out, rows_fc, rows_proj),
        [jnp.sum(square, axis=0) for square in squares],
        (cols_table, cols_qkv, cols_out, cols_fc, cols_proj),
        [table_sq] + [jnp.sum(value * value, axis=0) for value in weights[1:]],
        loss_part,
        (norm1, norm2, norm3),
        norm_params,
        second_norms,
        full,
    )
    steps = [
        grads[n] * lax.rsqrt(rows_new[n][:, None] * cols_new[n][None, :] / rates[n, 0])
        for n in range(5)
    ]
    factors = clip_rates(
        11, [jnp.sum(step * step, axis=0) for step in steps], rates, [r * c for r, c in full]
    )
    updated = [weights[n] - factors[n, 0] * steps[n] for n in range(5)]
    return (
        loss_sums,
        counts,
        grad_table,
        rows_new[0],
        cols_new[0],
        updated[0],
        grad_qkv,
        rows_new[1],
        cols_new[1],
        updated[1],
        grad_out,
        rows_new[2],
        cols_new[2],
        updated[2],
        grad_fc,
        rows_new[3],
        cols_new[3],
        updated[3],
        grad_proj,
        rows_new[4],
        cols_new[4],
        updated[4],
        grad_norms,
        second_new,
        norms_new,
    )


def solution(mesh):
    placed = (
        P("dp"),
        P("dp"),
        P("dp"),
        P("dp"),
        P("mp", "dp"),
        P("dp", "mp"),
        P("mp", "dp"),
        P("dp", "mp"),
        P("mp", "dp"),
        P(),
        P("mp"),
        P("dp"),
        P("dp"),
        P("mp"),
        P("mp"),
        P("dp"),
        P("dp"),
        P("mp"),
        P("mp"),
        P("dp"),
        P(),
    )
    return jax.shard_map(
        local,
        mesh=mesh,
        in_specs=placed,
        out_specs=(
            P(),
            P(),
            P("mp", "dp"),
            P("mp"),
            P("dp"),
            P("mp", "dp"),
            P("dp", "mp"),
            P("dp"),
            P("mp"),
            P("dp", "mp"),
            P("mp", "dp"),
            P("mp"),
            P("dp"),
            P("mp", "dp"),
            P("dp", "mp"),
            P("dp"),
            P("mp"),
            P("dp", "mp"),
            P("mp", "dp"),
            P("mp"),
            P("dp"),
            P("mp", "dp"),
            P(),
            P(),
            P(),
        ),
        check_vma=False,
    )
```

```python
import functools
import math

import jax
import jax.numpy as jnp
from jax import lax
from jax.experimental import pallas as pl
from jax.experimental.pallas import tpu as pltpu
from jax.sharding import PartitionSpec as P

HD = 64
VREAL = 50257
LEN = 1024
NSRC = 4
STEP = 10


EPS_NORM = 1e-05
EPS_ONE = 1e-30
CLIP = 1.0
RHO = 0.5
MASKED = -1e30
QUERIES = 256
HEAD_BLOCK = 640
MESH = pl.DeviceIdType.MESH
VMEM_CAP = 56 * 2**20


def cost_of(time):
    return pl.CostEstimate(
        flops=time * 1000000000, bytes_accessed=time * 3000000, transcendentals=0
    )


def row_slice(values, start, count):
    return lax.dynamic_slice_in_dim(values, start, count, 0)


def line_kernel(
    nr, ng, chunks, shapes, n_in, n_out, step, sides, turn, side_ticks, product, chunk_major, *refs
):
    (rows_r, width_r), (rows_g, width_g) = shapes
    if product:
        dl, *tables = refs[:3]
        first = 3
    else:
        part = refs[0] if nr else None
        first = 1 if nr else 0
    ins = refs[first : first + n_in]
    refs = refs[first + n_in :]
    side_ins, refs = refs[: len(sides)], refs[len(sides) :]
    if ng:
        whole, refs = refs[0], refs[1:]
    outs = refs[:n_out]
    refs = refs[n_out:]
    scatters = [index for index, (kind, unused) in enumerate(sides) if kind == "scatter"]
    side_outs, refs = refs[: len(sides)], refs[len(sides) :]
    twin_outs, scratch = (refs[:2], refs[2:]) if scatters else ([], refs)
    side_scratch, scratch = scratch[: 3 * len(sides)], scratch[3 * len(sides) :]
    if turn:
        cast, turn_send, turn_recv = scratch[-3:]
    if product:
        part, dl_buf, total_ref, dl_sem = scratch[-4:]
    size_dp = lax.axis_size("dp")
    dp = lax.axis_index("dp")
    mp = lax.axis_index("mp")
    z = mp // 2
    core = lax.rem(mp, 2)
    other = mp + 1 - 2 * core
    piece_r = rows_r // chunks
    piece_g = rows_g // chunks
    small = min(piece_r, piece_g)
    late = 1 if turn else 0
    ahead = 1 if product else 0
    most = max(nr, ng)
    zb = lax.rem(z, most)
    if nr:
        zr = lax.rem(z, nr)
        last_r = nr - 1
    if ng:
        zg = lax.rem(z, ng)
        last_g = ng - 1

    barrier = pltpu.get_barrier_semaphore()
    pl.semaphore_signal(barrier, inc=1, device_id=(dp, other), device_id_type=MESH)

    @pl.when(zb > 0)
    def _():
        pl.semaphore_signal(barrier, inc=1, device_id=(dp, mp - 2), device_id_type=MESH)

    @pl.when(zb < most - 1)
    def _():
        pl.semaphore_signal(barrier, inc=1, device_id=(dp, mp + 2), device_id_type=MESH)

    if sides or turn:
        for hop in range(1, size_dp):
            pl.semaphore_signal(
                barrier,
                inc=1,
                device_id=(lax.rem(dp + hop, size_dp), mp),
                device_id_type=MESH,
            )
    greeted = (size_dp if sides or turn else 1) + (zb > 0).astype(jnp.int32) + (zb < most - 1).astype(jnp.int32)
    pl.semaphore_wait(barrier, greeted)

    def share(axis, length, which):
        at = pl.ds(pl.multiple_of(which * length, length), length)
        return (at, slice(None)) if axis == 0 else (slice(None), at)

    def to_peer(src, dst, send, recv, peer):
        return pltpu.make_async_remote_copy(
            src_ref=src,
            dst_ref=dst,
            send_sem=send,
            recv_sem=recv,
            device_id=(peer, mp),
            device_id_type=MESH,
        )

    relay = size_dp == 4
    beside_x = dp + 1 - 2 * lax.rem(dp, 2)
    beside_y = lax.rem(dp + 2, 4)
    across = 3 - dp

    def half_share(axis, length, which, height, part):
        if axis == 0:
            return (pl.ds(pl.multiple_of(which * length + part * height, height), height), slice(None))
        at = pl.ds(pl.multiple_of(which * length, length), length)
        return (pl.ds(part * height, height), at)

    first_copies, more_copies, relays = [], [], []
    for index, (kind, axis) in enumerate(sides):
        src, dst = side_ins[index], side_outs[index]
        send, recv, slots = side_scratch[3 * index : 3 * index + 3]
        if kind == "gather":
            length, height = src.shape[axis], src.shape[0] // 2
        else:
            length = src.shape[axis] // size_dp
            height = (length if axis == 0 else src.shape[0]) // 2
        if not relay:
            for hop in range(1, size_dp):
                peer = lax.rem(dp + hop, size_dp)
                if kind == "gather":
                    source, target = src, dst.at[share(axis, length, dp)]
                else:
                    source, target = src.at[share(axis, length, peer)], slots.at[hop]
                more_copies.append(to_peer(source, target, send.at[hop], recv.at[hop], peer))
            continue
        for side, near_one, far_one in ((0, beside_x, beside_y), (1, beside_y, beside_x)):
            sems = [(send.at[3 * side + n], recv.at[3 * side + n]) for n in range(3)]
            if kind == "gather":
                mine = src.at[pl.ds(side * height, height)]
                here = dst.at[half_share(axis, length, dp, height, side)]
                passed = dst.at[half_share(axis, length, near_one, height, side)]
                arrives = to_peer(mine, here, *sems[0], near_one)
                first_copies.append(arrives)
                more_copies.append(to_peer(mine, here, *sems[1], far_one))
                relays.append((arrives, None, to_peer(passed, passed, *sems[2], far_one)))
            else:
                arrives = to_peer(
                    src.at[half_share(axis, length, across, height, side)],
                    slots.at[4 * side],
                    *sems[0],
                    near_one,
                )
                first_copies.append(arrives)
                more_copies.append(
                    to_peer(
                        src.at[half_share(axis, length, near_one, height, side)],
                        slots.at[4 * side + 1],
                        *sems[1],
                        near_one,
                    )
                )
                summed = to_peer(
                    slots.at[4 * side + 2], slots.at[4 * side + 3], *sems[2], far_one
                )
                own = src.at[half_share(axis, length, far_one, height, side)]
                relays.append((arrives, (own, slots, 4 * side, height), summed))

    def pass_on(arrives, adding, copy):
        arrives.wait_recv()
        if adding is not None:
            own, slots, at, height = adding
            both = own[...].astype(jnp.float32) + slots[at].astype(jnp.float32)
            slots[at + 2] = both.astype(slots.dtype)
        copy.start()

    jobs = [copy.start for copy in first_copies + more_copies]
    jobs += [functools.partial(pass_on, *one) for one in relays]

    def side_jobs(now):
        for spot in range(side_ticks if jobs else 0):
            chosen = jobs[len(jobs) * spot // side_ticks : len(jobs) * (spot + 1) // side_ticks]

            @pl.when(now == spot)
            def _():
                for job in chosen:
                    job()

    if nr:
        half, from_left, from_right, going = scratch[:4]
        half_send, half_recv, rs_send, left_recv, right_recv = scratch[4:9]
        scratch = scratch[9:]
    if ng:
        core_send, core_recv, to_right, to_left, ag_left, ag_right = scratch[:6]

    def part_rows(block, k):
        return pl.ds(pl.multiple_of(block * rows_r + k * piece_r, piece_r), piece_r)

    def whole_rows(block, k):
        if chunk_major:
            start = k * (2 * ng * piece_g) + block * piece_g
            return pl.ds(pl.multiple_of(start, piece_g), piece_g)
        return pl.ds(pl.multiple_of(block * rows_g + k * piece_g, piece_g), piece_g)

    def remote(src, dst, send, recv, target):
        return pltpu.make_async_remote_copy(
            src_ref=src,
            dst_ref=dst,
            send_sem=send,
            recv_sem=recv,
            device_id=(dp, target),
            device_id_type=MESH,
        )

    if nr:

        def half_copy(dest, k):
            return remote(
                part.at[part_rows(2 * dest + 1 - core, k)],
                half.at[dest, k],
                half_send.at[dest, k],
                half_recv.at[dest, k],
                other,
            )

        def send_halves(k, carry):
            for dest in range(nr):
                half_copy(dest, k).start()
            return carry

        if not product:
            lax.fori_loop(0, chunks, send_halves, 0)

        def right_copy(dest, k):
            return remote(
                going.at[dest, k],
                from_left.at[dest, k],
                rs_send.at[dest, k],
                left_recv.at[dest, k],
                mp + 2,
            )

        def left_copy(dest, k):
            return remote(
                going.at[dest, k],
                from_right.at[dest, k],
                rs_send.at[dest, k],
                right_recv.at[dest, k],
                mp - 2,
            )

        def chip_sum(dest, k):
            half_copy(dest, k).wait_recv()
            mine = part[part_rows(2 * dest + core, k), :].astype(jnp.float32)
            return mine + half[dest, k].astype(jnp.float32)

        def pass_right(dest, k):
            total = chip_sum(dest, k)

            @pl.when(zr == 0)
            def _():
                going[dest, k] = total.astype(jnp.bfloat16)

            @pl.when(zr > 0)
            def _():
                right_copy(dest, k).wait_recv()
                both = total + from_left[dest, k].astype(jnp.float32)
                going[dest, k] = both.astype(jnp.bfloat16)

            right_copy(dest, k).start()

        def pass_left(dest, k):
            total = chip_sum(dest, k)

            @pl.when(zr == last_r)
            def _():
                going[dest, k] = total.astype(jnp.bfloat16)

            @pl.when(zr < last_r)
            def _():
                left_copy(dest, k).wait_recv()
                both = total + from_right[dest, k].astype(jnp.float32)
                going[dest, k] = both.astype(jnp.bfloat16)

            left_copy(dest, k).start()

    if ng:

        def gathered(block, k, send, recv, target):
            where = whole.at[whole_rows(2 * block + core, k)]
            return remote(where, where, send.at[block, k], recv.at[block, k], target)

        def core_copy(block, k):
            return gathered(block, k, core_send, core_recv, other)

        def ag_right_copy(block, k):
            return gathered(block, k, to_right, ag_left, mp + 2)

        def ag_left_copy(block, k):
            return gathered(block, k, to_left, ag_right, mp - 2)

    def own_rows(k):
        total = None
        if nr:
            total = chip_sum(zr, k)
            zero = jnp.zeros((piece_r, width_r), jnp.float32)

            @pl.when(zr > 0)
            def _():
                right_copy(zr, k).wait_recv()

            @pl.when(zr < last_r)
            def _():
                left_copy(zr, k).wait_recv()

            total += jnp.where(zr > 0, from_left[zr, k].astype(jnp.float32), zero)
            total += jnp.where(zr < last_r, from_right[zr, k].astype(jnp.float32), zero)
        if turn == "gather":
            cast[k] = total.astype(cast.dtype)
            for hop in range(1, size_dp):
                turn_copy(hop, k).start()
            mine = pl.ds(pl.multiple_of(dp * small, small), small)
            outs[0][own_place(k, dp)] = cast[k, mine, :]
            return
        at = pl.ds(pl.multiple_of(k * piece_r, piece_r), piece_r)
        ready = step(total, at, ins, outs)
        if turn == "spread":
            cast[k] = ready.astype(cast.dtype)
            for hop in range(1, size_dp):
                turn_copy(hop, k).start()
            whole[own_place(k, dp)] = cast[
                k, :, pl.ds(pl.multiple_of(dp * width_g, width_g), width_g)
            ]
        elif ng:
            whole[whole_rows(2 * zg + core, k), :] = ready.astype(whole.dtype)
            start_gather(k)

    def own_place(k, peer):
        if turn == "gather":
            return (
                pl.ds(pl.multiple_of(k * small, small), small),
                pl.ds(pl.multiple_of(peer * width_r, width_r), width_r),
            )
        start = (2 * zg + core) * rows_g + k * piece_g + peer * small
        return (pl.ds(pl.multiple_of(start, small), small), slice(None))

    def turn_copy(hop, k):
        peer = lax.rem(dp + hop, size_dp)
        if turn == "gather":
            src = cast.at[k, pl.ds(pl.multiple_of(peer * small, small), small)]
            dst = outs[0].at[own_place(k, dp)]
        else:
            src = cast.at[k, :, pl.ds(pl.multiple_of(peer * width_g, width_g), width_g)]
            dst = whole.at[own_place(k, dp)]
        return to_peer(src, dst, turn_send.at[hop, k], turn_recv.at[hop, k], peer)

    def turned_rows(k):
        for hop in range(1, size_dp):
            turn_copy(hop, k).wait_recv()
        if turn == "gather":
            at = pl.ds(pl.multiple_of(k * piece_g, piece_g), piece_g)
            ready = step(None, at, ins, outs)
            whole[whole_rows(2 * zg + core, k), :] = ready.astype(whole.dtype)
        start_gather(k)

    def start_gather(k):
        core_copy(zg, k).start()

        @pl.when(zg < last_g)
        def _():
            ag_right_copy(zg, k).start()

        @pl.when(zg > 0)
        def _():
            ag_left_copy(zg, k).start()

    def inside(k):
        return (k >= 0) & (k < chunks)

    def own_lag(chip):
        if not nr:
            return 0
        at = lax.rem(chip, nr)
        return jnp.maximum(at, last_r - at) + ahead

    def dl_copy(k):
        columns = dl_buf.shape[2]
        return pltpu.make_async_copy(
            dl.at[:, pl.ds(pl.multiple_of(k * columns, columns), columns)],
            dl_buf.at[lax.rem(k, 2)],
            dl_sem.at[lax.rem(k, 2)],
        )

    def make_part(k):
        dl_copy(k).wait()

        @pl.when(k + 1 < chunks)
        def _():
            dl_copy(k + 1).start()

        slot = lax.rem(k, 2)

        start = 0
        for piece in tables:
            found = lax.dot_general(
                dl_buf[slot, start : start + piece.shape[0], :],
                piece[...],
                (((0,), (0,)), ((), ())),
                preferred_element_type=jnp.float32,
            )
            if start:
                total_ref[...] += found
            else:
                total_ref[...] = found
            start += piece.shape[0]
        for block in range(2 * nr):
            part[part_rows(block, k), :] = total_ref[
                block * piece_r : block * piece_r + piece_r, :
            ].astype(jnp.bfloat16)
        send_halves(k, 0)

    if product:
        dl_copy(0).start()

    def tick(now, carry):
        side_jobs(now)
        if nr:
            k_right = now - zr - ahead
            k_left = now - (last_r - zr) - ahead
            for far in range(last_r):

                @pl.when(inside(k_right) & (last_r - far > zr))
                def _():
                    pass_right(last_r - far, k_right)

                @pl.when(inside(k_left) & (far < zr))
                def _():
                    pass_left(far, k_left)

        k_own = now - own_lag(z)

        @pl.when(inside(k_own))
        def _():
            own_rows(k_own)

        if turn:

            @pl.when(inside(k_own - 1))
            def _():
                turned_rows(k_own - 1)

        if ng:
            for block in range(ng):
                k = now - (own_lag(z - zg + block) + late + jnp.abs(zg - block))

                @pl.when(inside(k) & (block < zg))
                def _():
                    ag_right_copy(block, k).wait_recv()
                    core_copy(block, k).start()

                    @pl.when(zg < last_g)
                    def _():
                        ag_right_copy(block, k).start()

                @pl.when(inside(k) & (block > zg))
                def _():
                    ag_left_copy(block, k).wait_recv()
                    core_copy(block, k).start()

                    @pl.when(zg > 0)
                    def _():
                        ag_left_copy(block, k).start()

        if product:

            @pl.when(now < chunks)
            def _():
                make_part(now)

        return carry

    ticks = ahead + chunks + (nr - 1 if nr else 0) + (ng - 1 if ng else 0) + late
    lax.fori_loop(0, ticks, tick, 0)

    def finish(k, carry):
        if turn:
            for hop in range(1, size_dp):
                turn_copy(hop, k).wait_send()
        if nr:
            for block in range(nr):
                half_copy(block, k).wait_send()

                @pl.when(block != zr)
                def _():
                    right_copy(block, k).wait_send()

        if ng:
            for block in range(ng):
                core_copy(block, k).wait()

                @pl.when((zg < last_g) & (block <= zg))
                def _():
                    ag_right_copy(block, k).wait_send()

                @pl.when((zg > 0) & (block >= zg))
                def _():
                    ag_left_copy(block, k).wait_send()

        return carry

    lax.fori_loop(0, chunks, finish, 0)
    for index, (kind, axis) in enumerate(sides):
        if kind == "gather":
            length = side_ins[index].shape[axis]
            side_outs[index][share(axis, length, dp)] = side_ins[index][...]
    for copy in first_copies:
        copy.wait_send()
    for copy in more_copies:
        copy.wait()
    for unused, unused, copy in relays:
        copy.wait()
    placed = [0, 0]
    for index in scatters:
        axis = sides[index][1]
        src, dst = side_ins[index], side_outs[index]
        slots = side_scratch[3 * index + 2]
        length = src.shape[axis] // size_dp
        height = (length if axis == 0 else src.shape[0]) // 2
        if relay:
            total = []
            for side in range(2):
                one = src[half_share(axis, length, dp, height, side)].astype(jnp.float32)
                one += slots[4 * side + 1].astype(jnp.float32)
                one += slots[4 * side + 3].astype(jnp.float32)
                total.append(one)
            total = jnp.concatenate(total)
        else:
            total = src[share(axis, length, dp)].astype(jnp.float32)
            for hop in range(1, size_dp):
                total += slots[hop].astype(jnp.float32)
        twins = twin_outs[axis]
        at = placed[axis]
        if axis == 0:
            own = dst.shape[1]
            dst[...] = total[:, :own]
            more = total.shape[1] - own
            twins[:, at : at + more] = total[:, own:].astype(twins.dtype)
        else:
            own = dst.shape[0]
            dst[...] = total[:own, :]
            more = total.shape[0] - own
            twins[at : at + more, :] = total[own:, :].astype(twins.dtype)
        placed[axis] += more


def line_call(
    name,
    cid,
    partial,
    ins,
    out_types,
    step,
    rows,
    width,
    chunks,
    nr,
    ng,
    time,
    sides=(),
    turn=None,
    side_ticks=0,
    product=False,
    chunk_major=False,
    seqs=1,
):
    piece = rows // chunks
    size_dp = lax.axis_size("dp")
    reduced = gathered = (rows, width)
    if turn == "gather":
        gathered = (rows // size_dp, width * size_dp)
    elif turn == "spread":
        gathered = (rows * size_dp, width // size_dp)
    out_shape = []
    if ng:
        out_shape.append(
            jax.ShapeDtypeStruct((2 * ng * gathered[0], gathered[1]), jnp.bfloat16)
        )
    out_shape += out_types
    dma = pltpu.SemaphoreType.DMA
    scratch = []
    twin_shapes = [[0, 0], [0, 0]]
    for kind, axis, values in sides:
        shape = list(values.shape)
        scratch += [dma((max(size_dp, 6),)), dma((max(size_dp, 6),))]
        if kind == "gather":
            shape[axis] *= size_dp
            out_shape.append(jax.ShapeDtypeStruct(tuple(shape), values.dtype))
            scratch.append(pltpu.VMEM((16, 128), values.dtype))
        else:
            shape[axis] //= size_dp
            own = list(shape)
            own[1 - axis] //= seqs
            out_shape.append(jax.ShapeDtypeStruct(tuple(own), jnp.float32))
            twin_shapes[axis][axis] = shape[axis]
            twin_shapes[axis][1 - axis] += shape[1 - axis] - own[1 - axis]
            slots = (8, shape[0] // 2, shape[1]) if size_dp == 4 else (size_dp, *shape)
            scratch.append(pltpu.VMEM(slots, values.dtype))
    if any(side[0] == "scatter" for side in sides):
        out_shape += [jax.ShapeDtypeStruct(tuple(shape), jnp.bfloat16) for shape in twin_shapes]
    if nr:
        scratch += [pltpu.VMEM((nr, chunks, piece, width), jnp.bfloat16)] * 4
        scratch += [dma((nr, chunks))] * 5
    if ng:
        scratch += [dma((ng, chunks))] * 6
    if turn:
        scratch.append(pltpu.VMEM((chunks, piece, width), jnp.bfloat16))
        scratch += [dma((size_dp, chunks))] * 2
    if product:
        dl = partial[0]
        columns = dl.shape[1] // chunks
        scratch += [
            pltpu.VMEM((2 * nr * rows, width), jnp.bfloat16),
            pltpu.VMEM((2, dl.shape[0], columns), jnp.bfloat16),
            pltpu.VMEM((columns, width), jnp.float32),
            dma((2,)),
        ]
        partial = list(partial)
    else:
        partial = [partial] if nr else []
    args = partial + list(ins) + [side[2] for side in sides]
    vmem = pl.BlockSpec(memory_space=pltpu.VMEM)
    call = pl.pallas_call(
        functools.partial(
            line_kernel,
            nr,
            ng,
            chunks,
            (reduced, gathered),
            len(ins),
            len(out_types),
            step,
            tuple(side[:2] for side in sides),
            turn,
            side_ticks,
            product,
            chunk_major,
        ),
        out_shape=out_shape,
        in_specs=[pl.BlockSpec(memory_space=pl.ANY) if product and n == 0 else vmem for n in range(len(args))],
        out_specs=[vmem] * len(out_shape),
        scratch_shapes=scratch,
        compiler_params=pltpu.CompilerParams(
            collective_id=cid, has_side_effects=True, vmem_limit_bytes=VMEM_CAP
        ),
        cost_estimate=cost_of(time),
        name=name,
    )
    return list(call(*args))


def head_stats_kernel(block, tile, early, early_ref, late_ref, final_ref, wanted_ref, edge_ref, exp_ref, top_ref, sum_ref, pick_ref):
    j = pl.program_id(0)
    tokens = final_ref.shape[0]
    place = j * block + lax.broadcasted_iota(jnp.int32, (block, 1), 0)
    valid = place < edge_ref[0]
    table = jnp.where(j < early, early_ref[...], late_ref[...])

    def one(i, carry):
        at = pl.ds(i * tile, tile)
        logits = lax.dot_general(
            table,
            final_ref[at, :],
            (((1,), (1,)), ((), ())),
            preferred_element_type=jnp.float32,
        )
        logits = jnp.where(valid, logits, MASKED)
        top = jnp.max(logits, axis=0, keepdims=True)
        weights = jnp.exp(logits - top)
        exp_ref[:, at] = weights.astype(jnp.bfloat16)
        top_ref[0, :, at] = top
        sum_ref[0, :, at] = jnp.sum(weights, axis=0, keepdims=True)
        pick_ref[0, :, at] = jnp.sum(
            jnp.where(place == wanted_ref[:, at], logits, 0.0), axis=0, keepdims=True
        )
        return carry

    for i in range(tokens // tile):
        one(i, 0)


def head_stats(tables, final, wanted, edge, block, tile=512):
    early = tables[0].shape[0] // block
    rows = sum(table.shape[0] for table in tables)
    width = tables[0].shape[1]
    tokens = final.shape[0]
    steps = rows // block
    row = jax.ShapeDtypeStruct((steps, 1, tokens), jnp.float32)
    row_spec = pl.BlockSpec((1, 1, tokens), lambda j: (j, 0, 0))
    return pl.pallas_call(
        functools.partial(head_stats_kernel, block, tile, early),
        grid=(steps,),
        out_shape=[jax.ShapeDtypeStruct((steps * block, tokens), jnp.bfloat16), row, row, row],
        in_specs=[
            pl.BlockSpec((block, width), lambda j: (jnp.minimum(j, early - 1), 0)),
            pl.BlockSpec((block, width), lambda j: (jnp.maximum(j - early, 0), 0)),
            pl.BlockSpec((tokens, width), lambda j: (0, 0)),
            pl.BlockSpec((1, tokens), lambda j: (0, 0)),
            pl.BlockSpec(memory_space=pltpu.SMEM),
        ],
        out_specs=[pl.BlockSpec((block, tokens), lambda j: (j, 0)), row_spec, row_spec, row_spec],
        compiler_params=pltpu.CompilerParams(vmem_limit_bytes=56 * 2**20),
        cost_estimate=pl.CostEstimate(
            flops=2 * rows * width * tokens,
            bytes_accessed=2 * rows * (width + tokens),
            transcendentals=rows * tokens,
        ),
        name="head_stats",
    )(*tables, final, wanted, edge)


def head_back_kernel(block, tile, exp_ref, final_ref, scale_ref, weight_ref, wanted_ref, dl_ref, grad_ref):
    j = pl.program_id(0)
    tokens = final_ref.shape[0]
    place = j * block + lax.broadcasted_iota(jnp.int32, (block, 1), 0)
    for start in range(0, tokens, tile):
        at = pl.ds(start, tile)
        dl = exp_ref[:, at].astype(jnp.float32) * scale_ref[0, :, at]
        dl = dl - jnp.where(place == wanted_ref[:, at], weight_ref[:, at], 0.0)
        dl_ref[:, at] = dl.astype(jnp.bfloat16)
    strip = block // max(1, block // 256)
    for start in range(0, block, strip):
        at = pl.ds(start, strip)
        grad_ref[at, :] = jnp.dot(
            dl_ref[at, :], final_ref[...], preferred_element_type=jnp.float32
        ).astype(jnp.bfloat16)


def head_back(exps, final, scale, weight, wanted, block, tile=256):
    rows, tokens = exps.shape
    width = final.shape[1]
    return pl.pallas_call(
        functools.partial(head_back_kernel, block, tile),
        grid=(rows // block,),
        out_shape=[
            jax.ShapeDtypeStruct((rows, tokens), jnp.bfloat16),
            jax.ShapeDtypeStruct((rows, width), jnp.bfloat16),
        ],
        in_specs=[
            pl.BlockSpec((block, tokens), lambda j: (j, 0)),
            pl.BlockSpec((tokens, width), lambda j: (0, 0)),
            pl.BlockSpec((1, 1, tokens), lambda j: (j, 0, 0)),
            pl.BlockSpec((1, tokens), lambda j: (0, 0)),
            pl.BlockSpec((1, tokens), lambda j: (0, 0)),
        ],
        out_specs=[
            pl.BlockSpec((block, tokens), lambda j: (j, 0)),
            pl.BlockSpec((block, width), lambda j: (j, 0)),
        ],
        compiler_params=pltpu.CompilerParams(vmem_limit_bytes=56 * 2**20),
        cost_estimate=pl.CostEstimate(
            flops=2 * rows * width * tokens,
            bytes_accessed=2 * rows * (width + 2 * tokens),
            transcendentals=0,
        ),
        name="head_back",
    )(exps, final, scale, weight, wanted)


def head_weights(mixed_ref, starts_ref, base, at, seen):
    query = mixed_ref[at : at + QUERIES, base : base + HD]
    keys = mixed_ref[0:seen, base + HD : base + 2 * HD]
    values = mixed_ref[0:seen, base + 2 * HD : base + 3 * HD]
    scores = lax.dot_general(
        query, keys, (((1,), (1,)), ((), ())), preferred_element_type=jnp.float32
    )
    row = at + lax.broadcasted_iota(jnp.int32, (QUERIES, seen), 0)
    column = lax.broadcasted_iota(jnp.int32, (QUERIES, seen), 1)
    allowed = (column <= row) & (column >= starts_ref[at : at + QUERIES, :])
    scores = jnp.where(allowed, scores * HD ** (-0.5), MASKED)
    weights = jnp.exp(scores - jnp.max(scores, axis=1, keepdims=True))
    probs = weights / jnp.sum(weights, axis=1, keepdims=True)
    return query, keys, values, probs


def attend_kernel(mixed_ref, starts_ref, out_ref):
    length = mixed_ref.shape[0]
    for at in range(0, length, QUERIES):
        found = []
        for head in range(2):
            unused, unused, values, probs = head_weights(
                mixed_ref, starts_ref, head * 3 * HD, at, at + QUERIES
            )
            found.append(
                jnp.dot(probs.astype(jnp.bfloat16), values, preferred_element_type=jnp.float32)
            )
        out_ref[at : at + QUERIES, :] = jnp.concatenate(found, axis=1).astype(jnp.bfloat16)


def attend(mixed, starts):
    length, columns = mixed.shape
    pairs = columns // (6 * HD)
    return pl.pallas_call(
        attend_kernel,
        grid=(pairs,),
        out_shape=jax.ShapeDtypeStruct((length, pairs * 2 * HD), jnp.bfloat16),
        in_specs=[
            pl.BlockSpec((length, 6 * HD), lambda j: (0, j)),
            pl.BlockSpec((length, 1), lambda j: (0, 0)),
        ],
        out_specs=pl.BlockSpec((length, 2 * HD), lambda j: (0, j)),
        compiler_params=pltpu.CompilerParams(vmem_limit_bytes=40 * 2**20),
        cost_estimate=pl.CostEstimate(
            flops=8 * pairs * length * length * HD,
            bytes_accessed=2 * length * columns,
            transcendentals=pairs * length * length,
        ),
        name="attend",
    )(mixed, starts)


def attend_back_kernel(mixed_ref, starts_ref, upstream_ref, out_ref, sums_ref):
    length = mixed_ref.shape[0]
    sums_ref[...] = jnp.zeros_like(sums_ref)
    rows = (((0,), (0,)), ((), ()))
    for at in range(0, length, QUERIES):
        seen = at + QUERIES
        for head in range(2):
            base = head * 3 * HD
            query, keys, values, probs = head_weights(mixed_ref, starts_ref, base, at, seen)
            upstream = upstream_ref[at:seen, head * HD : head * HD + HD]
            dprobs = lax.dot_general(
                upstream, values, (((1,), (1,)), ((), ())), preferred_element_type=jnp.float32
            )
            inner = jnp.sum(probs * dprobs, axis=1, keepdims=True)
            dscores = (probs * (dprobs - inner)).astype(jnp.bfloat16)
            dquery = jnp.dot(dscores, keys, preferred_element_type=jnp.float32)
            dkeys = lax.dot_general(dscores, query, rows, preferred_element_type=jnp.float32)
            dvalues = lax.dot_general(
                probs.astype(jnp.bfloat16), upstream, rows, preferred_element_type=jnp.float32
            )
            sums_ref[at:seen, base : base + HD] = dquery * HD ** (-0.5)
            sums_ref[0:seen, base + HD : base + 2 * HD] += dkeys * HD ** (-0.5)
            sums_ref[0:seen, base + 2 * HD : base + 3 * HD] += dvalues
    out_ref[...] = sums_ref[...].astype(jnp.bfloat16)


def attend_back(mixed, starts, upstream):
    length, columns = mixed.shape
    pairs = columns // (6 * HD)
    return pl.pallas_call(
        attend_back_kernel,
        grid=(pairs,),
        out_shape=jax.ShapeDtypeStruct((length, columns), jnp.bfloat16),
        in_specs=[
            pl.BlockSpec((length, 6 * HD), lambda j: (0, j)),
            pl.BlockSpec((length, 1), lambda j: (0, 0)),
            pl.BlockSpec((length, 2 * HD), lambda j: (0, j)),
        ],
        out_specs=pl.BlockSpec((length, 6 * HD), lambda j: (0, j)),
        scratch_shapes=[pltpu.VMEM((length, 6 * HD), jnp.float32)],
        compiler_params=pltpu.CompilerParams(vmem_limit_bytes=40 * 2**20),
        cost_estimate=pl.CostEstimate(
            flops=20 * pairs * length * length * HD,
            bytes_accessed=4 * length * columns,
            transcendentals=pairs * length * length,
        ),
        name="attend_back",
    )(mixed, starts, upstream)


def small_gather_kernel(axis, count, src_ref, out_ref, send, recv):
    dp = lax.axis_index("dp")
    mp = lax.axis_index("mp")
    me = dp if axis == "dp" else mp

    def device(peer):
        return (peer, mp) if axis == "dp" else (dp, peer)

    barrier = pltpu.get_barrier_semaphore()
    for hop in range(1, count):
        pl.semaphore_signal(
            barrier, inc=1, device_id=device(lax.rem(me + hop, count)), device_id_type=MESH
        )
    pl.semaphore_wait(barrier, count - 1)
    copies = []
    for hop in range(1, count):
        peer = lax.rem(me + hop, count)
        copy = pltpu.make_async_remote_copy(
            src_ref=src_ref,
            dst_ref=out_ref.at[me],
            send_sem=send.at[hop],
            recv_sem=recv.at[hop],
            device_id=device(peer),
            device_id_type=MESH,
        )
        copy.start()
        copies.append(copy)
    out_ref[me] = src_ref[...]
    for copy in copies:
        copy.wait()


def small_gather(name, cid, values, axis):
    count = lax.axis_size(axis)
    vmem = pl.BlockSpec(memory_space=pltpu.VMEM)
    return pl.pallas_call(
        functools.partial(small_gather_kernel, axis, count),
        out_shape=jax.ShapeDtypeStruct((count,) + values.shape, values.dtype),
        in_specs=[vmem],
        out_specs=vmem,
        scratch_shapes=[pltpu.SemaphoreType.DMA((count,)), pltpu.SemaphoreType.DMA((count,))],
        compiler_params=pltpu.CompilerParams(collective_id=cid, has_side_effects=True),
        cost_estimate=cost_of(6),
        name=name,
    )(values)


def exchange(axis, me, here, source, slots, send, recv, first):
    count = slots.shape[0]
    copies = []
    for hop in range(1, count):
        peer = lax.rem(me + hop, count)
        copy = pltpu.make_async_remote_copy(
            src_ref=source,
            dst_ref=slots.at[me],
            send_sem=send.at[first + hop],
            recv_sem=recv.at[first + hop],
            device_id=(peer, here) if axis == "dp" else (here, peer),
            device_id_type=MESH,
        )
        copy.start()
        copies.append(copy)
    slots[me] = source[...]
    for copy in copies:
        copy.wait()
    total = slots[0]
    for index in range(1, count):
        total = total + slots[index]
    return total


def greet_all(dp, mp, size_dp, size_mp):
    barrier = pltpu.get_barrier_semaphore()
    for hop in range(1, size_dp):
        pl.semaphore_signal(
            barrier, inc=1, device_id=(lax.rem(dp + hop, size_dp), mp), device_id_type=MESH
        )
    for hop in range(1, size_mp):
        pl.semaphore_signal(
            barrier, inc=1, device_id=(dp, lax.rem(mp + hop, size_mp)), device_id_type=MESH
        )
    pl.semaphore_wait(barrier, size_dp + size_mp - 2)


def lane_rows(values):
    values = values.reshape(-1)
    return jnp.pad(values, (0, -values.size % 128)).reshape(-1, 128)


def fold(values):
    return jnp.sum(values, axis=0, keepdims=True)


def stats_kernel(full, size_dp, size_mp, *refs):
    row_part, row_old, col_part, col_old, weight_sq = (refs[5 * n : 5 * n + 5] for n in range(5))
    loss_part, norm_one, norm_two, norm_three, norms, second_old = refs[25:31]
    refs = refs[31:]
    row_out, col_out = refs[0:5], refs[5:10]
    loss_out, grads_out, second_out, norms_out, rate_out = refs[10:15]
    send_dp, slots_dp, send_mp, slots_mp, parts, part_slots, whole, send, recv = refs[15:]
    dp = lax.axis_index("dp")
    mp = lax.axis_index("mp")
    greet_all(dp, mp, size_dp, size_mp)
    beta = 1.0 - STEP ** (-0.8)
    width = norms.shape[1]

    at = 0
    marks = []

    def put(values):
        nonlocal at
        rows = values.shape[0]
        send_dp[at : at + rows, :] = values
        marks.append((at, rows))
        at += rows

    norm_rows = width // 128
    for ref in (norm_one, norm_two, norm_three):
        for which in range(2):
            for piece in range(norm_rows):
                put(ref[which : which + 1, piece * 128 : piece * 128 + 128])
    marks.clear()
    count_norm = at
    for index in (0, 2, 4):
        put(row_part[index][...])
    for index in (1, 3):
        put(col_part[index][...])
    put(loss_part[...])
    for index in (1, 3):
        put(fold(row_old[index][...]))
    for index in range(5):
        put(fold(weight_sq[index][...]))
    if at < send_dp.shape[0]:
        send_dp[at:, :] = jnp.zeros((send_dp.shape[0] - at, 128), jnp.float32)
    over_dp = exchange("dp", dp, mp, send_dp, slots_dp, send, recv, 0)
    taken = [over_dp[start : start + rows] for start, rows in marks]
    loss_out[...] = taken[5]
    row_full = {0: taken[0], 2: taken[1], 4: taken[2]}
    col_full = {1: taken[3], 3: taken[4]}
    old_total = {1: taken[6], 3: taken[7]}
    weight_rows = taken[8:13]

    at = 0
    marks = []

    def put_mp(values):
        nonlocal at
        rows = values.shape[0]
        send_mp[at : at + rows, :] = values
        marks.append((at, rows))
        at += rows

    for index in (0, 2, 4):
        put_mp(col_part[index][...])
    for index in (1, 3):
        put_mp(row_part[index][...])
    for index in range(5):
        put_mp(fold(row_full[index] if index in row_full else col_full[index]))
    for index in (0, 2, 4):
        put_mp(fold(row_old[index][...]))
    for index in range(5):
        put_mp(weight_rows[index])
    if at < send_mp.shape[0]:
        send_mp[at:, :] = jnp.zeros((send_mp.shape[0] - at, 128), jnp.float32)
    each = count_norm // size_mp
    for index in range(size_mp):
        parts[index] = over_dp[index * each : index * each + each]
    first = size_dp + size_mp
    copies = []
    for hop in range(1, size_mp):
        peer = lax.rem(mp + hop, size_mp)
        copy = pltpu.make_async_remote_copy(
            src_ref=parts.at[peer],
            dst_ref=part_slots.at[mp],
            send_sem=send.at[first + hop],
            recv_sem=recv.at[first + hop],
            device_id=(dp, peer),
            device_id_type=MESH,
        )
        copy.start()
        copies.append(copy)
    part_slots[mp] = parts[mp]
    over_mp = exchange("mp", mp, dp, send_mp, slots_mp, send, recv, size_dp)
    for copy in copies:
        copy.wait()
    summed = part_slots[0]
    for index in range(1, size_mp):
        summed = summed + part_slots[index]
    whole[mp] = summed
    first += size_mp
    copies = []
    for hop in range(1, size_mp):
        peer = lax.rem(mp + hop, size_mp)
        copy = pltpu.make_async_remote_copy(
            src_ref=whole.at[mp],
            dst_ref=whole.at[mp],
            send_sem=send.at[first + hop],
            recv_sem=recv.at[first + hop],
            device_id=(dp, peer),
            device_id_type=MESH,
        )
        copies.append(copy)
    for copy in copies:
        copy.start()
    taken = [over_mp[start : start + rows] for start, rows in marks]
    for slot, index in enumerate((0, 2, 4)):
        col_full[index] = taken[slot]
        old_total[index] = taken[10 + slot]
    for slot, index in enumerate((1, 3)):
        row_full[index] = taken[3 + slot]
    square_total = taken[5:10]
    weight_total = taken[13:18]
    for index in range(5):
        full_rows, full_cols = full[index]
        row_new = beta * row_old[index][...] + (1.0 - beta) * row_full[index] / full_cols
        col_new = beta * col_old[index][...] + (1.0 - beta) * col_full[index] / full_rows
        row_out[index][...] = row_new
        col_out[index][...] = col_new
        mean = (
            beta * jnp.sum(old_total[index], axis=1, keepdims=True)
            + (1.0 - beta) * jnp.sum(square_total[index], axis=1, keepdims=True) / full_cols
        ) / full_rows
        rate = RHO * jnp.sqrt(
            jnp.sum(weight_total[index], axis=1, keepdims=True) / (full_rows * full_cols)
        )
        rate_out[index : index + 1, :] = jnp.broadcast_to(mean, (1, 128))
        rate_out[8 + index : 9 + index, :] = jnp.broadcast_to(rate, (1, 128))
    for copy in copies:
        copy.wait()
    for row in range(6):
        for piece in range(norm_rows):
            place = row * norm_rows + piece
            grads_out[row : row + 1, piece * 128 : piece * 128 + 128] = whole[
                place // each, place % each : place % each + 1, :
            ]
    grad = grads_out[...]
    second = beta * second_old[...] + (1.0 - beta) * (grad * grad + EPS_ONE)
    second_out[...] = second
    step = grad * lax.rsqrt(second)
    entries = step.size

    def mean_square(values):
        return jnp.sum(jnp.sum(values * values, axis=0, keepdims=True), axis=1, keepdims=True) / (
            entries
        )

    step = step / jnp.maximum(1.0, jnp.sqrt(mean_square(step)) / CLIP)
    old = norms[...]
    norms_out[...] = old - RHO * jnp.sqrt(mean_square(old)) * step


def update_stats(cid, row_parts, rows_old, col_parts, cols_old, weight_sq, loss, norm_parts, norms, second, full):
    size_dp = lax.axis_size("dp")
    size_mp = lax.axis_size("mp")
    f32 = jnp.float32
    rows_old2 = [lane_rows(v) for v in rows_old]
    cols_old2 = [lane_rows(v) for v in cols_old]
    args = (
        [lane_rows(v) for v in row_parts]
        + rows_old2
        + [lane_rows(v) for v in col_parts]
        + cols_old2
        + [v if v.ndim == 2 else lane_rows(v) for v in weight_sq]
        + [lane_rows(loss)]
        + list(norm_parts)
        + [norms, second]
    )
    width = norms.shape[1]
    count_norm = 6 * width // 128
    size_a = count_norm + sum(rows_old2[n].shape[0] for n in (0, 2, 4))
    size_a += sum(cols_old2[n].shape[0] for n in (1, 3)) + 8
    size_a += -size_a % 8
    size_b = sum(cols_old2[n].shape[0] for n in (0, 2, 4))
    size_b += sum(rows_old2[n].shape[0] for n in (1, 3)) + 13
    size_b += -size_b % 8
    each = count_norm // size_mp
    out_shape = [jax.ShapeDtypeStruct(v.shape, f32) for v in rows_old2 + cols_old2]
    out_shape += [
        jax.ShapeDtypeStruct((1, 128), f32),
        jax.ShapeDtypeStruct(norms.shape, f32),
        jax.ShapeDtypeStruct(norms.shape, f32),
        jax.ShapeDtypeStruct(norms.shape, f32),
        jax.ShapeDtypeStruct((16, 128), f32),
    ]
    sems = size_dp + 3 * size_mp
    vmem = pl.BlockSpec(memory_space=pltpu.VMEM)
    found = pl.pallas_call(
        functools.partial(stats_kernel, full, size_dp, size_mp),
        out_shape=out_shape,
        in_specs=[vmem] * len(args),
        out_specs=[vmem] * len(out_shape),
        scratch_shapes=[
            pltpu.VMEM((size_a, 128), f32),
            pltpu.VMEM((size_dp, size_a, 128), f32),
            pltpu.VMEM((size_b, 128), f32),
            pltpu.VMEM((size_mp, size_b, 128), f32),
            pltpu.VMEM((size_mp, each, 128), f32),
            pltpu.VMEM((size_mp, each, 128), f32),
            pltpu.VMEM((size_mp, each, 128), f32),
            pltpu.SemaphoreType.DMA((sems,)),
            pltpu.SemaphoreType.DMA((sems,)),
        ],
        compiler_params=pltpu.CompilerParams(collective_id=cid, has_side_effects=True),
        cost_estimate=cost_of(12),
        name="update_stats",
    )(*args)
    rows_new = [found[n].reshape(-1)[: rows_old[n].size] for n in range(5)]
    cols_new = [found[5 + n].reshape(-1)[: cols_old[n].size] for n in range(5)]
    loss_sums = found[10][0, :NSRC]
    return rows_new, cols_new, loss_sums, found[11], found[12], found[13], found[14]


def clip_kernel(entries, size_dp, size_mp, *refs):
    parts, rate = refs[:5], refs[5]
    out, mine, slots_dp, slots_mp, send, recv = refs[6:]
    dp = lax.axis_index("dp")
    mp = lax.axis_index("mp")
    greet_all(dp, mp, size_dp, size_mp)
    mine[...] = jnp.zeros_like(mine)
    for index in range(5):
        mine[index : index + 1, :] = fold(parts[index][...])
    mine[...] = exchange("dp", dp, mp, mine, slots_dp, send, recv, 0)
    total = exchange("mp", mp, dp, mine, slots_mp, send, recv, size_dp)
    total = jnp.sum(total, axis=1, keepdims=True)
    for index in range(5):
        clip = jnp.maximum(1.0, jnp.sqrt(total[index : index + 1] / entries[index]) / CLIP)
        out[index : index + 1, :] = rate[8 + index : 9 + index, :] / clip


def clip_rates(cid, step_parts, rate, entries):
    size_dp = lax.axis_size("dp")
    size_mp = lax.axis_size("mp")
    vmem = pl.BlockSpec(memory_space=pltpu.VMEM)
    sems = size_dp + size_mp
    return pl.pallas_call(
        functools.partial(clip_kernel, entries, size_dp, size_mp),
        out_shape=jax.ShapeDtypeStruct((8, 128), jnp.float32),
        in_specs=[vmem] * 6,
        out_specs=vmem,
        scratch_shapes=[
            pltpu.VMEM((8, 128), jnp.float32),
            pltpu.VMEM((size_dp, 8, 128), jnp.float32),
            pltpu.VMEM((size_mp, 8, 128), jnp.float32),
            pltpu.SemaphoreType.DMA((sems,)),
            pltpu.SemaphoreType.DMA((sems,)),
        ],
        compiler_params=pltpu.CompilerParams(collective_id=cid, has_side_effects=True),
        cost_estimate=cost_of(8),
        name="clip_rates",
    )(*[lane_rows(v) for v in step_parts], rate)


UNROLL = 8


def lookup_kernel(shift, early, count_ref, key_ref, table_ref, out_ref, low_ref, square_ref, rows_ref):
    spots = out_ref.shape[0]
    vocab, width = table_ref.shape
    rows_ref[...] = jnp.zeros_like(rows_ref)

    def some(i, carry):
        for j in range(UNROLL):
            key = key_ref[i * UNROLL + j]
            place = key & ((1 << shift) - 1)
            rows_ref[pl.ds(place, 1), :] = table_ref[pl.ds(key >> shift, 1), :]
        return carry

    lax.fori_loop(0, (count_ref[0] + UNROLL - 1) // UNROLL, some, 0)

    def narrow(i, carry):
        at = pl.ds(pl.multiple_of(i * 256, 256), 256)
        out_ref[at, :] = rows_ref[at, :].astype(jnp.bfloat16)
        return carry

    lax.fori_loop(0, spots // 256, narrow, 0)
    strip = 64
    rest = vocab % strip
    done = vocab - rest
    low_ref[done - early :, :] = jnp.zeros(
        (low_ref.shape[0] - done + early, width), jnp.bfloat16
    )

    def squares(values, total):
        for row in range(0, values.shape[0], 8):
            piece = values[row : row + 8, :]
            total = total + piece * piece
        return total

    def lower(i, total):
        at = pl.ds(pl.multiple_of(i * strip, strip), strip)
        values = table_ref[at, :]

        @pl.when(i >= early // strip)
        def _():
            start = pl.multiple_of(i * strip - early, 16)
            low_ref[pl.ds(start, strip), :] = values.astype(jnp.bfloat16)

        return squares(values, total)

    total = lax.fori_loop(0, done // strip, lower, jnp.zeros((8, width), jnp.float32))
    if rest:
        values = table_ref[done:, :]
        total = squares(values, total)
        values = jnp.concatenate([values, jnp.zeros((strip - rest, width), jnp.float32)])
        low_ref[done - early : done - early + strip, :] = values.astype(jnp.bfloat16)
    folded = total[:, 0:128]
    for start in range(128, width, 128):
        folded = folded + total[:, start : start + 128]
    square_ref[...] = folded


def lookup(keys, count, table, spots, shift, early):
    vocab, width = table.shape
    smem = pl.BlockSpec(memory_space=pltpu.SMEM)
    vmem = pl.BlockSpec(memory_space=pltpu.VMEM)
    return pl.pallas_call(
        functools.partial(lookup_kernel, shift, early),
        out_shape=[
            jax.ShapeDtypeStruct((spots, width), jnp.bfloat16),
            jax.ShapeDtypeStruct((vocab + -vocab % HEAD_BLOCK - early, width), jnp.bfloat16),
            jax.ShapeDtypeStruct((8, 128), jnp.float32),
        ],
        in_specs=[smem, smem, vmem],
        out_specs=[vmem] * 3,
        scratch_shapes=[pltpu.VMEM((spots + 8, width), jnp.float32)],
        compiler_params=pltpu.CompilerParams(vmem_limit_bytes=VMEM_CAP),
        cost_estimate=cost_of(20),
        name="lookup",
    )(count, keys, table)


def scatter_kernel(shift, count_ref, key_ref, head_ref, rows_in_ref, grad_ref, rows_ref):
    spots = rows_in_ref.shape[0]
    width = grad_ref.shape[1]

    def widen(i, carry):
        at = pl.ds(pl.multiple_of(i * 256, 256), 256)
        rows_ref[at, :] = rows_in_ref[at, :].astype(jnp.float32)
        return carry

    lax.fori_loop(0, spots // 256, widen, 0)
    rows_ref[spots:, :] = jnp.zeros((8, width), jnp.float32)
    grad_ref[...] = head_ref[...].astype(jnp.float32)[: grad_ref.shape[0]]

    def some(i, carry):
        for j in range(UNROLL):
            key = key_ref[i * UNROLL + j]
            place = key & ((1 << shift) - 1)
            grad_ref[pl.ds(key >> shift, 1), :] += rows_ref[pl.ds(place, 1), :]
        return carry

    lax.fori_loop(0, (count_ref[0] + UNROLL - 1) // UNROLL, some, 0)


def scatter(keys, count, head_grad, rows, vocab, shift):
    spots, width = rows.shape
    smem = pl.BlockSpec(memory_space=pltpu.SMEM)
    vmem = pl.BlockSpec(memory_space=pltpu.VMEM)
    return pl.pallas_call(
        functools.partial(scatter_kernel, shift),
        out_shape=jax.ShapeDtypeStruct((vocab, width), jnp.float32),
        in_specs=[smem, smem, vmem, vmem],
        out_specs=vmem,
        scratch_shapes=[pltpu.VMEM((spots + 8, width), jnp.float32)],
        compiler_params=pltpu.CompilerParams(vmem_limit_bytes=VMEM_CAP),
        cost_estimate=cost_of(23),
        name="scatter",
    )(count, keys, head_grad, rows)


def norm_parts(values):
    centre = jnp.mean(values, axis=-1, keepdims=True)
    centred = values - centre
    scale = lax.rsqrt(jnp.mean(centred * centred, axis=-1, keepdims=True) + EPS_NORM)
    return centred * scale, scale


def norm_pull(values, gain, upstream):
    normed, scale = norm_parts(values)
    weighted = upstream * gain
    pulled = scale * (
        weighted
        - jnp.mean(weighted, axis=-1, keepdims=True)
        - normed * jnp.mean(weighted * normed, axis=-1, keepdims=True)
    )
    return (
        pulled,
        jnp.sum(upstream * normed, axis=0, keepdims=True),
        jnp.sum(upstream, axis=0, keepdims=True),
    )


def step_first(total, at, ins, outs):
    stream, norms = outs[0], ins[0]
    normed, scale = norm_parts(stream[at, :].astype(jnp.float32))
    return normed * norms[0:1, :] + norms[1:2, :]


def step_forward(row, total, at, ins, outs):
    stream, norms = ins
    values = stream[at, :].astype(jnp.float32) + total
    outs[0][at, :] = values
    normed, scale = norm_parts(values)
    return normed * norms[row : row + 1, :] + norms[row + 1 : row + 2, :]


def step_backward(row, total, at, ins, outs):
    stream, norms = ins[:2]
    pulled, dgain, dshift = norm_pull(
        stream[at, :].astype(jnp.float32), norms[row : row + 1, :], total
    )
    if len(ins) > 2:
        pulled = pulled + ins[2][at, :]
    if len(outs) > 1:
        outs[0][at, :] = pulled
    sums = outs[-1]

    @pl.when(at.start == 0)
    def _():
        sums[...] = jnp.zeros_like(sums)

    sums[0:1, :] += dgain
    sums[1:2, :] += dshift
    return pulled


def gelu_tanh(values):
    return jax.nn.gelu(values, approximate=True)


def local(
    token_ids,
    targets,
    starts,
    sources,
    embedding,
    w_qkv,
    w_out,
    w_fc,
    w_proj,
    norm_params,
    rows_table,
    cols_table,
    rows_qkv,
    cols_qkv,
    rows_out,
    cols_out,
    rows_fc,
    cols_fc,
    rows_proj,
    cols_proj,
    second_norms,
):
    bf16 = jnp.bfloat16
    f32 = jnp.float32
    size_mp = lax.axis_size("mp")
    size_dp = lax.axis_size("dp")
    dp = lax.axis_index("dp")
    mp = lax.axis_index("mp")
    tokens = token_ids.shape[0]
    seqs = tokens // LEN
    chips = size_mp // 2
    near = chips // seqs
    sharers = size_mp // seqs
    rows = tokens // size_mp
    vocab, part_width = embedding.shape
    width = part_width * size_dp
    first_row = mp * vocab
    spots = tokens * size_dp
    chunks_full = max(1, min(8, rows // 32))
    chunks_near = max(1, min(4, rows // 32))
    chunks_turn = max(1, min(4, rows // 32))

    def own_and_twins(weights, axis):
        low = [weight.astype(bf16) for weight in weights]
        found = [[weight] for weight in low]
        sent = jnp.concatenate(low, axis=axis)
        for turn in range(1, seqs):
            shift = [(i, (i + turn * sharers) % size_mp) for i in range(size_mp)]
            arrived = lax.ppermute(sent, "mp", shift)
            start = 0
            for index, weight in enumerate(low):
                size = weight.shape[axis]
                found[index].append(lax.slice_in_dim(arrived, start, start + size, axis=axis))
                start += size
        return [jnp.concatenate(pieces, axis=axis) for pieces in found]

    pair_fc, pair_qkv = own_and_twins((w_fc, w_qkv), 1)
    pair_proj, pair_out = own_and_twins((w_proj, w_out), 0)

    early = (vocab + -vocab % HEAD_BLOCK) * 2 // (10 * HEAD_BLOCK) * HEAD_BLOCK
    early_table = lax.all_gather(embedding[:early].astype(bf16), "dp", axis=1, tiled=True)

    both = jnp.stack([token_ids, sources]).reshape(-1, 128)
    both = small_gather("gather_ids", 0, both, "dp").reshape(size_dp, 2, tokens)
    all_ids = both[:, 0]
    all_sources = both[:, 1].reshape(-1)
    counts = jnp.sum(
        (all_sources[:, None] == jnp.arange(NSRC, dtype=jnp.int32)[None, :]).astype(f32), axis=0
    )

    piece = rows // chunks_turn
    token = jnp.arange(tokens, dtype=jnp.int32)
    place = (
        token // piece * (size_dp * piece)
        + (jnp.arange(size_dp, dtype=jnp.int32) * piece)[:, None]
        + token % piece
    )
    local_ids = all_ids - first_row
    inside = (local_ids >= 0) & (local_ids < vocab)
    shift = spots.bit_length()
    idle = ((vocab - 1) << shift) + spots
    keys = jnp.where(inside, (local_ids << shift) + place, idle)
    keys = jnp.sort(keys.reshape(-1))
    owned = jnp.sum(inside.astype(jnp.int32)).reshape(1)
    found, low_table, table_sq = lookup(keys, owned, embedding, spots, shift, early)
    found, early_table = lax.optimization_barrier((found, early_table))
    inner_one, stream0, wide_qkv, wide_out, wide_fc, wide_proj = line_call(
        "lookup_sum",
        1,
        found,
        [norm_params],
        [jax.ShapeDtypeStruct((rows, width), bf16)],
        step_first,
        size_dp * rows,
        part_width,
        chunks_turn,
        chips,
        near,
        70,
        [
            ("gather", 0, pair_qkv),
            ("gather", 1, pair_out),
            ("gather", 0, pair_fc),
            ("gather", 1, pair_proj),
        ],
        "gather",
        8,
    )
    low_table, inner_one = lax.optimization_barrier((low_table, inner_one))
    wide_table = (early_table, lax.all_gather(low_table, "dp", axis=1, tiled=True))
    row_f32 = jax.ShapeDtypeStruct((rows, width), f32)
    pair_f32 = jax.ShapeDtypeStruct((8, width), f32)
    my_starts = row_slice(starts, (mp // sharers) * LEN, LEN)[:, None]
    mixed = jnp.dot(inner_one, wide_qkv, preferred_element_type=f32).astype(bf16)
    attended = attend(mixed, my_starts)
    partial = jnp.dot(attended, wide_out, preferred_element_type=f32).astype(bf16)
    inner_two, stream1 = line_call(
        "attn_sum",
        3,
        partial,
        [stream0, norm_params],
        [row_f32],
        functools.partial(step_forward, 2),
        rows,
        width,
        chunks_near,
        near,
        near,
        32,
    )
    before = jnp.dot(inner_two, wide_fc, preferred_element_type=f32)
    hidden = gelu_tanh(before).astype(bf16)
    partial = jnp.dot(hidden, wide_proj, preferred_element_type=f32).astype(bf16)
    final, stream2 = line_call(
        "mlp_sum",
        4,
        partial,
        [stream1, norm_params],
        [row_f32],
        functools.partial(step_forward, 4),
        rows,
        width,
        chunks_full,
        near,
        chips,
        58,
        chunk_major=True,
    )

    edge = jnp.clip(VREAL - first_row, 0, vocab).astype(jnp.int32).reshape(1)

    def by_chunk(values):
        return values.reshape(size_mp, chunks_full, -1).swapaxes(0, 1).reshape(tokens)

    sources = by_chunk(sources)
    wanted = by_chunk(targets) - first_row
    wanted = jnp.where((wanted >= 0) & (wanted < vocab), wanted, -1).reshape(1, tokens)
    block = HEAD_BLOCK
    exps, tops, sums, picks = head_stats(wide_table, final, wanted, edge, block)
    tops = tops[:, 0]
    top = jnp.max(tops, axis=0)
    total = jnp.sum(sums[:, 0] * jnp.exp(tops - top[None, :]), axis=0)
    pick = jnp.sum(picks[:, 0], axis=0)
    stats = jnp.concatenate([v.reshape(-1, 128) for v in (top, total, pick)])
    stats = small_gather("gather_stats", 5, stats, "mp").reshape(size_mp, 3, tokens)
    highest = jnp.max(stats[:, 0], axis=0)
    log_total = highest + jnp.log(
        jnp.sum(stats[:, 1] * jnp.exp(stats[:, 0] - highest[None, :]), axis=0)
    )
    token_loss = log_total - jnp.sum(stats[:, 2], axis=0)
    member = (sources[:, None] == jnp.arange(NSRC, dtype=jnp.int32)[None, :]).astype(f32)
    loss_part = jnp.sum(member * token_loss[:, None], axis=0)
    weight = jnp.sum(member / (NSRC * jnp.maximum(counts, 1.0))[None, :], axis=1)
    scale = jnp.exp(tops - log_total[None, :]) * weight[None, :]
    dlogits, table_grad = head_back(
        exps, final, scale[:, None, :], weight[None, :], wanted, block
    )
    head_grad = lax.psum_scatter(table_grad, "dp", scatter_dimension=1, tiled=True)

    dbranch2, dstream2, norm3 = line_call(
        "final_back",
        6,
        (dlogits, *wide_table),
        [stream2, norm_params],
        [row_f32, pair_f32],
        functools.partial(step_backward, 4),
        rows,
        width,
        chunks_full,
        chips,
        near,
        65,
        product=True,
    )
    grad_proj = jnp.einsum("tf,td->fd", hidden, dbranch2, preferred_element_type=f32).astype(bf16)
    grad_proj, head_grad = lax.optimization_barrier((grad_proj, head_grad))
    grad_proj = lax.psum_scatter(grad_proj, "dp", scatter_dimension=1, tiled=True)
    dhidden = jnp.einsum("td,fd->tf", dbranch2, wide_proj, preferred_element_type=f32)
    unused, gelu_pull = jax.vjp(gelu_tanh, before)
    dbefore = gelu_pull(dhidden)[0].astype(bf16)
    partial = jnp.einsum("tf,df->td", dbefore, wide_fc, preferred_element_type=f32).astype(bf16)
    dbranch1, dstream1, norm2 = line_call(
        "mlp_back",
        7,
        partial,
        [stream1, norm_params, dstream2],
        [row_f32, pair_f32],
        functools.partial(step_backward, 2),
        rows,
        width,
        chunks_near,
        near,
        near,
        34,
    )
    grad_fc = jnp.einsum("td,tf->df", inner_two, dbefore, preferred_element_type=f32).astype(bf16)
    grad_out = jnp.einsum("tf,td->fd", attended, dbranch1, preferred_element_type=f32).astype(bf16)
    dattended = jnp.einsum("td,fd->tf", dbranch1, wide_out, preferred_element_type=f32)
    dmixed = attend_back(mixed, my_starts, dattended.astype(bf16))
    partial = jnp.einsum("tc,dc->td", dmixed, wide_qkv, preferred_element_type=f32).astype(bf16)
    grad_qkv = jnp.einsum("td,tc->dc", inner_one, dmixed, preferred_element_type=f32).astype(bf16)
    drows, norm1, grad_out, grad_fc, grad_qkv, twins_wide, twins_out = line_call(
        "attn_back",
        8,
        partial,
        [stream0, norm_params, dstream1],
        [pair_f32],
        functools.partial(step_backward, 0),
        rows,
        width,
        chunks_turn,
        near,
        chips,
        70,
        [
            ("scatter", 1, grad_out),
            ("scatter", 0, grad_fc),
            ("scatter", 0, grad_qkv),
        ],
        "spread",
        9,
        seqs=seqs,
    )

    def from_twins(values, axis, sizes):
        starts = [(seqs - 1) * sum(sizes[:n]) for n in range(len(sizes))]
        found = []
        for turn in range(1, seqs):
            pieces = [
                lax.slice_in_dim(values, at + (turn - 1) * size, at + turn * size, axis=axis)
                for at, size in zip(starts, sizes)
            ]
            back = [(i, (i - turn * sharers) % size_mp) for i in range(size_mp)]
            found.append(lax.ppermute(jnp.concatenate(pieces, axis=axis), "mp", back))
        return found

    proj_rows = w_proj.shape[0]
    wide = [grad_fc.shape[1], grad_qkv.shape[1]]
    found_proj = from_twins(grad_proj[proj_rows:], 0, [proj_rows])
    found_out = from_twins(twins_out, 0, [w_out.shape[0]])
    found_wide = from_twins(twins_wide, 1, wide)
    grad_table = scatter(keys, owned, head_grad, drows, vocab, shift)
    found_proj, found_out, found_wide, grad_table = lax.optimization_barrier(
        (found_proj, found_out, found_wide, grad_table)
    )
    grad_proj = grad_proj[:proj_rows].astype(f32)
    for values in found_proj:
        grad_proj += values.astype(f32)
    for values in found_out:
        grad_out += values.astype(f32)
    for values in found_wide:
        grad_fc += values[:, : wide[0]].astype(f32)
        grad_qkv += values[:, wide[0] :].astype(f32)

    weights = (embedding, w_qkv, w_out, w_fc, w_proj)
    grads = (grad_table, grad_qkv, grad_out, grad_fc, grad_proj)
    row_span = (size_mp, size_dp, size_mp, size_dp, size_mp)
    col_span = (size_dp, size_mp, size_dp, size_mp, size_dp)
    full = tuple(
        (g.shape[0] * r, g.shape[1] * c) for g, r, c in zip(grads, row_span, col_span)
    )
    squares = [gradient * gradient + EPS_ONE for gradient in grads]
    rows_new, cols_new, loss_sums, grad_norms, second_new, norms_new, rates = update_stats(
        10,
        [jnp.sum(square, axis=1) for square in squares],
        (rows_table, rows_qkv, rows_out, rows_fc, rows_proj),
        [jnp.sum(square, axis=0) for square in squares],
        (cols_table, cols_qkv, cols_out, cols_fc, cols_proj),
        [table_sq] + [jnp.sum(value * value, axis=0) for value in weights[1:]],
        loss_part,
        (norm1, norm2, norm3),
        norm_params,
        second_norms,
        full,
    )
    steps = [
        grads[n] * lax.rsqrt(rows_new[n][:, None] * cols_new[n][None, :] / rates[n, 0])
        for n in range(5)
    ]
    factors = clip_rates(
        11, [jnp.sum(step * step, axis=0) for step in steps], rates, [r * c for r, c in full]
    )
    updated = [weights[n] - factors[n, 0] * steps[n] for n in range(5)]
    return (
        loss_sums,
        counts,
        grad_table,
        rows_new[0],
        cols_new[0],
        updated[0],
        grad_qkv,
        rows_new[1],
        cols_new[1],
        updated[1],
        grad_out,
        rows_new[2],
        cols_new[2],
        updated[2],
        grad_fc,
        rows_new[3],
        cols_new[3],
        updated[3],
        grad_proj,
        rows_new[4],
        cols_new[4],
        updated[4],
        grad_norms,
        second_new,
        norms_new,
    )


def solution(mesh):
    placed = (
        P("dp"),
        P("dp"),
        P("dp"),
        P("dp"),
        P("mp", "dp"),
        P("dp", "mp"),
        P("mp", "dp"),
        P("dp", "mp"),
        P("mp", "dp"),
        P(),
        P("mp"),
        P("dp"),
        P("dp"),
        P("mp"),
        P("mp"),
        P("dp"),
        P("dp"),
        P("mp"),
        P("mp"),
        P("dp"),
        P(),
    )
    return jax.shard_map(
        local,
        mesh=mesh,
        in_specs=placed,
        out_specs=(
            P(),
            P(),
            P("mp", "dp"),
            P("mp"),
            P("dp"),
            P("mp", "dp"),
            P("dp", "mp"),
            P("dp"),
            P("mp"),
            P("dp", "mp"),
            P("mp", "dp"),
            P("mp"),
            P("dp"),
            P("mp", "dp"),
            P("dp", "mp"),
            P("dp"),
            P("mp"),
            P("dp", "mp"),
            P("mp", "dp"),
            P("mp"),
            P("dp"),
            P("mp", "dp"),
            P(),
            P(),
            P(),
        ),
        check_vma=False,
    )
```

```python
import functools
import math

import jax
import jax.numpy as jnp
from jax import lax
from jax.experimental import pallas as pl
from jax.experimental.pallas import tpu as pltpu
from jax.sharding import PartitionSpec as P

HD = 64
VREAL = 50257
LEN = 1024
NSRC = 4
STEP = 10


EPS_NORM = 1e-05
EPS_ONE = 1e-30
CLIP = 1.0
RHO = 0.5
MASKED = -1e30
QUERIES = 256
HEAD_BLOCK = 640
MESH = pl.DeviceIdType.MESH
VMEM_CAP = 56 * 2**20


def cost_of(time):
    return pl.CostEstimate(
        flops=time * 1000000000, bytes_accessed=time * 3000000, transcendentals=0
    )


def row_slice(values, start, count):
    return lax.dynamic_slice_in_dim(values, start, count, 0)


def line_kernel(
    nr, ng, chunks, shapes, n_in, n_out, step, sides, turn, side_ticks, product, chunk_major, *refs
):
    (rows_r, width_r), (rows_g, width_g) = shapes
    if product:
        dl, *tables = refs[:3]
        first = 3
    else:
        part = refs[0] if nr else None
        first = 1 if nr else 0
    ins = refs[first : first + n_in]
    refs = refs[first + n_in :]
    side_ins, refs = refs[: len(sides)], refs[len(sides) :]
    if ng:
        whole, refs = refs[0], refs[1:]
    outs = refs[:n_out]
    refs = refs[n_out:]
    scatters = [index for index, (kind, unused) in enumerate(sides) if kind == "scatter"]
    side_outs, refs = refs[: len(sides)], refs[len(sides) :]
    twin_outs, scratch = (refs[:2], refs[2:]) if scatters else ([], refs)
    side_scratch, scratch = scratch[: 3 * len(sides)], scratch[3 * len(sides) :]
    if turn:
        cast, turn_send, turn_recv = scratch[-3:]
    if product:
        part, dl_buf, total_ref, dl_sem = scratch[-4:]
    size_dp = lax.axis_size("dp")
    dp = lax.axis_index("dp")
    mp = lax.axis_index("mp")
    z = mp // 2
    core = lax.rem(mp, 2)
    other = mp + 1 - 2 * core
    piece_r = rows_r // chunks
    piece_g = rows_g // chunks
    small = min(piece_r, piece_g)
    late = 1 if turn else 0
    ahead = 1 if product else 0
    most = max(nr, ng)
    zb = lax.rem(z, most)
    if nr:
        zr = lax.rem(z, nr)
        last_r = nr - 1
    if ng:
        zg = lax.rem(z, ng)
        last_g = ng - 1

    barrier = pltpu.get_barrier_semaphore()
    pl.semaphore_signal(barrier, inc=1, device_id=(dp, other), device_id_type=MESH)

    @pl.when(zb > 0)
    def _():
        pl.semaphore_signal(barrier, inc=1, device_id=(dp, mp - 2), device_id_type=MESH)

    @pl.when(zb < most - 1)
    def _():
        pl.semaphore_signal(barrier, inc=1, device_id=(dp, mp + 2), device_id_type=MESH)

    if sides or turn:
        for hop in range(1, size_dp):
            pl.semaphore_signal(
                barrier,
                inc=1,
                device_id=(lax.rem(dp + hop, size_dp), mp),
                device_id_type=MESH,
            )
    greeted = (size_dp if sides or turn else 1) + (zb > 0).astype(jnp.int32) + (zb < most - 1).astype(jnp.int32)
    pl.semaphore_wait(barrier, greeted)

    def share(axis, length, which):
        at = pl.ds(pl.multiple_of(which * length, length), length)
        return (at, slice(None)) if axis == 0 else (slice(None), at)

    def to_peer(src, dst, send, recv, peer):
        return pltpu.make_async_remote_copy(
            src_ref=src,
            dst_ref=dst,
            send_sem=send,
            recv_sem=recv,
            device_id=(peer, mp),
            device_id_type=MESH,
        )

    relay = size_dp == 4
    beside_x = dp + 1 - 2 * lax.rem(dp, 2)
    beside_y = lax.rem(dp + 2, 4)
    across = 3 - dp

    def half_share(axis, length, which, height, part):
        if axis == 0:
            return (pl.ds(pl.multiple_of(which * length + part * height, height), height), slice(None))
        at = pl.ds(pl.multiple_of(which * length, length), length)
        return (pl.ds(part * height, height), at)

    first_copies, more_copies, relays = [], [], []
    for index, (kind, axis) in enumerate(sides):
        src, dst = side_ins[index], side_outs[index]
        send, recv, slots = side_scratch[3 * index : 3 * index + 3]
        if kind == "gather":
            length, height = src.shape[axis], src.shape[0] // 2
        else:
            length = src.shape[axis] // size_dp
            height = (length if axis == 0 else src.shape[0]) // 2
        if not relay:
            for hop in range(1, size_dp):
                peer = lax.rem(dp + hop, size_dp)
                if kind == "gather":
                    source, target = src, dst.at[share(axis, length, dp)]
                else:
                    source, target = src.at[share(axis, length, peer)], slots.at[hop]
                more_copies.append(to_peer(source, target, send.at[hop], recv.at[hop], peer))
            continue
        for side, near_one, far_one in ((0, beside_x, beside_y), (1, beside_y, beside_x)):
            sems = [(send.at[3 * side + n], recv.at[3 * side + n]) for n in range(3)]
            if kind == "gather":
                mine = src.at[pl.ds(side * height, height)]
                here = dst.at[half_share(axis, length, dp, height, side)]
                passed = dst.at[half_share(axis, length, near_one, height, side)]
                arrives = to_peer(mine, here, *sems[0], near_one)
                first_copies.append(arrives)
                more_copies.append(to_peer(mine, here, *sems[1], far_one))
                relays.append((arrives, None, to_peer(passed, passed, *sems[2], far_one)))
            else:
                arrives = to_peer(
                    src.at[half_share(axis, length, across, height, side)],
                    slots.at[4 * side],
                    *sems[0],
                    near_one,
                )
                first_copies.append(arrives)
                more_copies.append(
                    to_peer(
                        src.at[half_share(axis, length, near_one, height, side)],
                        slots.at[4 * side + 1],
                        *sems[1],
                        near_one,
                    )
                )
                summed = to_peer(
                    slots.at[4 * side + 2], slots.at[4 * side + 3], *sems[2], far_one
                )
                own = src.at[half_share(axis, length, far_one, height, side)]
                relays.append((arrives, (own, slots, 4 * side, height), summed))

    def pass_on(arrives, adding, copy):
        arrives.wait_recv()
        if adding is not None:
            own, slots, at, height = adding
            both = own[...].astype(jnp.float32) + slots[at].astype(jnp.float32)
            slots[at + 2] = both.astype(slots.dtype)
        copy.start()

    jobs = [copy.start for copy in first_copies + more_copies]
    jobs += [functools.partial(pass_on, *one) for one in relays]

    def side_jobs(now):
        for spot in range(side_ticks if jobs else 0):
            chosen = jobs[len(jobs) * spot // side_ticks : len(jobs) * (spot + 1) // side_ticks]

            @pl.when(now == spot)
            def _():
                for job in chosen:
                    job()

    if nr:
        half, from_left, from_right, going = scratch[:4]
        half_send, half_recv, rs_send, left_recv, right_recv = scratch[4:9]
        scratch = scratch[9:]
    if ng:
        core_send, core_recv, to_right, to_left, ag_left, ag_right = scratch[:6]

    def part_rows(block, k):
        return pl.ds(pl.multiple_of(block * rows_r + k * piece_r, piece_r), piece_r)

    def whole_rows(block, k):
        if chunk_major:
            start = k * (2 * ng * piece_g) + block * piece_g
            return pl.ds(pl.multiple_of(start, piece_g), piece_g)
        return pl.ds(pl.multiple_of(block * rows_g + k * piece_g, piece_g), piece_g)

    def remote(src, dst, send, recv, target):
        return pltpu.make_async_remote_copy(
            src_ref=src,
            dst_ref=dst,
            send_sem=send,
            recv_sem=recv,
            device_id=(dp, target),
            device_id_type=MESH,
        )

    if nr:

        def half_copy(dest, k):
            return remote(
                part.at[part_rows(2 * dest + 1 - core, k)],
                half.at[dest, k],
                half_send.at[dest, k],
                half_recv.at[dest, k],
                other,
            )

        def send_halves(k, carry):
            for dest in range(nr):
                half_copy(dest, k).start()
            return carry

        if not product:
            lax.fori_loop(0, chunks, send_halves, 0)

        def right_copy(dest, k):
            return remote(
                going.at[dest, k],
                from_left.at[dest, k],
                rs_send.at[dest, k],
                left_recv.at[dest, k],
                mp + 2,
            )

        def left_copy(dest, k):
            return remote(
                going.at[dest, k],
                from_right.at[dest, k],
                rs_send.at[dest, k],
                right_recv.at[dest, k],
                mp - 2,
            )

        def chip_sum(dest, k):
            half_copy(dest, k).wait_recv()
            mine = part[part_rows(2 * dest + core, k), :].astype(jnp.float32)
            return mine + half[dest, k].astype(jnp.float32)

        def pass_right(dest, k):
            total = chip_sum(dest, k)

            @pl.when(zr == 0)
            def _():
                going[dest, k] = total.astype(jnp.bfloat16)

            @pl.when(zr > 0)
            def _():
                right_copy(dest, k).wait_recv()
                both = total + from_left[dest, k].astype(jnp.float32)
                going[dest, k] = both.astype(jnp.bfloat16)

            right_copy(dest, k).start()

        def pass_left(dest, k):
            total = chip_sum(dest, k)

            @pl.when(zr == last_r)
            def _():
                going[dest, k] = total.astype(jnp.bfloat16)

            @pl.when(zr < last_r)
            def _():
                left_copy(dest, k).wait_recv()
                both = total + from_right[dest, k].astype(jnp.float32)
                going[dest, k] = both.astype(jnp.bfloat16)

            left_copy(dest, k).start()

    if ng:

        def gathered(block, k, send, recv, target):
            where = whole.at[whole_rows(2 * block + core, k)]
            return remote(where, where, send.at[block, k], recv.at[block, k], target)

        def core_copy(block, k):
            return gathered(block, k, core_send, core_recv, other)

        def ag_right_copy(block, k):
            return gathered(block, k, to_right, ag_left, mp + 2)

        def ag_left_copy(block, k):
            return gathered(block, k, to_left, ag_right, mp - 2)

    def own_rows(k):
        total = None
        if nr:
            total = chip_sum(zr, k)
            zero = jnp.zeros((piece_r, width_r), jnp.float32)

            @pl.when(zr > 0)
            def _():
                right_copy(zr, k).wait_recv()

            @pl.when(zr < last_r)
            def _():
                left_copy(zr, k).wait_recv()

            total += jnp.where(zr > 0, from_left[zr, k].astype(jnp.float32), zero)
            total += jnp.where(zr < last_r, from_right[zr, k].astype(jnp.float32), zero)
        if turn == "gather":
            cast[k] = total.astype(cast.dtype)
            for hop in range(1, size_dp):
                turn_copy(hop, k).start()
            mine = pl.ds(pl.multiple_of(dp * small, small), small)
            outs[0][own_place(k, dp)] = cast[k, mine, :]
            return
        at = pl.ds(pl.multiple_of(k * piece_r, piece_r), piece_r)
        ready = step(total, at, ins, outs)
        if turn == "spread":
            cast[k] = ready.astype(cast.dtype)
            for hop in range(1, size_dp):
                turn_copy(hop, k).start()
            whole[own_place(k, dp)] = cast[
                k, :, pl.ds(pl.multiple_of(dp * width_g, width_g), width_g)
            ]
        elif ng:
            whole[whole_rows(2 * zg + core, k), :] = ready.astype(whole.dtype)
            start_gather(k)

    def own_place(k, peer):
        if turn == "gather":
            return (
                pl.ds(pl.multiple_of(k * small, small), small),
                pl.ds(pl.multiple_of(peer * width_r, width_r), width_r),
            )
        start = (2 * zg + core) * rows_g + k * piece_g + peer * small
        return (pl.ds(pl.multiple_of(start, small), small), slice(None))

    def turn_copy(hop, k):
        peer = lax.rem(dp + hop, size_dp)
        if turn == "gather":
            src = cast.at[k, pl.ds(pl.multiple_of(peer * small, small), small)]
            dst = outs[0].at[own_place(k, dp)]
        else:
            src = cast.at[k, :, pl.ds(pl.multiple_of(peer * width_g, width_g), width_g)]
            dst = whole.at[own_place(k, dp)]
        return to_peer(src, dst, turn_send.at[hop, k], turn_recv.at[hop, k], peer)

    def turned_rows(k):
        for hop in range(1, size_dp):
            turn_copy(hop, k).wait_recv()
        if turn == "gather":
            at = pl.ds(pl.multiple_of(k * piece_g, piece_g), piece_g)
            ready = step(None, at, ins, outs)
            whole[whole_rows(2 * zg + core, k), :] = ready.astype(whole.dtype)
        start_gather(k)

    def start_gather(k):
        core_copy(zg, k).start()

        @pl.when(zg < last_g)
        def _():
            ag_right_copy(zg, k).start()

        @pl.when(zg > 0)
        def _():
            ag_left_copy(zg, k).start()

    def inside(k):
        return (k >= 0) & (k < chunks)

    def own_lag(chip):
        if not nr:
            return 0
        at = lax.rem(chip, nr)
        return jnp.maximum(at, last_r - at) + ahead

    def dl_copy(k):
        columns = dl_buf.shape[2]
        return pltpu.make_async_copy(
            dl.at[:, pl.ds(pl.multiple_of(k * columns, columns), columns)],
            dl_buf.at[lax.rem(k, 2)],
            dl_sem.at[lax.rem(k, 2)],
        )

    def make_part(k):
        dl_copy(k).wait()

        @pl.when(k + 1 < chunks)
        def _():
            dl_copy(k + 1).start()

        slot = lax.rem(k, 2)

        start = 0
        for piece in tables:
            found = lax.dot_general(
                dl_buf[slot, start : start + piece.shape[0], :],
                piece[...],
                (((0,), (0,)), ((), ())),
                preferred_element_type=jnp.float32,
            )
            if start:
                total_ref[...] += found
            else:
                total_ref[...] = found
            start += piece.shape[0]
        for block in range(2 * nr):
            part[part_rows(block, k), :] = total_ref[
                block * piece_r : block * piece_r + piece_r, :
            ].astype(jnp.bfloat16)
        send_halves(k, 0)

    if product:
        dl_copy(0).start()

    def tick(now, carry):
        side_jobs(now)
        if nr:
            k_right = now - zr - ahead
            k_left = now - (last_r - zr) - ahead
            for far in range(last_r):

                @pl.when(inside(k_right) & (last_r - far > zr))
                def _():
                    pass_right(last_r - far, k_right)

                @pl.when(inside(k_left) & (far < zr))
                def _():
                    pass_left(far, k_left)

        k_own = now - own_lag(z)

        @pl.when(inside(k_own))
        def _():
            own_rows(k_own)

        if turn:

            @pl.when(inside(k_own - 1))
            def _():
                turned_rows(k_own - 1)

        if ng:
            for block in range(ng):
                k = now - (own_lag(z - zg + block) + late + jnp.abs(zg - block))

                @pl.when(inside(k) & (block < zg))
                def _():
                    ag_right_copy(block, k).wait_recv()
                    core_copy(block, k).start()

                    @pl.when(zg < last_g)
                    def _():
                        ag_right_copy(block, k).start()

                @pl.when(inside(k) & (block > zg))
                def _():
                    ag_left_copy(block, k).wait_recv()
                    core_copy(block, k).start()

                    @pl.when(zg > 0)
                    def _():
                        ag_left_copy(block, k).start()

        if product:

            @pl.when(now < chunks)
            def _():
                make_part(now)

        return carry

    ticks = ahead + chunks + (nr - 1 if nr else 0) + (ng - 1 if ng else 0) + late
    lax.fori_loop(0, ticks, tick, 0)

    def finish(k, carry):
        if turn:
            for hop in range(1, size_dp):
                turn_copy(hop, k).wait_send()
        if nr:
            for block in range(nr):
                half_copy(block, k).wait_send()

                @pl.when(block != zr)
                def _():
                    right_copy(block, k).wait_send()

        if ng:
            for block in range(ng):
                core_copy(block, k).wait()

                @pl.when((zg < last_g) & (block <= zg))
                def _():
                    ag_right_copy(block, k).wait_send()

                @pl.when((zg > 0) & (block >= zg))
                def _():
                    ag_left_copy(block, k).wait_send()

        return carry

    lax.fori_loop(0, chunks, finish, 0)
    for index, (kind, axis) in enumerate(sides):
        if kind == "gather":
            length = side_ins[index].shape[axis]
            side_outs[index][share(axis, length, dp)] = side_ins[index][...]
    for copy in first_copies:
        copy.wait_send()
    for copy in more_copies:
        copy.wait()
    for unused, unused, copy in relays:
        copy.wait()
    placed = [0, 0]
    for index in scatters:
        axis = sides[index][1]
        src, dst = side_ins[index], side_outs[index]
        slots = side_scratch[3 * index + 2]
        length = src.shape[axis] // size_dp
        height = (length if axis == 0 else src.shape[0]) // 2
        if relay:
            total = []
            for side in range(2):
                one = src[half_share(axis, length, dp, height, side)].astype(jnp.float32)
                one += slots[4 * side + 1].astype(jnp.float32)
                one += slots[4 * side + 3].astype(jnp.float32)
                total.append(one)
            total = jnp.concatenate(total)
        else:
            total = src[share(axis, length, dp)].astype(jnp.float32)
            for hop in range(1, size_dp):
                total += slots[hop].astype(jnp.float32)
        twins = twin_outs[axis]
        at = placed[axis]
        if axis == 0:
            own = dst.shape[1]
            dst[...] = total[:, :own]
            more = total.shape[1] - own
            twins[:, at : at + more] = total[:, own:].astype(twins.dtype)
        else:
            own = dst.shape[0]
            dst[...] = total[:own, :]
            more = total.shape[0] - own
            twins[at : at + more, :] = total[own:, :].astype(twins.dtype)
        placed[axis] += more


def line_call(
    name,
    cid,
    partial,
    ins,
    out_types,
    step,
    rows,
    width,
    chunks,
    nr,
    ng,
    time,
    sides=(),
    turn=None,
    side_ticks=0,
    product=False,
    chunk_major=False,
    seqs=1,
):
    piece = rows // chunks
    size_dp = lax.axis_size("dp")
    reduced = gathered = (rows, width)
    if turn == "gather":
        gathered = (rows // size_dp, width * size_dp)
    elif turn == "spread":
        gathered = (rows * size_dp, width // size_dp)
    out_shape = []
    if ng:
        out_shape.append(
            jax.ShapeDtypeStruct((2 * ng * gathered[0], gathered[1]), jnp.bfloat16)
        )
    out_shape += out_types
    dma = pltpu.SemaphoreType.DMA
    scratch = []
    twin_shapes = [[0, 0], [0, 0]]
    for kind, axis, values in sides:
        shape = list(values.shape)
        scratch += [dma((max(size_dp, 6),)), dma((max(size_dp, 6),))]
        if kind == "gather":
            shape[axis] *= size_dp
            out_shape.append(jax.ShapeDtypeStruct(tuple(shape), values.dtype))
            scratch.append(pltpu.VMEM((16, 128), values.dtype))
        else:
            shape[axis] //= size_dp
            own = list(shape)
            own[1 - axis] //= seqs
            out_shape.append(jax.ShapeDtypeStruct(tuple(own), jnp.float32))
            twin_shapes[axis][axis] = shape[axis]
            twin_shapes[axis][1 - axis] += shape[1 - axis] - own[1 - axis]
            slots = (8, shape[0] // 2, shape[1]) if size_dp == 4 else (size_dp, *shape)
            scratch.append(pltpu.VMEM(slots, values.dtype))
    if any(side[0] == "scatter" for side in sides):
        out_shape += [jax.ShapeDtypeStruct(tuple(shape), jnp.bfloat16) for shape in twin_shapes]
    if nr:
        scratch += [pltpu.VMEM((nr, chunks, piece, width), jnp.bfloat16)] * 4
        scratch += [dma((nr, chunks))] * 5
    if ng:
        scratch += [dma((ng, chunks))] * 6
    if turn:
        scratch.append(pltpu.VMEM((chunks, piece, width), jnp.bfloat16))
        scratch += [dma((size_dp, chunks))] * 2
    if product:
        dl = partial[0]
        columns = dl.shape[1] // chunks
        scratch += [
            pltpu.VMEM((2 * nr * rows, width), jnp.bfloat16),
            pltpu.VMEM((2, dl.shape[0], columns), jnp.bfloat16),
            pltpu.VMEM((columns, width), jnp.float32),
            dma((2,)),
        ]
        partial = list(partial)
    else:
        partial = [partial] if nr else []
    args = partial + list(ins) + [side[2] for side in sides]
    vmem = pl.BlockSpec(memory_space=pltpu.VMEM)
    call = pl.pallas_call(
        functools.partial(
            line_kernel,
            nr,
            ng,
            chunks,
            (reduced, gathered),
            len(ins),
            len(out_types),
            step,
            tuple(side[:2] for side in sides),
            turn,
            side_ticks,
            product,
            chunk_major,
        ),
        out_shape=out_shape,
        in_specs=[pl.BlockSpec(memory_space=pl.ANY) if product and n == 0 else vmem for n in range(len(args))],
        out_specs=[vmem] * len(out_shape),
        scratch_shapes=scratch,
        compiler_params=pltpu.CompilerParams(
            collective_id=cid, has_side_effects=True, vmem_limit_bytes=VMEM_CAP
        ),
        cost_estimate=cost_of(time),
        name=name,
    )
    return list(call(*args))


def head_stats_kernel(block, tile, early, early_ref, late_ref, final_ref, wanted_ref, edge_ref, exp_ref, top_ref, sum_ref, pick_ref):
    j = pl.program_id(0)
    tokens = final_ref.shape[0]
    place = j * block + lax.broadcasted_iota(jnp.int32, (block, 1), 0)
    valid = place < edge_ref[0]
    table = jnp.where(j < early, early_ref[...], late_ref[...])

    def weigh(masked):
        for start in range(0, tokens, tile):
            at = pl.ds(start, tile)
            logits = lax.dot_general(
                table,
                final_ref[at, :],
                (((1,), (1,)), ((), ())),
                preferred_element_type=jnp.float32,
            )
            if masked:
                logits = jnp.where(valid, logits, MASKED)
            top = jnp.max(logits, axis=0, keepdims=True)
            weights = jnp.exp(logits - top)
            exp_ref[:, at] = weights.astype(jnp.bfloat16)
            top_ref[0, :, at] = top
            sum_ref[0, :, at] = jnp.sum(weights, axis=0, keepdims=True)
            pick_ref[0, :, at] = jnp.sum(
                jnp.where(place == wanted_ref[:, at], logits, 0.0), axis=0, keepdims=True
            )

    whole = (j + 1) * block <= edge_ref[0]

    @pl.when(whole)
    def _():
        weigh(False)

    @pl.when(jnp.logical_not(whole))
    def _():
        weigh(True)


def head_stats(tables, final, wanted, edge, block, tile=512):
    early = tables[0].shape[0] // block
    rows = sum(table.shape[0] for table in tables)
    width = tables[0].shape[1]
    tokens = final.shape[0]
    steps = rows // block
    row = jax.ShapeDtypeStruct((steps, 1, tokens), jnp.float32)
    row_spec = pl.BlockSpec((1, 1, tokens), lambda j: (j, 0, 0))
    return pl.pallas_call(
        functools.partial(head_stats_kernel, block, tile, early),
        grid=(steps,),
        out_shape=[jax.ShapeDtypeStruct((steps * block, tokens), jnp.bfloat16), row, row, row],
        in_specs=[
            pl.BlockSpec((block, width), lambda j: (jnp.minimum(j, early - 1), 0)),
            pl.BlockSpec((block, width), lambda j: (jnp.maximum(j - early, 0), 0)),
            pl.BlockSpec((tokens, width), lambda j: (0, 0)),
            pl.BlockSpec((1, tokens), lambda j: (0, 0)),
            pl.BlockSpec(memory_space=pltpu.SMEM),
        ],
        out_specs=[pl.BlockSpec((block, tokens), lambda j: (j, 0)), row_spec, row_spec, row_spec],
        compiler_params=pltpu.CompilerParams(vmem_limit_bytes=56 * 2**20),
        cost_estimate=pl.CostEstimate(
            flops=2 * rows * width * tokens,
            bytes_accessed=2 * rows * (width + tokens),
            transcendentals=rows * tokens,
        ),
        name="head_stats",
    )(*tables, final, wanted, edge)


def head_back_kernel(block, tile, exp_ref, final_ref, scale_ref, weight_ref, wanted_ref, dl_ref, grad_ref):
    j = pl.program_id(0)
    tokens = final_ref.shape[0]
    place = j * block + lax.broadcasted_iota(jnp.int32, (block, 1), 0)
    for start in range(0, tokens, tile):
        at = pl.ds(start, tile)
        dl = exp_ref[:, at].astype(jnp.float32) * scale_ref[0, :, at]
        dl = dl - jnp.where(place == wanted_ref[:, at], weight_ref[:, at], 0.0)
        dl_ref[:, at] = dl.astype(jnp.bfloat16)
    strip = block // max(1, block // 256)
    for start in range(0, block, strip):
        at = pl.ds(start, strip)
        grad_ref[at, :] = jnp.dot(
            dl_ref[at, :], final_ref[...], preferred_element_type=jnp.float32
        ).astype(jnp.bfloat16)


def head_back(exps, final, scale, weight, wanted, block, tile=256):
    rows, tokens = exps.shape
    width = final.shape[1]
    return pl.pallas_call(
        functools.partial(head_back_kernel, block, tile),
        grid=(rows // block,),
        out_shape=[
            jax.ShapeDtypeStruct((rows, tokens), jnp.bfloat16),
            jax.ShapeDtypeStruct((rows, width), jnp.bfloat16),
        ],
        in_specs=[
            pl.BlockSpec((block, tokens), lambda j: (j, 0)),
            pl.BlockSpec((tokens, width), lambda j: (0, 0)),
            pl.BlockSpec((1, 1, tokens), lambda j: (j, 0, 0)),
            pl.BlockSpec((1, tokens), lambda j: (0, 0)),
            pl.BlockSpec((1, tokens), lambda j: (0, 0)),
        ],
        out_specs=[
            pl.BlockSpec((block, tokens), lambda j: (j, 0)),
            pl.BlockSpec((block, width), lambda j: (j, 0)),
        ],
        compiler_params=pltpu.CompilerParams(vmem_limit_bytes=56 * 2**20),
        cost_estimate=pl.CostEstimate(
            flops=2 * rows * width * tokens,
            bytes_accessed=2 * rows * (width + 2 * tokens),
            transcendentals=0,
        ),
        name="head_back",
    )(exps, final, scale, weight, wanted)


def head_weights(mixed_ref, starts_ref, base, at, seen):
    query = mixed_ref[at : at + QUERIES, base : base + HD]
    keys = mixed_ref[0:seen, base + HD : base + 2 * HD]
    values = mixed_ref[0:seen, base + 2 * HD : base + 3 * HD]
    scores = lax.dot_general(
        query, keys, (((1,), (1,)), ((), ())), preferred_element_type=jnp.float32
    )
    row = at + lax.broadcasted_iota(jnp.int32, (QUERIES, seen), 0)
    column = lax.broadcasted_iota(jnp.int32, (QUERIES, seen), 1)
    allowed = (column <= row) & (column >= starts_ref[at : at + QUERIES, :])
    scores = jnp.where(allowed, scores * HD ** (-0.5), MASKED)
    weights = jnp.exp(scores - jnp.max(scores, axis=1, keepdims=True))
    probs = weights / jnp.sum(weights, axis=1, keepdims=True)
    return query, keys, values, probs


def attend_kernel(mixed_ref, starts_ref, out_ref):
    length = mixed_ref.shape[0]
    for at in range(0, length, QUERIES):
        found = []
        for head in range(2):
            unused, unused, values, probs = head_weights(
                mixed_ref, starts_ref, head * 3 * HD, at, at + QUERIES
            )
            found.append(
                jnp.dot(probs.astype(jnp.bfloat16), values, preferred_element_type=jnp.float32)
            )
        out_ref[at : at + QUERIES, :] = jnp.concatenate(found, axis=1).astype(jnp.bfloat16)


def attend(mixed, starts):
    length, columns = mixed.shape
    pairs = columns // (6 * HD)
    return pl.pallas_call(
        attend_kernel,
        grid=(pairs,),
        out_shape=jax.ShapeDtypeStruct((length, pairs * 2 * HD), jnp.bfloat16),
        in_specs=[
            pl.BlockSpec((length, 6 * HD), lambda j: (0, j)),
            pl.BlockSpec((length, 1), lambda j: (0, 0)),
        ],
        out_specs=pl.BlockSpec((length, 2 * HD), lambda j: (0, j)),
        compiler_params=pltpu.CompilerParams(vmem_limit_bytes=40 * 2**20),
        cost_estimate=pl.CostEstimate(
            flops=8 * pairs * length * length * HD,
            bytes_accessed=2 * length * columns,
            transcendentals=pairs * length * length,
        ),
        name="attend",
    )(mixed, starts)


def attend_back_kernel(mixed_ref, starts_ref, upstream_ref, out_ref, sums_ref):
    length = mixed_ref.shape[0]
    sums_ref[...] = jnp.zeros_like(sums_ref)
    rows = (((0,), (0,)), ((), ()))
    for at in range(0, length, QUERIES):
        seen = at + QUERIES
        for head in range(2):
            base = head * 3 * HD
            query, keys, values, probs = head_weights(mixed_ref, starts_ref, base, at, seen)
            upstream = upstream_ref[at:seen, head * HD : head * HD + HD]
            dprobs = lax.dot_general(
                upstream, values, (((1,), (1,)), ((), ())), preferred_element_type=jnp.float32
            )
            inner = jnp.sum(probs * dprobs, axis=1, keepdims=True)
            dscores = (probs * (dprobs - inner)).astype(jnp.bfloat16)
            dquery = jnp.dot(dscores, keys, preferred_element_type=jnp.float32)
            dkeys = lax.dot_general(dscores, query, rows, preferred_element_type=jnp.float32)
            dvalues = lax.dot_general(
                probs.astype(jnp.bfloat16), upstream, rows, preferred_element_type=jnp.float32
            )
            sums_ref[at:seen, base : base + HD] = dquery * HD ** (-0.5)
            sums_ref[0:seen, base + HD : base + 2 * HD] += dkeys * HD ** (-0.5)
            sums_ref[0:seen, base + 2 * HD : base + 3 * HD] += dvalues
    out_ref[...] = sums_ref[...].astype(jnp.bfloat16)


def attend_back(mixed, starts, upstream):
    length, columns = mixed.shape
    pairs = columns // (6 * HD)
    return pl.pallas_call(
        attend_back_kernel,
        grid=(pairs,),
        out_shape=jax.ShapeDtypeStruct((length, columns), jnp.bfloat16),
        in_specs=[
            pl.BlockSpec((length, 6 * HD), lambda j: (0, j)),
            pl.BlockSpec((length, 1), lambda j: (0, 0)),
            pl.BlockSpec((length, 2 * HD), lambda j: (0, j)),
        ],
        out_specs=pl.BlockSpec((length, 6 * HD), lambda j: (0, j)),
        scratch_shapes=[pltpu.VMEM((length, 6 * HD), jnp.float32)],
        compiler_params=pltpu.CompilerParams(vmem_limit_bytes=40 * 2**20),
        cost_estimate=pl.CostEstimate(
            flops=20 * pairs * length * length * HD,
            bytes_accessed=4 * length * columns,
            transcendentals=pairs * length * length,
        ),
        name="attend_back",
    )(mixed, starts, upstream)


def small_gather_kernel(axis, count, src_ref, out_ref, send, recv):
    dp = lax.axis_index("dp")
    mp = lax.axis_index("mp")
    me = dp if axis == "dp" else mp

    def device(peer):
        return (peer, mp) if axis == "dp" else (dp, peer)

    barrier = pltpu.get_barrier_semaphore()
    for hop in range(1, count):
        pl.semaphore_signal(
            barrier, inc=1, device_id=device(lax.rem(me + hop, count)), device_id_type=MESH
        )
    pl.semaphore_wait(barrier, count - 1)
    copies = []
    for hop in range(1, count):
        peer = lax.rem(me + hop, count)
        copy = pltpu.make_async_remote_copy(
            src_ref=src_ref,
            dst_ref=out_ref.at[me],
            send_sem=send.at[hop],
            recv_sem=recv.at[hop],
            device_id=device(peer),
            device_id_type=MESH,
        )
        copy.start()
        copies.append(copy)
    out_ref[me] = src_ref[...]
    for copy in copies:
        copy.wait()


def small_gather(name, cid, values, axis):
    count = lax.axis_size(axis)
    vmem = pl.BlockSpec(memory_space=pltpu.VMEM)
    return pl.pallas_call(
        functools.partial(small_gather_kernel, axis, count),
        out_shape=jax.ShapeDtypeStruct((count,) + values.shape, values.dtype),
        in_specs=[vmem],
        out_specs=vmem,
        scratch_shapes=[pltpu.SemaphoreType.DMA((count,)), pltpu.SemaphoreType.DMA((count,))],
        compiler_params=pltpu.CompilerParams(collective_id=cid, has_side_effects=True),
        cost_estimate=cost_of(6),
        name=name,
    )(values)


def exchange(axis, me, here, source, slots, send, recv, first):
    count = slots.shape[0]
    copies = []
    for hop in range(1, count):
        peer = lax.rem(me + hop, count)
        copy = pltpu.make_async_remote_copy(
            src_ref=source,
            dst_ref=slots.at[me],
            send_sem=send.at[first + hop],
            recv_sem=recv.at[first + hop],
            device_id=(peer, here) if axis == "dp" else (here, peer),
            device_id_type=MESH,
        )
        copy.start()
        copies.append(copy)
    slots[me] = source[...]
    for copy in copies:
        copy.wait()
    total = slots[0]
    for index in range(1, count):
        total = total + slots[index]
    return total


def greet_all(dp, mp, size_dp, size_mp):
    barrier = pltpu.get_barrier_semaphore()
    for hop in range(1, size_dp):
        pl.semaphore_signal(
            barrier, inc=1, device_id=(lax.rem(dp + hop, size_dp), mp), device_id_type=MESH
        )
    for hop in range(1, size_mp):
        pl.semaphore_signal(
            barrier, inc=1, device_id=(dp, lax.rem(mp + hop, size_mp)), device_id_type=MESH
        )
    pl.semaphore_wait(barrier, size_dp + size_mp - 2)


def lane_rows(values):
    values = values.reshape(-1)
    return jnp.pad(values, (0, -values.size % 128)).reshape(-1, 128)


def fold(values):
    return jnp.sum(values, axis=0, keepdims=True)


def stats_kernel(full, size_dp, size_mp, *refs):
    row_part, row_old, col_part, col_old, weight_sq = (refs[5 * n : 5 * n + 5] for n in range(5))
    loss_part, norm_one, norm_two, norm_three, norms, second_old = refs[25:31]
    refs = refs[31:]
    row_out, col_out = refs[0:5], refs[5:10]
    loss_out, grads_out, second_out, norms_out, rate_out = refs[10:15]
    send_dp, slots_dp, send_mp, slots_mp, parts, part_slots, whole, send, recv = refs[15:]
    dp = lax.axis_index("dp")
    mp = lax.axis_index("mp")
    greet_all(dp, mp, size_dp, size_mp)
    beta = 1.0 - STEP ** (-0.8)
    width = norms.shape[1]

    at = 0
    marks = []

    def put(values):
        nonlocal at
        rows = values.shape[0]
        send_dp[at : at + rows, :] = values
        marks.append((at, rows))
        at += rows

    norm_rows = width // 128
    for ref in (norm_one, norm_two, norm_three):
        for which in range(2):
            for piece in range(norm_rows):
                put(ref[which : which + 1, piece * 128 : piece * 128 + 128])
    marks.clear()
    count_norm = at
    for index in (0, 2, 4):
        put(row_part[index][...])
    for index in (1, 3):
        put(col_part[index][...])
    put(loss_part[...])
    for index in (1, 3):
        put(fold(row_old[index][...]))
    for index in range(5):
        put(fold(weight_sq[index][...]))
    if at < send_dp.shape[0]:
        send_dp[at:, :] = jnp.zeros((send_dp.shape[0] - at, 128), jnp.float32)
    over_dp = exchange("dp", dp, mp, send_dp, slots_dp, send, recv, 0)
    taken = [over_dp[start : start + rows] for start, rows in marks]
    loss_out[...] = taken[5]
    row_full = {0: taken[0], 2: taken[1], 4: taken[2]}
    col_full = {1: taken[3], 3: taken[4]}
    old_total = {1: taken[6], 3: taken[7]}
    weight_rows = taken[8:13]

    at = 0
    marks = []

    def put_mp(values):
        nonlocal at
        rows = values.shape[0]
        send_mp[at : at + rows, :] = values
        marks.append((at, rows))
        at += rows

    for index in (0, 2, 4):
        put_mp(col_part[index][...])
    for index in (1, 3):
        put_mp(row_part[index][...])
    for index in range(5):
        put_mp(fold(row_full[index] if index in row_full else col_full[index]))
    for index in (0, 2, 4):
        put_mp(fold(row_old[index][...]))
    for index in range(5):
        put_mp(weight_rows[index])
    if at < send_mp.shape[0]:
        send_mp[at:, :] = jnp.zeros((send_mp.shape[0] - at, 128), jnp.float32)
    each = count_norm // size_mp
    for index in range(size_mp):
        parts[index] = over_dp[index * each : index * each + each]
    first = size_dp + size_mp
    copies = []
    for hop in range(1, size_mp):
        peer = lax.rem(mp + hop, size_mp)
        copy = pltpu.make_async_remote_copy(
            src_ref=parts.at[peer],
            dst_ref=part_slots.at[mp],
            send_sem=send.at[first + hop],
            recv_sem=recv.at[first + hop],
            device_id=(dp, peer),
            device_id_type=MESH,
        )
        copy.start()
        copies.append(copy)
    part_slots[mp] = parts[mp]
    over_mp = exchange("mp", mp, dp, send_mp, slots_mp, send, recv, size_dp)
    for copy in copies:
        copy.wait()
    summed = part_slots[0]
    for index in range(1, size_mp):
        summed = summed + part_slots[index]
    whole[mp] = summed
    first += size_mp
    copies = []
    for hop in range(1, size_mp):
        peer = lax.rem(mp + hop, size_mp)
        copy = pltpu.make_async_remote_copy(
            src_ref=whole.at[mp],
            dst_ref=whole.at[mp],
            send_sem=send.at[first + hop],
            recv_sem=recv.at[first + hop],
            device_id=(dp, peer),
            device_id_type=MESH,
        )
        copies.append(copy)
    for copy in copies:
        copy.start()
    taken = [over_mp[start : start + rows] for start, rows in marks]
    for slot, index in enumerate((0, 2, 4)):
        col_full[index] = taken[slot]
        old_total[index] = taken[10 + slot]
    for slot, index in enumerate((1, 3)):
        row_full[index] = taken[3 + slot]
    square_total = taken[5:10]
    weight_total = taken[13:18]
    for index in range(5):
        full_rows, full_cols = full[index]
        row_new = beta * row_old[index][...] + (1.0 - beta) * row_full[index] / full_cols
        col_new = beta * col_old[index][...] + (1.0 - beta) * col_full[index] / full_rows
        row_out[index][...] = row_new
        col_out[index][...] = col_new
        mean = (
            beta * jnp.sum(old_total[index], axis=1, keepdims=True)
            + (1.0 - beta) * jnp.sum(square_total[index], axis=1, keepdims=True) / full_cols
        ) / full_rows
        rate = RHO * jnp.sqrt(
            jnp.sum(weight_total[index], axis=1, keepdims=True) / (full_rows * full_cols)
        )
        rate_out[index : index + 1, :] = jnp.broadcast_to(mean, (1, 128))
        rate_out[8 + index : 9 + index, :] = jnp.broadcast_to(rate, (1, 128))
    for copy in copies:
        copy.wait()
    for row in range(6):
        for piece in range(norm_rows):
            place = row * norm_rows + piece
            grads_out[row : row + 1, piece * 128 : piece * 128 + 128] = whole[
                place // each, place % each : place % each + 1, :
            ]
    grad = grads_out[...]
    second = beta * second_old[...] + (1.0 - beta) * (grad * grad + EPS_ONE)
    second_out[...] = second
    step = grad * lax.rsqrt(second)
    entries = step.size

    def mean_square(values):
        return jnp.sum(jnp.sum(values * values, axis=0, keepdims=True), axis=1, keepdims=True) / (
            entries
        )

    step = step / jnp.maximum(1.0, jnp.sqrt(mean_square(step)) / CLIP)
    old = norms[...]
    norms_out[...] = old - RHO * jnp.sqrt(mean_square(old)) * step


def update_stats(cid, row_parts, rows_old, col_parts, cols_old, weight_sq, loss, norm_parts, norms, second, full):
    size_dp = lax.axis_size("dp")
    size_mp = lax.axis_size("mp")
    f32 = jnp.float32
    rows_old2 = [lane_rows(v) for v in rows_old]
    cols_old2 = [lane_rows(v) for v in cols_old]
    args = (
        [lane_rows(v) for v in row_parts]
        + rows_old2
        + [lane_rows(v) for v in col_parts]
        + cols_old2
        + [v if v.ndim == 2 else lane_rows(v) for v in weight_sq]
        + [lane_rows(loss)]
        + list(norm_parts)
        + [norms, second]
    )
    width = norms.shape[1]
    count_norm = 6 * width // 128
    size_a = count_norm + sum(rows_old2[n].shape[0] for n in (0, 2, 4))
    size_a += sum(cols_old2[n].shape[0] for n in (1, 3)) + 8
    size_a += -size_a % 8
    size_b = sum(cols_old2[n].shape[0] for n in (0, 2, 4))
    size_b += sum(rows_old2[n].shape[0] for n in (1, 3)) + 13
    size_b += -size_b % 8
    each = count_norm // size_mp
    out_shape = [jax.ShapeDtypeStruct(v.shape, f32) for v in rows_old2 + cols_old2]
    out_shape += [
        jax.ShapeDtypeStruct((1, 128), f32),
        jax.ShapeDtypeStruct(norms.shape, f32),
        jax.ShapeDtypeStruct(norms.shape, f32),
        jax.ShapeDtypeStruct(norms.shape, f32),
        jax.ShapeDtypeStruct((16, 128), f32),
    ]
    sems = size_dp + 3 * size_mp
    vmem = pl.BlockSpec(memory_space=pltpu.VMEM)
    found = pl.pallas_call(
        functools.partial(stats_kernel, full, size_dp, size_mp),
        out_shape=out_shape,
        in_specs=[vmem] * len(args),
        out_specs=[vmem] * len(out_shape),
        scratch_shapes=[
            pltpu.VMEM((size_a, 128), f32),
            pltpu.VMEM((size_dp, size_a, 128), f32),
            pltpu.VMEM((size_b, 128), f32),
            pltpu.VMEM((size_mp, size_b, 128), f32),
            pltpu.VMEM((size_mp, each, 128), f32),
            pltpu.VMEM((size_mp, each, 128), f32),
            pltpu.VMEM((size_mp, each, 128), f32),
            pltpu.SemaphoreType.DMA((sems,)),
            pltpu.SemaphoreType.DMA((sems,)),
        ],
        compiler_params=pltpu.CompilerParams(collective_id=cid, has_side_effects=True),
        cost_estimate=cost_of(12),
        name="update_stats",
    )(*args)
    rows_new = [found[n].reshape(-1)[: rows_old[n].size] for n in range(5)]
    cols_new = [found[5 + n].reshape(-1)[: cols_old[n].size] for n in range(5)]
    loss_sums = found[10][0, :NSRC]
    return rows_new, cols_new, loss_sums, found[11], found[12], found[13], found[14]


def clip_kernel(entries, size_dp, size_mp, *refs):
    parts, rate = refs[:5], refs[5]
    out, mine, slots_dp, slots_mp, send, recv = refs[6:]
    dp = lax.axis_index("dp")
    mp = lax.axis_index("mp")
    greet_all(dp, mp, size_dp, size_mp)
    mine[...] = jnp.zeros_like(mine)
    for index in range(5):
        mine[index : index + 1, :] = fold(parts[index][...])
    mine[...] = exchange("dp", dp, mp, mine, slots_dp, send, recv, 0)
    total = exchange("mp", mp, dp, mine, slots_mp, send, recv, size_dp)
    total = jnp.sum(total, axis=1, keepdims=True)
    for index in range(5):
        clip = jnp.maximum(1.0, jnp.sqrt(total[index : index + 1] / entries[index]) / CLIP)
        out[index : index + 1, :] = rate[8 + index : 9 + index, :] / clip


def clip_rates(cid, step_parts, rate, entries):
    size_dp = lax.axis_size("dp")
    size_mp = lax.axis_size("mp")
    vmem = pl.BlockSpec(memory_space=pltpu.VMEM)
    sems = size_dp + size_mp
    return pl.pallas_call(
        functools.partial(clip_kernel, entries, size_dp, size_mp),
        out_shape=jax.ShapeDtypeStruct((8, 128), jnp.float32),
        in_specs=[vmem] * 6,
        out_specs=vmem,
        scratch_shapes=[
            pltpu.VMEM((8, 128), jnp.float32),
            pltpu.VMEM((size_dp, 8, 128), jnp.float32),
            pltpu.VMEM((size_mp, 8, 128), jnp.float32),
            pltpu.SemaphoreType.DMA((sems,)),
            pltpu.SemaphoreType.DMA((sems,)),
        ],
        compiler_params=pltpu.CompilerParams(collective_id=cid, has_side_effects=True),
        cost_estimate=cost_of(8),
        name="clip_rates",
    )(*[lane_rows(v) for v in step_parts], rate)


UNROLL = 8


def lookup_kernel(shift, early, count_ref, key_ref, table_ref, out_ref, low_ref, square_ref, rows_ref):
    spots = out_ref.shape[0]
    vocab, width = table_ref.shape
    rows_ref[...] = jnp.zeros_like(rows_ref)

    def some(i, carry):
        for j in range(UNROLL):
            key = key_ref[i * UNROLL + j]
            place = key & ((1 << shift) - 1)
            rows_ref[pl.ds(place, 1), :] = table_ref[pl.ds(key >> shift, 1), :]
        return carry

    lax.fori_loop(0, (count_ref[0] + UNROLL - 1) // UNROLL, some, 0)

    def narrow(i, carry):
        at = pl.ds(pl.multiple_of(i * 256, 256), 256)
        out_ref[at, :] = rows_ref[at, :].astype(jnp.bfloat16)
        return carry

    lax.fori_loop(0, spots // 256, narrow, 0)
    strip = 64
    rest = vocab % strip
    done = vocab - rest
    low_ref[done - early :, :] = jnp.zeros(
        (low_ref.shape[0] - done + early, width), jnp.bfloat16
    )

    def squares(values, total):
        for row in range(0, values.shape[0], 8):
            piece = values[row : row + 8, :]
            total = total + piece * piece
        return total

    def lower(i, total):
        at = pl.ds(pl.multiple_of(i * strip, strip), strip)
        values = table_ref[at, :]
        start = pl.multiple_of(i * strip - early, strip)
        low_ref[pl.ds(start, strip), :] = values.astype(jnp.bfloat16)
        return squares(values, total)

    def square(i, total):
        at = pl.ds(pl.multiple_of(i * strip, strip), strip)
        return squares(table_ref[at, :], total)

    total = jnp.zeros((8, width), jnp.float32)
    total = lax.fori_loop(0, early // strip, square, total)
    total = lax.fori_loop(early // strip, done // strip, lower, total)
    if rest:
        values = table_ref[done:, :]
        total = squares(values, total)
        values = jnp.concatenate([values, jnp.zeros((strip - rest, width), jnp.float32)])
        low_ref[done - early : done - early + strip, :] = values.astype(jnp.bfloat16)
    folded = total[:, 0:128]
    for start in range(128, width, 128):
        folded = folded + total[:, start : start + 128]
    square_ref[...] = folded


def lookup(keys, count, table, spots, shift, early):
    vocab, width = table.shape
    smem = pl.BlockSpec(memory_space=pltpu.SMEM)
    vmem = pl.BlockSpec(memory_space=pltpu.VMEM)
    return pl.pallas_call(
        functools.partial(lookup_kernel, shift, early),
        out_shape=[
            jax.ShapeDtypeStruct((spots, width), jnp.bfloat16),
            jax.ShapeDtypeStruct((vocab + -vocab % HEAD_BLOCK - early, width), jnp.bfloat16),
            jax.ShapeDtypeStruct((8, 128), jnp.float32),
        ],
        in_specs=[smem, smem, vmem],
        out_specs=[vmem] * 3,
        scratch_shapes=[pltpu.VMEM((spots + 8, width), jnp.float32)],
        compiler_params=pltpu.CompilerParams(vmem_limit_bytes=VMEM_CAP),
        cost_estimate=cost_of(20),
        name="lookup",
    )(count, keys, table)


def scatter_kernel(shift, count_ref, key_ref, head_ref, rows_in_ref, grad_ref, rows_ref):
    spots = rows_in_ref.shape[0]
    width = grad_ref.shape[1]

    def widen(i, carry):
        at = pl.ds(pl.multiple_of(i * 256, 256), 256)
        rows_ref[at, :] = rows_in_ref[at, :].astype(jnp.float32)
        return carry

    lax.fori_loop(0, spots // 256, widen, 0)
    rows_ref[spots:, :] = jnp.zeros((8, width), jnp.float32)
    grad_ref[...] = head_ref[...].astype(jnp.float32)[: grad_ref.shape[0]]

    def some(i, carry):
        for j in range(UNROLL):
            key = key_ref[i * UNROLL + j]
            place = key & ((1 << shift) - 1)
            grad_ref[pl.ds(key >> shift, 1), :] += rows_ref[pl.ds(place, 1), :]
        return carry

    lax.fori_loop(0, (count_ref[0] + UNROLL - 1) // UNROLL, some, 0)


def scatter(keys, count, head_grad, rows, vocab, shift):
    spots, width = rows.shape
    smem = pl.BlockSpec(memory_space=pltpu.SMEM)
    vmem = pl.BlockSpec(memory_space=pltpu.VMEM)
    return pl.pallas_call(
        functools.partial(scatter_kernel, shift),
        out_shape=jax.ShapeDtypeStruct((vocab, width), jnp.float32),
        in_specs=[smem, smem, vmem, vmem],
        out_specs=vmem,
        scratch_shapes=[pltpu.VMEM((spots + 8, width), jnp.float32)],
        compiler_params=pltpu.CompilerParams(vmem_limit_bytes=VMEM_CAP),
        cost_estimate=cost_of(23),
        name="scatter",
    )(count, keys, head_grad, rows)


def norm_parts(values):
    centre = jnp.mean(values, axis=-1, keepdims=True)
    centred = values - centre
    scale = lax.rsqrt(jnp.mean(centred * centred, axis=-1, keepdims=True) + EPS_NORM)
    return centred * scale, scale


def norm_pull(values, gain, upstream):
    normed, scale = norm_parts(values)
    weighted = upstream * gain
    pulled = scale * (
        weighted
        - jnp.mean(weighted, axis=-1, keepdims=True)
        - normed * jnp.mean(weighted * normed, axis=-1, keepdims=True)
    )
    return (
        pulled,
        jnp.sum(upstream * normed, axis=0, keepdims=True),
        jnp.sum(upstream, axis=0, keepdims=True),
    )


def step_first(total, at, ins, outs):
    stream, norms = outs[0], ins[0]
    normed, scale = norm_parts(stream[at, :].astype(jnp.float32))
    return normed * norms[0:1, :] + norms[1:2, :]


def step_forward(row, total, at, ins, outs):
    stream, norms = ins
    values = stream[at, :].astype(jnp.float32) + total
    outs[0][at, :] = values
    normed, scale = norm_parts(values)
    return normed * norms[row : row + 1, :] + norms[row + 1 : row + 2, :]


def step_backward(row, total, at, ins, outs):
    stream, norms = ins[:2]
    pulled, dgain, dshift = norm_pull(
        stream[at, :].astype(jnp.float32), norms[row : row + 1, :], total
    )
    if len(ins) > 2:
        pulled = pulled + ins[2][at, :]
    if len(outs) > 1:
        outs[0][at, :] = pulled
    sums = outs[-1]

    @pl.when(at.start == 0)
    def _():
        sums[...] = jnp.zeros_like(sums)

    sums[0:1, :] += dgain
    sums[1:2, :] += dshift
    return pulled


def gelu_tanh(values):
    return jax.nn.gelu(values, approximate=True)


def local(
    token_ids,
    targets,
    starts,
    sources,
    embedding,
    w_qkv,
    w_out,
    w_fc,
    w_proj,
    norm_params,
    rows_table,
    cols_table,
    rows_qkv,
    cols_qkv,
    rows_out,
    cols_out,
    rows_fc,
    cols_fc,
    rows_proj,
    cols_proj,
    second_norms,
):
    bf16 = jnp.bfloat16
    f32 = jnp.float32
    size_mp = lax.axis_size("mp")
    size_dp = lax.axis_size("dp")
    dp = lax.axis_index("dp")
    mp = lax.axis_index("mp")
    tokens = token_ids.shape[0]
    seqs = tokens // LEN
    chips = size_mp // 2
    near = chips // seqs
    sharers = size_mp // seqs
    rows = tokens // size_mp
    vocab, part_width = embedding.shape
    width = part_width * size_dp
    first_row = mp * vocab
    spots = tokens * size_dp
    chunks_full = max(1, min(8, rows // 32))
    chunks_near = max(1, min(4, rows // 32))
    chunks_turn = max(1, min(4, rows // 32))

    def own_and_twins(weights, axis):
        low = [weight.astype(bf16) for weight in weights]
        found = [[weight] for weight in low]
        sent = jnp.concatenate(low, axis=axis)
        for turn in range(1, seqs):
            shift = [(i, (i + turn * sharers) % size_mp) for i in range(size_mp)]
            arrived = lax.ppermute(sent, "mp", shift)
            start = 0
            for index, weight in enumerate(low):
                size = weight.shape[axis]
                found[index].append(lax.slice_in_dim(arrived, start, start + size, axis=axis))
                start += size
        return [jnp.concatenate(pieces, axis=axis) for pieces in found]

    pair_fc, pair_qkv = own_and_twins((w_fc, w_qkv), 1)
    pair_proj, pair_out = own_and_twins((w_proj, w_out), 0)

    early = (vocab + -vocab % HEAD_BLOCK) * 2 // (10 * HEAD_BLOCK) * HEAD_BLOCK
    early_table = lax.all_gather(embedding[:early].astype(bf16), "dp", axis=1, tiled=True)

    both = jnp.stack([token_ids, sources]).reshape(-1, 128)
    both = small_gather("gather_ids", 0, both, "dp").reshape(size_dp, 2, tokens)
    all_ids = both[:, 0]
    all_sources = both[:, 1].reshape(-1)
    counts = jnp.sum(
        (all_sources[:, None] == jnp.arange(NSRC, dtype=jnp.int32)[None, :]).astype(f32), axis=0
    )

    piece = rows // chunks_turn
    token = jnp.arange(tokens, dtype=jnp.int32)
    place = (
        token // piece * (size_dp * piece)
        + (jnp.arange(size_dp, dtype=jnp.int32) * piece)[:, None]
        + token % piece
    )
    local_ids = all_ids - first_row
    inside = (local_ids >= 0) & (local_ids < vocab)
    shift = spots.bit_length()
    idle = ((vocab - 1) << shift) + spots
    keys = jnp.where(inside, (local_ids << shift) + place, idle)
    keys = jnp.sort(keys.reshape(-1))
    owned = jnp.sum(inside.astype(jnp.int32)).reshape(1)
    found, low_table, table_sq = lookup(keys, owned, embedding, spots, shift, early)
    found, early_table = lax.optimization_barrier((found, early_table))
    inner_one, stream0, wide_qkv, wide_out, wide_fc, wide_proj = line_call(
        "lookup_sum",
        1,
        found,
        [norm_params],
        [jax.ShapeDtypeStruct((rows, width), bf16)],
        step_first,
        size_dp * rows,
        part_width,
        chunks_turn,
        chips,
        near,
        70,
        [
            ("gather", 0, pair_qkv),
            ("gather", 1, pair_out),
            ("gather", 0, pair_fc),
            ("gather", 1, pair_proj),
        ],
        "gather",
        8,
    )
    low_table, inner_one = lax.optimization_barrier((low_table, inner_one))
    wide_table = (early_table, lax.all_gather(low_table, "dp", axis=1, tiled=True))
    row_f32 = jax.ShapeDtypeStruct((rows, width), f32)
    pair_f32 = jax.ShapeDtypeStruct((8, width), f32)
    my_starts = row_slice(starts, (mp // sharers) * LEN, LEN)[:, None]
    mixed = jnp.dot(inner_one, wide_qkv, preferred_element_type=f32).astype(bf16)
    attended = attend(mixed, my_starts)
    partial = jnp.dot(attended, wide_out, preferred_element_type=f32).astype(bf16)
    inner_two, stream1 = line_call(
        "attn_sum",
        3,
        partial,
        [stream0, norm_params],
        [row_f32],
        functools.partial(step_forward, 2),
        rows,
        width,
        chunks_near,
        near,
        near,
        32,
    )
    before = jnp.dot(inner_two, wide_fc, preferred_element_type=f32)
    hidden = gelu_tanh(before).astype(bf16)
    partial = jnp.dot(hidden, wide_proj, preferred_element_type=f32).astype(bf16)
    final, stream2 = line_call(
        "mlp_sum",
        4,
        partial,
        [stream1, norm_params],
        [row_f32],
        functools.partial(step_forward, 4),
        rows,
        width,
        chunks_full,
        near,
        chips,
        58,
        chunk_major=True,
    )

    edge = jnp.clip(VREAL - first_row, 0, vocab).astype(jnp.int32).reshape(1)

    def by_chunk(values):
        return values.reshape(size_mp, chunks_full, -1).swapaxes(0, 1).reshape(tokens)

    sources = by_chunk(sources)
    wanted = by_chunk(targets) - first_row
    wanted = jnp.where((wanted >= 0) & (wanted < vocab), wanted, -1).reshape(1, tokens)
    block = HEAD_BLOCK
    exps, tops, sums, picks = head_stats(wide_table, final, wanted, edge, block)
    tops = tops[:, 0]
    top = jnp.max(tops, axis=0)
    total = jnp.sum(sums[:, 0] * jnp.exp(tops - top[None, :]), axis=0)
    pick = jnp.sum(picks[:, 0], axis=0)
    stats = jnp.concatenate([v.reshape(-1, 128) for v in (top, total, pick)])
    stats = small_gather("gather_stats", 5, stats, "mp").reshape(size_mp, 3, tokens)
    highest = jnp.max(stats[:, 0], axis=0)
    log_total = highest + jnp.log(
        jnp.sum(stats[:, 1] * jnp.exp(stats[:, 0] - highest[None, :]), axis=0)
    )
    token_loss = log_total - jnp.sum(stats[:, 2], axis=0)
    member = (sources[:, None] == jnp.arange(NSRC, dtype=jnp.int32)[None, :]).astype(f32)
    loss_part = jnp.sum(member * token_loss[:, None], axis=0)
    weight = jnp.sum(member / (NSRC * jnp.maximum(counts, 1.0))[None, :], axis=1)
    scale = jnp.exp(tops - log_total[None, :]) * weight[None, :]
    dlogits, table_grad = head_back(
        exps, final, scale[:, None, :], weight[None, :], wanted, block
    )
    head_grad = lax.psum_scatter(table_grad, "dp", scatter_dimension=1, tiled=True)

    dbranch2, dstream2, norm3 = line_call(
        "final_back",
        6,
        (dlogits, *wide_table),
        [stream2, norm_params],
        [row_f32, pair_f32],
        functools.partial(step_backward, 4),
        rows,
        width,
        chunks_full,
        chips,
        near,
        65,
        product=True,
    )
    grad_proj = jnp.einsum("tf,td->fd", hidden, dbranch2, preferred_element_type=f32).astype(bf16)
    dhidden = jnp.einsum("td,fd->tf", dbranch2, wide_proj, preferred_element_type=f32)
    unused, gelu_pull = jax.vjp(gelu_tanh, before)
    dbefore = gelu_pull(dhidden)[0].astype(bf16)
    partial = jnp.einsum("tf,df->td", dbefore, wide_fc, preferred_element_type=f32).astype(bf16)
    partial, grad_proj = lax.optimization_barrier((partial, grad_proj))
    dbranch1, dstream1, norm2 = line_call(
        "mlp_back",
        7,
        partial,
        [stream1, norm_params, dstream2],
        [row_f32, pair_f32],
        functools.partial(step_backward, 2),
        rows,
        width,
        chunks_near,
        near,
        near,
        34,
    )
    grad_proj, head_grad = lax.optimization_barrier((grad_proj, head_grad))
    grad_proj = lax.psum_scatter(grad_proj, "dp", scatter_dimension=1, tiled=True)
    grad_fc = jnp.einsum("td,tf->df", inner_two, dbefore, preferred_element_type=f32).astype(bf16)
    grad_out = jnp.einsum("tf,td->fd", attended, dbranch1, preferred_element_type=f32).astype(bf16)
    dattended = jnp.einsum("td,fd->tf", dbranch1, wide_out, preferred_element_type=f32)
    dmixed = attend_back(mixed, my_starts, dattended.astype(bf16))
    partial = jnp.einsum("tc,dc->td", dmixed, wide_qkv, preferred_element_type=f32).astype(bf16)
    grad_qkv = jnp.einsum("td,tc->dc", inner_one, dmixed, preferred_element_type=f32).astype(bf16)
    drows, norm1, grad_out, grad_fc, grad_qkv, twins_wide, twins_out = line_call(
        "attn_back",
        8,
        partial,
        [stream0, norm_params, dstream1],
        [pair_f32],
        functools.partial(step_backward, 0),
        rows,
        width,
        chunks_turn,
        near,
        chips,
        70,
        [
            ("scatter", 1, grad_out),
            ("scatter", 0, grad_fc),
            ("scatter", 0, grad_qkv),
        ],
        "spread",
        9,
        seqs=seqs,
    )

    def from_twins(values, axis, sizes):
        starts = [(seqs - 1) * sum(sizes[:n]) for n in range(len(sizes))]
        found = []
        for turn in range(1, seqs):
            pieces = [
                lax.slice_in_dim(values, at + (turn - 1) * size, at + turn * size, axis=axis)
                for at, size in zip(starts, sizes)
            ]
            back = [(i, (i - turn * sharers) % size_mp) for i in range(size_mp)]
            found.append(lax.ppermute(jnp.concatenate(pieces, axis=axis), "mp", back))
        return found

    proj_rows = w_proj.shape[0]
    wide = [grad_fc.shape[1], grad_qkv.shape[1]]
    found_proj = from_twins(grad_proj[proj_rows:], 0, [proj_rows])
    found_out = from_twins(twins_out, 0, [w_out.shape[0]])
    found_wide = from_twins(twins_wide, 1, wide)
    grad_table = scatter(keys, owned, head_grad, drows, vocab, shift)
    found_proj, found_out, found_wide, grad_table = lax.optimization_barrier(
        (found_proj, found_out, found_wide, grad_table)
    )
    grad_proj = grad_proj[:proj_rows].astype(f32)
    for values in found_proj:
        grad_proj += values.astype(f32)
    for values in found_out:
        grad_out += values.astype(f32)
    for values in found_wide:
        grad_fc += values[:, : wide[0]].astype(f32)
        grad_qkv += values[:, wide[0] :].astype(f32)

    weights = (embedding, w_qkv, w_out, w_fc, w_proj)
    grads = (grad_table, grad_qkv, grad_out, grad_fc, grad_proj)
    row_span = (size_mp, size_dp, size_mp, size_dp, size_mp)
    col_span = (size_dp, size_mp, size_dp, size_mp, size_dp)
    full = tuple(
        (g.shape[0] * r, g.shape[1] * c) for g, r, c in zip(grads, row_span, col_span)
    )
    squares = [gradient * gradient + EPS_ONE for gradient in grads]
    rows_new, cols_new, loss_sums, grad_norms, second_new, norms_new, rates = update_stats(
        10,
        [jnp.sum(square, axis=1) for square in squares],
        (rows_table, rows_qkv, rows_out, rows_fc, rows_proj),
        [jnp.sum(square, axis=0) for square in squares],
        (cols_table, cols_qkv, cols_out, cols_fc, cols_proj),
        [table_sq] + [jnp.sum(value * value, axis=0) for value in weights[1:]],
        loss_part,
        (norm1, norm2, norm3),
        norm_params,
        second_norms,
        full,
    )
    steps = [
        grads[n] * lax.rsqrt(rows_new[n][:, None] * cols_new[n][None, :] / rates[n, 0])
        for n in range(5)
    ]
    factors = clip_rates(
        11, [jnp.sum(step * step, axis=0) for step in steps], rates, [r * c for r, c in full]
    )
    updated = [weights[n] - factors[n, 0] * steps[n] for n in range(5)]
    return (
        loss_sums,
        counts,
        grad_table,
        rows_new[0],
        cols_new[0],
        updated[0],
        grad_qkv,
        rows_new[1],
        cols_new[1],
        updated[1],
        grad_out,
        rows_new[2],
        cols_new[2],
        updated[2],
        grad_fc,
        rows_new[3],
        cols_new[3],
        updated[3],
        grad_proj,
        rows_new[4],
        cols_new[4],
        updated[4],
        grad_norms,
        second_new,
        norms_new,
    )


def solution(mesh):
    placed = (
        P("dp"),
        P("dp"),
        P("dp"),
        P("dp"),
        P("mp", "dp"),
        P("dp", "mp"),
        P("mp", "dp"),
        P("dp", "mp"),
        P("mp", "dp"),
        P(),
        P("mp"),
        P("dp"),
        P("dp"),
        P("mp"),
        P("mp"),
        P("dp"),
        P("dp"),
        P("mp"),
        P("mp"),
        P("dp"),
        P(),
    )
    return jax.shard_map(
        local,
        mesh=mesh,
        in_specs=placed,
        out_specs=(
            P(),
            P(),
            P("mp", "dp"),
            P("mp"),
            P("dp"),
            P("mp", "dp"),
            P("dp", "mp"),
            P("dp"),
            P("mp"),
            P("dp", "mp"),
            P("mp", "dp"),
            P("mp"),
            P("dp"),
            P("mp", "dp"),
            P("dp", "mp"),
            P("dp"),
            P("mp"),
            P("dp", "mp"),
            P("mp", "dp"),
            P("mp"),
            P("dp"),
            P("mp", "dp"),
            P(),
            P(),
            P(),
        ),
        check_vma=False,
    )
```

```python
import functools
import math

import jax
import jax.numpy as jnp
from jax import lax
from jax.experimental import pallas as pl
from jax.experimental.pallas import tpu as pltpu
from jax.sharding import PartitionSpec as P

HD = 64
VREAL = 50257
LEN = 1024
NSRC = 4
STEP = 10


EPS_NORM = 1e-05
EPS_ONE = 1e-30
CLIP = 1.0
RHO = 0.5
MASKED = -1e30
QUERIES = 256
HEAD_BLOCK = 640
MESH = pl.DeviceIdType.MESH
VMEM_CAP = 56 * 2**20


def cost_of(time):
    return pl.CostEstimate(
        flops=time * 1000000000, bytes_accessed=time * 3000000, transcendentals=0
    )


def row_slice(values, start, count):
    return lax.dynamic_slice_in_dim(values, start, count, 0)


def line_kernel(
    nr, ng, chunks, shapes, n_in, n_out, step, sides, turn, side_ticks, product, chunk_major, *refs
):
    (rows_r, width_r), (rows_g, width_g) = shapes
    if product:
        dl, *tables = refs[:3]
        first = 3
    else:
        part = refs[0] if nr else None
        first = 1 if nr else 0
    ins = refs[first : first + n_in]
    refs = refs[first + n_in :]
    side_ins, refs = refs[: len(sides)], refs[len(sides) :]
    if ng:
        whole, refs = refs[0], refs[1:]
    outs = refs[:n_out]
    refs = refs[n_out:]
    scatters = [index for index, (kind, unused) in enumerate(sides) if kind == "scatter"]
    side_outs, refs = refs[: len(sides)], refs[len(sides) :]
    twin_outs, scratch = (refs[:2], refs[2:]) if scatters else ([], refs)
    side_scratch, scratch = scratch[: 3 * len(sides)], scratch[3 * len(sides) :]
    if turn:
        cast, turn_send, turn_recv = scratch[-3:]
    if product:
        part, dl_buf, total_ref, dl_sem = scratch[-4:]
    size_dp = lax.axis_size("dp")
    dp = lax.axis_index("dp")
    mp = lax.axis_index("mp")
    z = mp // 2
    core = lax.rem(mp, 2)
    other = mp + 1 - 2 * core
    piece_r = rows_r // chunks
    piece_g = rows_g // chunks
    small = min(piece_r, piece_g)
    late = 1 if turn else 0
    ahead = 1 if product else 0
    most = max(nr, ng)
    zb = lax.rem(z, most)
    if nr:
        zr = lax.rem(z, nr)
        last_r = nr - 1
    if ng:
        zg = lax.rem(z, ng)
        last_g = ng - 1

    barrier = pltpu.get_barrier_semaphore()
    pl.semaphore_signal(barrier, inc=1, device_id=(dp, other), device_id_type=MESH)

    @pl.when(zb > 0)
    def _():
        pl.semaphore_signal(barrier, inc=1, device_id=(dp, mp - 2), device_id_type=MESH)

    @pl.when(zb < most - 1)
    def _():
        pl.semaphore_signal(barrier, inc=1, device_id=(dp, mp + 2), device_id_type=MESH)

    if sides or turn:
        for hop in range(1, size_dp):
            pl.semaphore_signal(
                barrier,
                inc=1,
                device_id=(lax.rem(dp + hop, size_dp), mp),
                device_id_type=MESH,
            )
    greeted = (size_dp if sides or turn else 1) + (zb > 0).astype(jnp.int32) + (zb < most - 1).astype(jnp.int32)
    pl.semaphore_wait(barrier, greeted)

    def share(axis, length, which):
        at = pl.ds(pl.multiple_of(which * length, length), length)
        return (at, slice(None)) if axis == 0 else (slice(None), at)

    def to_peer(src, dst, send, recv, peer):
        return pltpu.make_async_remote_copy(
            src_ref=src,
            dst_ref=dst,
            send_sem=send,
            recv_sem=recv,
            device_id=(peer, mp),
            device_id_type=MESH,
        )

    relay = size_dp == 4
    beside_x = dp + 1 - 2 * lax.rem(dp, 2)
    beside_y = lax.rem(dp + 2, 4)
    across = 3 - dp

    def half_share(axis, length, which, height, part):
        if axis == 0:
            return (pl.ds(pl.multiple_of(which * length + part * height, height), height), slice(None))
        at = pl.ds(pl.multiple_of(which * length, length), length)
        return (pl.ds(part * height, height), at)

    first_copies, more_copies, relays = [], [], []
    for index, (kind, axis) in enumerate(sides):
        src, dst = side_ins[index], side_outs[index]
        send, recv, slots = side_scratch[3 * index : 3 * index + 3]
        if kind == "gather":
            length, height = src.shape[axis], src.shape[0] // 2
        else:
            length = src.shape[axis] // size_dp
            height = (length if axis == 0 else src.shape[0]) // 2
        if not relay:
            for hop in range(1, size_dp):
                peer = lax.rem(dp + hop, size_dp)
                if kind == "gather":
                    source, target = src, dst.at[share(axis, length, dp)]
                else:
                    source, target = src.at[share(axis, length, peer)], slots.at[hop]
                more_copies.append(to_peer(source, target, send.at[hop], recv.at[hop], peer))
            continue
        for side, near_one, far_one in ((0, beside_x, beside_y), (1, beside_y, beside_x)):
            sems = [(send.at[3 * side + n], recv.at[3 * side + n]) for n in range(3)]
            if kind == "gather":
                mine = src.at[pl.ds(side * height, height)]
                here = dst.at[half_share(axis, length, dp, height, side)]
                passed = dst.at[half_share(axis, length, near_one, height, side)]
                arrives = to_peer(mine, here, *sems[0], near_one)
                first_copies.append(arrives)
                more_copies.append(to_peer(mine, here, *sems[1], far_one))
                relays.append((arrives, None, to_peer(passed, passed, *sems[2], far_one)))
            else:
                arrives = to_peer(
                    src.at[half_share(axis, length, across, height, side)],
                    slots.at[4 * side],
                    *sems[0],
                    near_one,
                )
                first_copies.append(arrives)
                more_copies.append(
                    to_peer(
                        src.at[half_share(axis, length, near_one, height, side)],
                        slots.at[4 * side + 1],
                        *sems[1],
                        near_one,
                    )
                )
                summed = to_peer(
                    slots.at[4 * side + 2], slots.at[4 * side + 3], *sems[2], far_one
                )
                own = src.at[half_share(axis, length, far_one, height, side)]
                relays.append((arrives, (own, slots, 4 * side, height), summed))

    def pass_on(arrives, adding, copy):
        arrives.wait_recv()
        if adding is not None:
            own, slots, at, height = adding
            both = own[...].astype(jnp.float32) + slots[at].astype(jnp.float32)
            slots[at + 2] = both.astype(slots.dtype)
        copy.start()

    jobs = [copy.start for copy in first_copies + more_copies]
    jobs += [functools.partial(pass_on, *one) for one in relays]

    def side_jobs(now):
        for spot in range(side_ticks if jobs else 0):
            chosen = jobs[len(jobs) * spot // side_ticks : len(jobs) * (spot + 1) // side_ticks]

            @pl.when(now == spot)
            def _():
                for job in chosen:
                    job()

    if nr:
        half, from_left, from_right, going = scratch[:4]
        half_send, half_recv, rs_send, left_recv, right_recv = scratch[4:9]
        scratch = scratch[9:]
    if ng:
        core_send, core_recv, to_right, to_left, ag_left, ag_right = scratch[:6]

    def part_rows(block, k):
        return pl.ds(pl.multiple_of(block * rows_r + k * piece_r, piece_r), piece_r)

    def whole_rows(block, k):
        if chunk_major:
            start = k * (2 * ng * piece_g) + block * piece_g
            return pl.ds(pl.multiple_of(start, piece_g), piece_g)
        return pl.ds(pl.multiple_of(block * rows_g + k * piece_g, piece_g), piece_g)

    def remote(src, dst, send, recv, target):
        return pltpu.make_async_remote_copy(
            src_ref=src,
            dst_ref=dst,
            send_sem=send,
            recv_sem=recv,
            device_id=(dp, target),
            device_id_type=MESH,
        )

    if nr:

        def half_copy(dest, k):
            return remote(
                part.at[part_rows(2 * dest + 1 - core, k)],
                half.at[dest, k],
                half_send.at[dest, k],
                half_recv.at[dest, k],
                other,
            )

        def send_halves(k, carry):
            for dest in range(nr):
                half_copy(dest, k).start()
            return carry

        if not product:
            lax.fori_loop(0, chunks, send_halves, 0)

        def right_copy(dest, k):
            return remote(
                going.at[dest, k],
                from_left.at[dest, k],
                rs_send.at[dest, k],
                left_recv.at[dest, k],
                mp + 2,
            )

        def left_copy(dest, k):
            return remote(
                going.at[dest, k],
                from_right.at[dest, k],
                rs_send.at[dest, k],
                right_recv.at[dest, k],
                mp - 2,
            )

        def chip_sum(dest, k):
            half_copy(dest, k).wait_recv()
            mine = part[part_rows(2 * dest + core, k), :].astype(jnp.float32)
            return mine + half[dest, k].astype(jnp.float32)

        def pass_right(dest, k):
            total = chip_sum(dest, k)

            @pl.when(zr == 0)
            def _():
                going[dest, k] = total.astype(jnp.bfloat16)

            @pl.when(zr > 0)
            def _():
                right_copy(dest, k).wait_recv()
                both = total + from_left[dest, k].astype(jnp.float32)
                going[dest, k] = both.astype(jnp.bfloat16)

            right_copy(dest, k).start()

        def pass_left(dest, k):
            total = chip_sum(dest, k)

            @pl.when(zr == last_r)
            def _():
                going[dest, k] = total.astype(jnp.bfloat16)

            @pl.when(zr < last_r)
            def _():
                left_copy(dest, k).wait_recv()
                both = total + from_right[dest, k].astype(jnp.float32)
                going[dest, k] = both.astype(jnp.bfloat16)

            left_copy(dest, k).start()

    if ng:

        def gathered(block, k, send, recv, target):
            where = whole.at[whole_rows(2 * block + core, k)]
            return remote(where, where, send.at[block, k], recv.at[block, k], target)

        def core_copy(block, k):
            return gathered(block, k, core_send, core_recv, other)

        def ag_right_copy(block, k):
            return gathered(block, k, to_right, ag_left, mp + 2)

        def ag_left_copy(block, k):
            return gathered(block, k, to_left, ag_right, mp - 2)

    def own_rows(k):
        total = None
        if nr:
            total = chip_sum(zr, k)
            zero = jnp.zeros((piece_r, width_r), jnp.float32)

            @pl.when(zr > 0)
            def _():
                right_copy(zr, k).wait_recv()

            @pl.when(zr < last_r)
            def _():
                left_copy(zr, k).wait_recv()

            total += jnp.where(zr > 0, from_left[zr, k].astype(jnp.float32), zero)
            total += jnp.where(zr < last_r, from_right[zr, k].astype(jnp.float32), zero)
        if turn == "gather":
            cast[k] = total.astype(cast.dtype)
            for hop in range(1, size_dp):
                turn_copy(hop, k).start()
            mine = pl.ds(pl.multiple_of(dp * small, small), small)
            outs[0][own_place(k, dp)] = cast[k, mine, :]
            return
        at = pl.ds(pl.multiple_of(k * piece_r, piece_r), piece_r)
        ready = step(total, at, ins, outs)
        if turn == "spread":
            cast[k] = ready.astype(cast.dtype)
            for hop in range(1, size_dp):
                turn_copy(hop, k).start()
            whole[own_place(k, dp)] = cast[
                k, :, pl.ds(pl.multiple_of(dp * width_g, width_g), width_g)
            ]
        elif ng:
            whole[whole_rows(2 * zg + core, k), :] = ready.astype(whole.dtype)
            start_gather(k)

    def own_place(k, peer):
        if turn == "gather":
            return (
                pl.ds(pl.multiple_of(k * small, small), small),
                pl.ds(pl.multiple_of(peer * width_r, width_r), width_r),
            )
        start = (2 * zg + core) * rows_g + k * piece_g + peer * small
        return (pl.ds(pl.multiple_of(start, small), small), slice(None))

    def turn_copy(hop, k):
        peer = lax.rem(dp + hop, size_dp)
        if turn == "gather":
            src = cast.at[k, pl.ds(pl.multiple_of(peer * small, small), small)]
            dst = outs[0].at[own_place(k, dp)]
        else:
            src = cast.at[k, :, pl.ds(pl.multiple_of(peer * width_g, width_g), width_g)]
            dst = whole.at[own_place(k, dp)]
        return to_peer(src, dst, turn_send.at[hop, k], turn_recv.at[hop, k], peer)

    def turned_rows(k):
        for hop in range(1, size_dp):
            turn_copy(hop, k).wait_recv()
        if turn == "gather":
            at = pl.ds(pl.multiple_of(k * piece_g, piece_g), piece_g)
            ready = step(None, at, ins, outs)
            whole[whole_rows(2 * zg + core, k), :] = ready.astype(whole.dtype)
        start_gather(k)

    def start_gather(k):
        core_copy(zg, k).start()

        @pl.when(zg < last_g)
        def _():
            ag_right_copy(zg, k).start()

        @pl.when(zg > 0)
        def _():
            ag_left_copy(zg, k).start()

    def inside(k):
        return (k >= 0) & (k < chunks)

    def own_lag(chip):
        if not nr:
            return 0
        at = lax.rem(chip, nr)
        return jnp.maximum(at, last_r - at) + ahead

    def dl_copy(k):
        columns = dl_buf.shape[2]
        return pltpu.make_async_copy(
            dl.at[:, pl.ds(pl.multiple_of(k * columns, columns), columns)],
            dl_buf.at[lax.rem(k, 2)],
            dl_sem.at[lax.rem(k, 2)],
        )

    def make_part(k):
        dl_copy(k).wait()

        @pl.when(k + 1 < chunks)
        def _():
            dl_copy(k + 1).start()

        slot = lax.rem(k, 2)

        start = 0
        for piece in tables:
            found = lax.dot_general(
                dl_buf[slot, start : start + piece.shape[0], :],
                piece[...],
                (((0,), (0,)), ((), ())),
                preferred_element_type=jnp.float32,
            )
            if start:
                total_ref[...] += found
            else:
                total_ref[...] = found
            start += piece.shape[0]
        for block in range(2 * nr):
            part[part_rows(block, k), :] = total_ref[
                block * piece_r : block * piece_r + piece_r, :
            ].astype(jnp.bfloat16)
        send_halves(k, 0)

    if product:
        dl_copy(0).start()

    def tick(now, carry):
        side_jobs(now)
        if nr:
            k_right = now - zr - ahead
            k_left = now - (last_r - zr) - ahead
            for far in range(last_r):

                @pl.when(inside(k_right) & (last_r - far > zr))
                def _():
                    pass_right(last_r - far, k_right)

                @pl.when(inside(k_left) & (far < zr))
                def _():
                    pass_left(far, k_left)

        k_own = now - own_lag(z)

        @pl.when(inside(k_own))
        def _():
            own_rows(k_own)

        if turn:

            @pl.when(inside(k_own - 1))
            def _():
                turned_rows(k_own - 1)

        if ng:
            for block in range(ng):
                k = now - (own_lag(z - zg + block) + late + jnp.abs(zg - block))

                @pl.when(inside(k) & (block < zg))
                def _():
                    ag_right_copy(block, k).wait_recv()
                    core_copy(block, k).start()

                    @pl.when(zg < last_g)
                    def _():
                        ag_right_copy(block, k).start()

                @pl.when(inside(k) & (block > zg))
                def _():
                    ag_left_copy(block, k).wait_recv()
                    core_copy(block, k).start()

                    @pl.when(zg > 0)
                    def _():
                        ag_left_copy(block, k).start()

        if product:

            @pl.when(now < chunks)
            def _():
                make_part(now)

        return carry

    ticks = ahead + chunks + (nr - 1 if nr else 0) + (ng - 1 if ng else 0) + late
    lax.fori_loop(0, ticks, tick, 0)

    def finish(k, carry):
        if turn:
            for hop in range(1, size_dp):
                turn_copy(hop, k).wait_send()
        if nr:
            for block in range(nr):
                half_copy(block, k).wait_send()

                @pl.when(block != zr)
                def _():
                    right_copy(block, k).wait_send()

        if ng:
            for block in range(ng):
                core_copy(block, k).wait()

                @pl.when((zg < last_g) & (block <= zg))
                def _():
                    ag_right_copy(block, k).wait_send()

                @pl.when((zg > 0) & (block >= zg))
                def _():
                    ag_left_copy(block, k).wait_send()

        return carry

    lax.fori_loop(0, chunks, finish, 0)
    for index, (kind, axis) in enumerate(sides):
        if kind == "gather":
            length = side_ins[index].shape[axis]
            side_outs[index][share(axis, length, dp)] = side_ins[index][...]
    for copy in first_copies:
        copy.wait_send()
    for copy in more_copies:
        copy.wait()
    for unused, unused, copy in relays:
        copy.wait()
    placed = [0, 0]
    for index in scatters:
        axis = sides[index][1]
        src, dst = side_ins[index], side_outs[index]
        slots = side_scratch[3 * index + 2]
        length = src.shape[axis] // size_dp
        height = (length if axis == 0 else src.shape[0]) // 2
        if relay:
            total = []
            for side in range(2):
                one = src[half_share(axis, length, dp, height, side)].astype(jnp.float32)
                one += slots[4 * side + 1].astype(jnp.float32)
                one += slots[4 * side + 3].astype(jnp.float32)
                total.append(one)
            total = jnp.concatenate(total)
        else:
            total = src[share(axis, length, dp)].astype(jnp.float32)
            for hop in range(1, size_dp):
                total += slots[hop].astype(jnp.float32)
        twins = twin_outs[axis]
        at = placed[axis]
        if axis == 0:
            own = dst.shape[1]
            dst[...] = total[:, :own]
            more = total.shape[1] - own
            twins[:, at : at + more] = total[:, own:].astype(twins.dtype)
        else:
            own = dst.shape[0]
            dst[...] = total[:own, :]
            more = total.shape[0] - own
            twins[at : at + more, :] = total[own:, :].astype(twins.dtype)
        placed[axis] += more


def line_call(
    name,
    cid,
    partial,
    ins,
    out_types,
    step,
    rows,
    width,
    chunks,
    nr,
    ng,
    time,
    sides=(),
    turn=None,
    side_ticks=0,
    product=False,
    chunk_major=False,
    seqs=1,
):
    piece = rows // chunks
    size_dp = lax.axis_size("dp")
    reduced = gathered = (rows, width)
    if turn == "gather":
        gathered = (rows // size_dp, width * size_dp)
    elif turn == "spread":
        gathered = (rows * size_dp, width // size_dp)
    out_shape = []
    if ng:
        out_shape.append(
            jax.ShapeDtypeStruct((2 * ng * gathered[0], gathered[1]), jnp.bfloat16)
        )
    out_shape += out_types
    dma = pltpu.SemaphoreType.DMA
    scratch = []
    twin_shapes = [[0, 0], [0, 0]]
    for kind, axis, values in sides:
        shape = list(values.shape)
        scratch += [dma((max(size_dp, 6),)), dma((max(size_dp, 6),))]
        if kind == "gather":
            shape[axis] *= size_dp
            out_shape.append(jax.ShapeDtypeStruct(tuple(shape), values.dtype))
            scratch.append(pltpu.VMEM((16, 128), values.dtype))
        else:
            shape[axis] //= size_dp
            own = list(shape)
            own[1 - axis] //= seqs
            out_shape.append(jax.ShapeDtypeStruct(tuple(own), jnp.float32))
            twin_shapes[axis][axis] = shape[axis]
            twin_shapes[axis][1 - axis] += shape[1 - axis] - own[1 - axis]
            slots = (8, shape[0] // 2, shape[1]) if size_dp == 4 else (size_dp, *shape)
            scratch.append(pltpu.VMEM(slots, values.dtype))
    if any(side[0] == "scatter" for side in sides):
        out_shape += [jax.ShapeDtypeStruct(tuple(shape), jnp.bfloat16) for shape in twin_shapes]
    if nr:
        scratch += [pltpu.VMEM((nr, chunks, piece, width), jnp.bfloat16)] * 4
        scratch += [dma((nr, chunks))] * 5
    if ng:
        scratch += [dma((ng, chunks))] * 6
    if turn:
        scratch.append(pltpu.VMEM((chunks, piece, width), jnp.bfloat16))
        scratch += [dma((size_dp, chunks))] * 2
    if product:
        dl = partial[0]
        columns = dl.shape[1] // chunks
        scratch += [
            pltpu.VMEM((2 * nr * rows, width), jnp.bfloat16),
            pltpu.VMEM((2, dl.shape[0], columns), jnp.bfloat16),
            pltpu.VMEM((columns, width), jnp.float32),
            dma((2,)),
        ]
        partial = list(partial)
    else:
        partial = [partial] if nr else []
    args = partial + list(ins) + [side[2] for side in sides]
    vmem = pl.BlockSpec(memory_space=pltpu.VMEM)
    call = pl.pallas_call(
        functools.partial(
            line_kernel,
            nr,
            ng,
            chunks,
            (reduced, gathered),
            len(ins),
            len(out_types),
            step,
            tuple(side[:2] for side in sides),
            turn,
            side_ticks,
            product,
            chunk_major,
        ),
        out_shape=out_shape,
        in_specs=[pl.BlockSpec(memory_space=pl.ANY) if product and n == 0 else vmem for n in range(len(args))],
        out_specs=[vmem] * len(out_shape),
        scratch_shapes=scratch,
        compiler_params=pltpu.CompilerParams(
            collective_id=cid, has_side_effects=True, vmem_limit_bytes=VMEM_CAP
        ),
        cost_estimate=cost_of(time),
        name=name,
    )
    return list(call(*args))


def head_stats_kernel(block, tile, early, early_ref, late_ref, final_ref, wanted_ref, edge_ref, exp_ref, top_ref, sum_ref, pick_ref):
    j = pl.program_id(0)
    tokens = final_ref.shape[0]
    place = j * block + lax.broadcasted_iota(jnp.int32, (block, 1), 0)
    valid = place < edge_ref[0]
    table = jnp.where(j < early, early_ref[...], late_ref[...])

    def weigh(masked):
        for start in range(0, tokens, tile):
            at = pl.ds(start, tile)
            logits = lax.dot_general(
                table,
                final_ref[at, :],
                (((1,), (1,)), ((), ())),
                preferred_element_type=jnp.float32,
            )
            if masked:
                logits = jnp.where(valid, logits, MASKED)
            top = jnp.max(logits, axis=0, keepdims=True)
            weights = jnp.exp(logits - top)
            exp_ref[:, at] = weights.astype(jnp.bfloat16)
            top_ref[0, :, at] = top
            sum_ref[0, :, at] = jnp.sum(weights, axis=0, keepdims=True)
            pick_ref[0, :, at] = jnp.sum(
                jnp.where(place == wanted_ref[:, at], logits, 0.0), axis=0, keepdims=True
            )

    whole = (j + 1) * block <= edge_ref[0]

    @pl.when(whole)
    def _():
        weigh(False)

    @pl.when(jnp.logical_not(whole))
    def _():
        weigh(True)


def head_stats(tables, final, wanted, edge, block, tile=512):
    early = tables[0].shape[0] // block
    rows = sum(table.shape[0] for table in tables)
    width = tables[0].shape[1]
    tokens = final.shape[0]
    steps = rows // block
    row = jax.ShapeDtypeStruct((steps, 1, tokens), jnp.float32)
    row_spec = pl.BlockSpec((1, 1, tokens), lambda j: (j, 0, 0))
    return pl.pallas_call(
        functools.partial(head_stats_kernel, block, tile, early),
        grid=(steps,),
        out_shape=[jax.ShapeDtypeStruct((steps * block, tokens), jnp.bfloat16), row, row, row],
        in_specs=[
            pl.BlockSpec((block, width), lambda j: (jnp.minimum(j, early - 1), 0)),
            pl.BlockSpec((block, width), lambda j: (jnp.maximum(j - early, 0), 0)),
            pl.BlockSpec((tokens, width), lambda j: (0, 0)),
            pl.BlockSpec((1, tokens), lambda j: (0, 0)),
            pl.BlockSpec(memory_space=pltpu.SMEM),
        ],
        out_specs=[pl.BlockSpec((block, tokens), lambda j: (j, 0)), row_spec, row_spec, row_spec],
        compiler_params=pltpu.CompilerParams(vmem_limit_bytes=56 * 2**20),
        cost_estimate=pl.CostEstimate(
            flops=2 * rows * width * tokens,
            bytes_accessed=2 * rows * (width + tokens),
            transcendentals=rows * tokens,
        ),
        name="head_stats",
    )(*tables, final, wanted, edge)


def head_back_kernel(block, tile, exp_ref, final_ref, scale_ref, weight_ref, wanted_ref, dl_ref, grad_ref):
    j = pl.program_id(0)
    tokens = final_ref.shape[0]
    place = j * block + lax.broadcasted_iota(jnp.int32, (block, 1), 0)
    for start in range(0, tokens, tile):
        at = pl.ds(start, tile)
        dl = exp_ref[:, at].astype(jnp.float32) * scale_ref[0, :, at]
        dl = dl - jnp.where(place == wanted_ref[:, at], weight_ref[:, at], 0.0)
        dl_ref[:, at] = dl.astype(jnp.bfloat16)
    strip = block // max(1, block // 256)
    for start in range(0, block, strip):
        at = pl.ds(start, strip)
        grad_ref[at, :] = jnp.dot(
            dl_ref[at, :], final_ref[...], preferred_element_type=jnp.float32
        ).astype(jnp.bfloat16)


def head_back(exps, final, scale, weight, wanted, block, tile=256):
    rows, tokens = exps.shape
    width = final.shape[1]
    return pl.pallas_call(
        functools.partial(head_back_kernel, block, tile),
        grid=(rows // block,),
        out_shape=[
            jax.ShapeDtypeStruct((rows, tokens), jnp.bfloat16),
            jax.ShapeDtypeStruct((rows, width), jnp.bfloat16),
        ],
        in_specs=[
            pl.BlockSpec((block, tokens), lambda j: (j, 0)),
            pl.BlockSpec((tokens, width), lambda j: (0, 0)),
            pl.BlockSpec((1, 1, tokens), lambda j: (j, 0, 0)),
            pl.BlockSpec((1, tokens), lambda j: (0, 0)),
            pl.BlockSpec((1, tokens), lambda j: (0, 0)),
        ],
        out_specs=[
            pl.BlockSpec((block, tokens), lambda j: (j, 0)),
            pl.BlockSpec((block, width), lambda j: (j, 0)),
        ],
        compiler_params=pltpu.CompilerParams(vmem_limit_bytes=56 * 2**20),
        cost_estimate=pl.CostEstimate(
            flops=2 * rows * width * tokens,
            bytes_accessed=2 * rows * (width + 2 * tokens),
            transcendentals=0,
        ),
        name="head_back",
    )(exps, final, scale, weight, wanted)


def head_weights(mixed_ref, starts_ref, base, at, seen):
    query = mixed_ref[at : at + QUERIES, base : base + HD]
    keys = mixed_ref[0:seen, base + HD : base + 2 * HD]
    values = mixed_ref[0:seen, base + 2 * HD : base + 3 * HD]
    scores = lax.dot_general(
        query, keys, (((1,), (1,)), ((), ())), preferred_element_type=jnp.float32
    )
    row = at + lax.broadcasted_iota(jnp.int32, (QUERIES, seen), 0)
    column = lax.broadcasted_iota(jnp.int32, (QUERIES, seen), 1)
    allowed = (column <= row) & (column >= starts_ref[at : at + QUERIES, :])
    scores = jnp.where(allowed, scores * HD ** (-0.5), MASKED)
    weights = jnp.exp(scores - jnp.max(scores, axis=1, keepdims=True))
    probs = weights / jnp.sum(weights, axis=1, keepdims=True)
    return query, keys, values, probs


def attend_kernel(mixed_ref, starts_ref, out_ref):
    length = mixed_ref.shape[0]
    for at in range(0, length, QUERIES):
        found = []
        for head in range(2):
            unused, unused, values, probs = head_weights(
                mixed_ref, starts_ref, head * 3 * HD, at, at + QUERIES
            )
            found.append(
                jnp.dot(probs.astype(jnp.bfloat16), values, preferred_element_type=jnp.float32)
            )
        out_ref[at : at + QUERIES, :] = jnp.concatenate(found, axis=1).astype(jnp.bfloat16)


def attend(mixed, starts):
    length, columns = mixed.shape
    pairs = columns // (6 * HD)
    return pl.pallas_call(
        attend_kernel,
        grid=(pairs,),
        out_shape=jax.ShapeDtypeStruct((length, pairs * 2 * HD), jnp.bfloat16),
        in_specs=[
            pl.BlockSpec((length, 6 * HD), lambda j: (0, j)),
            pl.BlockSpec((length, 1), lambda j: (0, 0)),
        ],
        out_specs=pl.BlockSpec((length, 2 * HD), lambda j: (0, j)),
        compiler_params=pltpu.CompilerParams(vmem_limit_bytes=40 * 2**20),
        cost_estimate=pl.CostEstimate(
            flops=8 * pairs * length * length * HD,
            bytes_accessed=2 * length * columns,
            transcendentals=pairs * length * length,
        ),
        name="attend",
    )(mixed, starts)


def attend_back_kernel(mixed_ref, starts_ref, upstream_ref, out_ref, sums_ref):
    length = mixed_ref.shape[0]
    sums_ref[...] = jnp.zeros_like(sums_ref)
    rows = (((0,), (0,)), ((), ()))
    for at in range(0, length, QUERIES):
        seen = at + QUERIES
        for head in range(2):
            base = head * 3 * HD
            query, keys, values, probs = head_weights(mixed_ref, starts_ref, base, at, seen)
            upstream = upstream_ref[at:seen, head * HD : head * HD + HD]
            dprobs = lax.dot_general(
                upstream, values, (((1,), (1,)), ((), ())), preferred_element_type=jnp.float32
            )
            inner = jnp.sum(probs * dprobs, axis=1, keepdims=True)
            dscores = (probs * (dprobs - inner)).astype(jnp.bfloat16)
            dquery = jnp.dot(dscores, keys, preferred_element_type=jnp.float32)
            dkeys = lax.dot_general(dscores, query, rows, preferred_element_type=jnp.float32)
            dvalues = lax.dot_general(
                probs.astype(jnp.bfloat16), upstream, rows, preferred_element_type=jnp.float32
            )
            sums_ref[at:seen, base : base + HD] = dquery * HD ** (-0.5)
            sums_ref[0:seen, base + HD : base + 2 * HD] += dkeys * HD ** (-0.5)
            sums_ref[0:seen, base + 2 * HD : base + 3 * HD] += dvalues
    out_ref[...] = sums_ref[...].astype(jnp.bfloat16)


def attend_back(mixed, starts, upstream):
    length, columns = mixed.shape
    pairs = columns // (6 * HD)
    return pl.pallas_call(
        attend_back_kernel,
        grid=(pairs,),
        out_shape=jax.ShapeDtypeStruct((length, columns), jnp.bfloat16),
        in_specs=[
            pl.BlockSpec((length, 6 * HD), lambda j: (0, j)),
            pl.BlockSpec((length, 1), lambda j: (0, 0)),
            pl.BlockSpec((length, 2 * HD), lambda j: (0, j)),
        ],
        out_specs=pl.BlockSpec((length, 6 * HD), lambda j: (0, j)),
        scratch_shapes=[pltpu.VMEM((length, 6 * HD), jnp.float32)],
        compiler_params=pltpu.CompilerParams(vmem_limit_bytes=40 * 2**20),
        cost_estimate=pl.CostEstimate(
            flops=20 * pairs * length * length * HD,
            bytes_accessed=4 * length * columns,
            transcendentals=pairs * length * length,
        ),
        name="attend_back",
    )(mixed, starts, upstream)


def small_gather_kernel(axis, count, src_ref, out_ref, send, recv):
    dp = lax.axis_index("dp")
    mp = lax.axis_index("mp")
    me = dp if axis == "dp" else mp

    def device(peer):
        return (peer, mp) if axis == "dp" else (dp, peer)

    barrier = pltpu.get_barrier_semaphore()
    for hop in range(1, count):
        pl.semaphore_signal(
            barrier, inc=1, device_id=device(lax.rem(me + hop, count)), device_id_type=MESH
        )
    pl.semaphore_wait(barrier, count - 1)
    copies = []
    for hop in range(1, count):
        peer = lax.rem(me + hop, count)
        copy = pltpu.make_async_remote_copy(
            src_ref=src_ref,
            dst_ref=out_ref.at[me],
            send_sem=send.at[hop],
            recv_sem=recv.at[hop],
            device_id=device(peer),
            device_id_type=MESH,
        )
        copy.start()
        copies.append(copy)
    out_ref[me] = src_ref[...]
    for copy in copies:
        copy.wait()


def small_gather(name, cid, values, axis):
    count = lax.axis_size(axis)
    vmem = pl.BlockSpec(memory_space=pltpu.VMEM)
    return pl.pallas_call(
        functools.partial(small_gather_kernel, axis, count),
        out_shape=jax.ShapeDtypeStruct((count,) + values.shape, values.dtype),
        in_specs=[vmem],
        out_specs=vmem,
        scratch_shapes=[pltpu.SemaphoreType.DMA((count,)), pltpu.SemaphoreType.DMA((count,))],
        compiler_params=pltpu.CompilerParams(collective_id=cid, has_side_effects=True),
        cost_estimate=cost_of(6),
        name=name,
    )(values)


def exchange(axis, me, here, source, slots, send, recv, first):
    count = slots.shape[0]
    copies = []
    for hop in range(1, count):
        peer = lax.rem(me + hop, count)
        copy = pltpu.make_async_remote_copy(
            src_ref=source,
            dst_ref=slots.at[me],
            send_sem=send.at[first + hop],
            recv_sem=recv.at[first + hop],
            device_id=(peer, here) if axis == "dp" else (here, peer),
            device_id_type=MESH,
        )
        copy.start()
        copies.append(copy)
    slots[me] = source[...]
    for copy in copies:
        copy.wait()
    total = slots[0]
    for index in range(1, count):
        total = total + slots[index]
    return total


def greet_all(dp, mp, size_dp, size_mp):
    barrier = pltpu.get_barrier_semaphore()
    for hop in range(1, size_dp):
        pl.semaphore_signal(
            barrier, inc=1, device_id=(lax.rem(dp + hop, size_dp), mp), device_id_type=MESH
        )
    for hop in range(1, size_mp):
        pl.semaphore_signal(
            barrier, inc=1, device_id=(dp, lax.rem(mp + hop, size_mp)), device_id_type=MESH
        )
    pl.semaphore_wait(barrier, size_dp + size_mp - 2)


def lane_rows(values):
    values = values.reshape(-1)
    return jnp.pad(values, (0, -values.size % 128)).reshape(-1, 128)


def fold(values):
    return jnp.sum(values, axis=0, keepdims=True)


def stats_kernel(full, size_dp, size_mp, *refs):
    row_part, row_old, col_part, col_old, weight_sq = (refs[5 * n : 5 * n + 5] for n in range(5))
    loss_part, norm_one, norm_two, norm_three, norms, second_old = refs[25:31]
    refs = refs[31:]
    row_out, col_out = refs[0:5], refs[5:10]
    loss_out, grads_out, second_out, norms_out, rate_out = refs[10:15]
    send_dp, slots_dp, send_mp, slots_mp, parts, part_slots, whole, send, recv = refs[15:]
    dp = lax.axis_index("dp")
    mp = lax.axis_index("mp")
    greet_all(dp, mp, size_dp, size_mp)
    beta = 1.0 - STEP ** (-0.8)
    width = norms.shape[1]

    at = 0
    marks = []

    def put(values):
        nonlocal at
        rows = values.shape[0]
        send_dp[at : at + rows, :] = values
        marks.append((at, rows))
        at += rows

    norm_rows = width // 128
    for ref in (norm_one, norm_two, norm_three):
        for which in range(2):
            for piece in range(norm_rows):
                put(ref[which : which + 1, piece * 128 : piece * 128 + 128])
    marks.clear()
    count_norm = at
    for index in (0, 2, 4):
        put(row_part[index][...])
    for index in (1, 3):
        put(col_part[index][...])
    put(loss_part[...])
    for index in (1, 3):
        put(fold(row_old[index][...]))
    for index in range(5):
        put(fold(weight_sq[index][...]))
    if at < send_dp.shape[0]:
        send_dp[at:, :] = jnp.zeros((send_dp.shape[0] - at, 128), jnp.float32)
    over_dp = exchange("dp", dp, mp, send_dp, slots_dp, send, recv, 0)
    taken = [over_dp[start : start + rows] for start, rows in marks]
    loss_out[...] = taken[5]
    row_full = {0: taken[0], 2: taken[1], 4: taken[2]}
    col_full = {1: taken[3], 3: taken[4]}
    old_total = {1: taken[6], 3: taken[7]}
    weight_rows = taken[8:13]

    at = 0
    marks = []

    def put_mp(values):
        nonlocal at
        rows = values.shape[0]
        send_mp[at : at + rows, :] = values
        marks.append((at, rows))
        at += rows

    for index in (0, 2, 4):
        put_mp(col_part[index][...])
    for index in (1, 3):
        put_mp(row_part[index][...])
    for index in range(5):
        put_mp(fold(row_full[index] if index in row_full else col_full[index]))
    for index in (0, 2, 4):
        put_mp(fold(row_old[index][...]))
    for index in range(5):
        put_mp(weight_rows[index])
    if at < send_mp.shape[0]:
        send_mp[at:, :] = jnp.zeros((send_mp.shape[0] - at, 128), jnp.float32)
    each = count_norm // size_mp
    for index in range(size_mp):
        parts[index] = over_dp[index * each : index * each + each]
    first = size_dp + size_mp
    copies = []
    for hop in range(1, size_mp):
        peer = lax.rem(mp + hop, size_mp)
        copy = pltpu.make_async_remote_copy(
            src_ref=parts.at[peer],
            dst_ref=part_slots.at[mp],
            send_sem=send.at[first + hop],
            recv_sem=recv.at[first + hop],
            device_id=(dp, peer),
            device_id_type=MESH,
        )
        copy.start()
        copies.append(copy)
    part_slots[mp] = parts[mp]
    over_mp = exchange("mp", mp, dp, send_mp, slots_mp, send, recv, size_dp)
    for copy in copies:
        copy.wait()
    summed = part_slots[0]
    for index in range(1, size_mp):
        summed = summed + part_slots[index]
    whole[mp] = summed
    first += size_mp
    copies = []
    for hop in range(1, size_mp):
        peer = lax.rem(mp + hop, size_mp)
        copy = pltpu.make_async_remote_copy(
            src_ref=whole.at[mp],
            dst_ref=whole.at[mp],
            send_sem=send.at[first + hop],
            recv_sem=recv.at[first + hop],
            device_id=(dp, peer),
            device_id_type=MESH,
        )
        copies.append(copy)
    for copy in copies:
        copy.start()
    taken = [over_mp[start : start + rows] for start, rows in marks]
    for slot, index in enumerate((0, 2, 4)):
        col_full[index] = taken[slot]
        old_total[index] = taken[10 + slot]
    for slot, index in enumerate((1, 3)):
        row_full[index] = taken[3 + slot]
    square_total = taken[5:10]
    weight_total = taken[13:18]
    for index in range(5):
        full_rows, full_cols = full[index]
        row_new = beta * row_old[index][...] + (1.0 - beta) * row_full[index] / full_cols
        col_new = beta * col_old[index][...] + (1.0 - beta) * col_full[index] / full_rows
        row_out[index][...] = row_new
        col_out[index][...] = col_new
        mean = (
            beta * jnp.sum(old_total[index], axis=1, keepdims=True)
            + (1.0 - beta) * jnp.sum(square_total[index], axis=1, keepdims=True) / full_cols
        ) / full_rows
        rate = RHO * jnp.sqrt(
            jnp.sum(weight_total[index], axis=1, keepdims=True) / (full_rows * full_cols)
        )
        rate_out[index : index + 1, :] = jnp.broadcast_to(mean, (1, 128))
        rate_out[8 + index : 9 + index, :] = jnp.broadcast_to(rate, (1, 128))
    for copy in copies:
        copy.wait()
    for row in range(6):
        for piece in range(norm_rows):
            place = row * norm_rows + piece
            grads_out[row : row + 1, piece * 128 : piece * 128 + 128] = whole[
                place // each, place % each : place % each + 1, :
            ]
    grad = grads_out[...]
    second = beta * second_old[...] + (1.0 - beta) * (grad * grad + EPS_ONE)
    second_out[...] = second
    step = grad * lax.rsqrt(second)
    entries = step.size

    def mean_square(values):
        return jnp.sum(jnp.sum(values * values, axis=0, keepdims=True), axis=1, keepdims=True) / (
            entries
        )

    step = step / jnp.maximum(1.0, jnp.sqrt(mean_square(step)) / CLIP)
    old = norms[...]
    norms_out[...] = old - RHO * jnp.sqrt(mean_square(old)) * step


def update_stats(cid, row_parts, rows_old, col_parts, cols_old, weight_sq, loss, norm_parts, norms, second, full):
    size_dp = lax.axis_size("dp")
    size_mp = lax.axis_size("mp")
    f32 = jnp.float32
    rows_old2 = [lane_rows(v) for v in rows_old]
    cols_old2 = [lane_rows(v) for v in cols_old]
    args = (
        [lane_rows(v) for v in row_parts]
        + rows_old2
        + [lane_rows(v) for v in col_parts]
        + cols_old2
        + [v if v.ndim == 2 else lane_rows(v) for v in weight_sq]
        + [lane_rows(loss)]
        + list(norm_parts)
        + [norms, second]
    )
    width = norms.shape[1]
    count_norm = 6 * width // 128
    size_a = count_norm + sum(rows_old2[n].shape[0] for n in (0, 2, 4))
    size_a += sum(cols_old2[n].shape[0] for n in (1, 3)) + 8
    size_a += -size_a % 8
    size_b = sum(cols_old2[n].shape[0] for n in (0, 2, 4))
    size_b += sum(rows_old2[n].shape[0] for n in (1, 3)) + 13
    size_b += -size_b % 8
    each = count_norm // size_mp
    out_shape = [jax.ShapeDtypeStruct(v.shape, f32) for v in rows_old2 + cols_old2]
    out_shape += [
        jax.ShapeDtypeStruct((1, 128), f32),
        jax.ShapeDtypeStruct(norms.shape, f32),
        jax.ShapeDtypeStruct(norms.shape, f32),
        jax.ShapeDtypeStruct(norms.shape, f32),
        jax.ShapeDtypeStruct((16, 128), f32),
    ]
    sems = size_dp + 3 * size_mp
    vmem = pl.BlockSpec(memory_space=pltpu.VMEM)
    found = pl.pallas_call(
        functools.partial(stats_kernel, full, size_dp, size_mp),
        out_shape=out_shape,
        in_specs=[vmem] * len(args),
        out_specs=[vmem] * len(out_shape),
        scratch_shapes=[
            pltpu.VMEM((size_a, 128), f32),
            pltpu.VMEM((size_dp, size_a, 128), f32),
            pltpu.VMEM((size_b, 128), f32),
            pltpu.VMEM((size_mp, size_b, 128), f32),
            pltpu.VMEM((size_mp, each, 128), f32),
            pltpu.VMEM((size_mp, each, 128), f32),
            pltpu.VMEM((size_mp, each, 128), f32),
            pltpu.SemaphoreType.DMA((sems,)),
            pltpu.SemaphoreType.DMA((sems,)),
        ],
        compiler_params=pltpu.CompilerParams(collective_id=cid, has_side_effects=True),
        cost_estimate=cost_of(12),
        name="update_stats",
    )(*args)
    rows_new = [found[n].reshape(-1)[: rows_old[n].size] for n in range(5)]
    cols_new = [found[5 + n].reshape(-1)[: cols_old[n].size] for n in range(5)]
    loss_sums = found[10][0, :NSRC]
    return rows_new, cols_new, loss_sums, found[11], found[12], found[13], found[14]


def clip_kernel(entries, size_dp, size_mp, *refs):
    parts, rate = refs[:5], refs[5]
    out, mine, slots_dp, slots_mp, send, recv = refs[6:]
    dp = lax.axis_index("dp")
    mp = lax.axis_index("mp")
    greet_all(dp, mp, size_dp, size_mp)
    mine[...] = jnp.zeros_like(mine)
    for index in range(5):
        mine[index : index + 1, :] = fold(parts[index][...])
    mine[...] = exchange("dp", dp, mp, mine, slots_dp, send, recv, 0)
    total = exchange("mp", mp, dp, mine, slots_mp, send, recv, size_dp)
    total = jnp.sum(total, axis=1, keepdims=True)
    for index in range(5):
        clip = jnp.maximum(1.0, jnp.sqrt(total[index : index + 1] / entries[index]) / CLIP)
        out[index : index + 1, :] = rate[8 + index : 9 + index, :] / clip


def clip_rates(cid, step_parts, rate, entries):
    size_dp = lax.axis_size("dp")
    size_mp = lax.axis_size("mp")
    vmem = pl.BlockSpec(memory_space=pltpu.VMEM)
    sems = size_dp + size_mp
    return pl.pallas_call(
        functools.partial(clip_kernel, entries, size_dp, size_mp),
        out_shape=jax.ShapeDtypeStruct((8, 128), jnp.float32),
        in_specs=[vmem] * 6,
        out_specs=vmem,
        scratch_shapes=[
            pltpu.VMEM((8, 128), jnp.float32),
            pltpu.VMEM((size_dp, 8, 128), jnp.float32),
            pltpu.VMEM((size_mp, 8, 128), jnp.float32),
            pltpu.SemaphoreType.DMA((sems,)),
            pltpu.SemaphoreType.DMA((sems,)),
        ],
        compiler_params=pltpu.CompilerParams(collective_id=cid, has_side_effects=True),
        cost_estimate=cost_of(8),
        name="clip_rates",
    )(*[lane_rows(v) for v in step_parts], rate)


UNROLL = 8


def lookup_kernel(shift, early, count_ref, key_ref, table_ref, out_ref, low_ref, square_ref, rows_ref):
    spots = out_ref.shape[0]
    vocab, width = table_ref.shape
    rows_ref[...] = jnp.zeros_like(rows_ref)

    def some(i, carry):
        for j in range(UNROLL):
            key = key_ref[i * UNROLL + j]
            place = key & ((1 << shift) - 1)
            rows_ref[pl.ds(place, 1), :] = table_ref[pl.ds(key >> shift, 1), :]
        return carry

    lax.fori_loop(0, (count_ref[0] + UNROLL - 1) // UNROLL, some, 0)

    def narrow(i, carry):
        at = pl.ds(pl.multiple_of(i * 256, 256), 256)
        out_ref[at, :] = rows_ref[at, :].astype(jnp.bfloat16)
        return carry

    lax.fori_loop(0, spots // 256, narrow, 0)
    strip = 64
    rest = vocab % strip
    done = vocab - rest
    low_ref[done - early :, :] = jnp.zeros(
        (low_ref.shape[0] - done + early, width), jnp.bfloat16
    )

    def squares(values, total):
        for row in range(0, values.shape[0], 8):
            piece = values[row : row + 8, :]
            total = total + piece * piece
        return total

    def lower(i, total):
        at = pl.ds(pl.multiple_of(i * strip, strip), strip)
        values = table_ref[at, :]
        start = pl.multiple_of(i * strip - early, strip)
        low_ref[pl.ds(start, strip), :] = values.astype(jnp.bfloat16)
        return squares(values, total)

    def square(i, total):
        at = pl.ds(pl.multiple_of(i * strip, strip), strip)
        return squares(table_ref[at, :], total)

    total = jnp.zeros((8, width), jnp.float32)
    total = lax.fori_loop(0, early // strip, square, total)
    total = lax.fori_loop(early // strip, done // strip, lower, total)
    if rest:
        values = table_ref[done:, :]
        total = squares(values, total)
        values = jnp.concatenate([values, jnp.zeros((strip - rest, width), jnp.float32)])
        low_ref[done - early : done - early + strip, :] = values.astype(jnp.bfloat16)
    folded = total[:, 0:128]
    for start in range(128, width, 128):
        folded = folded + total[:, start : start + 128]
    square_ref[...] = folded


def lookup(keys, count, table, spots, shift, early):
    vocab, width = table.shape
    smem = pl.BlockSpec(memory_space=pltpu.SMEM)
    vmem = pl.BlockSpec(memory_space=pltpu.VMEM)
    return pl.pallas_call(
        functools.partial(lookup_kernel, shift, early),
        out_shape=[
            jax.ShapeDtypeStruct((spots, width), jnp.bfloat16),
            jax.ShapeDtypeStruct((vocab + -vocab % HEAD_BLOCK - early, width), jnp.bfloat16),
            jax.ShapeDtypeStruct((8, 128), jnp.float32),
        ],
        in_specs=[smem, smem, vmem],
        out_specs=[vmem] * 3,
        scratch_shapes=[pltpu.VMEM((spots + 8, width), jnp.float32)],
        compiler_params=pltpu.CompilerParams(vmem_limit_bytes=VMEM_CAP),
        cost_estimate=cost_of(20),
        name="lookup",
    )(count, keys, table)


def scatter_kernel(shift, count_ref, key_ref, head_ref, rows_in_ref, grad_ref, rows_ref):
    spots = rows_in_ref.shape[0]
    width = grad_ref.shape[1]

    def widen(i, carry):
        at = pl.ds(pl.multiple_of(i * 256, 256), 256)
        rows_ref[at, :] = rows_in_ref[at, :].astype(jnp.float32)
        return carry

    lax.fori_loop(0, spots // 256, widen, 0)
    rows_ref[spots:, :] = jnp.zeros((8, width), jnp.float32)
    grad_ref[...] = head_ref[...].astype(jnp.float32)[: grad_ref.shape[0]]

    def some(i, carry):
        for j in range(UNROLL):
            key = key_ref[i * UNROLL + j]
            place = key & ((1 << shift) - 1)
            grad_ref[pl.ds(key >> shift, 1), :] += rows_ref[pl.ds(place, 1), :]
        return carry

    lax.fori_loop(0, (count_ref[0] + UNROLL - 1) // UNROLL, some, 0)


def scatter(keys, count, head_grad, rows, vocab, shift):
    spots, width = rows.shape
    smem = pl.BlockSpec(memory_space=pltpu.SMEM)
    vmem = pl.BlockSpec(memory_space=pltpu.VMEM)
    return pl.pallas_call(
        functools.partial(scatter_kernel, shift),
        out_shape=jax.ShapeDtypeStruct((vocab, width), jnp.float32),
        in_specs=[smem, smem, vmem, vmem],
        out_specs=vmem,
        scratch_shapes=[pltpu.VMEM((spots + 8, width), jnp.float32)],
        compiler_params=pltpu.CompilerParams(vmem_limit_bytes=VMEM_CAP),
        cost_estimate=cost_of(23),
        name="scatter",
    )(count, keys, head_grad, rows)


def norm_parts(values):
    centre = jnp.mean(values, axis=-1, keepdims=True)
    centred = values - centre
    scale = lax.rsqrt(jnp.mean(centred * centred, axis=-1, keepdims=True) + EPS_NORM)
    return centred * scale, scale


def norm_pull(values, gain, upstream):
    normed, scale = norm_parts(values)
    weighted = upstream * gain
    pulled = scale * (
        weighted
        - jnp.mean(weighted, axis=-1, keepdims=True)
        - normed * jnp.mean(weighted * normed, axis=-1, keepdims=True)
    )
    return (
        pulled,
        jnp.sum(upstream * normed, axis=0, keepdims=True),
        jnp.sum(upstream, axis=0, keepdims=True),
    )


def step_first(total, at, ins, outs):
    stream, norms = outs[0], ins[0]
    normed, scale = norm_parts(stream[at, :].astype(jnp.float32))
    return normed * norms[0:1, :] + norms[1:2, :]


def step_forward(row, total, at, ins, outs):
    stream, norms = ins
    values = stream[at, :].astype(jnp.float32) + total
    outs[0][at, :] = values
    normed, scale = norm_parts(values)
    return normed * norms[row : row + 1, :] + norms[row + 1 : row + 2, :]


def step_backward(row, total, at, ins, outs):
    stream, norms = ins[:2]
    pulled, dgain, dshift = norm_pull(
        stream[at, :].astype(jnp.float32), norms[row : row + 1, :], total
    )
    if len(ins) > 2:
        pulled = pulled + ins[2][at, :]
    if len(outs) > 1:
        outs[0][at, :] = pulled
    sums = outs[-1]

    @pl.when(at.start == 0)
    def _():
        sums[...] = jnp.zeros_like(sums)

    sums[0:1, :] += dgain
    sums[1:2, :] += dshift
    return pulled


def gelu_tanh(values):
    return jax.nn.gelu(values, approximate=True)


def local(
    token_ids,
    targets,
    starts,
    sources,
    embedding,
    w_qkv,
    w_out,
    w_fc,
    w_proj,
    norm_params,
    rows_table,
    cols_table,
    rows_qkv,
    cols_qkv,
    rows_out,
    cols_out,
    rows_fc,
    cols_fc,
    rows_proj,
    cols_proj,
    second_norms,
):
    bf16 = jnp.bfloat16
    f32 = jnp.float32
    size_mp = lax.axis_size("mp")
    size_dp = lax.axis_size("dp")
    dp = lax.axis_index("dp")
    mp = lax.axis_index("mp")
    tokens = token_ids.shape[0]
    seqs = tokens // LEN
    chips = size_mp // 2
    near = chips // seqs
    sharers = size_mp // seqs
    rows = tokens // size_mp
    vocab, part_width = embedding.shape
    width = part_width * size_dp
    first_row = mp * vocab
    spots = tokens * size_dp
    chunks_full = max(1, min(4, rows // 32))
    chunks_near = max(1, min(4, rows // 32))
    chunks_turn = max(1, min(4, rows // 32))

    def own_and_twins(weights, axis):
        low = [weight.astype(bf16) for weight in weights]
        found = [[weight] for weight in low]
        sent = jnp.concatenate(low, axis=axis)
        for turn in range(1, seqs):
            shift = [(i, (i + turn * sharers) % size_mp) for i in range(size_mp)]
            arrived = lax.ppermute(sent, "mp", shift)
            start = 0
            for index, weight in enumerate(low):
                size = weight.shape[axis]
                found[index].append(lax.slice_in_dim(arrived, start, start + size, axis=axis))
                start += size
        return [jnp.concatenate(pieces, axis=axis) for pieces in found]

    pair_fc, pair_qkv = own_and_twins((w_fc, w_qkv), 1)
    pair_proj, pair_out = own_and_twins((w_proj, w_out), 0)

    early = (vocab + -vocab % HEAD_BLOCK) * 2 // (10 * HEAD_BLOCK) * HEAD_BLOCK
    early_table = lax.all_gather(embedding[:early].astype(bf16), "dp", axis=1, tiled=True)

    both = jnp.stack([token_ids, sources]).reshape(-1, 128)
    both = small_gather("gather_ids", 0, both, "dp").reshape(size_dp, 2, tokens)
    all_ids = both[:, 0]
    all_sources = both[:, 1].reshape(-1)
    counts = jnp.sum(
        (all_sources[:, None] == jnp.arange(NSRC, dtype=jnp.int32)[None, :]).astype(f32), axis=0
    )

    piece = rows // chunks_turn
    token = jnp.arange(tokens, dtype=jnp.int32)
    place = (
        token // piece * (size_dp * piece)
        + (jnp.arange(size_dp, dtype=jnp.int32) * piece)[:, None]
        + token % piece
    )
    local_ids = all_ids - first_row
    inside = (local_ids >= 0) & (local_ids < vocab)
    shift = spots.bit_length()
    idle = ((vocab - 1) << shift) + spots
    keys = jnp.where(inside, (local_ids << shift) + place, idle)
    keys = jnp.sort(keys.reshape(-1))
    owned = jnp.sum(inside.astype(jnp.int32)).reshape(1)
    found, low_table, table_sq = lookup(keys, owned, embedding, spots, shift, early)
    found, early_table = lax.optimization_barrier((found, early_table))
    inner_one, stream0, wide_qkv, wide_out, wide_fc, wide_proj = line_call(
        "lookup_sum",
        1,
        found,
        [norm_params],
        [jax.ShapeDtypeStruct((rows, width), bf16)],
        step_first,
        size_dp * rows,
        part_width,
        chunks_turn,
        chips,
        near,
        70,
        [
            ("gather", 0, pair_qkv),
            ("gather", 1, pair_out),
            ("gather", 0, pair_fc),
            ("gather", 1, pair_proj),
        ],
        "gather",
        8,
    )
    low_table, inner_one = lax.optimization_barrier((low_table, inner_one))
    wide_table = (early_table, lax.all_gather(low_table, "dp", axis=1, tiled=True))
    row_f32 = jax.ShapeDtypeStruct((rows, width), f32)
    pair_f32 = jax.ShapeDtypeStruct((8, width), f32)
    my_starts = row_slice(starts, (mp // sharers) * LEN, LEN)[:, None]
    mixed = jnp.dot(inner_one, wide_qkv, preferred_element_type=f32).astype(bf16)
    attended = attend(mixed, my_starts)
    partial = jnp.dot(attended, wide_out, preferred_element_type=f32).astype(bf16)
    inner_two, stream1 = line_call(
        "attn_sum",
        3,
        partial,
        [stream0, norm_params],
        [row_f32],
        functools.partial(step_forward, 2),
        rows,
        width,
        chunks_near,
        near,
        near,
        32,
    )
    before = jnp.dot(inner_two, wide_fc, preferred_element_type=f32)
    hidden = gelu_tanh(before).astype(bf16)
    partial = jnp.dot(hidden, wide_proj, preferred_element_type=f32).astype(bf16)
    final, stream2 = line_call(
        "mlp_sum",
        4,
        partial,
        [stream1, norm_params],
        [row_f32],
        functools.partial(step_forward, 4),
        rows,
        width,
        chunks_full,
        near,
        chips,
        58,
        chunk_major=True,
    )

    edge = jnp.clip(VREAL - first_row, 0, vocab).astype(jnp.int32).reshape(1)

    def by_chunk(values):
        return values.reshape(size_mp, chunks_full, -1).swapaxes(0, 1).reshape(tokens)

    sources = by_chunk(sources)
    wanted = by_chunk(targets) - first_row
    wanted = jnp.where((wanted >= 0) & (wanted < vocab), wanted, -1).reshape(1, tokens)
    block = HEAD_BLOCK
    exps, tops, sums, picks = head_stats(wide_table, final, wanted, edge, block)
    tops = tops[:, 0]
    top = jnp.max(tops, axis=0)
    total = jnp.sum(sums[:, 0] * jnp.exp(tops - top[None, :]), axis=0)
    pick = jnp.sum(picks[:, 0], axis=0)
    stats = jnp.concatenate([v.reshape(-1, 128) for v in (top, total, pick)])
    stats = small_gather("gather_stats", 5, stats, "mp").reshape(size_mp, 3, tokens)
    highest = jnp.max(stats[:, 0], axis=0)
    log_total = highest + jnp.log(
        jnp.sum(stats[:, 1] * jnp.exp(stats[:, 0] - highest[None, :]), axis=0)
    )
    token_loss = log_total - jnp.sum(stats[:, 2], axis=0)
    member = (sources[:, None] == jnp.arange(NSRC, dtype=jnp.int32)[None, :]).astype(f32)
    loss_part = jnp.sum(member * token_loss[:, None], axis=0)
    weight = jnp.sum(member / (NSRC * jnp.maximum(counts, 1.0))[None, :], axis=1)
    scale = jnp.exp(tops - log_total[None, :]) * weight[None, :]
    dlogits, table_grad = head_back(
        exps, final, scale[:, None, :], weight[None, :], wanted, block
    )
    head_grad = lax.psum_scatter(table_grad, "dp", scatter_dimension=1, tiled=True)

    dbranch2, dstream2, norm3 = line_call(
        "final_back",
        6,
        (dlogits, *wide_table),
        [stream2, norm_params],
        [row_f32, pair_f32],
        functools.partial(step_backward, 4),
        rows,
        width,
        chunks_full,
        chips,
        near,
        65,
        product=True,
    )
    grad_proj = jnp.einsum("tf,td->fd", hidden, dbranch2, preferred_element_type=f32).astype(bf16)
    dhidden = jnp.einsum("td,fd->tf", dbranch2, wide_proj, preferred_element_type=f32)
    unused, gelu_pull = jax.vjp(gelu_tanh, before)
    dbefore = gelu_pull(dhidden)[0].astype(bf16)
    partial = jnp.einsum("tf,df->td", dbefore, wide_fc, preferred_element_type=f32).astype(bf16)
    dbranch1, dstream1, norm2 = line_call(
        "mlp_back",
        7,
        partial,
        [stream1, norm_params, dstream2],
        [row_f32, pair_f32],
        functools.partial(step_backward, 2),
        rows,
        width,
        chunks_near,
        near,
        near,
        34,
    )
    grad_fc = jnp.einsum("td,tf->df", inner_two, dbefore, preferred_element_type=f32).astype(bf16)
    grad_out = jnp.einsum("tf,td->fd", attended, dbranch1, preferred_element_type=f32).astype(bf16)
    dattended = jnp.einsum("td,fd->tf", dbranch1, wide_out, preferred_element_type=f32)
    dmixed = attend_back(mixed, my_starts, dattended.astype(bf16))
    partial = jnp.einsum("tc,dc->td", dmixed, wide_qkv, preferred_element_type=f32).astype(bf16)
    grad_qkv = jnp.einsum("td,tc->dc", inner_one, dmixed, preferred_element_type=f32).astype(bf16)
    drows, norm1, grad_proj, grad_out, grad_fc, grad_qkv, twins_wide, twins_tall = line_call(
        "attn_back",
        8,
        partial,
        [stream0, norm_params, dstream1],
        [pair_f32],
        functools.partial(step_backward, 0),
        rows,
        width,
        chunks_turn,
        near,
        chips,
        70,
        [
            ("scatter", 1, grad_proj),
            ("scatter", 1, grad_out),
            ("scatter", 0, grad_fc),
            ("scatter", 0, grad_qkv),
        ],
        "spread",
        9,
        seqs=seqs,
    )

    def from_twins(values, axis, sizes):
        starts = [(seqs - 1) * sum(sizes[:n]) for n in range(len(sizes))]
        found = []
        for turn in range(1, seqs):
            pieces = [
                lax.slice_in_dim(values, at + (turn - 1) * size, at + turn * size, axis=axis)
                for at, size in zip(starts, sizes)
            ]
            back = [(i, (i - turn * sharers) % size_mp) for i in range(size_mp)]
            found.append(lax.ppermute(jnp.concatenate(pieces, axis=axis), "mp", back))
        return found

    tall = [grad_proj.shape[0], grad_out.shape[0]]
    wide = [grad_fc.shape[1], grad_qkv.shape[1]]
    found_tall = from_twins(twins_tall, 0, tall)
    found_wide = from_twins(twins_wide, 1, wide)
    grad_table = scatter(keys, owned, head_grad, drows, vocab, shift)
    table_squares = grad_table * grad_table + EPS_ONE
    table_rows = jnp.sum(table_squares, axis=1)
    table_cols = jnp.sum(table_squares, axis=0)
    found_tall, found_wide, table_rows = lax.optimization_barrier(
        (found_tall, found_wide, table_rows)
    )
    for values in found_tall:
        grad_proj += values[: tall[0]].astype(f32)
        grad_out += values[tall[0] :].astype(f32)
    for values in found_wide:
        grad_fc += values[:, : wide[0]].astype(f32)
        grad_qkv += values[:, wide[0] :].astype(f32)

    weights = (embedding, w_qkv, w_out, w_fc, w_proj)
    grads = (grad_table, grad_qkv, grad_out, grad_fc, grad_proj)
    row_span = (size_mp, size_dp, size_mp, size_dp, size_mp)
    col_span = (size_dp, size_mp, size_dp, size_mp, size_dp)
    full = tuple(
        (g.shape[0] * r, g.shape[1] * c) for g, r, c in zip(grads, row_span, col_span)
    )
    squares = [gradient * gradient + EPS_ONE for gradient in grads[1:]]
    rows_new, cols_new, loss_sums, grad_norms, second_new, norms_new, rates = update_stats(
        10,
        [table_rows] + [jnp.sum(square, axis=1) for square in squares],
        (rows_table, rows_qkv, rows_out, rows_fc, rows_proj),
        [table_cols] + [jnp.sum(square, axis=0) for square in squares],
        (cols_table, cols_qkv, cols_out, cols_fc, cols_proj),
        [table_sq] + [jnp.sum(value * value, axis=0) for value in weights[1:]],
        loss_part,
        (norm1, norm2, norm3),
        norm_params,
        second_norms,
        full,
    )
    steps = [
        grads[n] * lax.rsqrt(rows_new[n][:, None] * cols_new[n][None, :] / rates[n, 0])
        for n in range(5)
    ]
    factors = clip_rates(
        11, [jnp.sum(step * step, axis=0) for step in steps], rates, [r * c for r, c in full]
    )
    updated = [weights[n] - factors[n, 0] * steps[n] for n in range(5)]
    return (
        loss_sums,
        counts,
        grad_table,
        rows_new[0],
        cols_new[0],
        updated[0],
        grad_qkv,
        rows_new[1],
        cols_new[1],
        updated[1],
        grad_out,
        rows_new[2],
        cols_new[2],
        updated[2],
        grad_fc,
        rows_new[3],
        cols_new[3],
        updated[3],
        grad_proj,
        rows_new[4],
        cols_new[4],
        updated[4],
        grad_norms,
        second_new,
        norms_new,
    )


def solution(mesh):
    placed = (
        P("dp"),
        P("dp"),
        P("dp"),
        P("dp"),
        P("mp", "dp"),
        P("dp", "mp"),
        P("mp", "dp"),
        P("dp", "mp"),
        P("mp", "dp"),
        P(),
        P("mp"),
        P("dp"),
        P("dp"),
        P("mp"),
        P("mp"),
        P("dp"),
        P("dp"),
        P("mp"),
        P("mp"),
        P("dp"),
        P(),
    )
    return jax.shard_map(
        local,
        mesh=mesh,
        in_specs=placed,
        out_specs=(
            P(),
            P(),
            P("mp", "dp"),
            P("mp"),
            P("dp"),
            P("mp", "dp"),
            P("dp", "mp"),
            P("dp"),
            P("mp"),
            P("dp", "mp"),
            P("mp", "dp"),
            P("mp"),
            P("dp"),
            P("mp", "dp"),
            P("dp", "mp"),
            P("dp"),
            P("mp"),
            P("dp", "mp"),
            P("mp", "dp"),
            P("mp"),
            P("dp"),
            P("mp", "dp"),
            P(),
            P(),
            P(),
        ),
        check_vma=False,
    )
```

```python
import functools
import math

import jax
import jax.numpy as jnp
from jax import lax
from jax.experimental import pallas as pl
from jax.experimental.pallas import tpu as pltpu
from jax.sharding import PartitionSpec as P

HD = 64
VREAL = 50257
LEN = 1024
NSRC = 4
STEP = 10


EPS_NORM = 1e-05
EPS_ONE = 1e-30
CLIP = 1.0
RHO = 0.5
MASKED = -1e30
QUERIES = 256
HEAD_BLOCK = 640
MESH = pl.DeviceIdType.MESH
VMEM_CAP = 56 * 2**20


def cost_of(time):
    return pl.CostEstimate(
        flops=time * 1000000000, bytes_accessed=time * 3000000, transcendentals=0
    )


def row_slice(values, start, count):
    return lax.dynamic_slice_in_dim(values, start, count, 0)


def line_kernel(
    nr, ng, chunks, shapes, n_in, n_out, step, sides, turn, side_ticks, product, chunk_major, *refs
):
    (rows_r, width_r), (rows_g, width_g) = shapes
    if product:
        dl, *tables = refs[:3]
        first = 3
    else:
        part = refs[0] if nr else None
        first = 1 if nr else 0
    ins = refs[first : first + n_in]
    refs = refs[first + n_in :]
    side_ins, refs = refs[: len(sides)], refs[len(sides) :]
    if ng:
        whole, refs = refs[0], refs[1:]
    outs = refs[:n_out]
    refs = refs[n_out:]
    scatters = [index for index, (kind, unused) in enumerate(sides) if kind == "scatter"]
    side_outs, refs = refs[: len(sides)], refs[len(sides) :]
    twin_outs, scratch = (refs[:2], refs[2:]) if scatters else ([], refs)
    side_scratch, scratch = scratch[: 3 * len(sides)], scratch[3 * len(sides) :]
    if turn:
        cast, turn_send, turn_recv = scratch[-3:]
    if product:
        part, dl_buf, total_ref, dl_sem = scratch[-4:]
    size_dp = lax.axis_size("dp")
    dp = lax.axis_index("dp")
    mp = lax.axis_index("mp")
    z = mp // 2
    core = lax.rem(mp, 2)
    other = mp + 1 - 2 * core
    piece_r = rows_r // chunks
    piece_g = rows_g // chunks
    small = min(piece_r, piece_g)
    late = 1 if turn else 0
    ahead = 1 if product else 0
    most = max(nr, ng)
    zb = lax.rem(z, most)
    if nr:
        zr = lax.rem(z, nr)
        last_r = nr - 1
    if ng:
        zg = lax.rem(z, ng)
        last_g = ng - 1

    barrier = pltpu.get_barrier_semaphore()
    pl.semaphore_signal(barrier, inc=1, device_id=(dp, other), device_id_type=MESH)

    @pl.when(zb > 0)
    def _():
        pl.semaphore_signal(barrier, inc=1, device_id=(dp, mp - 2), device_id_type=MESH)

    @pl.when(zb < most - 1)
    def _():
        pl.semaphore_signal(barrier, inc=1, device_id=(dp, mp + 2), device_id_type=MESH)

    if sides or turn:
        for hop in range(1, size_dp):
            pl.semaphore_signal(
                barrier,
                inc=1,
                device_id=(lax.rem(dp + hop, size_dp), mp),
                device_id_type=MESH,
            )
    greeted = (size_dp if sides or turn else 1) + (zb > 0).astype(jnp.int32) + (zb < most - 1).astype(jnp.int32)
    pl.semaphore_wait(barrier, greeted)

    def share(axis, length, which):
        at = pl.ds(pl.multiple_of(which * length, length), length)
        return (at, slice(None)) if axis == 0 else (slice(None), at)

    def to_peer(src, dst, send, recv, peer):
        return pltpu.make_async_remote_copy(
            src_ref=src,
            dst_ref=dst,
            send_sem=send,
            recv_sem=recv,
            device_id=(peer, mp),
            device_id_type=MESH,
        )

    relay = size_dp == 4
    beside_x = dp + 1 - 2 * lax.rem(dp, 2)
    beside_y = lax.rem(dp + 2, 4)
    across = 3 - dp

    def half_share(axis, length, which, height, part):
        if axis == 0:
            return (pl.ds(pl.multiple_of(which * length + part * height, height), height), slice(None))
        at = pl.ds(pl.multiple_of(which * length, length), length)
        return (pl.ds(part * height, height), at)

    first_copies, more_copies, relays = [], [], []
    for index, (kind, axis) in enumerate(sides):
        src, dst = side_ins[index], side_outs[index]
        send, recv, slots = side_scratch[3 * index : 3 * index + 3]
        if kind == "gather":
            length, height = src.shape[axis], src.shape[0] // 2
        else:
            length = src.shape[axis] // size_dp
            height = (length if axis == 0 else src.shape[0]) // 2
        if not relay:
            for hop in range(1, size_dp):
                peer = lax.rem(dp + hop, size_dp)
                if kind == "gather":
                    source, target = src, dst.at[share(axis, length, dp)]
                else:
                    source, target = src.at[share(axis, length, peer)], slots.at[hop]
                more_copies.append(to_peer(source, target, send.at[hop], recv.at[hop], peer))
            continue
        for side, near_one, far_one in ((0, beside_x, beside_y), (1, beside_y, beside_x)):
            sems = [(send.at[3 * side + n], recv.at[3 * side + n]) for n in range(3)]
            if kind == "gather":
                mine = src.at[pl.ds(side * height, height)]
                here = dst.at[half_share(axis, length, dp, height, side)]
                passed = dst.at[half_share(axis, length, near_one, height, side)]
                arrives = to_peer(mine, here, *sems[0], near_one)
                first_copies.append(arrives)
                more_copies.append(to_peer(mine, here, *sems[1], far_one))
                relays.append((arrives, None, to_peer(passed, passed, *sems[2], far_one)))
            else:
                arrives = to_peer(
                    src.at[half_share(axis, length, across, height, side)],
                    slots.at[4 * side],
                    *sems[0],
                    near_one,
                )
                first_copies.append(arrives)
                more_copies.append(
                    to_peer(
                        src.at[half_share(axis, length, near_one, height, side)],
                        slots.at[4 * side + 1],
                        *sems[1],
                        near_one,
                    )
                )
                summed = to_peer(
                    slots.at[4 * side + 2], slots.at[4 * side + 3], *sems[2], far_one
                )
                own = src.at[half_share(axis, length, far_one, height, side)]
                relays.append((arrives, (own, slots, 4 * side, height), summed))

    def pass_on(arrives, adding, copy):
        arrives.wait_recv()
        if adding is not None:
            own, slots, at, height = adding
            both = own[...].astype(jnp.float32) + slots[at].astype(jnp.float32)
            slots[at + 2] = both.astype(slots.dtype)
        copy.start()

    jobs = [copy.start for copy in first_copies + more_copies]
    jobs += [functools.partial(pass_on, *one) for one in relays]

    def side_jobs(now):
        for spot in range(side_ticks if jobs else 0):
            chosen = jobs[len(jobs) * spot // side_ticks : len(jobs) * (spot + 1) // side_ticks]

            @pl.when(now == spot)
            def _():
                for job in chosen:
                    job()

    if nr:
        half, from_left, from_right, going = scratch[:4]
        half_send, half_recv, rs_send, left_recv, right_recv = scratch[4:9]
        scratch = scratch[9:]
    if ng:
        core_send, core_recv, to_right, to_left, ag_left, ag_right = scratch[:6]

    def part_rows(block, k):
        return pl.ds(pl.multiple_of(block * rows_r + k * piece_r, piece_r), piece_r)

    def whole_rows(block, k):
        if chunk_major:
            start = k * (2 * ng * piece_g) + block * piece_g
            return pl.ds(pl.multiple_of(start, piece_g), piece_g)
        return pl.ds(pl.multiple_of(block * rows_g + k * piece_g, piece_g), piece_g)

    def remote(src, dst, send, recv, target):
        return pltpu.make_async_remote_copy(
            src_ref=src,
            dst_ref=dst,
            send_sem=send,
            recv_sem=recv,
            device_id=(dp, target),
            device_id_type=MESH,
        )

    if nr:

        def half_copy(dest, k):
            return remote(
                part.at[part_rows(2 * dest + 1 - core, k)],
                half.at[dest, k],
                half_send.at[dest, k],
                half_recv.at[dest, k],
                other,
            )

        def send_halves(k, carry):
            for dest in range(nr):
                half_copy(dest, k).start()
            return carry

        if not product:
            lax.fori_loop(0, chunks, send_halves, 0)

        def right_copy(dest, k):
            return remote(
                going.at[dest, k],
                from_left.at[dest, k],
                rs_send.at[dest, k],
                left_recv.at[dest, k],
                mp + 2,
            )

        def left_copy(dest, k):
            return remote(
                going.at[dest, k],
                from_right.at[dest, k],
                rs_send.at[dest, k],
                right_recv.at[dest, k],
                mp - 2,
            )

        def chip_sum(dest, k):
            half_copy(dest, k).wait_recv()
            mine = part[part_rows(2 * dest + core, k), :].astype(jnp.float32)
            return mine + half[dest, k].astype(jnp.float32)

        def pass_right(dest, k):
            total = chip_sum(dest, k)

            @pl.when(zr == 0)
            def _():
                going[dest, k] = total.astype(jnp.bfloat16)

            @pl.when(zr > 0)
            def _():
                right_copy(dest, k).wait_recv()
                both = total + from_left[dest, k].astype(jnp.float32)
                going[dest, k] = both.astype(jnp.bfloat16)

            right_copy(dest, k).start()

        def pass_left(dest, k):
            total = chip_sum(dest, k)

            @pl.when(zr == last_r)
            def _():
                going[dest, k] = total.astype(jnp.bfloat16)

            @pl.when(zr < last_r)
            def _():
                left_copy(dest, k).wait_recv()
                both = total + from_right[dest, k].astype(jnp.float32)
                going[dest, k] = both.astype(jnp.bfloat16)

            left_copy(dest, k).start()

    if ng:

        def gathered(block, k, send, recv, target):
            where = whole.at[whole_rows(2 * block + core, k)]
            return remote(where, where, send.at[block, k], recv.at[block, k], target)

        def core_copy(block, k):
            return gathered(block, k, core_send, core_recv, other)

        def ag_right_copy(block, k):
            return gathered(block, k, to_right, ag_left, mp + 2)

        def ag_left_copy(block, k):
            return gathered(block, k, to_left, ag_right, mp - 2)

    def own_rows(k):
        total = None
        if nr:
            total = chip_sum(zr, k)
            zero = jnp.zeros((piece_r, width_r), jnp.float32)

            @pl.when(zr > 0)
            def _():
                right_copy(zr, k).wait_recv()

            @pl.when(zr < last_r)
            def _():
                left_copy(zr, k).wait_recv()

            total += jnp.where(zr > 0, from_left[zr, k].astype(jnp.float32), zero)
            total += jnp.where(zr < last_r, from_right[zr, k].astype(jnp.float32), zero)
        if turn == "gather":
            cast[k] = total.astype(cast.dtype)
            for hop in range(1, size_dp):
                turn_copy(hop, k).start()
            mine = pl.ds(pl.multiple_of(dp * small, small), small)
            outs[0][own_place(k, dp)] = cast[k, mine, :]
            return
        at = pl.ds(pl.multiple_of(k * piece_r, piece_r), piece_r)
        ready = step(total, at, ins, outs)
        if turn == "spread":
            cast[k] = ready.astype(cast.dtype)
            for hop in range(1, size_dp):
                turn_copy(hop, k).start()
            whole[own_place(k, dp)] = cast[
                k, :, pl.ds(pl.multiple_of(dp * width_g, width_g), width_g)
            ]
        elif ng:
            whole[whole_rows(2 * zg + core, k), :] = ready.astype(whole.dtype)
            start_gather(k)

    def own_place(k, peer):
        if turn == "gather":
            return (
                pl.ds(pl.multiple_of(k * small, small), small),
                pl.ds(pl.multiple_of(peer * width_r, width_r), width_r),
            )
        start = (2 * zg + core) * rows_g + k * piece_g + peer * small
        return (pl.ds(pl.multiple_of(start, small), small), slice(None))

    def turn_copy(hop, k):
        peer = lax.rem(dp + hop, size_dp)
        if turn == "gather":
            src = cast.at[k, pl.ds(pl.multiple_of(peer * small, small), small)]
            dst = outs[0].at[own_place(k, dp)]
        else:
            src = cast.at[k, :, pl.ds(pl.multiple_of(peer * width_g, width_g), width_g)]
            dst = whole.at[own_place(k, dp)]
        return to_peer(src, dst, turn_send.at[hop, k], turn_recv.at[hop, k], peer)

    def turned_rows(k):
        for hop in range(1, size_dp):
            turn_copy(hop, k).wait_recv()
        if turn == "gather":
            at = pl.ds(pl.multiple_of(k * piece_g, piece_g), piece_g)
            ready = step(None, at, ins, outs)
            whole[whole_rows(2 * zg + core, k), :] = ready.astype(whole.dtype)
        start_gather(k)

    def start_gather(k):
        core_copy(zg, k).start()

        @pl.when(zg < last_g)
        def _():
            ag_right_copy(zg, k).start()

        @pl.when(zg > 0)
        def _():
            ag_left_copy(zg, k).start()

    def inside(k):
        return (k >= 0) & (k < chunks)

    def own_lag(chip):
        if not nr:
            return 0
        at = lax.rem(chip, nr)
        return jnp.maximum(at, last_r - at) + ahead

    def dl_copy(k):
        columns = dl_buf.shape[2]
        return pltpu.make_async_copy(
            dl.at[:, pl.ds(pl.multiple_of(k * columns, columns), columns)],
            dl_buf.at[lax.rem(k, 2)],
            dl_sem.at[lax.rem(k, 2)],
        )

    def make_part(k):
        dl_copy(k).wait()

        @pl.when(k + 1 < chunks)
        def _():
            dl_copy(k + 1).start()

        slot = lax.rem(k, 2)

        start = 0
        for piece in tables:
            found = lax.dot_general(
                dl_buf[slot, start : start + piece.shape[0], :],
                piece[...],
                (((0,), (0,)), ((), ())),
                preferred_element_type=jnp.float32,
            )
            if start:
                total_ref[...] += found
            else:
                total_ref[...] = found
            start += piece.shape[0]
        for block in range(2 * nr):
            part[part_rows(block, k), :] = total_ref[
                block * piece_r : block * piece_r + piece_r, :
            ].astype(jnp.bfloat16)
        send_halves(k, 0)

    if product:
        dl_copy(0).start()

    def tick(now, carry):
        side_jobs(now)
        if nr:
            k_right = now - zr - ahead
            k_left = now - (last_r - zr) - ahead
            for far in range(last_r):

                @pl.when(inside(k_right) & (last_r - far > zr))
                def _():
                    pass_right(last_r - far, k_right)

                @pl.when(inside(k_left) & (far < zr))
                def _():
                    pass_left(far, k_left)

        k_own = now - own_lag(z)

        @pl.when(inside(k_own))
        def _():
            own_rows(k_own)

        if turn:

            @pl.when(inside(k_own - 1))
            def _():
                turned_rows(k_own - 1)

        if ng:
            for block in range(ng):
                k = now - (own_lag(z - zg + block) + late + jnp.abs(zg - block))

                @pl.when(inside(k) & (block < zg))
                def _():
                    ag_right_copy(block, k).wait_recv()
                    core_copy(block, k).start()

                    @pl.when(zg < last_g)
                    def _():
                        ag_right_copy(block, k).start()

                @pl.when(inside(k) & (block > zg))
                def _():
                    ag_left_copy(block, k).wait_recv()
                    core_copy(block, k).start()

                    @pl.when(zg > 0)
                    def _():
                        ag_left_copy(block, k).start()

        if product:

            @pl.when(now < chunks)
            def _():
                make_part(now)

        return carry

    ticks = ahead + chunks + (nr - 1 if nr else 0) + (ng - 1 if ng else 0) + late
    lax.fori_loop(0, ticks, tick, 0)

    def finish(k, carry):
        if turn:
            for hop in range(1, size_dp):
                turn_copy(hop, k).wait_send()
        if nr:
            for block in range(nr):
                half_copy(block, k).wait_send()

                @pl.when(block != zr)
                def _():
                    right_copy(block, k).wait_send()

        if ng:
            for block in range(ng):
                core_copy(block, k).wait()

                @pl.when((zg < last_g) & (block <= zg))
                def _():
                    ag_right_copy(block, k).wait_send()

                @pl.when((zg > 0) & (block >= zg))
                def _():
                    ag_left_copy(block, k).wait_send()

        return carry

    lax.fori_loop(0, chunks, finish, 0)
    for index, (kind, axis) in enumerate(sides):
        if kind == "gather":
            length = side_ins[index].shape[axis]
            side_outs[index][share(axis, length, dp)] = side_ins[index][...]
    for copy in first_copies:
        copy.wait_send()
    for copy in more_copies:
        copy.wait()
    for unused, unused, copy in relays:
        copy.wait()
    placed = [0, 0]
    for index in scatters:
        axis = sides[index][1]
        src, dst = side_ins[index], side_outs[index]
        slots = side_scratch[3 * index + 2]
        length = src.shape[axis] // size_dp
        height = (length if axis == 0 else src.shape[0]) // 2
        if relay:
            total = []
            for side in range(2):
                one = src[half_share(axis, length, dp, height, side)].astype(jnp.float32)
                one += slots[4 * side + 1].astype(jnp.float32)
                one += slots[4 * side + 3].astype(jnp.float32)
                total.append(one)
            total = jnp.concatenate(total)
        else:
            total = src[share(axis, length, dp)].astype(jnp.float32)
            for hop in range(1, size_dp):
                total += slots[hop].astype(jnp.float32)
        twins = twin_outs[axis]
        at = placed[axis]
        if axis == 0:
            own = dst.shape[1]
            dst[...] = total[:, :own]
            more = total.shape[1] - own
            twins[:, at : at + more] = total[:, own:].astype(twins.dtype)
        else:
            own = dst.shape[0]
            dst[...] = total[:own, :]
            more = total.shape[0] - own
            twins[at : at + more, :] = total[own:, :].astype(twins.dtype)
        placed[axis] += more


def line_call(
    name,
    cid,
    partial,
    ins,
    out_types,
    step,
    rows,
    width,
    chunks,
    nr,
    ng,
    time,
    sides=(),
    turn=None,
    side_ticks=0,
    product=False,
    chunk_major=False,
    seqs=1,
):
    piece = rows // chunks
    size_dp = lax.axis_size("dp")
    reduced = gathered = (rows, width)
    if turn == "gather":
        gathered = (rows // size_dp, width * size_dp)
    elif turn == "spread":
        gathered = (rows * size_dp, width // size_dp)
    out_shape = []
    if ng:
        out_shape.append(
            jax.ShapeDtypeStruct((2 * ng * gathered[0], gathered[1]), jnp.bfloat16)
        )
    out_shape += out_types
    dma = pltpu.SemaphoreType.DMA
    scratch = []
    twin_shapes = [[0, 0], [0, 0]]
    for kind, axis, values in sides:
        shape = list(values.shape)
        scratch += [dma((max(size_dp, 6),)), dma((max(size_dp, 6),))]
        if kind == "gather":
            shape[axis] *= size_dp
            out_shape.append(jax.ShapeDtypeStruct(tuple(shape), values.dtype))
            scratch.append(pltpu.VMEM((16, 128), values.dtype))
        else:
            shape[axis] //= size_dp
            own = list(shape)
            own[1 - axis] //= seqs
            out_shape.append(jax.ShapeDtypeStruct(tuple(own), jnp.float32))
            twin_shapes[axis][axis] = shape[axis]
            twin_shapes[axis][1 - axis] += shape[1 - axis] - own[1 - axis]
            slots = (8, shape[0] // 2, shape[1]) if size_dp == 4 else (size_dp, *shape)
            scratch.append(pltpu.VMEM(slots, values.dtype))
    if any(side[0] == "scatter" for side in sides):
        out_shape += [jax.ShapeDtypeStruct(tuple(shape), jnp.bfloat16) for shape in twin_shapes]
    if nr:
        scratch += [pltpu.VMEM((nr, chunks, piece, width), jnp.bfloat16)] * 4
        scratch += [dma((nr, chunks))] * 5
    if ng:
        scratch += [dma((ng, chunks))] * 6
    if turn:
        scratch.append(pltpu.VMEM((chunks, piece, width), jnp.bfloat16))
        scratch += [dma((size_dp, chunks))] * 2
    if product:
        dl = partial[0]
        columns = dl.shape[1] // chunks
        scratch += [
            pltpu.VMEM((2 * nr * rows, width), jnp.bfloat16),
            pltpu.VMEM((2, dl.shape[0], columns), jnp.bfloat16),
            pltpu.VMEM((columns, width), jnp.float32),
            dma((2,)),
        ]
        partial = list(partial)
    else:
        partial = [partial] if nr else []
    args = partial + list(ins) + [side[2] for side in sides]
    vmem = pl.BlockSpec(memory_space=pltpu.VMEM)
    call = pl.pallas_call(
        functools.partial(
            line_kernel,
            nr,
            ng,
            chunks,
            (reduced, gathered),
            len(ins),
            len(out_types),
            step,
            tuple(side[:2] for side in sides),
            turn,
            side_ticks,
            product,
            chunk_major,
        ),
        out_shape=out_shape,
        in_specs=[pl.BlockSpec(memory_space=pl.ANY) if product and n == 0 else vmem for n in range(len(args))],
        out_specs=[vmem] * len(out_shape),
        scratch_shapes=scratch,
        compiler_params=pltpu.CompilerParams(
            collective_id=cid, has_side_effects=True, vmem_limit_bytes=VMEM_CAP
        ),
        cost_estimate=cost_of(time),
        name=name,
    )
    return list(call(*args))


def head_stats_kernel(block, tile, early, early_ref, late_ref, final_ref, wanted_ref, edge_ref, exp_ref, top_ref, sum_ref, pick_ref):
    j = pl.program_id(0)
    tokens = final_ref.shape[0]
    place = j * block + lax.broadcasted_iota(jnp.int32, (block, 1), 0)
    valid = place < edge_ref[0]
    table = jnp.where(j < early, early_ref[...], late_ref[...])

    def weigh(masked):
        for start in range(0, tokens, tile):
            at = pl.ds(start, tile)
            logits = lax.dot_general(
                table,
                final_ref[at, :],
                (((1,), (1,)), ((), ())),
                preferred_element_type=jnp.float32,
            )
            if masked:
                logits = jnp.where(valid, logits, MASKED)
            top = jnp.max(logits, axis=0, keepdims=True)
            weights = jnp.exp(logits - top)
            exp_ref[:, at] = weights.astype(jnp.bfloat16)
            top_ref[0, :, at] = top
            sum_ref[0, :, at] = jnp.sum(weights, axis=0, keepdims=True)
            pick_ref[0, :, at] = jnp.sum(
                jnp.where(place == wanted_ref[:, at], logits, 0.0), axis=0, keepdims=True
            )

    whole = (j + 1) * block <= edge_ref[0]

    @pl.when(whole)
    def _():
        weigh(False)

    @pl.when(jnp.logical_not(whole))
    def _():
        weigh(True)


def head_stats(tables, final, wanted, edge, block, tile=512):
    early = tables[0].shape[0] // block
    rows = sum(table.shape[0] for table in tables)
    width = tables[0].shape[1]
    tokens = final.shape[0]
    steps = rows // block
    row = jax.ShapeDtypeStruct((steps, 1, tokens), jnp.float32)
    row_spec = pl.BlockSpec((1, 1, tokens), lambda j: (j, 0, 0))
    return pl.pallas_call(
        functools.partial(head_stats_kernel, block, tile, early),
        grid=(steps,),
        out_shape=[jax.ShapeDtypeStruct((steps * block, tokens), jnp.bfloat16), row, row, row],
        in_specs=[
            pl.BlockSpec((block, width), lambda j: (jnp.minimum(j, early - 1), 0)),
            pl.BlockSpec((block, width), lambda j: (jnp.maximum(j - early, 0), 0)),
            pl.BlockSpec((tokens, width), lambda j: (0, 0)),
            pl.BlockSpec((1, tokens), lambda j: (0, 0)),
            pl.BlockSpec(memory_space=pltpu.SMEM),
        ],
        out_specs=[pl.BlockSpec((block, tokens), lambda j: (j, 0)), row_spec, row_spec, row_spec],
        compiler_params=pltpu.CompilerParams(vmem_limit_bytes=56 * 2**20),
        cost_estimate=pl.CostEstimate(
            flops=2 * rows * width * tokens,
            bytes_accessed=2 * rows * (width + tokens),
            transcendentals=rows * tokens,
        ),
        name="head_stats",
    )(*tables, final, wanted, edge)


def head_back_kernel(block, tile, exp_ref, final_ref, scale_ref, weight_ref, wanted_ref, dl_ref, grad_ref):
    j = pl.program_id(0)
    tokens = final_ref.shape[0]
    place = j * block + lax.broadcasted_iota(jnp.int32, (block, 1), 0)
    for start in range(0, tokens, tile):
        at = pl.ds(start, tile)
        dl = exp_ref[:, at].astype(jnp.float32) * scale_ref[0, :, at]
        dl = dl - jnp.where(place == wanted_ref[:, at], weight_ref[:, at], 0.0)
        dl_ref[:, at] = dl.astype(jnp.bfloat16)
    strip = block // max(1, block // 256)
    for start in range(0, block, strip):
        at = pl.ds(start, strip)
        grad_ref[at, :] = jnp.dot(
            dl_ref[at, :], final_ref[...], preferred_element_type=jnp.float32
        ).astype(jnp.bfloat16)


def head_back(exps, final, scale, weight, wanted, block, tile=256):
    rows, tokens = exps.shape
    width = final.shape[1]
    return pl.pallas_call(
        functools.partial(head_back_kernel, block, tile),
        grid=(rows // block,),
        out_shape=[
            jax.ShapeDtypeStruct((rows, tokens), jnp.bfloat16),
            jax.ShapeDtypeStruct((rows, width), jnp.bfloat16),
        ],
        in_specs=[
            pl.BlockSpec((block, tokens), lambda j: (j, 0)),
            pl.BlockSpec((tokens, width), lambda j: (0, 0)),
            pl.BlockSpec((1, 1, tokens), lambda j: (j, 0, 0)),
            pl.BlockSpec((1, tokens), lambda j: (0, 0)),
            pl.BlockSpec((1, tokens), lambda j: (0, 0)),
        ],
        out_specs=[
            pl.BlockSpec((block, tokens), lambda j: (j, 0)),
            pl.BlockSpec((block, width), lambda j: (j, 0)),
        ],
        compiler_params=pltpu.CompilerParams(vmem_limit_bytes=56 * 2**20),
        cost_estimate=pl.CostEstimate(
            flops=2 * rows * width * tokens,
            bytes_accessed=2 * rows * (width + 2 * tokens),
            transcendentals=0,
        ),
        name="head_back",
    )(exps, final, scale, weight, wanted)


def head_weights(mixed_ref, starts_ref, base, at, seen):
    query = mixed_ref[at : at + QUERIES, base : base + HD]
    keys = mixed_ref[0:seen, base + HD : base + 2 * HD]
    values = mixed_ref[0:seen, base + 2 * HD : base + 3 * HD]
    scores = lax.dot_general(
        query, keys, (((1,), (1,)), ((), ())), preferred_element_type=jnp.float32
    )
    row = at + lax.broadcasted_iota(jnp.int32, (QUERIES, seen), 0)
    column = lax.broadcasted_iota(jnp.int32, (QUERIES, seen), 1)
    allowed = (column <= row) & (column >= starts_ref[at : at + QUERIES, :])
    scores = jnp.where(allowed, scores * HD ** (-0.5), MASKED)
    weights = jnp.exp(scores - jnp.max(scores, axis=1, keepdims=True))
    probs = weights / jnp.sum(weights, axis=1, keepdims=True)
    return query, keys, values, probs


def attend_kernel(mixed_ref, starts_ref, out_ref):
    length = mixed_ref.shape[0]
    for at in range(0, length, QUERIES):
        found = []
        for head in range(2):
            unused, unused, values, probs = head_weights(
                mixed_ref, starts_ref, head * 3 * HD, at, at + QUERIES
            )
            found.append(
                jnp.dot(probs.astype(jnp.bfloat16), values, preferred_element_type=jnp.float32)
            )
        out_ref[at : at + QUERIES, :] = jnp.concatenate(found, axis=1).astype(jnp.bfloat16)


def attend(mixed, starts):
    length, columns = mixed.shape
    pairs = columns // (6 * HD)
    return pl.pallas_call(
        attend_kernel,
        grid=(pairs,),
        out_shape=jax.ShapeDtypeStruct((length, pairs * 2 * HD), jnp.bfloat16),
        in_specs=[
            pl.BlockSpec((length, 6 * HD), lambda j: (0, j)),
            pl.BlockSpec((length, 1), lambda j: (0, 0)),
        ],
        out_specs=pl.BlockSpec((length, 2 * HD), lambda j: (0, j)),
        compiler_params=pltpu.CompilerParams(vmem_limit_bytes=40 * 2**20),
        cost_estimate=pl.CostEstimate(
            flops=8 * pairs * length * length * HD,
            bytes_accessed=2 * length * columns,
            transcendentals=pairs * length * length,
        ),
        name="attend",
    )(mixed, starts)


def attend_back_kernel(mixed_ref, starts_ref, upstream_ref, out_ref, sums_ref):
    length = mixed_ref.shape[0]
    sums_ref[...] = jnp.zeros_like(sums_ref)
    rows = (((0,), (0,)), ((), ()))
    for at in range(0, length, QUERIES):
        seen = at + QUERIES
        for head in range(2):
            base = head * 3 * HD
            query, keys, values, probs = head_weights(mixed_ref, starts_ref, base, at, seen)
            upstream = upstream_ref[at:seen, head * HD : head * HD + HD]
            dprobs = lax.dot_general(
                upstream, values, (((1,), (1,)), ((), ())), preferred_element_type=jnp.float32
            )
            inner = jnp.sum(probs * dprobs, axis=1, keepdims=True)
            dscores = (probs * (dprobs - inner)).astype(jnp.bfloat16)
            dquery = jnp.dot(dscores, keys, preferred_element_type=jnp.float32)
            dkeys = lax.dot_general(dscores, query, rows, preferred_element_type=jnp.float32)
            dvalues = lax.dot_general(
                probs.astype(jnp.bfloat16), upstream, rows, preferred_element_type=jnp.float32
            )
            sums_ref[at:seen, base : base + HD] = dquery * HD ** (-0.5)
            sums_ref[0:seen, base + HD : base + 2 * HD] += dkeys * HD ** (-0.5)
            sums_ref[0:seen, base + 2 * HD : base + 3 * HD] += dvalues
    out_ref[...] = sums_ref[...].astype(jnp.bfloat16)


def attend_back(mixed, starts, upstream):
    length, columns = mixed.shape
    pairs = columns // (6 * HD)
    return pl.pallas_call(
        attend_back_kernel,
        grid=(pairs,),
        out_shape=jax.ShapeDtypeStruct((length, columns), jnp.bfloat16),
        in_specs=[
            pl.BlockSpec((length, 6 * HD), lambda j: (0, j)),
            pl.BlockSpec((length, 1), lambda j: (0, 0)),
            pl.BlockSpec((length, 2 * HD), lambda j: (0, j)),
        ],
        out_specs=pl.BlockSpec((length, 6 * HD), lambda j: (0, j)),
        scratch_shapes=[pltpu.VMEM((length, 6 * HD), jnp.float32)],
        compiler_params=pltpu.CompilerParams(vmem_limit_bytes=40 * 2**20),
        cost_estimate=pl.CostEstimate(
            flops=20 * pairs * length * length * HD,
            bytes_accessed=4 * length * columns,
            transcendentals=pairs * length * length,
        ),
        name="attend_back",
    )(mixed, starts, upstream)


def small_gather_kernel(axis, count, src_ref, out_ref, send, recv):
    dp = lax.axis_index("dp")
    mp = lax.axis_index("mp")
    me = dp if axis == "dp" else mp

    def device(peer):
        return (peer, mp) if axis == "dp" else (dp, peer)

    barrier = pltpu.get_barrier_semaphore()
    for hop in range(1, count):
        pl.semaphore_signal(
            barrier, inc=1, device_id=device(lax.rem(me + hop, count)), device_id_type=MESH
        )
    pl.semaphore_wait(barrier, count - 1)
    copies = []
    for hop in range(1, count):
        peer = lax.rem(me + hop, count)
        copy = pltpu.make_async_remote_copy(
            src_ref=src_ref,
            dst_ref=out_ref.at[me],
            send_sem=send.at[hop],
            recv_sem=recv.at[hop],
            device_id=device(peer),
            device_id_type=MESH,
        )
        copy.start()
        copies.append(copy)
    out_ref[me] = src_ref[...]
    for copy in copies:
        copy.wait()


def small_gather(name, cid, values, axis):
    count = lax.axis_size(axis)
    vmem = pl.BlockSpec(memory_space=pltpu.VMEM)
    return pl.pallas_call(
        functools.partial(small_gather_kernel, axis, count),
        out_shape=jax.ShapeDtypeStruct((count,) + values.shape, values.dtype),
        in_specs=[vmem],
        out_specs=vmem,
        scratch_shapes=[pltpu.SemaphoreType.DMA((count,)), pltpu.SemaphoreType.DMA((count,))],
        compiler_params=pltpu.CompilerParams(collective_id=cid, has_side_effects=True),
        cost_estimate=cost_of(6),
        name=name,
    )(values)


def exchange(axis, me, here, source, slots, send, recv, first):
    count = slots.shape[0]
    copies = []
    for hop in range(1, count):
        peer = lax.rem(me + hop, count)
        copy = pltpu.make_async_remote_copy(
            src_ref=source,
            dst_ref=slots.at[me],
            send_sem=send.at[first + hop],
            recv_sem=recv.at[first + hop],
            device_id=(peer, here) if axis == "dp" else (here, peer),
            device_id_type=MESH,
        )
        copy.start()
        copies.append(copy)
    slots[me] = source[...]
    for copy in copies:
        copy.wait()
    total = slots[0]
    for index in range(1, count):
        total = total + slots[index]
    return total


def greet_all(dp, mp, size_dp, size_mp):
    barrier = pltpu.get_barrier_semaphore()
    for hop in range(1, size_dp):
        pl.semaphore_signal(
            barrier, inc=1, device_id=(lax.rem(dp + hop, size_dp), mp), device_id_type=MESH
        )
    for hop in range(1, size_mp):
        pl.semaphore_signal(
            barrier, inc=1, device_id=(dp, lax.rem(mp + hop, size_mp)), device_id_type=MESH
        )
    pl.semaphore_wait(barrier, size_dp + size_mp - 2)


def lane_rows(values):
    values = values.reshape(-1)
    return jnp.pad(values, (0, -values.size % 128)).reshape(-1, 128)


def fold(values):
    return jnp.sum(values, axis=0, keepdims=True)


def stats_kernel(full, size_dp, size_mp, *refs):
    row_part, row_old, col_part, col_old, weight_sq = (refs[5 * n : 5 * n + 5] for n in range(5))
    loss_part, norm_one, norm_two, norm_three = refs[25:29]
    refs = refs[29:]
    row_out, col_out = refs[0:5], refs[5:10]
    loss_out, part_out, rate_out = refs[10:13]
    send_dp, slots_dp, send_mp, slots_mp, parts, part_slots, send, recv = refs[13:]
    dp = lax.axis_index("dp")
    mp = lax.axis_index("mp")
    greet_all(dp, mp, size_dp, size_mp)
    beta = 1.0 - STEP ** (-0.8)
    width = norm_one.shape[1]

    at = 0
    marks = []

    def put(values):
        nonlocal at
        rows = values.shape[0]
        send_dp[at : at + rows, :] = values
        marks.append((at, rows))
        at += rows

    norm_rows = width // 128
    for ref in (norm_one, norm_two, norm_three):
        for which in range(2):
            for piece in range(norm_rows):
                put(ref[which : which + 1, piece * 128 : piece * 128 + 128])
    marks.clear()
    count_norm = at
    for index in (0, 2, 4):
        put(row_part[index][...])
    for index in (1, 3):
        put(col_part[index][...])
    put(loss_part[...])
    for index in (1, 3):
        put(fold(row_old[index][...]))
    for index in range(5):
        put(fold(weight_sq[index][...]))
    if at < send_dp.shape[0]:
        send_dp[at:, :] = jnp.zeros((send_dp.shape[0] - at, 128), jnp.float32)
    over_dp = exchange("dp", dp, mp, send_dp, slots_dp, send, recv, 0)
    taken = [over_dp[start : start + rows] for start, rows in marks]
    loss_row = taken[5]
    row_full = {0: taken[0], 2: taken[1], 4: taken[2]}
    col_full = {1: taken[3], 3: taken[4]}
    old_total = {1: taken[6], 3: taken[7]}
    weight_rows = taken[8:13]

    at = 0
    marks = []

    def put_mp(values):
        nonlocal at
        rows = values.shape[0]
        send_mp[at : at + rows, :] = values
        marks.append((at, rows))
        at += rows

    for index in (0, 2, 4):
        put_mp(col_part[index][...])
    for index in (1, 3):
        put_mp(row_part[index][...])
    for index in range(5):
        put_mp(fold(row_full[index] if index in row_full else col_full[index]))
    for index in (0, 2, 4):
        put_mp(fold(row_old[index][...]))
    for index in range(5):
        put_mp(weight_rows[index])
    put_mp(loss_row)
    if at < send_mp.shape[0]:
        send_mp[at:, :] = jnp.zeros((send_mp.shape[0] - at, 128), jnp.float32)
    each = count_norm // size_mp
    for index in range(size_mp):
        parts[index] = over_dp[index * each : index * each + each]
    first = size_dp + size_mp
    copies = []
    for hop in range(1, size_mp):
        peer = lax.rem(mp + hop, size_mp)
        copy = pltpu.make_async_remote_copy(
            src_ref=parts.at[peer],
            dst_ref=part_slots.at[mp],
            send_sem=send.at[first + hop],
            recv_sem=recv.at[first + hop],
            device_id=(dp, peer),
            device_id_type=MESH,
        )
        copy.start()
        copies.append(copy)
    part_slots[mp] = parts[mp]
    over_mp = exchange("mp", mp, dp, send_mp, slots_mp, send, recv, size_dp)
    for copy in copies:
        copy.wait()
    summed = part_slots[0]
    for index in range(1, size_mp):
        summed = summed + part_slots[index]
    part_out[...] = summed
    taken = [over_mp[start : start + rows] for start, rows in marks]
    for slot, index in enumerate((0, 2, 4)):
        col_full[index] = taken[slot]
        old_total[index] = taken[10 + slot]
    for slot, index in enumerate((1, 3)):
        row_full[index] = taken[3 + slot]
    square_total = taken[5:10]
    weight_total = taken[13:18]
    loss_out[...] = taken[18]
    for index in range(5):
        full_rows, full_cols = full[index]
        row_new = beta * row_old[index][...] + (1.0 - beta) * row_full[index] / full_cols
        col_new = beta * col_old[index][...] + (1.0 - beta) * col_full[index] / full_rows
        row_out[index][...] = row_new
        col_out[index][...] = col_new
        mean = (
            beta * jnp.sum(old_total[index], axis=1, keepdims=True)
            + (1.0 - beta) * jnp.sum(square_total[index], axis=1, keepdims=True) / full_cols
        ) / full_rows
        rate = RHO * jnp.sqrt(
            jnp.sum(weight_total[index], axis=1, keepdims=True) / (full_rows * full_cols)
        )
        rate_out[index : index + 1, :] = jnp.broadcast_to(mean, (1, 128))
        rate_out[8 + index : 9 + index, :] = jnp.broadcast_to(rate, (1, 128))


def update_stats(cid, row_parts, rows_old, col_parts, cols_old, weight_sq, loss, norm_parts, full):
    size_dp = lax.axis_size("dp")
    size_mp = lax.axis_size("mp")
    f32 = jnp.float32
    rows_old2 = [lane_rows(v) for v in rows_old]
    cols_old2 = [lane_rows(v) for v in cols_old]
    args = (
        [lane_rows(v) for v in row_parts]
        + rows_old2
        + [lane_rows(v) for v in col_parts]
        + cols_old2
        + [v if v.ndim == 2 else lane_rows(v) for v in weight_sq]
        + [lane_rows(loss)]
        + list(norm_parts)
    )
    width = norm_parts[0].shape[1]
    count_norm = 6 * width // 128
    size_a = count_norm + sum(rows_old2[n].shape[0] for n in (0, 2, 4))
    size_a += sum(cols_old2[n].shape[0] for n in (1, 3)) + 8
    size_a += -size_a % 8
    size_b = sum(cols_old2[n].shape[0] for n in (0, 2, 4))
    size_b += sum(rows_old2[n].shape[0] for n in (1, 3)) + 14
    size_b += -size_b % 8
    each = count_norm // size_mp
    out_shape = [jax.ShapeDtypeStruct(v.shape, f32) for v in rows_old2 + cols_old2]
    out_shape += [
        jax.ShapeDtypeStruct((1, 128), f32),
        jax.ShapeDtypeStruct((each, 128), f32),
        jax.ShapeDtypeStruct((16, 128), f32),
    ]
    sems = size_dp + 2 * size_mp
    vmem = pl.BlockSpec(memory_space=pltpu.VMEM)
    found = pl.pallas_call(
        functools.partial(stats_kernel, full, size_dp, size_mp),
        out_shape=out_shape,
        in_specs=[vmem] * len(args),
        out_specs=[vmem] * len(out_shape),
        scratch_shapes=[
            pltpu.VMEM((size_a, 128), f32),
            pltpu.VMEM((size_dp, size_a, 128), f32),
            pltpu.VMEM((size_b, 128), f32),
            pltpu.VMEM((size_mp, size_b, 128), f32),
            pltpu.VMEM((size_mp, each, 128), f32),
            pltpu.VMEM((size_mp, each, 128), f32),
            pltpu.SemaphoreType.DMA((sems,)),
            pltpu.SemaphoreType.DMA((sems,)),
        ],
        compiler_params=pltpu.CompilerParams(collective_id=cid, has_side_effects=True),
        cost_estimate=cost_of(12),
        name="update_stats",
    )(*args)
    rows_new = [found[n].reshape(-1)[: rows_old[n].size] for n in range(5)]
    cols_new = [found[5 + n].reshape(-1)[: cols_old[n].size] for n in range(5)]
    loss_sums = found[10][0, :NSRC]
    return rows_new, cols_new, loss_sums, found[11], found[12]


def clip_kernel(entries, size_dp, size_mp, *refs):
    parts, rate, part, norms, second_old = refs[:5], *refs[5:9]
    out, grads_out, second_out, norms_out = refs[9:13]
    mine, slots_dp, slots_mp, whole, send, recv = refs[13:]
    dp = lax.axis_index("dp")
    mp = lax.axis_index("mp")
    greet_all(dp, mp, size_dp, size_mp)
    first = size_dp + size_mp
    copies = []
    for hop in range(1, size_mp):
        copy = pltpu.make_async_remote_copy(
            src_ref=part,
            dst_ref=whole.at[mp],
            send_sem=send.at[first + hop],
            recv_sem=recv.at[first + hop],
            device_id=(dp, lax.rem(mp + hop, size_mp)),
            device_id_type=MESH,
        )
        copy.start()
        copies.append(copy)
    whole[mp] = part[...]
    mine[...] = jnp.zeros_like(mine)
    for index in range(5):
        mine[index : index + 1, :] = fold(parts[index][...])
    over_dp = exchange("dp", dp, mp, mine, slots_dp, send, recv, 0)
    mine[...] = over_dp
    total = exchange("mp", mp, dp, mine, slots_mp, send, recv, size_dp)
    total = jnp.sum(total, axis=1, keepdims=True)
    for index in range(5):
        clip = jnp.maximum(1.0, jnp.sqrt(total[index : index + 1] / entries[index]) / CLIP)
        out[index : index + 1, :] = rate[8 + index : 9 + index, :] / clip
    for copy in copies:
        copy.wait()
    beta = 1.0 - STEP ** (-0.8)
    each = part.shape[0]
    norm_rows = norms.shape[1] // 128
    for row in range(6):
        for piece in range(norm_rows):
            place = row * norm_rows + piece
            grads_out[row : row + 1, piece * 128 : piece * 128 + 128] = whole[
                place // each, place % each : place % each + 1, :
            ]
    grad = grads_out[...]
    second = beta * second_old[...] + (1.0 - beta) * (grad * grad + EPS_ONE)
    second_out[...] = second
    step = grad * lax.rsqrt(second)
    entries = step.size

    def mean_square(values):
        return jnp.sum(jnp.sum(values * values, axis=0, keepdims=True), axis=1, keepdims=True) / (
            entries
        )

    step = step / jnp.maximum(1.0, jnp.sqrt(mean_square(step)) / CLIP)
    old = norms[...]
    norms_out[...] = old - RHO * jnp.sqrt(mean_square(old)) * step


def clip_rates(cid, step_parts, rate, part, norms, second, entries):
    size_dp = lax.axis_size("dp")
    size_mp = lax.axis_size("mp")
    vmem = pl.BlockSpec(memory_space=pltpu.VMEM)
    sems = size_dp + 2 * size_mp
    norm_type = jax.ShapeDtypeStruct(norms.shape, jnp.float32)
    return pl.pallas_call(
        functools.partial(clip_kernel, entries, size_dp, size_mp),
        out_shape=[jax.ShapeDtypeStruct((8, 128), jnp.float32)] + [norm_type] * 3,
        in_specs=[vmem] * 9,
        out_specs=[vmem] * 4,
        scratch_shapes=[
            pltpu.VMEM((8, 128), jnp.float32),
            pltpu.VMEM((size_dp, 8, 128), jnp.float32),
            pltpu.VMEM((size_mp, 8, 128), jnp.float32),
            pltpu.VMEM((size_mp, *part.shape), jnp.float32),
            pltpu.SemaphoreType.DMA((sems,)),
            pltpu.SemaphoreType.DMA((sems,)),
        ],
        compiler_params=pltpu.CompilerParams(collective_id=cid, has_side_effects=True),
        cost_estimate=cost_of(8),
        name="clip_rates",
    )(*[lane_rows(v) for v in step_parts], rate, part, norms, second)


UNROLL = 8


def lookup_kernel(shift, early, count_ref, key_ref, table_ref, out_ref, low_ref, square_ref, rows_ref):
    spots = out_ref.shape[0]
    vocab, width = table_ref.shape
    rows_ref[...] = jnp.zeros_like(rows_ref)

    def some(i, carry):
        for j in range(UNROLL):
            key = key_ref[i * UNROLL + j]
            place = key & ((1 << shift) - 1)
            rows_ref[pl.ds(place, 1), :] = table_ref[pl.ds(key >> shift, 1), :]
        return carry

    lax.fori_loop(0, (count_ref[0] + UNROLL - 1) // UNROLL, some, 0)

    def narrow(i, carry):
        at = pl.ds(pl.multiple_of(i * 256, 256), 256)
        out_ref[at, :] = rows_ref[at, :].astype(jnp.bfloat16)
        return carry

    lax.fori_loop(0, spots // 256, narrow, 0)
    strip = 64
    rest = vocab % strip
    done = vocab - rest
    low_ref[done - early :, :] = jnp.zeros(
        (low_ref.shape[0] - done + early, width), jnp.bfloat16
    )

    def squares(values, total):
        for row in range(0, values.shape[0], 8):
            piece = values[row : row + 8, :]
            total = total + piece * piece
        return total

    def lower(i, total):
        at = pl.ds(pl.multiple_of(i * strip, strip), strip)
        values = table_ref[at, :]
        start = pl.multiple_of(i * strip - early, strip)
        low_ref[pl.ds(start, strip), :] = values.astype(jnp.bfloat16)
        return squares(values, total)

    def square(i, total):
        at = pl.ds(pl.multiple_of(i * strip, strip), strip)
        return squares(table_ref[at, :], total)

    total = jnp.zeros((8, width), jnp.float32)
    total = lax.fori_loop(0, early // strip, square, total)
    total = lax.fori_loop(early // strip, done // strip, lower, total)
    if rest:
        values = table_ref[done:, :]
        total = squares(values, total)
        values = jnp.concatenate([values, jnp.zeros((strip - rest, width), jnp.float32)])
        low_ref[done - early : done - early + strip, :] = values.astype(jnp.bfloat16)
    folded = total[:, 0:128]
    for start in range(128, width, 128):
        folded = folded + total[:, start : start + 128]
    square_ref[...] = folded


def lookup(keys, count, table, spots, shift, early):
    vocab, width = table.shape
    smem = pl.BlockSpec(memory_space=pltpu.SMEM)
    vmem = pl.BlockSpec(memory_space=pltpu.VMEM)
    return pl.pallas_call(
        functools.partial(lookup_kernel, shift, early),
        out_shape=[
            jax.ShapeDtypeStruct((spots, width), jnp.bfloat16),
            jax.ShapeDtypeStruct((vocab + -vocab % HEAD_BLOCK - early, width), jnp.bfloat16),
            jax.ShapeDtypeStruct((8, 128), jnp.float32),
        ],
        in_specs=[smem, smem, vmem],
        out_specs=[vmem] * 3,
        scratch_shapes=[pltpu.VMEM((spots + 8, width), jnp.float32)],
        compiler_params=pltpu.CompilerParams(vmem_limit_bytes=VMEM_CAP),
        cost_estimate=cost_of(20),
        name="lookup",
    )(count, keys, table)


def scatter_kernel(shift, count_ref, key_ref, head_ref, rows_in_ref, grad_ref, rows_ref):
    spots = rows_in_ref.shape[0]
    width = grad_ref.shape[1]

    def widen(i, carry):
        at = pl.ds(pl.multiple_of(i * 256, 256), 256)
        rows_ref[at, :] = rows_in_ref[at, :].astype(jnp.float32)
        return carry

    lax.fori_loop(0, spots // 256, widen, 0)
    rows_ref[spots:, :] = jnp.zeros((8, width), jnp.float32)
    grad_ref[...] = head_ref[...].astype(jnp.float32)[: grad_ref.shape[0]]

    def some(i, carry):
        for j in range(UNROLL):
            key = key_ref[i * UNROLL + j]
            place = key & ((1 << shift) - 1)
            grad_ref[pl.ds(key >> shift, 1), :] += rows_ref[pl.ds(place, 1), :]
        return carry

    lax.fori_loop(0, (count_ref[0] + UNROLL - 1) // UNROLL, some, 0)


def scatter(keys, count, head_grad, rows, vocab, shift):
    spots, width = rows.shape
    smem = pl.BlockSpec(memory_space=pltpu.SMEM)
    vmem = pl.BlockSpec(memory_space=pltpu.VMEM)
    return pl.pallas_call(
        functools.partial(scatter_kernel, shift),
        out_shape=jax.ShapeDtypeStruct((vocab, width), jnp.float32),
        in_specs=[smem, smem, vmem, vmem],
        out_specs=vmem,
        scratch_shapes=[pltpu.VMEM((spots + 8, width), jnp.float32)],
        compiler_params=pltpu.CompilerParams(vmem_limit_bytes=VMEM_CAP),
        cost_estimate=cost_of(23),
        name="scatter",
    )(count, keys, head_grad, rows)


def norm_parts(values):
    centre = jnp.mean(values, axis=-1, keepdims=True)
    centred = values - centre
    scale = lax.rsqrt(jnp.mean(centred * centred, axis=-1, keepdims=True) + EPS_NORM)
    return centred * scale, scale


def norm_pull(values, gain, upstream):
    normed, scale = norm_parts(values)
    weighted = upstream * gain
    pulled = scale * (
        weighted
        - jnp.mean(weighted, axis=-1, keepdims=True)
        - normed * jnp.mean(weighted * normed, axis=-1, keepdims=True)
    )
    return (
        pulled,
        jnp.sum(upstream * normed, axis=0, keepdims=True),
        jnp.sum(upstream, axis=0, keepdims=True),
    )


def step_first(total, at, ins, outs):
    stream, norms = outs[0], ins[0]
    normed, scale = norm_parts(stream[at, :].astype(jnp.float32))
    return normed * norms[0:1, :] + norms[1:2, :]


def step_forward(row, total, at, ins, outs):
    stream, norms = ins
    values = stream[at, :].astype(jnp.float32) + total
    outs[0][at, :] = values
    normed, scale = norm_parts(values)
    return normed * norms[row : row + 1, :] + norms[row + 1 : row + 2, :]


def step_backward(row, total, at, ins, outs):
    stream, norms = ins[:2]
    pulled, dgain, dshift = norm_pull(
        stream[at, :].astype(jnp.float32), norms[row : row + 1, :], total
    )
    if len(ins) > 2:
        pulled = pulled + ins[2][at, :]
    if len(outs) > 1:
        outs[0][at, :] = pulled
    sums = outs[-1]

    @pl.when(at.start == 0)
    def _():
        sums[...] = jnp.zeros_like(sums)

    sums[0:1, :] += dgain
    sums[1:2, :] += dshift
    return pulled


def gelu_tanh(values):
    return jax.nn.gelu(values, approximate=True)


def local(
    token_ids,
    targets,
    starts,
    sources,
    embedding,
    w_qkv,
    w_out,
    w_fc,
    w_proj,
    norm_params,
    rows_table,
    cols_table,
    rows_qkv,
    cols_qkv,
    rows_out,
    cols_out,
    rows_fc,
    cols_fc,
    rows_proj,
    cols_proj,
    second_norms,
):
    bf16 = jnp.bfloat16
    f32 = jnp.float32
    size_mp = lax.axis_size("mp")
    size_dp = lax.axis_size("dp")
    dp = lax.axis_index("dp")
    mp = lax.axis_index("mp")
    tokens = token_ids.shape[0]
    seqs = tokens // LEN
    chips = size_mp // 2
    near = chips // seqs
    sharers = size_mp // seqs
    rows = tokens // size_mp
    vocab, part_width = embedding.shape
    width = part_width * size_dp
    first_row = mp * vocab
    spots = tokens * size_dp
    chunks_full = max(1, min(4, rows // 32))
    chunks_near = max(1, min(4, rows // 32))
    chunks_turn = max(1, min(4, rows // 32))

    def own_and_twins(weights, axis):
        low = [weight.astype(bf16) for weight in weights]
        found = [[weight] for weight in low]
        sent = jnp.concatenate(low, axis=axis)
        for turn in range(1, seqs):
            shift = [(i, (i + turn * sharers) % size_mp) for i in range(size_mp)]
            arrived = lax.ppermute(sent, "mp", shift)
            start = 0
            for index, weight in enumerate(low):
                size = weight.shape[axis]
                found[index].append(lax.slice_in_dim(arrived, start, start + size, axis=axis))
                start += size
        return [jnp.concatenate(pieces, axis=axis) for pieces in found]

    pair_fc, pair_qkv = own_and_twins((w_fc, w_qkv), 1)
    pair_proj, pair_out = own_and_twins((w_proj, w_out), 0)

    early = (vocab + -vocab % HEAD_BLOCK) * 2 // (10 * HEAD_BLOCK) * HEAD_BLOCK
    early_table = lax.all_gather(embedding[:early].astype(bf16), "dp", axis=1, tiled=True)

    both = jnp.stack([token_ids, sources]).reshape(-1, 128)
    both = small_gather("gather_ids", 0, both, "dp").reshape(size_dp, 2, tokens)
    all_ids = both[:, 0]
    all_sources = both[:, 1].reshape(-1)
    counts = jnp.sum(
        (all_sources[:, None] == jnp.arange(NSRC, dtype=jnp.int32)[None, :]).astype(f32), axis=0
    )

    piece = rows // chunks_turn
    token = jnp.arange(tokens, dtype=jnp.int32)
    place = (
        token // piece * (size_dp * piece)
        + (jnp.arange(size_dp, dtype=jnp.int32) * piece)[:, None]
        + token % piece
    )
    local_ids = all_ids - first_row
    inside = (local_ids >= 0) & (local_ids < vocab)
    shift = spots.bit_length()
    idle = ((vocab - 1) << shift) + spots
    keys = jnp.where(inside, (local_ids << shift) + place, idle)
    keys = jnp.sort(keys.reshape(-1))
    owned = jnp.sum(inside.astype(jnp.int32)).reshape(1)
    found, low_table, table_sq = lookup(keys, owned, embedding, spots, shift, early)
    found, early_table = lax.optimization_barrier((found, early_table))
    inner_one, stream0, wide_qkv, wide_out, wide_fc, wide_proj = line_call(
        "lookup_sum",
        1,
        found,
        [norm_params],
        [jax.ShapeDtypeStruct((rows, width), bf16)],
        step_first,
        size_dp * rows,
        part_width,
        chunks_turn,
        chips,
        near,
        70,
        [
            ("gather", 0, pair_qkv),
            ("gather", 1, pair_out),
            ("gather", 0, pair_fc),
            ("gather", 1, pair_proj),
        ],
        "gather",
        8,
    )
    low_table, inner_one = lax.optimization_barrier((low_table, inner_one))
    wide_table = (early_table, lax.all_gather(low_table, "dp", axis=1, tiled=True))
    row_f32 = jax.ShapeDtypeStruct((rows, width), f32)
    pair_f32 = jax.ShapeDtypeStruct((8, width), f32)
    my_starts = row_slice(starts, (mp // sharers) * LEN, LEN)[:, None]
    mixed = jnp.dot(inner_one, wide_qkv, preferred_element_type=f32).astype(bf16)
    attended = attend(mixed, my_starts)
    partial = jnp.dot(attended, wide_out, preferred_element_type=f32).astype(bf16)
    inner_two, stream1 = line_call(
        "attn_sum",
        3,
        partial,
        [stream0, norm_params],
        [row_f32],
        functools.partial(step_forward, 2),
        rows,
        width,
        chunks_near,
        near,
        near,
        32,
    )
    before = jnp.dot(inner_two, wide_fc, preferred_element_type=f32)
    hidden = gelu_tanh(before).astype(bf16)
    partial = jnp.dot(hidden, wide_proj, preferred_element_type=f32).astype(bf16)
    final, stream2 = line_call(
        "mlp_sum",
        4,
        partial,
        [stream1, norm_params],
        [row_f32],
        functools.partial(step_forward, 4),
        rows,
        width,
        chunks_full,
        near,
        chips,
        58,
        chunk_major=True,
    )

    edge = jnp.clip(VREAL - first_row, 0, vocab).astype(jnp.int32).reshape(1)

    def by_chunk(values):
        return values.reshape(size_mp, chunks_full, -1).swapaxes(0, 1).reshape(tokens)

    sources = by_chunk(sources)
    wanted = by_chunk(targets) - first_row
    wanted = jnp.where((wanted >= 0) & (wanted < vocab), wanted, -1).reshape(1, tokens)
    block = HEAD_BLOCK
    exps, tops, sums, picks = head_stats(wide_table, final, wanted, edge, block)
    tops = tops[:, 0]
    top = jnp.max(tops, axis=0)
    total = jnp.sum(sums[:, 0] * jnp.exp(tops - top[None, :]), axis=0)
    pick = jnp.sum(picks[:, 0], axis=0)
    stats = jnp.concatenate([v.reshape(-1, 128) for v in (top, total)])
    stats = small_gather("gather_stats", 5, stats, "mp").reshape(size_mp, 2, tokens)
    highest = jnp.max(stats[:, 0], axis=0)
    log_total = highest + jnp.log(
        jnp.sum(stats[:, 1] * jnp.exp(stats[:, 0] - highest[None, :]), axis=0)
    )
    token_loss = jnp.where(mp == 0, log_total, 0.0) - pick
    member = (sources[:, None] == jnp.arange(NSRC, dtype=jnp.int32)[None, :]).astype(f32)
    loss_part = jnp.sum(member * token_loss[:, None], axis=0)
    weight = jnp.sum(member / (NSRC * jnp.maximum(counts, 1.0))[None, :], axis=1)
    scale = jnp.exp(tops - log_total[None, :]) * weight[None, :]
    dlogits, table_grad = head_back(
        exps, final, scale[:, None, :], weight[None, :], wanted, block
    )
    head_grad = lax.psum_scatter(table_grad, "dp", scatter_dimension=1, tiled=True)

    dbranch2, dstream2, norm3 = line_call(
        "final_back",
        6,
        (dlogits, *wide_table),
        [stream2, norm_params],
        [row_f32, pair_f32],
        functools.partial(step_backward, 4),
        rows,
        width,
        chunks_full,
        chips,
        near,
        65,
        product=True,
    )
    grad_proj = jnp.einsum("tf,td->fd", hidden, dbranch2, preferred_element_type=f32).astype(bf16)
    dhidden = jnp.einsum("td,fd->tf", dbranch2, wide_proj, preferred_element_type=f32)
    unused, gelu_pull = jax.vjp(gelu_tanh, before)
    dbefore = gelu_pull(dhidden)[0].astype(bf16)
    partial = jnp.einsum("tf,df->td", dbefore, wide_fc, preferred_element_type=f32).astype(bf16)
    dbranch1, dstream1, norm2 = line_call(
        "mlp_back",
        7,
        partial,
        [stream1, norm_params, dstream2],
        [row_f32, pair_f32],
        functools.partial(step_backward, 2),
        rows,
        width,
        chunks_near,
        near,
        near,
        34,
    )
    grad_fc = jnp.einsum("td,tf->df", inner_two, dbefore, preferred_element_type=f32).astype(bf16)
    grad_out = jnp.einsum("tf,td->fd", attended, dbranch1, preferred_element_type=f32).astype(bf16)
    dattended = jnp.einsum("td,fd->tf", dbranch1, wide_out, preferred_element_type=f32)
    dmixed = attend_back(mixed, my_starts, dattended.astype(bf16))
    partial = jnp.einsum("tc,dc->td", dmixed, wide_qkv, preferred_element_type=f32).astype(bf16)
    grad_qkv = jnp.einsum("td,tc->dc", inner_one, dmixed, preferred_element_type=f32).astype(bf16)
    drows, norm1, grad_proj, grad_out, grad_fc, grad_qkv, twins_wide, twins_tall = line_call(
        "attn_back",
        8,
        partial,
        [stream0, norm_params, dstream1],
        [pair_f32],
        functools.partial(step_backward, 0),
        rows,
        width,
        chunks_turn,
        near,
        chips,
        70,
        [
            ("scatter", 1, grad_proj),
            ("scatter", 1, grad_out),
            ("scatter", 0, grad_fc),
            ("scatter", 0, grad_qkv),
        ],
        "spread",
        9,
        seqs=seqs,
    )

    def from_twins(values, axis, sizes):
        starts = [(seqs - 1) * sum(sizes[:n]) for n in range(len(sizes))]
        found = []
        for turn in range(1, seqs):
            pieces = [
                lax.slice_in_dim(values, at + (turn - 1) * size, at + turn * size, axis=axis)
                for at, size in zip(starts, sizes)
            ]
            back = [(i, (i - turn * sharers) % size_mp) for i in range(size_mp)]
            found.append(lax.ppermute(jnp.concatenate(pieces, axis=axis), "mp", back))
        return found

    tall = [grad_proj.shape[0], grad_out.shape[0]]
    wide = [grad_fc.shape[1], grad_qkv.shape[1]]
    found_tall = from_twins(twins_tall, 0, tall)
    found_wide = from_twins(twins_wide, 1, wide)
    grad_table = scatter(keys, owned, head_grad, drows, vocab, shift)
    table_squares = grad_table * grad_table + EPS_ONE
    table_rows = jnp.sum(table_squares, axis=1)
    table_cols = jnp.sum(table_squares, axis=0)
    found_tall, found_wide, table_rows = lax.optimization_barrier(
        (found_tall, found_wide, table_rows)
    )
    for values in found_tall:
        grad_proj += values[: tall[0]].astype(f32)
        grad_out += values[tall[0] :].astype(f32)
    for values in found_wide:
        grad_fc += values[:, : wide[0]].astype(f32)
        grad_qkv += values[:, wide[0] :].astype(f32)

    weights = (embedding, w_qkv, w_out, w_fc, w_proj)
    grads = (grad_table, grad_qkv, grad_out, grad_fc, grad_proj)
    row_span = (size_mp, size_dp, size_mp, size_dp, size_mp)
    col_span = (size_dp, size_mp, size_dp, size_mp, size_dp)
    full = tuple(
        (g.shape[0] * r, g.shape[1] * c) for g, r, c in zip(grads, row_span, col_span)
    )
    squares = [gradient * gradient + EPS_ONE for gradient in grads[1:]]
    rows_new, cols_new, loss_sums, norm_part, rates = update_stats(
        10,
        [table_rows] + [jnp.sum(square, axis=1) for square in squares],
        (rows_table, rows_qkv, rows_out, rows_fc, rows_proj),
        [table_cols] + [jnp.sum(square, axis=0) for square in squares],
        (cols_table, cols_qkv, cols_out, cols_fc, cols_proj),
        [table_sq] + [jnp.sum(value * value, axis=0) for value in weights[1:]],
        loss_part,
        (norm1, norm2, norm3),
        full,
    )
    steps = [
        grads[n] * lax.rsqrt(rows_new[n][:, None] * cols_new[n][None, :] / rates[n, 0])
        for n in range(5)
    ]
    factors, grad_norms, second_new, norms_new = clip_rates(
        11,
        [jnp.sum(step * step, axis=0) for step in steps],
        rates,
        norm_part,
        norm_params,
        second_norms,
        [r * c for r, c in full],
    )
    updated = [weights[n] - factors[n, 0] * steps[n] for n in range(5)]
    return (
        loss_sums,
        counts,
        grad_table,
        rows_new[0],
        cols_new[0],
        updated[0],
        grad_qkv,
        rows_new[1],
        cols_new[1],
        updated[1],
        grad_out,
        rows_new[2],
        cols_new[2],
        updated[2],
        grad_fc,
        rows_new[3],
        cols_new[3],
        updated[3],
        grad_proj,
        rows_new[4],
        cols_new[4],
        updated[4],
        grad_norms,
        second_new,
        norms_new,
    )


def solution(mesh):
    placed = (
        P("dp"),
        P("dp"),
        P("dp"),
        P("dp"),
        P("mp", "dp"),
        P("dp", "mp"),
        P("mp", "dp"),
        P("dp", "mp"),
        P("mp", "dp"),
        P(),
        P("mp"),
        P("dp"),
        P("dp"),
        P("mp"),
        P("mp"),
        P("dp"),
        P("dp"),
        P("mp"),
        P("mp"),
        P("dp"),
        P(),
    )
    return jax.shard_map(
        local,
        mesh=mesh,
        in_specs=placed,
        out_specs=(
            P(),
            P(),
            P("mp", "dp"),
            P("mp"),
            P("dp"),
            P("mp", "dp"),
            P("dp", "mp"),
            P("dp"),
            P("mp"),
            P("dp", "mp"),
            P("mp", "dp"),
            P("mp"),
            P("dp"),
            P("mp", "dp"),
            P("dp", "mp"),
            P("dp"),
            P("mp"),
            P("dp", "mp"),
            P("mp", "dp"),
            P("mp"),
            P("dp"),
            P("mp", "dp"),
            P(),
            P(),
            P(),
        ),
        check_vma=False,
    )
```

```python
import functools
import math

import jax
import jax.numpy as jnp
from jax import lax
from jax.experimental import pallas as pl
from jax.experimental.pallas import tpu as pltpu
from jax.sharding import PartitionSpec as P

HD = 64
VREAL = 50257
LEN = 1024
NSRC = 4
STEP = 10


EPS_NORM = 1e-05
EPS_ONE = 1e-30
CLIP = 1.0
RHO = 0.5
MASKED = -1e30
QUERIES = 256
HEAD_BLOCK = 640
MESH = pl.DeviceIdType.MESH
VMEM_CAP = 56 * 2**20


def cost_of(time):
    return pl.CostEstimate(
        flops=time * 1000000000, bytes_accessed=time * 3000000, transcendentals=0
    )


def row_slice(values, start, count):
    return lax.dynamic_slice_in_dim(values, start, count, 0)


def line_kernel(
    nr, ng, chunks, shapes, n_in, n_out, step, sides, turn, side_ticks, product, chunk_major, *refs
):
    (rows_r, width_r), (rows_g, width_g) = shapes
    if product:
        dl, *tables = refs[:3]
        first = 3
    else:
        part = refs[0] if nr else None
        first = 1 if nr else 0
    ins = refs[first : first + n_in]
    refs = refs[first + n_in :]
    side_ins, refs = refs[: len(sides)], refs[len(sides) :]
    if ng:
        whole, refs = refs[0], refs[1:]
    outs = refs[:n_out]
    refs = refs[n_out:]
    scatters = [index for index, (kind, unused) in enumerate(sides) if kind == "scatter"]
    side_outs, refs = refs[: len(sides)], refs[len(sides) :]
    twin_outs, scratch = (refs[:2], refs[2:]) if scatters else ([], refs)
    side_scratch, scratch = scratch[: 3 * len(sides)], scratch[3 * len(sides) :]
    if turn:
        cast, turn_send, turn_recv = scratch[-3:]
    if product:
        part, dl_buf, total_ref, dl_sem = scratch[-4:]
    size_dp = lax.axis_size("dp")
    dp = lax.axis_index("dp")
    mp = lax.axis_index("mp")
    z = mp // 2
    core = lax.rem(mp, 2)
    other = mp + 1 - 2 * core
    piece_r = rows_r // chunks
    piece_g = rows_g // chunks
    small = min(piece_r, piece_g)
    late = 1 if turn else 0
    ahead = 1 if product else 0
    most = max(nr, ng)
    zb = lax.rem(z, most)
    if nr:
        zr = lax.rem(z, nr)
        last_r = nr - 1
    if ng:
        zg = lax.rem(z, ng)
        last_g = ng - 1

    barrier = pltpu.get_barrier_semaphore()
    pl.semaphore_signal(barrier, inc=1, device_id=(dp, other), device_id_type=MESH)

    @pl.when(zb > 0)
    def _():
        pl.semaphore_signal(barrier, inc=1, device_id=(dp, mp - 2), device_id_type=MESH)

    @pl.when(zb < most - 1)
    def _():
        pl.semaphore_signal(barrier, inc=1, device_id=(dp, mp + 2), device_id_type=MESH)

    if sides or turn:
        for hop in range(1, size_dp):
            pl.semaphore_signal(
                barrier,
                inc=1,
                device_id=(lax.rem(dp + hop, size_dp), mp),
                device_id_type=MESH,
            )
    greeted = (size_dp if sides or turn else 1) + (zb > 0).astype(jnp.int32) + (zb < most - 1).astype(jnp.int32)
    pl.semaphore_wait(barrier, greeted)

    def share(axis, length, which):
        at = pl.ds(pl.multiple_of(which * length, length), length)
        return (at, slice(None)) if axis == 0 else (slice(None), at)

    def to_peer(src, dst, send, recv, peer):
        return pltpu.make_async_remote_copy(
            src_ref=src,
            dst_ref=dst,
            send_sem=send,
            recv_sem=recv,
            device_id=(peer, mp),
            device_id_type=MESH,
        )

    relay = size_dp == 4
    beside_x = dp + 1 - 2 * lax.rem(dp, 2)
    beside_y = lax.rem(dp + 2, 4)
    across = 3 - dp

    def half_share(axis, length, which, height, part):
        if axis == 0:
            return (pl.ds(pl.multiple_of(which * length + part * height, height), height), slice(None))
        at = pl.ds(pl.multiple_of(which * length, length), length)
        return (pl.ds(part * height, height), at)

    first_copies, more_copies, relays = [], [], []
    for index, (kind, axis) in enumerate(sides):
        src, dst = side_ins[index], side_outs[index]
        send, recv, slots = side_scratch[3 * index : 3 * index + 3]
        if kind == "gather":
            length, height = src.shape[axis], src.shape[0] // 2
        else:
            length = src.shape[axis] // size_dp
            height = (length if axis == 0 else src.shape[0]) // 2
        if not relay:
            for hop in range(1, size_dp):
                peer = lax.rem(dp + hop, size_dp)
                if kind == "gather":
                    source, target = src, dst.at[share(axis, length, dp)]
                else:
                    source, target = src.at[share(axis, length, peer)], slots.at[hop]
                more_copies.append(to_peer(source, target, send.at[hop], recv.at[hop], peer))
            continue
        for side, near_one, far_one in ((0, beside_x, beside_y), (1, beside_y, beside_x)):
            sems = [(send.at[3 * side + n], recv.at[3 * side + n]) for n in range(3)]
            if kind == "gather":
                mine = src.at[pl.ds(side * height, height)]
                here = dst.at[half_share(axis, length, dp, height, side)]
                passed = dst.at[half_share(axis, length, near_one, height, side)]
                arrives = to_peer(mine, here, *sems[0], near_one)
                first_copies.append(arrives)
                more_copies.append(to_peer(mine, here, *sems[1], far_one))
                relays.append((arrives, None, to_peer(passed, passed, *sems[2], far_one)))
            else:
                arrives = to_peer(
                    src.at[half_share(axis, length, across, height, side)],
                    slots.at[4 * side],
                    *sems[0],
                    near_one,
                )
                first_copies.append(arrives)
                more_copies.append(
                    to_peer(
                        src.at[half_share(axis, length, near_one, height, side)],
                        slots.at[4 * side + 1],
                        *sems[1],
                        near_one,
                    )
                )
                summed = to_peer(
                    slots.at[4 * side + 2], slots.at[4 * side + 3], *sems[2], far_one
                )
                own = src.at[half_share(axis, length, far_one, height, side)]
                relays.append((arrives, (own, slots, 4 * side, height), summed))

    def pass_on(arrives, adding, copy):
        arrives.wait_recv()
        if adding is not None:
            own, slots, at, height = adding
            both = own[...].astype(jnp.float32) + slots[at].astype(jnp.float32)
            slots[at + 2] = both.astype(slots.dtype)
        copy.start()

    jobs = [copy.start for copy in first_copies + more_copies]
    jobs += [functools.partial(pass_on, *one) for one in relays]

    def side_jobs(now):
        for spot in range(side_ticks if jobs else 0):
            chosen = jobs[len(jobs) * spot // side_ticks : len(jobs) * (spot + 1) // side_ticks]

            @pl.when(now == spot)
            def _():
                for job in chosen:
                    job()

    if nr:
        half, from_left, from_right, going = scratch[:4]
        half_send, half_recv, rs_send, left_recv, right_recv = scratch[4:9]
        scratch = scratch[9:]
    if ng:
        core_send, core_recv, to_right, to_left, ag_left, ag_right = scratch[:6]

    def part_rows(block, k):
        return pl.ds(pl.multiple_of(block * rows_r + k * piece_r, piece_r), piece_r)

    def whole_rows(block, k):
        if chunk_major:
            start = k * (2 * ng * piece_g) + block * piece_g
            return pl.ds(pl.multiple_of(start, piece_g), piece_g)
        return pl.ds(pl.multiple_of(block * rows_g + k * piece_g, piece_g), piece_g)

    def remote(src, dst, send, recv, target):
        return pltpu.make_async_remote_copy(
            src_ref=src,
            dst_ref=dst,
            send_sem=send,
            recv_sem=recv,
            device_id=(dp, target),
            device_id_type=MESH,
        )

    if nr:

        def half_copy(dest, k):
            return remote(
                part.at[part_rows(2 * dest + 1 - core, k)],
                half.at[dest, k],
                half_send.at[dest, k],
                half_recv.at[dest, k],
                other,
            )

        def send_halves(k, carry):
            for dest in range(nr):
                half_copy(dest, k).start()
            return carry

        if not product:
            lax.fori_loop(0, chunks, send_halves, 0)

        def right_copy(dest, k):
            return remote(
                going.at[dest, k],
                from_left.at[dest, k],
                rs_send.at[dest, k],
                left_recv.at[dest, k],
                mp + 2,
            )

        def left_copy(dest, k):
            return remote(
                going.at[dest, k],
                from_right.at[dest, k],
                rs_send.at[dest, k],
                right_recv.at[dest, k],
                mp - 2,
            )

        def chip_sum(dest, k):
            half_copy(dest, k).wait_recv()
            mine = part[part_rows(2 * dest + core, k), :].astype(jnp.float32)
            return mine + half[dest, k].astype(jnp.float32)

        def pass_right(dest, k):
            total = chip_sum(dest, k)

            @pl.when(zr == 0)
            def _():
                going[dest, k] = total.astype(jnp.bfloat16)

            @pl.when(zr > 0)
            def _():
                right_copy(dest, k).wait_recv()
                both = total + from_left[dest, k].astype(jnp.float32)
                going[dest, k] = both.astype(jnp.bfloat16)

            right_copy(dest, k).start()

        def pass_left(dest, k):
            total = chip_sum(dest, k)

            @pl.when(zr == last_r)
            def _():
                going[dest, k] = total.astype(jnp.bfloat16)

            @pl.when(zr < last_r)
            def _():
                left_copy(dest, k).wait_recv()
                both = total + from_right[dest, k].astype(jnp.float32)
                going[dest, k] = both.astype(jnp.bfloat16)

            left_copy(dest, k).start()

    if ng:

        def gathered(block, k, send, recv, target):
            where = whole.at[whole_rows(2 * block + core, k)]
            return remote(where, where, send.at[block, k], recv.at[block, k], target)

        def core_copy(block, k):
            return gathered(block, k, core_send, core_recv, other)

        def ag_right_copy(block, k):
            return gathered(block, k, to_right, ag_left, mp + 2)

        def ag_left_copy(block, k):
            return gathered(block, k, to_left, ag_right, mp - 2)

    def own_rows(k):
        total = None
        if nr:
            total = chip_sum(zr, k)
            zero = jnp.zeros((piece_r, width_r), jnp.float32)

            @pl.when(zr > 0)
            def _():
                right_copy(zr, k).wait_recv()

            @pl.when(zr < last_r)
            def _():
                left_copy(zr, k).wait_recv()

            total += jnp.where(zr > 0, from_left[zr, k].astype(jnp.float32), zero)
            total += jnp.where(zr < last_r, from_right[zr, k].astype(jnp.float32), zero)
        if turn == "gather":
            cast[k] = total.astype(cast.dtype)
            for hop in range(1, size_dp):
                turn_copy(hop, k).start()
            mine = pl.ds(pl.multiple_of(dp * small, small), small)
            outs[0][own_place(k, dp)] = cast[k, mine, :]
            return
        at = pl.ds(pl.multiple_of(k * piece_r, piece_r), piece_r)
        ready = step(total, at, ins, outs)
        if turn == "spread":
            cast[k] = ready.astype(cast.dtype)
            for hop in range(1, size_dp):
                turn_copy(hop, k).start()
            whole[own_place(k, dp)] = cast[
                k, :, pl.ds(pl.multiple_of(dp * width_g, width_g), width_g)
            ]
        elif ng:
            whole[whole_rows(2 * zg + core, k), :] = ready.astype(whole.dtype)
            start_gather(k)

    def own_place(k, peer):
        if turn == "gather":
            return (
                pl.ds(pl.multiple_of(k * small, small), small),
                pl.ds(pl.multiple_of(peer * width_r, width_r), width_r),
            )
        start = (2 * zg + core) * rows_g + k * piece_g + peer * small
        return (pl.ds(pl.multiple_of(start, small), small), slice(None))

    def turn_copy(hop, k):
        peer = lax.rem(dp + hop, size_dp)
        if turn == "gather":
            src = cast.at[k, pl.ds(pl.multiple_of(peer * small, small), small)]
            dst = outs[0].at[own_place(k, dp)]
        else:
            src = cast.at[k, :, pl.ds(pl.multiple_of(peer * width_g, width_g), width_g)]
            dst = whole.at[own_place(k, dp)]
        return to_peer(src, dst, turn_send.at[hop, k], turn_recv.at[hop, k], peer)

    def turned_rows(k):
        for hop in range(1, size_dp):
            turn_copy(hop, k).wait_recv()
        if turn == "gather":
            at = pl.ds(pl.multiple_of(k * piece_g, piece_g), piece_g)
            ready = step(None, at, ins, outs)
            whole[whole_rows(2 * zg + core, k), :] = ready.astype(whole.dtype)
        start_gather(k)

    def start_gather(k):
        core_copy(zg, k).start()

        @pl.when(zg < last_g)
        def _():
            ag_right_copy(zg, k).start()

        @pl.when(zg > 0)
        def _():
            ag_left_copy(zg, k).start()

    def inside(k):
        return (k >= 0) & (k < chunks)

    def own_lag(chip):
        if not nr:
            return 0
        at = lax.rem(chip, nr)
        return jnp.maximum(at, last_r - at) + ahead

    def dl_copy(k):
        columns = dl_buf.shape[2]
        return pltpu.make_async_copy(
            dl.at[:, pl.ds(pl.multiple_of(k * columns, columns), columns)],
            dl_buf.at[lax.rem(k, 2)],
            dl_sem.at[lax.rem(k, 2)],
        )

    def make_part(k):
        dl_copy(k).wait()

        @pl.when(k + 1 < chunks)
        def _():
            dl_copy(k + 1).start()

        slot = lax.rem(k, 2)

        start = 0
        for piece in tables:
            found = lax.dot_general(
                dl_buf[slot, start : start + piece.shape[0], :],
                piece[...],
                (((0,), (0,)), ((), ())),
                preferred_element_type=jnp.float32,
            )
            if start:
                total_ref[...] += found
            else:
                total_ref[...] = found
            start += piece.shape[0]
        for block in range(2 * nr):
            part[part_rows(block, k), :] = total_ref[
                block * piece_r : block * piece_r + piece_r, :
            ].astype(jnp.bfloat16)
        send_halves(k, 0)

    if product:
        dl_copy(0).start()

    def tick(now, carry):
        side_jobs(now)
        if nr:
            k_right = now - zr - ahead
            k_left = now - (last_r - zr) - ahead
            for far in range(last_r):

                @pl.when(inside(k_right) & (last_r - far > zr))
                def _():
                    pass_right(last_r - far, k_right)

                @pl.when(inside(k_left) & (far < zr))
                def _():
                    pass_left(far, k_left)

        k_own = now - own_lag(z)

        @pl.when(inside(k_own))
        def _():
            own_rows(k_own)

        if turn:

            @pl.when(inside(k_own - 1))
            def _():
                turned_rows(k_own - 1)

        if ng:
            for block in range(ng):
                k = now - (own_lag(z - zg + block) + late + jnp.abs(zg - block))

                @pl.when(inside(k) & (block < zg))
                def _():
                    ag_right_copy(block, k).wait_recv()
                    core_copy(block, k).start()

                    @pl.when(zg < last_g)
                    def _():
                        ag_right_copy(block, k).start()

                @pl.when(inside(k) & (block > zg))
                def _():
                    ag_left_copy(block, k).wait_recv()
                    core_copy(block, k).start()

                    @pl.when(zg > 0)
                    def _():
                        ag_left_copy(block, k).start()

        if product:

            @pl.when(now < chunks)
            def _():
                make_part(now)

        return carry

    ticks = ahead + chunks + (nr - 1 if nr else 0) + (ng - 1 if ng else 0) + late
    lax.fori_loop(0, ticks, tick, 0)

    def finish(k, carry):
        if turn:
            for hop in range(1, size_dp):
                turn_copy(hop, k).wait_send()
        if nr:
            for block in range(nr):
                half_copy(block, k).wait_send()

                @pl.when(block != zr)
                def _():
                    right_copy(block, k).wait_send()

        if ng:
            for block in range(ng):
                core_copy(block, k).wait()

                @pl.when((zg < last_g) & (block <= zg))
                def _():
                    ag_right_copy(block, k).wait_send()

                @pl.when((zg > 0) & (block >= zg))
                def _():
                    ag_left_copy(block, k).wait_send()

        return carry

    lax.fori_loop(0, chunks, finish, 0)
    for index, (kind, axis) in enumerate(sides):
        if kind == "gather":
            length = side_ins[index].shape[axis]
            side_outs[index][share(axis, length, dp)] = side_ins[index][...]
    for copy in first_copies:
        copy.wait_send()
    for copy in more_copies:
        copy.wait()
    for unused, unused, copy in relays:
        copy.wait()
    placed = [0, 0]
    for index in scatters:
        axis = sides[index][1]
        src, dst = side_ins[index], side_outs[index]
        slots = side_scratch[3 * index + 2]
        length = src.shape[axis] // size_dp
        height = (length if axis == 0 else src.shape[0]) // 2
        if relay:
            total = []
            for side in range(2):
                one = src[half_share(axis, length, dp, height, side)].astype(jnp.float32)
                one += slots[4 * side + 1].astype(jnp.float32)
                one += slots[4 * side + 3].astype(jnp.float32)
                total.append(one)
            total = jnp.concatenate(total)
        else:
            total = src[share(axis, length, dp)].astype(jnp.float32)
            for hop in range(1, size_dp):
                total += slots[hop].astype(jnp.float32)
        twins = twin_outs[axis]
        at = placed[axis]
        if axis == 0:
            own = dst.shape[1]
            dst[...] = total[:, :own]
            more = total.shape[1] - own
            twins[:, at : at + more] = total[:, own:].astype(twins.dtype)
        else:
            own = dst.shape[0]
            dst[...] = total[:own, :]
            more = total.shape[0] - own
            twins[at : at + more, :] = total[own:, :].astype(twins.dtype)
        placed[axis] += more


def line_call(
    name,
    cid,
    partial,
    ins,
    out_types,
    step,
    rows,
    width,
    chunks,
    nr,
    ng,
    time,
    sides=(),
    turn=None,
    side_ticks=0,
    product=False,
    chunk_major=False,
    seqs=1,
):
    piece = rows // chunks
    size_dp = lax.axis_size("dp")
    reduced = gathered = (rows, width)
    if turn == "gather":
        gathered = (rows // size_dp, width * size_dp)
    elif turn == "spread":
        gathered = (rows * size_dp, width // size_dp)
    out_shape = []
    if ng:
        out_shape.append(
            jax.ShapeDtypeStruct((2 * ng * gathered[0], gathered[1]), jnp.bfloat16)
        )
    out_shape += out_types
    dma = pltpu.SemaphoreType.DMA
    scratch = []
    twin_shapes = [[0, 0], [0, 0]]
    for kind, axis, values in sides:
        shape = list(values.shape)
        scratch += [dma((max(size_dp, 6),)), dma((max(size_dp, 6),))]
        if kind == "gather":
            shape[axis] *= size_dp
            out_shape.append(jax.ShapeDtypeStruct(tuple(shape), values.dtype))
            scratch.append(pltpu.VMEM((16, 128), values.dtype))
        else:
            shape[axis] //= size_dp
            own = list(shape)
            own[1 - axis] //= seqs
            out_shape.append(jax.ShapeDtypeStruct(tuple(own), jnp.float32))
            twin_shapes[axis][axis] = shape[axis]
            twin_shapes[axis][1 - axis] += shape[1 - axis] - own[1 - axis]
            slots = (8, shape[0] // 2, shape[1]) if size_dp == 4 else (size_dp, *shape)
            scratch.append(pltpu.VMEM(slots, values.dtype))
    if any(side[0] == "scatter" for side in sides):
        out_shape += [jax.ShapeDtypeStruct(tuple(shape), jnp.bfloat16) for shape in twin_shapes]
    if nr:
        scratch += [pltpu.VMEM((nr, chunks, piece, width), jnp.bfloat16)] * 4
        scratch += [dma((nr, chunks))] * 5
    if ng:
        scratch += [dma((ng, chunks))] * 6
    if turn:
        scratch.append(pltpu.VMEM((chunks, piece, width), jnp.bfloat16))
        scratch += [dma((size_dp, chunks))] * 2
    if product:
        dl = partial[0]
        columns = dl.shape[1] // chunks
        scratch += [
            pltpu.VMEM((2 * nr * rows, width), jnp.bfloat16),
            pltpu.VMEM((2, dl.shape[0], columns), jnp.bfloat16),
            pltpu.VMEM((columns, width), jnp.float32),
            dma((2,)),
        ]
        partial = list(partial)
    else:
        partial = [partial] if nr else []
    args = partial + list(ins) + [side[2] for side in sides]
    vmem = pl.BlockSpec(memory_space=pltpu.VMEM)
    call = pl.pallas_call(
        functools.partial(
            line_kernel,
            nr,
            ng,
            chunks,
            (reduced, gathered),
            len(ins),
            len(out_types),
            step,
            tuple(side[:2] for side in sides),
            turn,
            side_ticks,
            product,
            chunk_major,
        ),
        out_shape=out_shape,
        in_specs=[pl.BlockSpec(memory_space=pl.ANY) if product and n == 0 else vmem for n in range(len(args))],
        out_specs=[vmem] * len(out_shape),
        scratch_shapes=scratch,
        compiler_params=pltpu.CompilerParams(
            collective_id=cid, has_side_effects=True, vmem_limit_bytes=VMEM_CAP
        ),
        cost_estimate=cost_of(time),
        name=name,
    )
    return list(call(*args))


def head_stats_kernel(block, tile, early, early_ref, late_ref, final_ref, wanted_ref, edge_ref, exp_ref, top_ref, sum_ref, pick_ref):
    j = pl.program_id(0)
    tokens = final_ref.shape[0]
    place = j * block + lax.broadcasted_iota(jnp.int32, (block, 1), 0)
    valid = place < edge_ref[0]
    table = jnp.where(j < early, early_ref[...], late_ref[...])

    def weigh(masked):
        for start in range(0, tokens, tile):
            at = pl.ds(start, tile)
            logits = lax.dot_general(
                table,
                final_ref[at, :],
                (((1,), (1,)), ((), ())),
                preferred_element_type=jnp.float32,
            )
            if masked:
                logits = jnp.where(valid, logits, MASKED)
            top = jnp.max(logits, axis=0, keepdims=True)
            weights = jnp.exp(logits - top)
            exp_ref[:, at] = weights.astype(jnp.bfloat16)
            top_ref[0, :, at] = top
            sum_ref[0, :, at] = jnp.sum(weights, axis=0, keepdims=True)
            pick_ref[0, :, at] = jnp.sum(
                jnp.where(place == wanted_ref[:, at], logits, 0.0), axis=0, keepdims=True
            )

    whole = (j + 1) * block <= edge_ref[0]

    @pl.when(whole)
    def _():
        weigh(False)

    @pl.when(jnp.logical_not(whole))
    def _():
        weigh(True)


def head_stats(tables, final, wanted, edge, block, tile=512):
    early = tables[0].shape[0] // block
    rows = sum(table.shape[0] for table in tables)
    width = tables[0].shape[1]
    tokens = final.shape[0]
    steps = rows // block
    row = jax.ShapeDtypeStruct((steps, 1, tokens), jnp.float32)
    row_spec = pl.BlockSpec((1, 1, tokens), lambda j: (j, 0, 0))
    return pl.pallas_call(
        functools.partial(head_stats_kernel, block, tile, early),
        grid=(steps,),
        out_shape=[jax.ShapeDtypeStruct((steps * block, tokens), jnp.bfloat16), row, row, row],
        in_specs=[
            pl.BlockSpec((block, width), lambda j: (jnp.minimum(j, early - 1), 0)),
            pl.BlockSpec((block, width), lambda j: (jnp.maximum(j - early, 0), 0)),
            pl.BlockSpec((tokens, width), lambda j: (0, 0)),
            pl.BlockSpec((1, tokens), lambda j: (0, 0)),
            pl.BlockSpec(memory_space=pltpu.SMEM),
        ],
        out_specs=[pl.BlockSpec((block, tokens), lambda j: (j, 0)), row_spec, row_spec, row_spec],
        compiler_params=pltpu.CompilerParams(vmem_limit_bytes=56 * 2**20),
        cost_estimate=pl.CostEstimate(
            flops=2 * rows * width * tokens,
            bytes_accessed=2 * rows * (width + tokens),
            transcendentals=rows * tokens,
        ),
        name="head_stats",
    )(*tables, final, wanted, edge)


def head_back_kernel(block, tile, exp_ref, final_ref, scale_ref, weight_ref, wanted_ref, dl_ref, grad_ref):
    j = pl.program_id(0)
    tokens = final_ref.shape[0]
    place = j * block + lax.broadcasted_iota(jnp.int32, (block, 1), 0)
    for start in range(0, tokens, tile):
        at = pl.ds(start, tile)
        dl = exp_ref[:, at].astype(jnp.float32) * scale_ref[0, :, at]
        dl = dl - jnp.where(place == wanted_ref[:, at], weight_ref[:, at], 0.0)
        dl_ref[:, at] = dl.astype(jnp.bfloat16)
    strip = block // max(1, block // 256)
    for start in range(0, block, strip):
        at = pl.ds(start, strip)
        grad_ref[at, :] = jnp.dot(
            dl_ref[at, :], final_ref[...], preferred_element_type=jnp.float32
        ).astype(jnp.bfloat16)


def head_back(exps, final, scale, weight, wanted, block, tile=256):
    rows, tokens = exps.shape
    width = final.shape[1]
    return pl.pallas_call(
        functools.partial(head_back_kernel, block, tile),
        grid=(rows // block,),
        out_shape=[
            jax.ShapeDtypeStruct((rows, tokens), jnp.bfloat16),
            jax.ShapeDtypeStruct((rows, width), jnp.bfloat16),
        ],
        in_specs=[
            pl.BlockSpec((block, tokens), lambda j: (j, 0)),
            pl.BlockSpec((tokens, width), lambda j: (0, 0)),
            pl.BlockSpec((1, 1, tokens), lambda j: (j, 0, 0)),
            pl.BlockSpec((1, tokens), lambda j: (0, 0)),
            pl.BlockSpec((1, tokens), lambda j: (0, 0)),
        ],
        out_specs=[
            pl.BlockSpec((block, tokens), lambda j: (j, 0)),
            pl.BlockSpec((block, width), lambda j: (j, 0)),
        ],
        compiler_params=pltpu.CompilerParams(vmem_limit_bytes=56 * 2**20),
        cost_estimate=pl.CostEstimate(
            flops=2 * rows * width * tokens,
            bytes_accessed=2 * rows * (width + 2 * tokens),
            transcendentals=0,
        ),
        name="head_back",
    )(exps, final, scale, weight, wanted)


def head_weights(mixed_ref, starts_ref, base, at, seen):
    query = mixed_ref[at : at + QUERIES, base : base + HD]
    keys = mixed_ref[0:seen, base + HD : base + 2 * HD]
    values = mixed_ref[0:seen, base + 2 * HD : base + 3 * HD]
    scores = lax.dot_general(
        query, keys, (((1,), (1,)), ((), ())), preferred_element_type=jnp.float32
    )
    row = at + lax.broadcasted_iota(jnp.int32, (QUERIES, seen), 0)
    column = lax.broadcasted_iota(jnp.int32, (QUERIES, seen), 1)
    allowed = (column <= row) & (column >= starts_ref[at : at + QUERIES, :])
    scores = jnp.where(allowed, scores * HD ** (-0.5), MASKED)
    weights = jnp.exp(scores - jnp.max(scores, axis=1, keepdims=True))
    probs = weights / jnp.sum(weights, axis=1, keepdims=True)
    return query, keys, values, probs


def attend_kernel(mixed_ref, starts_ref, out_ref):
    length = mixed_ref.shape[0]
    for at in range(0, length, QUERIES):
        found = []
        for head in range(2):
            unused, unused, values, probs = head_weights(
                mixed_ref, starts_ref, head * 3 * HD, at, at + QUERIES
            )
            found.append(
                jnp.dot(probs.astype(jnp.bfloat16), values, preferred_element_type=jnp.float32)
            )
        out_ref[at : at + QUERIES, :] = jnp.concatenate(found, axis=1).astype(jnp.bfloat16)


def attend(mixed, starts):
    length, columns = mixed.shape
    pairs = columns // (6 * HD)
    return pl.pallas_call(
        attend_kernel,
        grid=(pairs,),
        out_shape=jax.ShapeDtypeStruct((length, pairs * 2 * HD), jnp.bfloat16),
        in_specs=[
            pl.BlockSpec((length, 6 * HD), lambda j: (0, j)),
            pl.BlockSpec((length, 1), lambda j: (0, 0)),
        ],
        out_specs=pl.BlockSpec((length, 2 * HD), lambda j: (0, j)),
        compiler_params=pltpu.CompilerParams(vmem_limit_bytes=40 * 2**20),
        cost_estimate=pl.CostEstimate(
            flops=8 * pairs * length * length * HD,
            bytes_accessed=2 * length * columns,
            transcendentals=pairs * length * length,
        ),
        name="attend",
    )(mixed, starts)


def attend_back_kernel(mixed_ref, starts_ref, upstream_ref, out_ref, sums_ref):
    length = mixed_ref.shape[0]
    sums_ref[...] = jnp.zeros_like(sums_ref)
    rows = (((0,), (0,)), ((), ()))
    for at in range(0, length, QUERIES):
        seen = at + QUERIES
        for head in range(2):
            base = head * 3 * HD
            query, keys, values, probs = head_weights(mixed_ref, starts_ref, base, at, seen)
            upstream = upstream_ref[at:seen, head * HD : head * HD + HD]
            dprobs = lax.dot_general(
                upstream, values, (((1,), (1,)), ((), ())), preferred_element_type=jnp.float32
            )
            inner = jnp.sum(probs * dprobs, axis=1, keepdims=True)
            dscores = (probs * (dprobs - inner)).astype(jnp.bfloat16)
            dquery = jnp.dot(dscores, keys, preferred_element_type=jnp.float32)
            dkeys = lax.dot_general(dscores, query, rows, preferred_element_type=jnp.float32)
            dvalues = lax.dot_general(
                probs.astype(jnp.bfloat16), upstream, rows, preferred_element_type=jnp.float32
            )
            sums_ref[at:seen, base : base + HD] = dquery * HD ** (-0.5)
            sums_ref[0:seen, base + HD : base + 2 * HD] += dkeys * HD ** (-0.5)
            sums_ref[0:seen, base + 2 * HD : base + 3 * HD] += dvalues
    out_ref[...] = sums_ref[...].astype(jnp.bfloat16)


def attend_back(mixed, starts, upstream):
    length, columns = mixed.shape
    pairs = columns // (6 * HD)
    return pl.pallas_call(
        attend_back_kernel,
        grid=(pairs,),
        out_shape=jax.ShapeDtypeStruct((length, columns), jnp.bfloat16),
        in_specs=[
            pl.BlockSpec((length, 6 * HD), lambda j: (0, j)),
            pl.BlockSpec((length, 1), lambda j: (0, 0)),
            pl.BlockSpec((length, 2 * HD), lambda j: (0, j)),
        ],
        out_specs=pl.BlockSpec((length, 6 * HD), lambda j: (0, j)),
        scratch_shapes=[pltpu.VMEM((length, 6 * HD), jnp.float32)],
        compiler_params=pltpu.CompilerParams(vmem_limit_bytes=40 * 2**20),
        cost_estimate=pl.CostEstimate(
            flops=20 * pairs * length * length * HD,
            bytes_accessed=4 * length * columns,
            transcendentals=pairs * length * length,
        ),
        name="attend_back",
    )(mixed, starts, upstream)


def small_gather_kernel(axis, count, src_ref, out_ref, send, recv):
    dp = lax.axis_index("dp")
    mp = lax.axis_index("mp")
    me = dp if axis == "dp" else mp

    def device(peer):
        return (peer, mp) if axis == "dp" else (dp, peer)

    barrier = pltpu.get_barrier_semaphore()
    for hop in range(1, count):
        pl.semaphore_signal(
            barrier, inc=1, device_id=device(lax.rem(me + hop, count)), device_id_type=MESH
        )
    pl.semaphore_wait(barrier, count - 1)
    copies = []
    for hop in range(1, count):
        peer = lax.rem(me + hop, count)
        copy = pltpu.make_async_remote_copy(
            src_ref=src_ref,
            dst_ref=out_ref.at[me],
            send_sem=send.at[hop],
            recv_sem=recv.at[hop],
            device_id=device(peer),
            device_id_type=MESH,
        )
        copy.start()
        copies.append(copy)
    out_ref[me] = src_ref[...]
    for copy in copies:
        copy.wait()


def small_gather(name, cid, values, axis):
    count = lax.axis_size(axis)
    vmem = pl.BlockSpec(memory_space=pltpu.VMEM)
    return pl.pallas_call(
        functools.partial(small_gather_kernel, axis, count),
        out_shape=jax.ShapeDtypeStruct((count,) + values.shape, values.dtype),
        in_specs=[vmem],
        out_specs=vmem,
        scratch_shapes=[pltpu.SemaphoreType.DMA((count,)), pltpu.SemaphoreType.DMA((count,))],
        compiler_params=pltpu.CompilerParams(collective_id=cid, has_side_effects=True),
        cost_estimate=cost_of(6),
        name=name,
    )(values)


def exchange(axis, me, here, source, slots, send, recv, first):
    count = slots.shape[0]
    copies = []
    for hop in range(1, count):
        peer = lax.rem(me + hop, count)
        copy = pltpu.make_async_remote_copy(
            src_ref=source,
            dst_ref=slots.at[me],
            send_sem=send.at[first + hop],
            recv_sem=recv.at[first + hop],
            device_id=(peer, here) if axis == "dp" else (here, peer),
            device_id_type=MESH,
        )
        copy.start()
        copies.append(copy)
    slots[me] = source[...]
    for copy in copies:
        copy.wait()
    total = slots[0]
    for index in range(1, count):
        total = total + slots[index]
    return total


def greet_all(dp, mp, size_dp, size_mp):
    barrier = pltpu.get_barrier_semaphore()
    for hop in range(1, size_dp):
        pl.semaphore_signal(
            barrier, inc=1, device_id=(lax.rem(dp + hop, size_dp), mp), device_id_type=MESH
        )
    for hop in range(1, size_mp):
        pl.semaphore_signal(
            barrier, inc=1, device_id=(dp, lax.rem(mp + hop, size_mp)), device_id_type=MESH
        )
    pl.semaphore_wait(barrier, size_dp + size_mp - 2)


def lane_rows(values):
    values = values.reshape(-1)
    return jnp.pad(values, (0, -values.size % 128)).reshape(-1, 128)


def fold(values):
    return jnp.sum(values, axis=0, keepdims=True)


def stats_kernel(full, size_dp, size_mp, *refs):
    row_part, row_old, col_part, col_old, weight_sq = (refs[5 * n : 5 * n + 5] for n in range(5))
    loss_part, norm_one, norm_two, norm_three = refs[25:29]
    refs = refs[29:]
    row_out, col_out = refs[0:5], refs[5:10]
    loss_out, part_out, rate_out = refs[10:13]
    send_dp, slots_dp, send_mp, slots_mp, parts, part_slots, send, recv = refs[13:]
    dp = lax.axis_index("dp")
    mp = lax.axis_index("mp")
    greet_all(dp, mp, size_dp, size_mp)
    beta = 1.0 - STEP ** (-0.8)
    width = norm_one.shape[1]

    at = 0
    marks = []

    def put(values):
        nonlocal at
        rows = values.shape[0]
        send_dp[at : at + rows, :] = values
        marks.append((at, rows))
        at += rows

    norm_rows = width // 128
    for ref in (norm_one, norm_two, norm_three):
        for which in range(2):
            for piece in range(norm_rows):
                put(ref[which : which + 1, piece * 128 : piece * 128 + 128])
    marks.clear()
    count_norm = at
    for index in (0, 2, 4):
        put(row_part[index][...])
    for index in (1, 3):
        put(col_part[index][...])
    put(loss_part[...])
    for index in (1, 3):
        put(fold(row_old[index][...]))
    for index in range(5):
        put(fold(weight_sq[index][...]))
    if at < send_dp.shape[0]:
        send_dp[at:, :] = jnp.zeros((send_dp.shape[0] - at, 128), jnp.float32)
    over_dp = exchange("dp", dp, mp, send_dp, slots_dp, send, recv, 0)
    taken = [over_dp[start : start + rows] for start, rows in marks]
    loss_row = taken[5]
    row_full = {0: taken[0], 2: taken[1], 4: taken[2]}
    col_full = {1: taken[3], 3: taken[4]}
    old_total = {1: taken[6], 3: taken[7]}
    weight_rows = taken[8:13]

    at = 0
    marks = []

    def put_mp(values):
        nonlocal at
        rows = values.shape[0]
        send_mp[at : at + rows, :] = values
        marks.append((at, rows))
        at += rows

    for index in (0, 2, 4):
        put_mp(col_part[index][...])
    for index in (1, 3):
        put_mp(row_part[index][...])
    for index in range(5):
        put_mp(fold(row_full[index] if index in row_full else col_full[index]))
    for index in (0, 2, 4):
        put_mp(fold(row_old[index][...]))
    for index in range(5):
        put_mp(weight_rows[index])
    put_mp(loss_row)
    if at < send_mp.shape[0]:
        send_mp[at:, :] = jnp.zeros((send_mp.shape[0] - at, 128), jnp.float32)
    each = count_norm // size_mp
    for index in range(size_mp):
        parts[index] = over_dp[index * each : index * each + each]
    first = size_dp + size_mp
    copies = []
    for hop in range(1, size_mp):
        peer = lax.rem(mp + hop, size_mp)
        copy = pltpu.make_async_remote_copy(
            src_ref=parts.at[peer],
            dst_ref=part_slots.at[mp],
            send_sem=send.at[first + hop],
            recv_sem=recv.at[first + hop],
            device_id=(dp, peer),
            device_id_type=MESH,
        )
        copy.start()
        copies.append(copy)
    part_slots[mp] = parts[mp]
    over_mp = exchange("mp", mp, dp, send_mp, slots_mp, send, recv, size_dp)
    for copy in copies:
        copy.wait()
    summed = part_slots[0]
    for index in range(1, size_mp):
        summed = summed + part_slots[index]
    part_out[...] = summed
    taken = [over_mp[start : start + rows] for start, rows in marks]
    for slot, index in enumerate((0, 2, 4)):
        col_full[index] = taken[slot]
        old_total[index] = taken[10 + slot]
    for slot, index in enumerate((1, 3)):
        row_full[index] = taken[3 + slot]
    square_total = taken[5:10]
    weight_total = taken[13:18]
    loss_out[...] = taken[18]
    for index in range(5):
        full_rows, full_cols = full[index]
        row_new = beta * row_old[index][...] + (1.0 - beta) * row_full[index] / full_cols
        col_new = beta * col_old[index][...] + (1.0 - beta) * col_full[index] / full_rows
        row_out[index][...] = row_new
        col_out[index][...] = col_new
        mean = (
            beta * jnp.sum(old_total[index], axis=1, keepdims=True)
            + (1.0 - beta) * jnp.sum(square_total[index], axis=1, keepdims=True) / full_cols
        ) / full_rows
        rate = RHO * jnp.sqrt(
            jnp.sum(weight_total[index], axis=1, keepdims=True) / (full_rows * full_cols)
        )
        rate_out[index : index + 1, :] = jnp.broadcast_to(mean, (1, 128))
        rate_out[8 + index : 9 + index, :] = jnp.broadcast_to(rate, (1, 128))


def update_stats(cid, row_parts, rows_old, col_parts, cols_old, weight_sq, loss, norm_parts, full):
    size_dp = lax.axis_size("dp")
    size_mp = lax.axis_size("mp")
    f32 = jnp.float32
    rows_old2 = [lane_rows(v) for v in rows_old]
    cols_old2 = [lane_rows(v) for v in cols_old]
    args = (
        [lane_rows(v) for v in row_parts]
        + rows_old2
        + [lane_rows(v) for v in col_parts]
        + cols_old2
        + [v if v.ndim == 2 else lane_rows(v) for v in weight_sq]
        + [lane_rows(loss)]
        + list(norm_parts)
    )
    width = norm_parts[0].shape[1]
    count_norm = 6 * width // 128
    size_a = count_norm + sum(rows_old2[n].shape[0] for n in (0, 2, 4))
    size_a += sum(cols_old2[n].shape[0] for n in (1, 3)) + 8
    size_a += -size_a % 8
    size_b = sum(cols_old2[n].shape[0] for n in (0, 2, 4))
    size_b += sum(rows_old2[n].shape[0] for n in (1, 3)) + 14
    size_b += -size_b % 8
    each = count_norm // size_mp
    out_shape = [jax.ShapeDtypeStruct(v.shape, f32) for v in rows_old2 + cols_old2]
    out_shape += [
        jax.ShapeDtypeStruct((1, 128), f32),
        jax.ShapeDtypeStruct((each, 128), f32),
        jax.ShapeDtypeStruct((16, 128), f32),
    ]
    sems = size_dp + 2 * size_mp
    vmem = pl.BlockSpec(memory_space=pltpu.VMEM)
    found = pl.pallas_call(
        functools.partial(stats_kernel, full, size_dp, size_mp),
        out_shape=out_shape,
        in_specs=[vmem] * len(args),
        out_specs=[vmem] * len(out_shape),
        scratch_shapes=[
            pltpu.VMEM((size_a, 128), f32),
            pltpu.VMEM((size_dp, size_a, 128), f32),
            pltpu.VMEM((size_b, 128), f32),
            pltpu.VMEM((size_mp, size_b, 128), f32),
            pltpu.VMEM((size_mp, each, 128), f32),
            pltpu.VMEM((size_mp, each, 128), f32),
            pltpu.SemaphoreType.DMA((sems,)),
            pltpu.SemaphoreType.DMA((sems,)),
        ],
        compiler_params=pltpu.CompilerParams(collective_id=cid, has_side_effects=True),
        cost_estimate=cost_of(12),
        name="update_stats",
    )(*args)
    rows_new = [found[n].reshape(-1)[: rows_old[n].size] for n in range(5)]
    cols_new = [found[5 + n].reshape(-1)[: cols_old[n].size] for n in range(5)]
    loss_sums = found[10][0, :NSRC]
    return rows_new, cols_new, loss_sums, found[11], found[12]


def clip_kernel(entries, size_dp, size_mp, *refs):
    parts, rate, part, norms, second_old = refs[:5], *refs[5:9]
    out, grads_out, second_out, norms_out = refs[9:13]
    mine, slots_dp, slots_mp, whole, send, recv = refs[13:]
    dp = lax.axis_index("dp")
    mp = lax.axis_index("mp")
    greet_all(dp, mp, size_dp, size_mp)
    first = size_dp + size_mp
    copies = []
    for hop in range(1, size_mp):
        copy = pltpu.make_async_remote_copy(
            src_ref=part,
            dst_ref=whole.at[mp],
            send_sem=send.at[first + hop],
            recv_sem=recv.at[first + hop],
            device_id=(dp, lax.rem(mp + hop, size_mp)),
            device_id_type=MESH,
        )
        copy.start()
        copies.append(copy)
    whole[mp] = part[...]
    mine[...] = jnp.zeros_like(mine)
    for index in range(5):
        mine[index : index + 1, :] = fold(parts[index][...])
    over_dp = exchange("dp", dp, mp, mine, slots_dp, send, recv, 0)
    mine[...] = over_dp
    total = exchange("mp", mp, dp, mine, slots_mp, send, recv, size_dp)
    total = jnp.sum(total, axis=1, keepdims=True)
    for index in range(5):
        clip = jnp.maximum(1.0, jnp.sqrt(total[index : index + 1] / entries[index]) / CLIP)
        out[index : index + 1, :] = rate[8 + index : 9 + index, :] / clip
    for copy in copies:
        copy.wait()
    beta = 1.0 - STEP ** (-0.8)
    each = part.shape[0]
    norm_rows = norms.shape[1] // 128
    for row in range(6):
        for piece in range(norm_rows):
            place = row * norm_rows + piece
            grads_out[row : row + 1, piece * 128 : piece * 128 + 128] = whole[
                place // each, place % each : place % each + 1, :
            ]
    grad = grads_out[...]
    second = beta * second_old[...] + (1.0 - beta) * (grad * grad + EPS_ONE)
    second_out[...] = second
    step = grad * lax.rsqrt(second)
    entries = step.size

    def mean_square(values):
        return jnp.sum(jnp.sum(values * values, axis=0, keepdims=True), axis=1, keepdims=True) / (
            entries
        )

    step = step / jnp.maximum(1.0, jnp.sqrt(mean_square(step)) / CLIP)
    old = norms[...]
    norms_out[...] = old - RHO * jnp.sqrt(mean_square(old)) * step


def clip_rates(cid, step_parts, rate, part, norms, second, entries):
    size_dp = lax.axis_size("dp")
    size_mp = lax.axis_size("mp")
    vmem = pl.BlockSpec(memory_space=pltpu.VMEM)
    sems = size_dp + 2 * size_mp
    norm_type = jax.ShapeDtypeStruct(norms.shape, jnp.float32)
    return pl.pallas_call(
        functools.partial(clip_kernel, entries, size_dp, size_mp),
        out_shape=[jax.ShapeDtypeStruct((8, 128), jnp.float32)] + [norm_type] * 3,
        in_specs=[vmem] * 9,
        out_specs=[vmem] * 4,
        scratch_shapes=[
            pltpu.VMEM((8, 128), jnp.float32),
            pltpu.VMEM((size_dp, 8, 128), jnp.float32),
            pltpu.VMEM((size_mp, 8, 128), jnp.float32),
            pltpu.VMEM((size_mp, *part.shape), jnp.float32),
            pltpu.SemaphoreType.DMA((sems,)),
            pltpu.SemaphoreType.DMA((sems,)),
        ],
        compiler_params=pltpu.CompilerParams(collective_id=cid, has_side_effects=True),
        cost_estimate=cost_of(8),
        name="clip_rates",
    )(*[lane_rows(v) for v in step_parts], rate, part, norms, second)


UNROLL = 16


def lookup_kernel(shift, early, count_ref, key_ref, table_ref, out_ref, low_ref, square_ref, rows_ref):
    spots = out_ref.shape[0]
    vocab, width = table_ref.shape
    rows_ref[...] = jnp.zeros_like(rows_ref)

    def some(i, carry):
        for j in range(UNROLL):
            key = key_ref[i * UNROLL + j]
            place = key & ((1 << shift) - 1)
            rows_ref[pl.ds(place, 1), :] = table_ref[pl.ds(key >> shift, 1), :]
        return carry

    lax.fori_loop(0, (count_ref[0] + UNROLL - 1) // UNROLL, some, 0)

    def narrow(i, carry):
        at = pl.ds(pl.multiple_of(i * 256, 256), 256)
        out_ref[at, :] = rows_ref[at, :].astype(jnp.bfloat16)
        return carry

    lax.fori_loop(0, spots // 256, narrow, 0)
    strip = 64
    rest = vocab % strip
    done = vocab - rest
    low_ref[done - early :, :] = jnp.zeros(
        (low_ref.shape[0] - done + early, width), jnp.bfloat16
    )

    def squares(values, total):
        for row in range(0, values.shape[0], 8):
            piece = values[row : row + 8, :]
            total = total + piece * piece
        return total

    def lower(i, total):
        at = pl.ds(pl.multiple_of(i * strip, strip), strip)
        values = table_ref[at, :]
        start = pl.multiple_of(i * strip - early, strip)
        low_ref[pl.ds(start, strip), :] = values.astype(jnp.bfloat16)
        return squares(values, total)

    def square(i, total):
        at = pl.ds(pl.multiple_of(i * strip, strip), strip)
        return squares(table_ref[at, :], total)

    total = jnp.zeros((8, width), jnp.float32)
    total = lax.fori_loop(0, early // strip, square, total)
    total = lax.fori_loop(early // strip, done // strip, lower, total)
    if rest:
        values = table_ref[done:, :]
        total = squares(values, total)
        values = jnp.concatenate([values, jnp.zeros((strip - rest, width), jnp.float32)])
        low_ref[done - early : done - early + strip, :] = values.astype(jnp.bfloat16)
    folded = total[:, 0:128]
    for start in range(128, width, 128):
        folded = folded + total[:, start : start + 128]
    square_ref[...] = folded


def lookup(keys, count, table, spots, shift, early):
    vocab, width = table.shape
    smem = pl.BlockSpec(memory_space=pltpu.SMEM)
    vmem = pl.BlockSpec(memory_space=pltpu.VMEM)
    return pl.pallas_call(
        functools.partial(lookup_kernel, shift, early),
        out_shape=[
            jax.ShapeDtypeStruct((spots, width), jnp.bfloat16),
            jax.ShapeDtypeStruct((vocab + -vocab % HEAD_BLOCK - early, width), jnp.bfloat16),
            jax.ShapeDtypeStruct((8, 128), jnp.float32),
        ],
        in_specs=[smem, smem, vmem],
        out_specs=[vmem] * 3,
        scratch_shapes=[pltpu.VMEM((spots + 8, width), jnp.float32)],
        compiler_params=pltpu.CompilerParams(vmem_limit_bytes=VMEM_CAP),
        cost_estimate=cost_of(20),
        name="lookup",
    )(count, keys, table)


def scatter_kernel(shift, count_ref, key_ref, head_ref, rows_in_ref, grad_ref, rows_ref):
    spots = rows_in_ref.shape[0]
    width = grad_ref.shape[1]

    def widen(i, carry):
        at = pl.ds(pl.multiple_of(i * 256, 256), 256)
        rows_ref[at, :] = rows_in_ref[at, :].astype(jnp.float32)
        return carry

    lax.fori_loop(0, spots // 256, widen, 0)
    rows_ref[spots:, :] = jnp.zeros((8, width), jnp.float32)
    grad_ref[...] = head_ref[...].astype(jnp.float32)[: grad_ref.shape[0]]

    def some(i, carry):
        for j in range(UNROLL):
            key = key_ref[i * UNROLL + j]
            place = key & ((1 << shift) - 1)
            grad_ref[pl.ds(key >> shift, 1), :] += rows_ref[pl.ds(place, 1), :]
        return carry

    lax.fori_loop(0, (count_ref[0] + UNROLL - 1) // UNROLL, some, 0)


def scatter(keys, count, head_grad, rows, vocab, shift):
    spots, width = rows.shape
    smem = pl.BlockSpec(memory_space=pltpu.SMEM)
    vmem = pl.BlockSpec(memory_space=pltpu.VMEM)
    return pl.pallas_call(
        functools.partial(scatter_kernel, shift),
        out_shape=jax.ShapeDtypeStruct((vocab, width), jnp.float32),
        in_specs=[smem, smem, vmem, vmem],
        out_specs=vmem,
        scratch_shapes=[pltpu.VMEM((spots + 8, width), jnp.float32)],
        compiler_params=pltpu.CompilerParams(vmem_limit_bytes=VMEM_CAP),
        cost_estimate=cost_of(23),
        name="scatter",
    )(count, keys, head_grad, rows)


def norm_parts(values):
    centre = jnp.mean(values, axis=-1, keepdims=True)
    centred = values - centre
    scale = lax.rsqrt(jnp.mean(centred * centred, axis=-1, keepdims=True) + EPS_NORM)
    return centred * scale, scale


def norm_pull(values, gain, upstream):
    normed, scale = norm_parts(values)
    weighted = upstream * gain
    pulled = scale * (
        weighted
        - jnp.mean(weighted, axis=-1, keepdims=True)
        - normed * jnp.mean(weighted * normed, axis=-1, keepdims=True)
    )
    return (
        pulled,
        jnp.sum(upstream * normed, axis=0, keepdims=True),
        jnp.sum(upstream, axis=0, keepdims=True),
    )


def step_first(total, at, ins, outs):
    stream, norms = outs[0], ins[0]
    normed, scale = norm_parts(stream[at, :].astype(jnp.float32))
    return normed * norms[0:1, :] + norms[1:2, :]


def step_forward(row, total, at, ins, outs):
    stream, norms = ins
    values = stream[at, :].astype(jnp.float32) + total
    outs[0][at, :] = values
    normed, scale = norm_parts(values)
    return normed * norms[row : row + 1, :] + norms[row + 1 : row + 2, :]


def step_backward(row, total, at, ins, outs):
    stream, norms = ins[:2]
    pulled, dgain, dshift = norm_pull(
        stream[at, :].astype(jnp.float32), norms[row : row + 1, :], total
    )
    if len(ins) > 2:
        pulled = pulled + ins[2][at, :]
    if len(outs) > 1:
        outs[0][at, :] = pulled
    sums = outs[-1]

    @pl.when(at.start == 0)
    def _():
        sums[...] = jnp.zeros_like(sums)

    sums[0:1, :] += dgain
    sums[1:2, :] += dshift
    return pulled


def gelu_tanh(values):
    return jax.nn.gelu(values, approximate=True)


def local(
    token_ids,
    targets,
    starts,
    sources,
    embedding,
    w_qkv,
    w_out,
    w_fc,
    w_proj,
    norm_params,
    rows_table,
    cols_table,
    rows_qkv,
    cols_qkv,
    rows_out,
    cols_out,
    rows_fc,
    cols_fc,
    rows_proj,
    cols_proj,
    second_norms,
):
    bf16 = jnp.bfloat16
    f32 = jnp.float32
    size_mp = lax.axis_size("mp")
    size_dp = lax.axis_size("dp")
    dp = lax.axis_index("dp")
    mp = lax.axis_index("mp")
    tokens = token_ids.shape[0]
    seqs = tokens // LEN
    chips = size_mp // 2
    near = chips // seqs
    sharers = size_mp // seqs
    rows = tokens // size_mp
    vocab, part_width = embedding.shape
    width = part_width * size_dp
    first_row = mp * vocab
    spots = tokens * size_dp
    chunks_full = max(1, min(4, rows // 32))
    chunks_near = max(1, min(4, rows // 32))
    chunks_turn = max(1, min(4, rows // 32))

    def own_and_twins(weights, axis):
        low = [weight.astype(bf16) for weight in weights]
        found = [[weight] for weight in low]
        sent = jnp.concatenate(low, axis=axis)
        for turn in range(1, seqs):
            shift = [(i, (i + turn * sharers) % size_mp) for i in range(size_mp)]
            arrived = lax.ppermute(sent, "mp", shift)
            start = 0
            for index, weight in enumerate(low):
                size = weight.shape[axis]
                found[index].append(lax.slice_in_dim(arrived, start, start + size, axis=axis))
                start += size
        return [jnp.concatenate(pieces, axis=axis) for pieces in found]

    pair_fc, pair_qkv = own_and_twins((w_fc, w_qkv), 1)
    pair_proj, pair_out = own_and_twins((w_proj, w_out), 0)

    early = (vocab + -vocab % HEAD_BLOCK) * 2 // (10 * HEAD_BLOCK) * HEAD_BLOCK
    early_table = lax.all_gather(embedding[:early].astype(bf16), "dp", axis=1, tiled=True)

    both = jnp.stack([token_ids, sources]).reshape(-1, 128)
    both = small_gather("gather_ids", 0, both, "dp").reshape(size_dp, 2, tokens)
    all_ids = both[:, 0]
    all_sources = both[:, 1].reshape(-1)
    counts = jnp.sum(
        (all_sources[:, None] == jnp.arange(NSRC, dtype=jnp.int32)[None, :]).astype(f32), axis=0
    )

    piece = rows // chunks_turn
    token = jnp.arange(tokens, dtype=jnp.int32)
    place = (
        token // piece * (size_dp * piece)
        + (jnp.arange(size_dp, dtype=jnp.int32) * piece)[:, None]
        + token % piece
    )
    local_ids = all_ids - first_row
    inside = (local_ids >= 0) & (local_ids < vocab)
    shift = spots.bit_length()
    idle = ((vocab - 1) << shift) + spots
    keys = jnp.where(inside, (local_ids << shift) + place, idle)
    keys = jnp.sort(keys.reshape(-1))
    owned = jnp.sum(inside.astype(jnp.int32)).reshape(1)
    found, low_table, table_sq = lookup(keys, owned, embedding, spots, shift, early)
    found, early_table = lax.optimization_barrier((found, early_table))
    inner_one, stream0, wide_qkv, wide_out, wide_fc, wide_proj = line_call(
        "lookup_sum",
        1,
        found,
        [norm_params],
        [jax.ShapeDtypeStruct((rows, width), bf16)],
        step_first,
        size_dp * rows,
        part_width,
        chunks_turn,
        chips,
        near,
        70,
        [
            ("gather", 0, pair_qkv),
            ("gather", 1, pair_out),
            ("gather", 0, pair_fc),
            ("gather", 1, pair_proj),
        ],
        "gather",
        8,
    )
    low_table, inner_one = lax.optimization_barrier((low_table, inner_one))
    wide_table = (early_table, lax.all_gather(low_table, "dp", axis=1, tiled=True))
    row_f32 = jax.ShapeDtypeStruct((rows, width), f32)
    pair_f32 = jax.ShapeDtypeStruct((8, width), f32)
    my_starts = row_slice(starts, (mp // sharers) * LEN, LEN)[:, None]
    mixed = jnp.dot(inner_one, wide_qkv, preferred_element_type=f32).astype(bf16)
    attended = attend(mixed, my_starts)
    partial = jnp.dot(attended, wide_out, preferred_element_type=f32).astype(bf16)
    inner_two, stream1 = line_call(
        "attn_sum",
        3,
        partial,
        [stream0, norm_params],
        [row_f32],
        functools.partial(step_forward, 2),
        rows,
        width,
        chunks_near,
        near,
        near,
        32,
    )
    before = jnp.dot(inner_two, wide_fc, preferred_element_type=f32)
    hidden = gelu_tanh(before).astype(bf16)
    partial = jnp.dot(hidden, wide_proj, preferred_element_type=f32).astype(bf16)
    final, stream2 = line_call(
        "mlp_sum",
        4,
        partial,
        [stream1, norm_params],
        [row_f32],
        functools.partial(step_forward, 4),
        rows,
        width,
        chunks_full,
        near,
        chips,
        58,
        chunk_major=True,
    )

    edge = jnp.clip(VREAL - first_row, 0, vocab).astype(jnp.int32).reshape(1)

    def by_chunk(values):
        return values.reshape(size_mp, chunks_full, -1).swapaxes(0, 1).reshape(tokens)

    sources = by_chunk(sources)
    wanted = by_chunk(targets) - first_row
    wanted = jnp.where((wanted >= 0) & (wanted < vocab), wanted, -1).reshape(1, tokens)
    block = HEAD_BLOCK
    exps, tops, sums, picks = head_stats(wide_table, final, wanted, edge, block)
    tops = tops[:, 0]
    top = jnp.max(tops, axis=0)
    total = jnp.sum(sums[:, 0] * jnp.exp(tops - top[None, :]), axis=0)
    pick = jnp.sum(picks[:, 0], axis=0)
    stats = jnp.concatenate([v.reshape(-1, 128) for v in (top, total)])
    stats = small_gather("gather_stats", 5, stats, "mp").reshape(size_mp, 2, tokens)
    highest = jnp.max(stats[:, 0], axis=0)
    log_total = highest + jnp.log(
        jnp.sum(stats[:, 1] * jnp.exp(stats[:, 0] - highest[None, :]), axis=0)
    )
    token_loss = jnp.where(mp == 0, log_total, 0.0) - pick
    member = (sources[:, None] == jnp.arange(NSRC, dtype=jnp.int32)[None, :]).astype(f32)
    loss_part = jnp.sum(member * token_loss[:, None], axis=0)
    weight = jnp.sum(member / (NSRC * jnp.maximum(counts, 1.0))[None, :], axis=1)
    scale = jnp.exp(tops - log_total[None, :]) * weight[None, :]
    dlogits, table_grad = head_back(
        exps, final, scale[:, None, :], weight[None, :], wanted, block
    )
    head_grad = lax.psum_scatter(table_grad, "dp", scatter_dimension=1, tiled=True)

    dbranch2, dstream2, norm3 = line_call(
        "final_back",
        6,
        (dlogits, *wide_table),
        [stream2, norm_params],
        [row_f32, pair_f32],
        functools.partial(step_backward, 4),
        rows,
        width,
        chunks_full,
        chips,
        near,
        65,
        product=True,
    )
    grad_proj = jnp.einsum("tf,td->fd", hidden, dbranch2, preferred_element_type=f32).astype(bf16)
    dhidden = jnp.einsum("td,fd->tf", dbranch2, wide_proj, preferred_element_type=f32)
    unused, gelu_pull = jax.vjp(gelu_tanh, before)
    dbefore = gelu_pull(dhidden)[0].astype(bf16)
    partial = jnp.einsum("tf,df->td", dbefore, wide_fc, preferred_element_type=f32).astype(bf16)
    dbranch1, dstream1, norm2 = line_call(
        "mlp_back",
        7,
        partial,
        [stream1, norm_params, dstream2],
        [row_f32, pair_f32],
        functools.partial(step_backward, 2),
        rows,
        width,
        chunks_near,
        near,
        near,
        34,
    )
    grad_fc = jnp.einsum("td,tf->df", inner_two, dbefore, preferred_element_type=f32).astype(bf16)
    grad_out = jnp.einsum("tf,td->fd", attended, dbranch1, preferred_element_type=f32).astype(bf16)
    dattended = jnp.einsum("td,fd->tf", dbranch1, wide_out, preferred_element_type=f32)
    dmixed = attend_back(mixed, my_starts, dattended.astype(bf16))
    partial = jnp.einsum("tc,dc->td", dmixed, wide_qkv, preferred_element_type=f32).astype(bf16)
    grad_qkv = jnp.einsum("td,tc->dc", inner_one, dmixed, preferred_element_type=f32).astype(bf16)
    drows, norm1, grad_proj, grad_out, grad_fc, grad_qkv, twins_wide, twins_tall = line_call(
        "attn_back",
        8,
        partial,
        [stream0, norm_params, dstream1],
        [pair_f32],
        functools.partial(step_backward, 0),
        rows,
        width,
        chunks_turn,
        near,
        chips,
        70,
        [
            ("scatter", 1, grad_proj),
            ("scatter", 1, grad_out),
            ("scatter", 0, grad_fc),
            ("scatter", 0, grad_qkv),
        ],
        "spread",
        9,
        seqs=seqs,
    )

    def from_twins(values, axis, sizes):
        starts = [(seqs - 1) * sum(sizes[:n]) for n in range(len(sizes))]
        found = []
        for turn in range(1, seqs):
            pieces = [
                lax.slice_in_dim(values, at + (turn - 1) * size, at + turn * size, axis=axis)
                for at, size in zip(starts, sizes)
            ]
            back = [(i, (i - turn * sharers) % size_mp) for i in range(size_mp)]
            found.append(lax.ppermute(jnp.concatenate(pieces, axis=axis), "mp", back))
        return found

    tall = [grad_proj.shape[0], grad_out.shape[0]]
    wide = [grad_fc.shape[1], grad_qkv.shape[1]]
    found_tall = from_twins(twins_tall, 0, tall)
    found_wide = from_twins(twins_wide, 1, wide)
    grad_table = scatter(keys, owned, head_grad, drows, vocab, shift)
    table_squares = grad_table * grad_table + EPS_ONE
    table_rows = jnp.sum(table_squares, axis=1)
    table_cols = jnp.sum(table_squares, axis=0)
    found_tall, found_wide, table_rows = lax.optimization_barrier(
        (found_tall, found_wide, table_rows)
    )
    for values in found_tall:
        grad_proj += values[: tall[0]].astype(f32)
        grad_out += values[tall[0] :].astype(f32)
    for values in found_wide:
        grad_fc += values[:, : wide[0]].astype(f32)
        grad_qkv += values[:, wide[0] :].astype(f32)

    weights = (embedding, w_qkv, w_out, w_fc, w_proj)
    grads = (grad_table, grad_qkv, grad_out, grad_fc, grad_proj)
    row_span = (size_mp, size_dp, size_mp, size_dp, size_mp)
    col_span = (size_dp, size_mp, size_dp, size_mp, size_dp)
    full = tuple(
        (g.shape[0] * r, g.shape[1] * c) for g, r, c in zip(grads, row_span, col_span)
    )
    squares = [gradient * gradient + EPS_ONE for gradient in grads[1:]]
    rows_new, cols_new, loss_sums, norm_part, rates = update_stats(
        10,
        [table_rows] + [jnp.sum(square, axis=1) for square in squares],
        (rows_table, rows_qkv, rows_out, rows_fc, rows_proj),
        [table_cols] + [jnp.sum(square, axis=0) for square in squares],
        (cols_table, cols_qkv, cols_out, cols_fc, cols_proj),
        [table_sq] + [jnp.sum(value * value, axis=0) for value in weights[1:]],
        loss_part,
        (norm1, norm2, norm3),
        full,
    )
    steps = [
        grads[n] * lax.rsqrt(rows_new[n][:, None] * cols_new[n][None, :] / rates[n, 0])
        for n in range(5)
    ]
    factors, grad_norms, second_new, norms_new = clip_rates(
        11,
        [jnp.sum(step * step, axis=0) for step in steps],
        rates,
        norm_part,
        norm_params,
        second_norms,
        [r * c for r, c in full],
    )
    updated = [weights[n] - factors[n, 0] * steps[n] for n in range(5)]
    return (
        loss_sums,
        counts,
        grad_table,
        rows_new[0],
        cols_new[0],
        updated[0],
        grad_qkv,
        rows_new[1],
        cols_new[1],
        updated[1],
        grad_out,
        rows_new[2],
        cols_new[2],
        updated[2],
        grad_fc,
        rows_new[3],
        cols_new[3],
        updated[3],
        grad_proj,
        rows_new[4],
        cols_new[4],
        updated[4],
        grad_norms,
        second_new,
        norms_new,
    )


def solution(mesh):
    placed = (
        P("dp"),
        P("dp"),
        P("dp"),
        P("dp"),
        P("mp", "dp"),
        P("dp", "mp"),
        P("mp", "dp"),
        P("dp", "mp"),
        P("mp", "dp"),
        P(),
        P("mp"),
        P("dp"),
        P("dp"),
        P("mp"),
        P("mp"),
        P("dp"),
        P("dp"),
        P("mp"),
        P("mp"),
        P("dp"),
        P(),
    )
    return jax.shard_map(
        local,
        mesh=mesh,
        in_specs=placed,
        out_specs=(
            P(),
            P(),
            P("mp", "dp"),
            P("mp"),
            P("dp"),
            P("mp", "dp"),
            P("dp", "mp"),
            P("dp"),
            P("mp"),
            P("dp", "mp"),
            P("mp", "dp"),
            P("mp"),
            P("dp"),
            P("mp", "dp"),
            P("dp", "mp"),
            P("dp"),
            P("mp"),
            P("dp", "mp"),
            P("mp", "dp"),
            P("mp"),
            P("dp"),
            P("mp", "dp"),
            P(),
            P(),
            P(),
        ),
        check_vma=False,
    )
```
